32 devices in a mesh: dp: 8 (over z, y), seq: 4 (over x, core).
Axes of the slice: x: 2, y: 2, z: 4, core: 2. Of those that a mesh axis runs over, the one named last changes fastest.
Arguments:
- tokens: bfloat16 [8, 16, 256, 768], P(None, 'seq', 'dp'), may hold values from -6 to 6
- condition: bfloat16 [8, 768], replicated, may hold values from -6 to 6
- loss_grad: bfloat16 [8, 16, 256, 768], P(None, 'seq', 'dp'), may hold values from -6 to 6
- cell_counts: int32 [8], replicated, may hold values from 64 to 256, as said below
- frame_tasks: int32 [8, 16], replicated, may hold values 0 or 1
- destinations: int32 [8], replicated, may hold values from 0 to 7, each once
- w_ada: bfloat16 [768, 6912], replicated, may hold values from -0.21875 to 0.21875
- b_ada: bfloat16 [6912], replicated, may hold values from -2 to 2
- w_qkv_s: bfloat16 [768, 2304], replicated, may hold values from -0.21875 to 0.21875
- w_out_s: bfloat16 [768, 768], replicated, may hold values from -0.875 to 0.875
- b_out_s: bfloat16 [768], replicated, may hold values from -2 to 2
- w_qkv_t: bfloat16 [768, 2304], replicated, may hold values from -0.21875 to 0.21875
- w_out_t: bfloat16 [768, 768], replicated, may hold values from -0.4375 to 0.4375
- b_out_t: bfloat16 [768], replicated, may hold values from -2 to 2
- w_up: bfloat16 [768, 3072], replicated, may hold values from -0.21875 to 0.21875
- b_up: bfloat16 [3072], replicated, may hold values from -2 to 2
- w_down: bfloat16 [3072, 768], replicated, may hold values from -0.109375 to 0.109375
- b_down: bfloat16 [768], replicated, may hold values from -2 to 2
Outputs:
- layer_out: bfloat16 [8, 16, 256, 768], P(None, 'seq', 'dp')
- grad_tokens: bfloat16 [8, 16, 256, 768], P(None, 'seq', 'dp')
- grad_w_ada: float32 [768, 6912], P('seq')
- grad_b_ada: float32 [6912], P('seq')
- grad_w_qkv_s: float32 [768, 2304], P('seq')
- grad_w_out_s: float32 [768, 768], P('seq')
- grad_b_out_s: float32 [768], P('seq')
- grad_w_qkv_t: float32 [768, 2304], P('seq')
- grad_w_out_t: float32 [768, 768], P('seq')
- grad_b_out_t: float32 [768], P('seq')
- grad_w_up: float32 [768, 3072], P('seq')
- grad_b_up: float32 [3072], P('seq')
- grad_w_down: float32 [3072, 768], P('seq')
- grad_b_down: float32 [768], P('seq')
The draws below stay inside these ranges and needn't reach their ends.
Inputs may be any that keep to these rules, and one draw needn't show every extreme that they name: `cell_counts`: each clip has 64, 128 or 256 valid cells, the first ones of its frames; some clip has 256 and some clip has 64. `destinations`: each slot of the data axis is named by exactly one clip.
All inputs are finite; a program needn't handle non-finite values.
Results may differ from the reference program's by a relative error of at most 0.02.
Values may be sent and summed in bfloat16 or wider, within the bound.
A program may use at most 256 MiB of HBM per device.

```python
import jax
import jax.numpy as jnp
from jax import lax

D = 768
HEADS = 12
HEAD = 64
FF = 3072
FRAMES = 16
CELLS = 256
CLIPS = 8


def draw_cell_counts(key, part):
    key = jax.random.fold_in(key, 11)
    level_key, pick_key = jax.random.split(key)
    levels = jax.random.randint(level_key, (CLIPS,), 0, 3)
    shuffled = jax.random.permutation(pick_key, CLIPS)
    levels = levels.at[shuffled[0]].set(2).at[shuffled[1]].set(0)
    counts = jnp.where(levels == 2, CELLS, jnp.where(levels == 1, CELLS // 2, CELLS // 4))
    return counts.astype(jnp.int32)


def touch_ends(values, rng, least, largest):
    longest = values.shape.index(max(values.shape))
    spots = []
    for shift in (0, 1):
        where = [jax.random.randint(jax.random.fold_in(rng, axis), (), 0, length) for axis, length in enumerate(values.shape)]
        where[longest] = (where[longest] + shift) % values.shape[longest]
        spots.append(tuple(where))
    return values.at[spots[0]].set(least).at[spots[1]].set(largest)


def level_of(rng, dims, cuts, least, top_value):
    factor_of = 1.0
    for dim, shards_of in cuts:
        draws = jax.random.uniform(jax.random.fold_in(jax.random.fold_in(rng, 6), dim), (shards_of,), jnp.float32, least / len(cuts), top_value / len(cuts))
        factor_of = factor_of * jnp.repeat(jnp.exp(draws), dims[dim] // shards_of).reshape((-1,) + (1,) * (len(dims) - 1 - dim))
    return factor_of


def normal_values(own_key, extent, width, limit, cuts=(), kind=jnp.bfloat16):
    array = jax.random.normal(own_key, extent, jnp.float32) * width
    if len(cuts) > 0:
        array = level_of(own_key, extent, cuts, -0.22, 0.18) * array
    return jnp.clip(array, min=-limit, max=limit).astype(kind)


def setup_inputs(seed: int = 0) -> dict:
    splits = jax.random.split(jax.random.key(seed), 19)
    tokens = normal_values(splits[0], (CLIPS, FRAMES, CELLS, D), 1.0, 6.0, ((1, 4), (2, 8)))
    condition = normal_values(splits[1], (CLIPS, D), 1.0, 6.0)
    loss_grad = normal_values(splits[2], (CLIPS, FRAMES, CELLS, D), 1.0, 6.0, ((1, 4), (2, 8)))
    cell_counts = draw_cell_counts(jax.random.fold_in(splits[18], 71), 0)
    frame_tasks = touch_ends((jax.random.randint(splits[4], (CLIPS, FRAMES), 0, 2) < 1).astype(jnp.int32), jax.random.fold_in(splits[4], 1), 0, 1)
    destinations = jax.random.permutation(splits[5], CLIPS).astype(jnp.int32)
    w_ada = normal_values(splits[6], (D, 9 * D), D ** -0.5, 0.21875)
    b_ada = normal_values(splits[7], (9 * D,), 0.3, 2.0)
    w_qkv_s = normal_values(splits[8], (D, 3 * D), D ** -0.5, 0.21875)
    w_out_s = normal_values(splits[9], (D, D), (D // 16) ** -0.5, 0.875)
    b_out_s = normal_values(splits[10], (D,), 0.3, 2.0)
    w_qkv_t = normal_values(splits[11], (D, 3 * D), D ** -0.5, 0.21875)
    w_out_t = normal_values(splits[12], (D, D), (D // 4) ** -0.5, 0.4375)
    b_out_t = normal_values(splits[13], (D,), 0.3, 2.0)
    w_up = normal_values(splits[14], (D, FF), D ** -0.5, 0.21875)
    b_up = normal_values(splits[15], (FF,), 0.3, 2.0)
    w_down = normal_values(splits[16], (FF, D), FF ** -0.5, 0.109375)
    b_down = normal_values(splits[17], (D,), 0.3, 2.0)
    return dict(tokens=tokens, condition=condition, loss_grad=loss_grad, cell_counts=cell_counts, frame_tasks=frame_tasks, destinations=destinations, w_ada=w_ada, b_ada=b_ada, w_qkv_s=w_qkv_s, w_out_s=w_out_s, b_out_s=b_out_s, w_qkv_t=w_qkv_t, w_out_t=w_out_t, b_out_t=b_out_t, w_up=w_up, b_up=b_up, w_down=w_down, b_down=b_down)


@jax.custom_vjp
def low(v):
    return lax.optimization_barrier(v.astype(jnp.bfloat16)).astype(jnp.float32)

@jax.custom_vjp
def low_back(v):
    return v

def low_keep(v):
    return (low(v), None)

def low_pass(kept, grad):
    return (grad,)

def back_keep(v):
    return (v, None)

def back_low(kept, grad):
    return (low(grad),)
low.defvjp(low_keep, low_pass)
low_back.defvjp(back_keep, back_low)
PRECISE = lax.Precision.HIGHEST

def project(inputs, weight):
    return jnp.einsum('cfpd,de->cfpe', inputs, weight, precision=PRECISE)

def standard(field):
    centred = field - lax.optimization_barrier(jnp.mean(field, axis=-1, keepdims=True))
    return centred * lax.rsqrt(lax.optimization_barrier(jnp.mean(centred * centred, axis=-1, keepdims=True)) + 1e-06)

def softmax_rows(scores):
    row_top = lax.optimization_barrier(jnp.max(scores, axis=-1, keepdims=True))
    exponent = jnp.exp(scores - row_top)
    return exponent / lax.optimization_barrier(jnp.sum(exponent, axis=-1, keepdims=True))

def attend_space(normed_in, w_qkv, key_valid):
    clip_count, frame_count, cell_count = (normed_in.shape[0], normed_in.shape[1], normed_in.shape[2])
    triple = low_back(low(project(normed_in, w_qkv))).reshape(clip_count, frame_count, cell_count, 3, HEADS, HEAD)
    queries = triple[:, :, :, 0]
    key_rows = triple[:, :, :, 1]
    value_rows = triple[:, :, :, 2]
    scores = low_back(jnp.einsum('cfphe,cfqhe->cfhpq', queries, key_rows, precision=PRECISE) * 0.125)
    scores = jnp.where(key_valid[:, None, None, None, :] == 1, scores, -1e+30)
    probs_low = low(softmax_rows(scores))
    mixed_out = jnp.einsum('cfhpq,cfqhe->cfphe', probs_low, value_rows, precision=PRECISE)
    return low_back(low(mixed_out.reshape(clip_count, frame_count, cell_count, D)))

def attend_time(normed_in, w_qkv):
    clip_count, frame_count, cell_count = (normed_in.shape[0], normed_in.shape[1], normed_in.shape[2])
    triple = low_back(low(project(normed_in, w_qkv))).reshape(clip_count, frame_count, cell_count, 3, HEADS, HEAD)
    queries = triple[:, :, :, 0]
    key_rows = triple[:, :, :, 1]
    value_rows = triple[:, :, :, 2]
    scores = low_back(jnp.einsum('cfphe,cgphe->cphfg', queries, key_rows, precision=PRECISE) * 0.125)
    probs_low = low(softmax_rows(scores))
    mixed_out = jnp.einsum('cphfg,cgphe->cfphe', probs_low, value_rows, precision=PRECISE)
    return low_back(low(mixed_out.reshape(clip_count, frame_count, cell_count, D)))

def layer_forward(tokens, w_ada, b_ada, w_qkv_s, w_out_s, b_out_s, w_qkv_t, w_out_t, b_out_t, w_up, b_up, w_down, b_down, cond_act, key_valid):
    modulation = jnp.dot(cond_act, w_ada, precision=PRECISE) + b_ada
    pieces = [modulation[:, piece_index * D:(piece_index + 1) * D][:, None, None, :] for piece_index in range(9)]
    shift_one, scale_one, gate_one, shift_two, scale_two, gate_two, shift_three, scale_three, gate_three = pieces
    act_one = low(standard(tokens) * (1.0 + scale_one) + shift_one)
    spatial = low_back(project(attend_space(act_one, w_qkv_s, key_valid), w_out_s) + b_out_s)
    state_one = low_back(low(tokens + gate_one * spatial))
    act_two = low(standard(state_one) * (1.0 + scale_two) + shift_two)
    temporal = low_back(project(attend_time(act_two, w_qkv_t), w_out_t) + b_out_t)
    state_two = state_one + gate_two * temporal
    act_three = low(standard(state_two) * (1.0 + scale_three) + shift_three)
    lifted = low_back(project(act_three, w_up) + b_up)
    hidden = low(jax.nn.gelu(lifted, approximate=True))
    branch = low_back(project(hidden, w_down) + b_down)
    return state_two + gate_three * branch

def reference(tokens, condition, loss_grad, cell_counts, frame_tasks, destinations, w_ada, b_ada, w_qkv_s, w_out_s, b_out_s, w_qkv_t, w_out_t, b_out_t, w_up, b_up, w_down, b_down):
    floats = [weight.astype(jnp.float32) for weight in (w_ada, b_ada, w_qkv_s, w_out_s, b_out_s, w_qkv_t, w_out_t, b_out_t, w_up, b_up, w_down, b_down)]
    cond_act = low(jax.nn.silu(condition.astype(jnp.float32)[destinations]))
    cell_index = jnp.arange(CELLS, dtype=jnp.int32)
    key_valid = (cell_index[None, :] < cell_counts[:, None]).astype(jnp.int32)
    loss_mask = frame_tasks[:, :, None] * key_valid[:, None, :]
    out_grad = loss_grad.astype(jnp.float32) * loss_mask[..., None].astype(jnp.float32)

    def forward(token_field, *weight_list):
        return layer_forward(token_field, *weight_list, cond_act, key_valid)
    result, pullback = jax.vjp(forward, tokens.astype(jnp.float32), *floats)
    grads = pullback(out_grad)
    return (result.astype(jnp.bfloat16), grads[0].astype(jnp.bfloat16), grads[1], grads[2], grads[3], grads[4], grads[5], grads[6], grads[7], grads[8], grads[9], grads[10], grads[11], grads[12])
```

```python
import jax
import jax.numpy as jnp
from jax import lax
from jax.experimental import pallas as pl
from jax.experimental.pallas import tpu as pltpu
from jax.sharding import PartitionSpec as P

D = 768
HEADS = 12
HEAD = 64


def standard(field):
    centred = field - jnp.mean(field, axis=-1, keepdims=True)
    inverse = lax.rsqrt(jnp.mean(centred * centred, axis=-1, keepdims=True) + 1e-06)
    return (centred * inverse, inverse)


def standard_back(normed, inverse, grad_normed):
    return inverse * (
        grad_normed
        - jnp.mean(grad_normed, axis=-1, keepdims=True)
        - normed * jnp.mean(grad_normed * normed, axis=-1, keepdims=True)
    )


def gelu_back(lifted, grad_hidden):
    return jax.vjp(lambda inner: jax.nn.gelu(inner, approximate=True), lifted)[1](grad_hidden)[0]


def attend(triple, key_valid, einsum_forms):
    queries = triple[:, :, 0]
    key_rows = triple[:, :, 1]
    value_rows = triple[:, :, 2]
    scores = (
        jnp.einsum(einsum_forms[0], queries, key_rows, preferred_element_type=jnp.float32) * 0.125
    )
    scores = jnp.where(key_valid, scores, -1e30)
    row_top = jnp.max(scores, axis=-1, keepdims=True)
    exponent = jnp.exp(scores - row_top)
    probs_full = exponent / jnp.sum(exponent, axis=-1, keepdims=True)
    probs_low = probs_full.astype(jnp.bfloat16)
    mixed_out = jnp.einsum(
        einsum_forms[1], probs_low, value_rows, preferred_element_type=jnp.float32
    ).astype(jnp.bfloat16)
    return (mixed_out, probs_full, probs_low)


def attend_back(triple, probs_full, probs_low, grad_mixed, einsum_forms):
    queries = triple[:, :, 0]
    key_rows = triple[:, :, 1]
    value_rows = triple[:, :, 2]
    grad_probs = jnp.einsum(
        einsum_forms[0], grad_mixed, value_rows, preferred_element_type=jnp.float32
    )
    row_delta = jnp.sum(probs_full * grad_probs, axis=-1, keepdims=True)
    grad_scores = (probs_full * (grad_probs - row_delta)).astype(jnp.bfloat16)
    grad_values = jnp.einsum(
        einsum_forms[2], probs_low, grad_mixed, preferred_element_type=jnp.float32
    )
    grad_queries = (
        jnp.einsum(einsum_forms[1], grad_scores, key_rows, preferred_element_type=jnp.float32)
        * 0.125
    )
    grad_keys = (
        jnp.einsum(einsum_forms[2], grad_scores, queries, preferred_element_type=jnp.float32)
        * 0.125
    )
    return jnp.stack([grad_queries, grad_keys, grad_values], axis=2)


def per_device_general(
    tokens,
    condition,
    loss_grad,
    cell_counts,
    frame_tasks,
    destinations,
    w_ada,
    b_ada,
    w_qkv_s,
    w_out_s,
    b_out_s,
    w_qkv_t,
    w_out_t,
    b_out_t,
    w_up,
    b_up,
    w_down,
    b_down,
):
    groups = lax.axis_size("dp")
    ranks = lax.axis_size("seq")
    own_slot = lax.axis_index("dp")
    own_rank = lax.axis_index("seq")
    frame_part = tokens.shape[1]
    cell_total = tokens.shape[2] * groups
    cell_part = cell_total // ranks
    frame_total = frame_part * ranks
    slot_ids = jnp.arange(groups, dtype=jnp.int32)
    routing = (destinations[None, :] == slot_ids[:, None]).astype(jnp.bfloat16)
    outgoing = jnp.einsum(
        "jc,cfbd->jfbd", routing, tokens, preferred_element_type=jnp.float32
    ).astype(jnp.bfloat16)
    outgoing_grad = jnp.einsum(
        "jc,cfbd->jfbd", routing, loss_grad, preferred_element_type=jnp.float32
    ).astype(jnp.bfloat16)
    arrived, arrived_grad = (
        lax.all_to_all(outgoing, "dp", split_axis=0, concat_axis=2, tiled=True),
        lax.all_to_all(outgoing_grad, "dp", split_axis=0, concat_axis=2, tiled=True),
    )
    own_clip = jnp.sum(jnp.where(destinations == own_slot, slot_ids, 0))
    own_count = jnp.sum(jnp.where(slot_ids == own_clip, cell_counts, 0))
    own_tasks = lax.dynamic_index_in_dim(frame_tasks, own_clip, 0, keepdims=False)
    cond_row = lax.dynamic_index_in_dim(condition, own_slot, 0, keepdims=False)
    cond_low = jax.nn.silu(cond_row.astype(jnp.float32)).astype(jnp.bfloat16)
    modulation = jnp.dot(cond_low[None, :], w_ada, preferred_element_type=jnp.float32)[
        0
    ] + b_ada.astype(jnp.float32)
    pieces = [modulation[piece_index * D : (piece_index + 1) * D] for piece_index in range(9)]
    (
        shift_one,
        scale_one,
        gate_one,
        shift_two,
        scale_two,
        gate_two,
        shift_three,
        scale_three,
        gate_three,
    ) = pieces
    space_forms = ("fphe,fqhe->fhpq", "fhpq,fqhe->fphe", "fhpq,fphe->fqhe")
    frames_in = arrived[0].astype(jnp.float32)
    normed_one, inverse_one = standard(frames_in)
    act_one = (normed_one * (1.0 + scale_one) + shift_one).astype(jnp.bfloat16)
    triple_one = (
        jnp.einsum("fpd,de->fpe", act_one, w_qkv_s, preferred_element_type=jnp.float32)
        .astype(jnp.bfloat16)
        .reshape(frame_part, cell_total, 3, HEADS, HEAD)
    )
    key_valid = (jnp.arange(cell_total, dtype=jnp.int32) < own_count)[None, None, None, :]
    mixed_one, probs_one, low_one = attend(triple_one, key_valid, space_forms)
    flat_one = mixed_one.reshape(frame_part, cell_total, D)
    spatial_out = jnp.einsum(
        "fpd,de->fpe", flat_one, w_out_s, preferred_element_type=jnp.float32
    ) + b_out_s.astype(jnp.float32)
    state_one = (frames_in + gate_one * spatial_out).astype(jnp.bfloat16)
    cells_in, cells_grad = (
        lax.all_to_all(state_one, "seq", split_axis=1, concat_axis=0, tiled=True),
        lax.all_to_all(arrived_grad[0], "seq", split_axis=1, concat_axis=0, tiled=True),
    )
    time_forms = ("fqhe,gqhe->qhfg", "qhfg,gqhe->fqhe", "qhfg,fqhe->gqhe")
    state_cells = cells_in.astype(jnp.float32)
    normed_two, inverse_two = standard(state_cells)
    act_two = (normed_two * (1.0 + scale_two) + shift_two).astype(jnp.bfloat16)
    triple_two = (
        jnp.einsum("fqd,de->fqe", act_two, w_qkv_t, preferred_element_type=jnp.float32)
        .astype(jnp.bfloat16)
        .reshape(frame_total, cell_part, 3, HEADS, HEAD)
    )
    mixed_two, probs_two, low_two = attend(triple_two, True, time_forms)
    flat_two = mixed_two.reshape(frame_total, cell_part, D)
    temporal_out = jnp.einsum(
        "fqd,de->fqe", flat_two, w_out_t, preferred_element_type=jnp.float32
    ) + b_out_t.astype(jnp.float32)
    state_two = state_cells + gate_two * temporal_out
    normed_three, inverse_three = standard(state_two)
    act_three = (normed_three * (1.0 + scale_three) + shift_three).astype(jnp.bfloat16)
    lifted = jnp.einsum(
        "fqd,dk->fqk", act_three, w_up, preferred_element_type=jnp.float32
    ) + b_up.astype(jnp.float32)
    hidden = jax.nn.gelu(lifted, approximate=True).astype(jnp.bfloat16)
    branch_out = jnp.einsum(
        "fqk,kd->fqd", hidden, w_down, preferred_element_type=jnp.float32
    ) + b_down.astype(jnp.float32)
    result = (state_two + gate_three * branch_out).astype(jnp.bfloat16)
    cell_ids = own_rank * cell_part + jnp.arange(cell_part, dtype=jnp.int32)
    loss_mask = jnp.logical_and(own_tasks[:, None] == 1, cell_ids[None, :] < own_count)
    out_grad = cells_grad.astype(jnp.float32) * loss_mask[:, :, None].astype(jnp.float32)
    grad_gate_three = jnp.sum(out_grad * branch_out, axis=(0, 1))
    grad_branch = (gate_three * out_grad).astype(jnp.bfloat16)
    grad_b_down = jnp.sum(grad_branch.astype(jnp.float32), axis=(0, 1))
    grad_w_down = jnp.einsum("fqk,fqd->kd", hidden, grad_branch, preferred_element_type=jnp.float32)
    grad_hidden = jnp.einsum("fqd,kd->fqk", grad_branch, w_down, preferred_element_type=jnp.float32)
    grad_lifted = gelu_back(lifted, grad_hidden).astype(jnp.bfloat16)
    grad_b_up = jnp.sum(grad_lifted.astype(jnp.float32), axis=(0, 1))
    grad_w_up = jnp.einsum(
        "fqd,fqk->dk", act_three, grad_lifted, preferred_element_type=jnp.float32
    )
    grad_act_three = jnp.einsum(
        "fqk,dk->fqd", grad_lifted, w_up, preferred_element_type=jnp.float32
    )
    grad_shift_three = jnp.sum(grad_act_three, axis=(0, 1))
    grad_scale_three = jnp.sum(grad_act_three * normed_three, axis=(0, 1))
    grad_state_two = out_grad + standard_back(
        normed_three, inverse_three, grad_act_three * (1.0 + scale_three)
    )
    grad_gate_two = jnp.sum(grad_state_two * temporal_out, axis=(0, 1))
    grad_temporal = (gate_two * grad_state_two).astype(jnp.bfloat16)
    grad_b_out_t = jnp.sum(grad_temporal.astype(jnp.float32), axis=(0, 1))
    grad_w_out_t = jnp.einsum(
        "fqd,fqe->de", flat_two, grad_temporal, preferred_element_type=jnp.float32
    )
    grad_mixed_two = (
        jnp.einsum("fqe,de->fqd", grad_temporal, w_out_t, preferred_element_type=jnp.float32)
        .astype(jnp.bfloat16)
        .reshape(frame_total, cell_part, HEADS, HEAD)
    )
    grad_triple_two = (
        attend_back(triple_two, probs_two, low_two, grad_mixed_two, time_forms)
        .reshape(frame_total, cell_part, 3 * D)
        .astype(jnp.bfloat16)
    )
    grad_w_qkv_t = jnp.einsum(
        "fqd,fqe->de", act_two, grad_triple_two, preferred_element_type=jnp.float32
    )
    grad_act_two = jnp.einsum(
        "fqe,de->fqd", grad_triple_two, w_qkv_t, preferred_element_type=jnp.float32
    )
    grad_shift_two = jnp.sum(grad_act_two, axis=(0, 1))
    grad_scale_two = jnp.sum(grad_act_two * normed_two, axis=(0, 1))
    grad_state_one = (
        grad_state_two + standard_back(normed_two, inverse_two, grad_act_two * (1.0 + scale_two))
    ).astype(jnp.bfloat16)
    frames_out, frames_grad = (
        lax.all_to_all(result, "seq", split_axis=0, concat_axis=1, tiled=True),
        lax.all_to_all(grad_state_one, "seq", split_axis=0, concat_axis=1, tiled=True),
    )
    grad_frames = frames_grad.astype(jnp.float32)
    grad_gate_one = jnp.sum(grad_frames * spatial_out, axis=(0, 1))
    grad_spatial = (gate_one * grad_frames).astype(jnp.bfloat16)
    grad_b_out_s = jnp.sum(grad_spatial.astype(jnp.float32), axis=(0, 1))
    grad_w_out_s = jnp.einsum(
        "fpd,fpe->de", flat_one, grad_spatial, preferred_element_type=jnp.float32
    )
    grad_mixed_one = (
        jnp.einsum("fpe,de->fpd", grad_spatial, w_out_s, preferred_element_type=jnp.float32)
        .astype(jnp.bfloat16)
        .reshape(frame_part, cell_total, HEADS, HEAD)
    )
    grad_triple_one = (
        attend_back(triple_one, probs_one, low_one, grad_mixed_one, space_forms)
        .reshape(frame_part, cell_total, 3 * D)
        .astype(jnp.bfloat16)
    )
    grad_w_qkv_s = jnp.einsum(
        "fpd,fpe->de", act_one, grad_triple_one, preferred_element_type=jnp.float32
    )
    grad_act_one = jnp.einsum(
        "fpe,de->fpd", grad_triple_one, w_qkv_s, preferred_element_type=jnp.float32
    )
    grad_shift_one = jnp.sum(grad_act_one, axis=(0, 1))
    grad_scale_one = jnp.sum(grad_act_one * normed_one, axis=(0, 1))
    grad_input = (
        grad_frames + standard_back(normed_one, inverse_one, grad_act_one * (1.0 + scale_one))
    ).astype(jnp.bfloat16)
    home_out, home_grad = (
        lax.all_to_all(frames_out[None], "dp", split_axis=2, concat_axis=0, tiled=True),
        lax.all_to_all(grad_input[None], "dp", split_axis=2, concat_axis=0, tiled=True),
    )
    layer_out = jnp.einsum(
        "jc,jfbd->cfbd", routing, home_out, preferred_element_type=jnp.float32
    ).astype(jnp.bfloat16)
    grad_tokens = jnp.einsum(
        "jc,jfbd->cfbd", routing, home_grad, preferred_element_type=jnp.float32
    ).astype(jnp.bfloat16)
    grad_mod = jnp.concatenate(
        [
            grad_shift_one,
            grad_scale_one,
            grad_gate_one,
            grad_shift_two,
            grad_scale_two,
            grad_gate_two,
            grad_shift_three,
            grad_scale_three,
            grad_gate_three,
        ]
    )
    ada_term = cond_low.astype(jnp.float32)[:, None] * grad_mod[None, :]
    partials = (
        lax.psum_scatter(
            ada_term.astype(jnp.bfloat16), "seq", scatter_dimension=0, tiled=True
        ).astype(jnp.float32),
        lax.psum_scatter(
            grad_mod.astype(jnp.bfloat16), "seq", scatter_dimension=0, tiled=True
        ).astype(jnp.float32),
        lax.psum_scatter(
            grad_w_qkv_s.astype(jnp.bfloat16), "seq", scatter_dimension=0, tiled=True
        ).astype(jnp.float32),
        lax.psum_scatter(
            grad_w_out_s.astype(jnp.bfloat16), "seq", scatter_dimension=0, tiled=True
        ).astype(jnp.float32),
        lax.psum_scatter(
            grad_b_out_s.astype(jnp.bfloat16), "seq", scatter_dimension=0, tiled=True
        ).astype(jnp.float32),
        lax.psum_scatter(
            grad_w_qkv_t.astype(jnp.bfloat16), "seq", scatter_dimension=0, tiled=True
        ).astype(jnp.float32),
        lax.psum_scatter(
            grad_w_out_t.astype(jnp.bfloat16), "seq", scatter_dimension=0, tiled=True
        ).astype(jnp.float32),
        lax.psum_scatter(
            grad_b_out_t.astype(jnp.bfloat16), "seq", scatter_dimension=0, tiled=True
        ).astype(jnp.float32),
        lax.psum_scatter(
            grad_w_up.astype(jnp.bfloat16), "seq", scatter_dimension=0, tiled=True
        ).astype(jnp.float32),
        lax.psum_scatter(
            grad_b_up.astype(jnp.bfloat16), "seq", scatter_dimension=0, tiled=True
        ).astype(jnp.float32),
        lax.psum_scatter(
            grad_w_down.astype(jnp.bfloat16), "seq", scatter_dimension=0, tiled=True
        ).astype(jnp.float32),
        lax.psum_scatter(
            grad_b_down.astype(jnp.bfloat16), "seq", scatter_dimension=0, tiled=True
        ).astype(jnp.float32),
    )
    totals = lax.psum(
        (
            partials[0],
            partials[1],
            partials[2],
            partials[3],
            partials[4],
            partials[5],
            partials[6],
            partials[7],
            partials[8],
            partials[9],
            partials[10],
            partials[11],
        ),
        "dp",
    )
    ada_grad = totals[0]
    ada_bias = totals[1]
    rest = totals[2:]
    return (
        layer_out,
        grad_tokens,
        ada_grad,
        ada_bias,
        rest[0],
        rest[1],
        rest[2],
        rest[3],
        rest[4],
        rest[5],
        rest[6],
        rest[7],
        rest[8],
        rest[9],
    )


MESH = pl.DeviceIdType.MESH
ANY = pl.BlockSpec(memory_space=pl.ANY)
VMEM = pl.BlockSpec(memory_space=pltpu.VMEM)
NEG = -1e30
CLIPS = 8
RANKS = 4
FRAME_PART = 4
CELLS = 256
CELL_HOME = CELLS // CLIPS
CELL_PART = CELLS // RANKS


def f32(value):
    return value.astype(jnp.float32)


def bf16(value):
    return value.astype(jnp.bfloat16)


def dot(left, right):
    return lax.dot_general(left, right, (((1,), (0,)), ((), ())), preferred_element_type=jnp.float32)


def dot_nt(left, right):
    return lax.dot_general(left, right, (((1,), (1,)), ((), ())), preferred_element_type=jnp.float32)


def dot_tn(left, right):
    return lax.dot_general(left, right, (((0,), (0,)), ((), ())), preferred_element_type=jnp.float32)


def heads_forward(qkv, mixed, valid, probs=None):
    lane = lax.broadcasted_iota(jnp.int32, (1, 2 * HEAD), 1) < HEAD
    for pair in range(HEADS // 2):
        lanes = pl.ds(pair * 2 * HEAD, 2 * HEAD)
        queries = qkv[:, pl.ds(pair * 2 * HEAD, 2 * HEAD)] * jnp.bfloat16(0.125)
        keys = qkv[:, pl.ds(D + pair * 2 * HEAD, 2 * HEAD)]
        values = qkv[:, pl.ds(2 * D + pair * 2 * HEAD, 2 * HEAD)]
        parts = []
        for half in range(2):
            mine = lane if half == 0 else jnp.logical_not(lane)
            scores = dot_nt(jnp.where(mine, queries, jnp.bfloat16(0)), keys)
            scores = jnp.where(valid, scores, NEG)
            exponent = jnp.exp(scores - jnp.max(scores, axis=-1, keepdims=True))
            full = exponent * (1.0 / jnp.sum(exponent, axis=-1, keepdims=True))
            if probs is not None:
                probs[2 * pair + half] = full
            parts.append(dot(bf16(full), values))
        mixed[:, lanes] = bf16(jnp.where(lane, parts[0], parts[1]))


def space_forward_body(
    tokens,
    loss_grad,
    cond,
    valid,
    w_ada,
    b_ada,
    w_qkv,
    w_out,
    b_out,
    arrived,
    qkv_all,
    mixed_all,
    state_cells,
    grad_cells,
    modulation,
    x_scr,
    ada_scr,
    wqkv_scr,
    wout_scr,
    qkv_scr,
    mixed_scr,
    state_scr,
    local_sem,
    in_send,
    in_recv,
    grad_send,
    grad_recv,
    out_send,
    out_recv,
    save_sem,
):
    slot = lax.axis_index("dp")
    rank = lax.axis_index("seq")

    def arrival(frame, hop):
        peer = lax.rem(slot + hop, CLIPS)
        rows = pl.ds(pl.multiple_of(slot * CELL_HOME, CELL_HOME), CELL_HOME)
        return pltpu.make_async_remote_copy(
            src_ref=tokens.at[peer, frame],
            dst_ref=x_scr.at[frame, rows],
            send_sem=in_send.at[frame, hop],
            recv_sem=in_recv.at[frame, hop],
            device_id=(peer, rank),
            device_id_type=MESH,
        )

    def loss_route(hop):
        peer = lax.rem(slot + hop, CLIPS)
        target = slot // 2
        rows = pl.ds(pl.multiple_of(lax.rem(slot, 2) * CELL_HOME, CELL_HOME), CELL_HOME)
        place = grad_cells.at[pl.ds(rank * FRAME_PART, FRAME_PART), rows]
        spot = lax.rem(slot, 2) * RANKS + rank
        return peer, target, place, spot

    def loss_send(hop):
        peer, target, place, spot = loss_route(hop)
        return pltpu.make_async_remote_copy(
            src_ref=loss_grad.at[peer],
            dst_ref=place,
            send_sem=grad_send.at[hop],
            recv_sem=grad_recv.at[spot],
            device_id=(peer, target),
            device_id_type=MESH,
        )

    def loss_keep():
        peer, target, place, spot = loss_route(0)
        return pltpu.make_async_copy(loss_grad.at[peer], place, grad_recv.at[spot])

    def leave(frame, hop):
        peer = lax.rem(rank + hop, RANKS)
        rows = pl.ds(pl.multiple_of(peer * CELL_PART, CELL_PART), CELL_PART)
        return pltpu.make_async_remote_copy(
            src_ref=state_scr.at[frame, rows],
            dst_ref=state_cells.at[rank * FRAME_PART + frame],
            send_sem=out_send.at[frame, hop],
            recv_sem=out_recv.at[frame, hop],
            device_id=(slot, peer),
            device_id_type=MESH,
        )

    def keep(frame):
        rows = pl.ds(pl.multiple_of(rank * CELL_PART, CELL_PART), CELL_PART)
        return pltpu.make_async_copy(
            state_scr.at[frame, rows], state_cells.at[rank * FRAME_PART + frame], out_recv.at[frame, 0]
        )

    def saves(frame):
        return (
            pltpu.make_async_copy(x_scr.at[frame], arrived.at[frame], save_sem.at[frame, 0]),
            pltpu.make_async_copy(qkv_scr.at[frame], qkv_all.at[frame], save_sem.at[frame, 1]),
            pltpu.make_async_copy(mixed_scr.at[frame], mixed_all.at[frame], save_sem.at[frame, 2]),
        )

    own_rows = pl.ds(pl.multiple_of(slot * CELL_HOME, CELL_HOME), CELL_HOME)
    own_copy = pltpu.make_async_copy(tokens.at[slot], x_scr.at[:, own_rows], local_sem.at[0])
    ada_copy = pltpu.make_async_copy(w_ada, ada_scr, local_sem.at[1])
    qkv_copy = pltpu.make_async_copy(w_qkv, wqkv_scr, local_sem.at[2])
    out_copy = pltpu.make_async_copy(w_out, wout_scr, local_sem.at[3])
    for hop in range(1, CLIPS):
        arrival(0, hop).start()
    own_copy.start()
    ada_copy.start()
    for frame in range(1, FRAME_PART):
        for hop in range(1, CLIPS):
            arrival(frame, hop).start()
    qkv_copy.start()
    out_copy.start()
    self_loss = slot // 2 == rank

    ada_copy.wait()
    for piece in range(9):
        row = dot(cond[...], ada_scr[:, pl.ds(piece * D, D)])[0:1]
        modulation[pl.ds(piece, 1)] = row + b_ada[pl.ds(piece, 1)]
    own_copy.wait()
    qkv_copy.wait()
    out_copy.wait()

    def frame_step(frame, carry):
        for hop in range(1, CLIPS):
            arrival(frame, hop).wait_recv()
        for extra in range(2):
            hop = 2 * frame + extra
            alone = jnp.logical_and(self_loss, hop == 0)

            @pl.when(alone)
            def _():
                loss_keep().start()

            @pl.when(jnp.logical_not(alone))
            def _():
                loss_send(hop).start()

        x = f32(x_scr[frame])
        centred = x - jnp.mean(x, axis=-1, keepdims=True)
        normed = centred * lax.rsqrt(jnp.mean(centred * centred, axis=-1, keepdims=True) + 1e-06)
        act = bf16(normed * (1.0 + modulation[1:2]) + modulation[0:1])
        qkv_scr[frame] = bf16(dot(act, wqkv_scr[...]))
        heads_forward(qkv_scr.at[frame], mixed_scr.at[frame], valid[0:1] > 0.5)
        spatial = dot(mixed_scr[frame], wout_scr[...]) + b_out[...]
        state_scr[frame] = bf16(f32(x_scr[frame]) + modulation[2:3] * spatial)
        for hop in range(1, RANKS):
            leave(frame, hop).start()
        keep(frame).start()
        for save in saves(frame):
            save.start()
        return carry

    lax.fori_loop(0, FRAME_PART, frame_step, 0)

    def frame_end(frame, carry):
        for hop in range(1, CLIPS):
            arrival(frame, hop).wait_send()
        for hop in range(1, RANKS):
            leave(frame, hop).wait()
        keep(frame).wait()
        for save in saves(frame):
            save.wait()
        return carry

    lax.fori_loop(0, FRAME_PART, frame_end, 0)

    @pl.when(jnp.logical_not(self_loss))
    def _():
        loss_send(0).wait_send()

    for hop in range(1, CLIPS):
        loss_send(hop).wait_send()
    for spot in range(2 * RANKS):
        rows = pl.ds((spot // RANKS) * CELL_HOME, CELL_HOME)
        place = grad_cells.at[pl.ds((spot % RANKS) * FRAME_PART, FRAME_PART), rows]
        pltpu.make_async_copy(loss_grad.at[0], place, grad_recv.at[spot]).wait()


def space_forward(tokens, loss_grad, cond, valid, w_ada, b_ada, w_qkv, w_out, b_out):
    low = jnp.bfloat16
    return pl.pallas_call(
        space_forward_body,
        out_shape=(
            jax.ShapeDtypeStruct((FRAME_PART, CELLS, D), low),
            jax.ShapeDtypeStruct((FRAME_PART, CELLS, 3 * D), low),
            jax.ShapeDtypeStruct((FRAME_PART, CELLS, D), low),
            jax.ShapeDtypeStruct((FRAME_PART * RANKS, CELL_PART, D), low),
            jax.ShapeDtypeStruct((FRAME_PART * RANKS, CELL_PART, D), low),
            jax.ShapeDtypeStruct((16, D), jnp.float32),
        ),
        in_specs=[ANY, ANY, VMEM, VMEM, ANY, VMEM, ANY, ANY, VMEM],
        out_specs=(ANY, ANY, ANY, ANY, ANY, VMEM),
        scratch_shapes=[
            pltpu.VMEM((FRAME_PART, CELLS, D), low),
            pltpu.VMEM((D, 9 * D), low),
            pltpu.VMEM((D, 3 * D), low),
            pltpu.VMEM((D, D), low),
            pltpu.VMEM((FRAME_PART, CELLS, 3 * D), low),
            pltpu.VMEM((FRAME_PART, CELLS, D), low),
            pltpu.VMEM((FRAME_PART, CELLS, D), low),
            pltpu.SemaphoreType.DMA((4,)),
            pltpu.SemaphoreType.DMA((FRAME_PART, CLIPS)),
            pltpu.SemaphoreType.DMA((FRAME_PART, CLIPS)),
            pltpu.SemaphoreType.DMA((CLIPS,)),
            pltpu.SemaphoreType.DMA((2 * RANKS,)),
            pltpu.SemaphoreType.DMA((FRAME_PART, RANKS)),
            pltpu.SemaphoreType.DMA((FRAME_PART, RANKS)),
            pltpu.SemaphoreType.DMA((FRAME_PART, 3)),
        ],
        compiler_params=pltpu.CompilerParams(has_side_effects=True, vmem_limit_bytes=48 * 1024 * 1024),
        cost_estimate=pl.CostEstimate(flops=8 * 10**9, bytes_accessed=40 * 10**6, transcendentals=3 * 10**6),
        name="space_forward",
    )(tokens, loss_grad, cond, valid, w_ada, b_ada, w_qkv, w_out, b_out)


def per_device_fast(
    tokens,
    condition,
    loss_grad,
    cell_counts,
    frame_tasks,
    destinations,
    w_ada,
    b_ada,
    w_qkv_s,
    w_out_s,
    b_out_s,
    w_qkv_t,
    w_out_t,
    b_out_t,
    w_up,
    b_up,
    w_down,
    b_down,
):
    groups = lax.axis_size("dp")
    ranks = lax.axis_size("seq")
    own_slot = lax.axis_index("dp")
    own_rank = lax.axis_index("seq")
    frame_part = tokens.shape[1]
    cell_total = tokens.shape[2] * groups
    cell_part = cell_total // ranks
    frame_total = frame_part * ranks
    own_count = lax.dynamic_index_in_dim(cell_counts, own_slot, 0, keepdims=False)
    own_tasks = lax.dynamic_index_in_dim(frame_tasks, own_slot, 0, keepdims=False)
    own_row = lax.dynamic_index_in_dim(destinations, own_slot, 0, keepdims=False)
    cond_row = lax.dynamic_index_in_dim(condition, own_row, 0, keepdims=False)
    cond_low = jax.nn.silu(cond_row.astype(jnp.float32)).astype(jnp.bfloat16)
    cell_range = jnp.arange(cell_total, dtype=jnp.int32)
    valid_row = jnp.broadcast_to((cell_range < own_count).astype(jnp.float32)[None], (8, cell_total))
    arrived, qkv_one, flat_one, cells_in, cells_grad, modulation = space_forward(
        tokens,
        loss_grad,
        jnp.broadcast_to(cond_low[None], (16, D)),
        valid_row,
        w_ada,
        b_ada.astype(jnp.float32).reshape(9, D),
        w_qkv_s,
        w_out_s,
        b_out_s.astype(jnp.float32)[None],
    )
    pieces = [modulation[piece_index] for piece_index in range(9)]
    (
        shift_one,
        scale_one,
        gate_one,
        shift_two,
        scale_two,
        gate_two,
        shift_three,
        scale_three,
        gate_three,
    ) = pieces
    space_forms = ("fphe,fqhe->fhpq", "fhpq,fqhe->fphe", "fhpq,fphe->fqhe")
    frames_in = arrived.astype(jnp.float32)
    normed_one, inverse_one = standard(frames_in)
    act_one = (normed_one * (1.0 + scale_one) + shift_one).astype(jnp.bfloat16)
    triple_one = qkv_one.reshape(frame_part, cell_total, 3, HEADS, HEAD)
    key_valid = (jnp.arange(cell_total, dtype=jnp.int32) < own_count)[None, None, None, :]
    _, probs_one, low_one = attend(triple_one, key_valid, space_forms)
    spatial_out = jnp.einsum(
        "fpd,de->fpe", flat_one, w_out_s, preferred_element_type=jnp.float32
    ) + b_out_s.astype(jnp.float32)
    time_forms = ("fqhe,gqhe->qhfg", "qhfg,gqhe->fqhe", "qhfg,fqhe->gqhe")
    state_cells = cells_in.astype(jnp.float32)
    normed_two, inverse_two = standard(state_cells)
    act_two = (normed_two * (1.0 + scale_two) + shift_two).astype(jnp.bfloat16)
    triple_two = (
        jnp.einsum("fqd,de->fqe", act_two, w_qkv_t, preferred_element_type=jnp.float32)
        .astype(jnp.bfloat16)
        .reshape(frame_total, cell_part, 3, HEADS, HEAD)
    )
    mixed_two, probs_two, low_two = attend(triple_two, True, time_forms)
    flat_two = mixed_two.reshape(frame_total, cell_part, D)
    temporal_out = jnp.einsum(
        "fqd,de->fqe", flat_two, w_out_t, preferred_element_type=jnp.float32
    ) + b_out_t.astype(jnp.float32)
    state_two = state_cells + gate_two * temporal_out
    normed_three, inverse_three = standard(state_two)
    act_three = (normed_three * (1.0 + scale_three) + shift_three).astype(jnp.bfloat16)
    lifted = jnp.einsum(
        "fqd,dk->fqk", act_three, w_up, preferred_element_type=jnp.float32
    ) + b_up.astype(jnp.float32)
    hidden = jax.nn.gelu(lifted, approximate=True).astype(jnp.bfloat16)
    branch_out = jnp.einsum(
        "fqk,kd->fqd", hidden, w_down, preferred_element_type=jnp.float32
    ) + b_down.astype(jnp.float32)
    result = (state_two + gate_three * branch_out).astype(jnp.bfloat16)
    cell_ids = own_rank * cell_part + jnp.arange(cell_part, dtype=jnp.int32)
    loss_mask = jnp.logical_and(own_tasks[:, None] == 1, cell_ids[None, :] < own_count)
    out_grad = cells_grad.astype(jnp.float32) * loss_mask[:, :, None].astype(jnp.float32)
    grad_gate_three = jnp.sum(out_grad * branch_out, axis=(0, 1))
    grad_branch = (gate_three * out_grad).astype(jnp.bfloat16)
    grad_b_down = jnp.sum(grad_branch.astype(jnp.float32), axis=(0, 1))
    grad_w_down = jnp.einsum("fqk,fqd->kd", hidden, grad_branch, preferred_element_type=jnp.float32)
    grad_hidden = jnp.einsum("fqd,kd->fqk", grad_branch, w_down, preferred_element_type=jnp.float32)
    grad_lifted = gelu_back(lifted, grad_hidden).astype(jnp.bfloat16)
    grad_b_up = jnp.sum(grad_lifted.astype(jnp.float32), axis=(0, 1))
    grad_w_up = jnp.einsum(
        "fqd,fqk->dk", act_three, grad_lifted, preferred_element_type=jnp.float32
    )
    grad_act_three = jnp.einsum(
        "fqk,dk->fqd", grad_lifted, w_up, preferred_element_type=jnp.float32
    )
    grad_shift_three = jnp.sum(grad_act_three, axis=(0, 1))
    grad_scale_three = jnp.sum(grad_act_three * normed_three, axis=(0, 1))
    grad_state_two = out_grad + standard_back(
        normed_three, inverse_three, grad_act_three * (1.0 + scale_three)
    )
    grad_gate_two = jnp.sum(grad_state_two * temporal_out, axis=(0, 1))
    grad_temporal = (gate_two * grad_state_two).astype(jnp.bfloat16)
    grad_b_out_t = jnp.sum(grad_temporal.astype(jnp.float32), axis=(0, 1))
    grad_w_out_t = jnp.einsum(
        "fqd,fqe->de", flat_two, grad_temporal, preferred_element_type=jnp.float32
    )
    grad_mixed_two = (
        jnp.einsum("fqe,de->fqd", grad_temporal, w_out_t, preferred_element_type=jnp.float32)
        .astype(jnp.bfloat16)
        .reshape(frame_total, cell_part, HEADS, HEAD)
    )
    grad_triple_two = (
        attend_back(triple_two, probs_two, low_two, grad_mixed_two, time_forms)
        .reshape(frame_total, cell_part, 3 * D)
        .astype(jnp.bfloat16)
    )
    grad_w_qkv_t = jnp.einsum(
        "fqd,fqe->de", act_two, grad_triple_two, preferred_element_type=jnp.float32
    )
    grad_act_two = jnp.einsum(
        "fqe,de->fqd", grad_triple_two, w_qkv_t, preferred_element_type=jnp.float32
    )
    grad_shift_two = jnp.sum(grad_act_two, axis=(0, 1))
    grad_scale_two = jnp.sum(grad_act_two * normed_two, axis=(0, 1))
    grad_state_one = (
        grad_state_two + standard_back(normed_two, inverse_two, grad_act_two * (1.0 + scale_two))
    ).astype(jnp.bfloat16)
    frames_out, frames_grad = (
        lax.all_to_all(result, "seq", split_axis=0, concat_axis=1, tiled=True),
        lax.all_to_all(grad_state_one, "seq", split_axis=0, concat_axis=1, tiled=True),
    )
    grad_frames = frames_grad.astype(jnp.float32)
    grad_gate_one = jnp.sum(grad_frames * spatial_out, axis=(0, 1))
    grad_spatial = (gate_one * grad_frames).astype(jnp.bfloat16)
    grad_b_out_s = jnp.sum(grad_spatial.astype(jnp.float32), axis=(0, 1))
    grad_w_out_s = jnp.einsum(
        "fpd,fpe->de", flat_one, grad_spatial, preferred_element_type=jnp.float32
    )
    grad_mixed_one = (
        jnp.einsum("fpe,de->fpd", grad_spatial, w_out_s, preferred_element_type=jnp.float32)
        .astype(jnp.bfloat16)
        .reshape(frame_part, cell_total, HEADS, HEAD)
    )
    grad_triple_one = (
        attend_back(triple_one, probs_one, low_one, grad_mixed_one, space_forms)
        .reshape(frame_part, cell_total, 3 * D)
        .astype(jnp.bfloat16)
    )
    grad_w_qkv_s = jnp.einsum(
        "fpd,fpe->de", act_one, grad_triple_one, preferred_element_type=jnp.float32
    )
    grad_act_one = jnp.einsum(
        "fpe,de->fpd", grad_triple_one, w_qkv_s, preferred_element_type=jnp.float32
    )
    grad_shift_one = jnp.sum(grad_act_one, axis=(0, 1))
    grad_scale_one = jnp.sum(grad_act_one * normed_one, axis=(0, 1))
    grad_input = (
        grad_frames + standard_back(normed_one, inverse_one, grad_act_one * (1.0 + scale_one))
    ).astype(jnp.bfloat16)
    home_out, home_grad = (
        lax.all_to_all(frames_out[None], "dp", split_axis=2, concat_axis=0, tiled=True),
        lax.all_to_all(grad_input[None], "dp", split_axis=2, concat_axis=0, tiled=True),
    )
    layer_out = home_out
    grad_tokens = home_grad
    grad_mod = jnp.concatenate(
        [
            grad_shift_one,
            grad_scale_one,
            grad_gate_one,
            grad_shift_two,
            grad_scale_two,
            grad_gate_two,
            grad_shift_three,
            grad_scale_three,
            grad_gate_three,
        ]
    )
    ada_term = cond_low.astype(jnp.float32)[:, None] * grad_mod[None, :]
    partials = (
        lax.psum_scatter(
            ada_term.astype(jnp.bfloat16), "seq", scatter_dimension=0, tiled=True
        ).astype(jnp.float32),
        lax.psum_scatter(
            grad_mod.astype(jnp.bfloat16), "seq", scatter_dimension=0, tiled=True
        ).astype(jnp.float32),
        lax.psum_scatter(
            grad_w_qkv_s.astype(jnp.bfloat16), "seq", scatter_dimension=0, tiled=True
        ).astype(jnp.float32),
        lax.psum_scatter(
            grad_w_out_s.astype(jnp.bfloat16), "seq", scatter_dimension=0, tiled=True
        ).astype(jnp.float32),
        lax.psum_scatter(
            grad_b_out_s.astype(jnp.bfloat16), "seq", scatter_dimension=0, tiled=True
        ).astype(jnp.float32),
        lax.psum_scatter(
            grad_w_qkv_t.astype(jnp.bfloat16), "seq", scatter_dimension=0, tiled=True
        ).astype(jnp.float32),
        lax.psum_scatter(
            grad_w_out_t.astype(jnp.bfloat16), "seq", scatter_dimension=0, tiled=True
        ).astype(jnp.float32),
        lax.psum_scatter(
            grad_b_out_t.astype(jnp.bfloat16), "seq", scatter_dimension=0, tiled=True
        ).astype(jnp.float32),
        lax.psum_scatter(
            grad_w_up.astype(jnp.bfloat16), "seq", scatter_dimension=0, tiled=True
        ).astype(jnp.float32),
        lax.psum_scatter(
            grad_b_up.astype(jnp.bfloat16), "seq", scatter_dimension=0, tiled=True
        ).astype(jnp.float32),
        lax.psum_scatter(
            grad_w_down.astype(jnp.bfloat16), "seq", scatter_dimension=0, tiled=True
        ).astype(jnp.float32),
        lax.psum_scatter(
            grad_b_down.astype(jnp.bfloat16), "seq", scatter_dimension=0, tiled=True
        ).astype(jnp.float32),
    )
    totals = lax.psum(
        (
            partials[0],
            partials[1],
            partials[2],
            partials[3],
            partials[4],
            partials[5],
            partials[6],
            partials[7],
            partials[8],
            partials[9],
            partials[10],
            partials[11],
        ),
        "dp",
    )
    ada_grad = totals[0]
    ada_bias = totals[1]
    rest = totals[2:]
    return (
        layer_out,
        grad_tokens,
        ada_grad,
        ada_bias,
        rest[0],
        rest[1],
        rest[2],
        rest[3],
        rest[4],
        rest[5],
        rest[6],
        rest[7],
        rest[8],
        rest[9],
    )


def solution(mesh):
    placed = (
        P(None, "seq", "dp", None),
        P(),
        P(None, "seq", "dp", None),
        P(),
        P(),
        P(),
        P(),
        P(),
        P(),
        P(),
        P(),
        P(),
        P(),
        P(),
        P(),
        P(),
        P(),
        P(),
    )
    fast = mesh.shape["dp"] == 8 and mesh.shape["seq"] == 4
    return jax.shard_map(
        per_device_fast if fast else per_device_general,
        mesh=mesh,
        in_specs=placed,
        out_specs=(
            P(None, "seq", "dp", None),
            P(None, "seq", "dp", None),
            P("seq", None),
            P("seq"),
            P("seq", None),
            P("seq", None),
            P("seq"),
            P("seq", None),
            P("seq", None),
            P("seq"),
            P("seq", None),
            P("seq"),
            P("seq", None),
            P("seq"),
        ),
        check_vma=False,
    )
```

```python
import jax
import jax.numpy as jnp
from jax import lax
from jax.experimental import pallas as pl
from jax.experimental.pallas import tpu as pltpu
from jax.sharding import PartitionSpec as P

D = 768
HEADS = 12
HEAD = 64


def standard(field):
    centred = field - jnp.mean(field, axis=-1, keepdims=True)
    inverse = lax.rsqrt(jnp.mean(centred * centred, axis=-1, keepdims=True) + 1e-06)
    return (centred * inverse, inverse)


def standard_back(normed, inverse, grad_normed):
    return inverse * (
        grad_normed
        - jnp.mean(grad_normed, axis=-1, keepdims=True)
        - normed * jnp.mean(grad_normed * normed, axis=-1, keepdims=True)
    )


def gelu_back(lifted, grad_hidden):
    return jax.vjp(lambda inner: jax.nn.gelu(inner, approximate=True), lifted)[1](grad_hidden)[0]


def attend(triple, key_valid, einsum_forms):
    queries = triple[:, :, 0]
    key_rows = triple[:, :, 1]
    value_rows = triple[:, :, 2]
    scores = (
        jnp.einsum(einsum_forms[0], queries, key_rows, preferred_element_type=jnp.float32) * 0.125
    )
    scores = jnp.where(key_valid, scores, -1e30)
    row_top = jnp.max(scores, axis=-1, keepdims=True)
    exponent = jnp.exp(scores - row_top)
    probs_full = exponent / jnp.sum(exponent, axis=-1, keepdims=True)
    probs_low = probs_full.astype(jnp.bfloat16)
    mixed_out = jnp.einsum(
        einsum_forms[1], probs_low, value_rows, preferred_element_type=jnp.float32
    ).astype(jnp.bfloat16)
    return (mixed_out, probs_full, probs_low)


def attend_back(triple, probs_full, probs_low, grad_mixed, einsum_forms):
    queries = triple[:, :, 0]
    key_rows = triple[:, :, 1]
    value_rows = triple[:, :, 2]
    grad_probs = jnp.einsum(
        einsum_forms[0], grad_mixed, value_rows, preferred_element_type=jnp.float32
    )
    row_delta = jnp.sum(probs_full * grad_probs, axis=-1, keepdims=True)
    grad_scores = (probs_full * (grad_probs - row_delta)).astype(jnp.bfloat16)
    grad_values = jnp.einsum(
        einsum_forms[2], probs_low, grad_mixed, preferred_element_type=jnp.float32
    )
    grad_queries = (
        jnp.einsum(einsum_forms[1], grad_scores, key_rows, preferred_element_type=jnp.float32)
        * 0.125
    )
    grad_keys = (
        jnp.einsum(einsum_forms[2], grad_scores, queries, preferred_element_type=jnp.float32)
        * 0.125
    )
    return jnp.stack([grad_queries, grad_keys, grad_values], axis=2)


def per_device_general(
    tokens,
    condition,
    loss_grad,
    cell_counts,
    frame_tasks,
    destinations,
    w_ada,
    b_ada,
    w_qkv_s,
    w_out_s,
    b_out_s,
    w_qkv_t,
    w_out_t,
    b_out_t,
    w_up,
    b_up,
    w_down,
    b_down,
):
    groups = lax.axis_size("dp")
    ranks = lax.axis_size("seq")
    own_slot = lax.axis_index("dp")
    own_rank = lax.axis_index("seq")
    frame_part = tokens.shape[1]
    cell_total = tokens.shape[2] * groups
    cell_part = cell_total // ranks
    frame_total = frame_part * ranks
    slot_ids = jnp.arange(groups, dtype=jnp.int32)
    routing = (destinations[None, :] == slot_ids[:, None]).astype(jnp.bfloat16)
    outgoing = jnp.einsum(
        "jc,cfbd->jfbd", routing, tokens, preferred_element_type=jnp.float32
    ).astype(jnp.bfloat16)
    outgoing_grad = jnp.einsum(
        "jc,cfbd->jfbd", routing, loss_grad, preferred_element_type=jnp.float32
    ).astype(jnp.bfloat16)
    arrived, arrived_grad = (
        lax.all_to_all(outgoing, "dp", split_axis=0, concat_axis=2, tiled=True),
        lax.all_to_all(outgoing_grad, "dp", split_axis=0, concat_axis=2, tiled=True),
    )
    own_clip = jnp.sum(jnp.where(destinations == own_slot, slot_ids, 0))
    own_count = jnp.sum(jnp.where(slot_ids == own_clip, cell_counts, 0))
    own_tasks = lax.dynamic_index_in_dim(frame_tasks, own_clip, 0, keepdims=False)
    cond_row = lax.dynamic_index_in_dim(condition, own_slot, 0, keepdims=False)
    cond_low = jax.nn.silu(cond_row.astype(jnp.float32)).astype(jnp.bfloat16)
    modulation = jnp.dot(cond_low[None, :], w_ada, preferred_element_type=jnp.float32)[
        0
    ] + b_ada.astype(jnp.float32)
    pieces = [modulation[piece_index * D : (piece_index + 1) * D] for piece_index in range(9)]
    (
        shift_one,
        scale_one,
        gate_one,
        shift_two,
        scale_two,
        gate_two,
        shift_three,
        scale_three,
        gate_three,
    ) = pieces
    space_forms = ("fphe,fqhe->fhpq", "fhpq,fqhe->fphe", "fhpq,fphe->fqhe")
    frames_in = arrived[0].astype(jnp.float32)
    normed_one, inverse_one = standard(frames_in)
    act_one = (normed_one * (1.0 + scale_one) + shift_one).astype(jnp.bfloat16)
    triple_one = (
        jnp.einsum("fpd,de->fpe", act_one, w_qkv_s, preferred_element_type=jnp.float32)
        .astype(jnp.bfloat16)
        .reshape(frame_part, cell_total, 3, HEADS, HEAD)
    )
    key_valid = (jnp.arange(cell_total, dtype=jnp.int32) < own_count)[None, None, None, :]
    mixed_one, probs_one, low_one = attend(triple_one, key_valid, space_forms)
    flat_one = mixed_one.reshape(frame_part, cell_total, D)
    spatial_out = jnp.einsum(
        "fpd,de->fpe", flat_one, w_out_s, preferred_element_type=jnp.float32
    ) + b_out_s.astype(jnp.float32)
    state_one = (frames_in + gate_one * spatial_out).astype(jnp.bfloat16)
    cells_in, cells_grad = (
        lax.all_to_all(state_one, "seq", split_axis=1, concat_axis=0, tiled=True),
        lax.all_to_all(arrived_grad[0], "seq", split_axis=1, concat_axis=0, tiled=True),
    )
    time_forms = ("fqhe,gqhe->qhfg", "qhfg,gqhe->fqhe", "qhfg,fqhe->gqhe")
    state_cells = cells_in.astype(jnp.float32)
    normed_two, inverse_two = standard(state_cells)
    act_two = (normed_two * (1.0 + scale_two) + shift_two).astype(jnp.bfloat16)
    triple_two = (
        jnp.einsum("fqd,de->fqe", act_two, w_qkv_t, preferred_element_type=jnp.float32)
        .astype(jnp.bfloat16)
        .reshape(frame_total, cell_part, 3, HEADS, HEAD)
    )
    mixed_two, probs_two, low_two = attend(triple_two, True, time_forms)
    flat_two = mixed_two.reshape(frame_total, cell_part, D)
    temporal_out = jnp.einsum(
        "fqd,de->fqe", flat_two, w_out_t, preferred_element_type=jnp.float32
    ) + b_out_t.astype(jnp.float32)
    state_two = state_cells + gate_two * temporal_out
    normed_three, inverse_three = standard(state_two)
    act_three = (normed_three * (1.0 + scale_three) + shift_three).astype(jnp.bfloat16)
    lifted = jnp.einsum(
        "fqd,dk->fqk", act_three, w_up, preferred_element_type=jnp.float32
    ) + b_up.astype(jnp.float32)
    hidden = jax.nn.gelu(lifted, approximate=True).astype(jnp.bfloat16)
    branch_out = jnp.einsum(
        "fqk,kd->fqd", hidden, w_down, preferred_element_type=jnp.float32
    ) + b_down.astype(jnp.float32)
    result = (state_two + gate_three * branch_out).astype(jnp.bfloat16)
    cell_ids = own_rank * cell_part + jnp.arange(cell_part, dtype=jnp.int32)
    loss_mask = jnp.logical_and(own_tasks[:, None] == 1, cell_ids[None, :] < own_count)
    out_grad = cells_grad.astype(jnp.float32) * loss_mask[:, :, None].astype(jnp.float32)
    grad_gate_three = jnp.sum(out_grad * branch_out, axis=(0, 1))
    grad_branch = (gate_three * out_grad).astype(jnp.bfloat16)
    grad_b_down = jnp.sum(grad_branch.astype(jnp.float32), axis=(0, 1))
    grad_w_down = jnp.einsum("fqk,fqd->kd", hidden, grad_branch, preferred_element_type=jnp.float32)
    grad_hidden = jnp.einsum("fqd,kd->fqk", grad_branch, w_down, preferred_element_type=jnp.float32)
    grad_lifted = gelu_back(lifted, grad_hidden).astype(jnp.bfloat16)
    grad_b_up = jnp.sum(grad_lifted.astype(jnp.float32), axis=(0, 1))
    grad_w_up = jnp.einsum(
        "fqd,fqk->dk", act_three, grad_lifted, preferred_element_type=jnp.float32
    )
    grad_act_three = jnp.einsum(
        "fqk,dk->fqd", grad_lifted, w_up, preferred_element_type=jnp.float32
    )
    grad_shift_three = jnp.sum(grad_act_three, axis=(0, 1))
    grad_scale_three = jnp.sum(grad_act_three * normed_three, axis=(0, 1))
    grad_state_two = out_grad + standard_back(
        normed_three, inverse_three, grad_act_three * (1.0 + scale_three)
    )
    grad_gate_two = jnp.sum(grad_state_two * temporal_out, axis=(0, 1))
    grad_temporal = (gate_two * grad_state_two).astype(jnp.bfloat16)
    grad_b_out_t = jnp.sum(grad_temporal.astype(jnp.float32), axis=(0, 1))
    grad_w_out_t = jnp.einsum(
        "fqd,fqe->de", flat_two, grad_temporal, preferred_element_type=jnp.float32
    )
    grad_mixed_two = (
        jnp.einsum("fqe,de->fqd", grad_temporal, w_out_t, preferred_element_type=jnp.float32)
        .astype(jnp.bfloat16)
        .reshape(frame_total, cell_part, HEADS, HEAD)
    )
    grad_triple_two = (
        attend_back(triple_two, probs_two, low_two, grad_mixed_two, time_forms)
        .reshape(frame_total, cell_part, 3 * D)
        .astype(jnp.bfloat16)
    )
    grad_w_qkv_t = jnp.einsum(
        "fqd,fqe->de", act_two, grad_triple_two, preferred_element_type=jnp.float32
    )
    grad_act_two = jnp.einsum(
        "fqe,de->fqd", grad_triple_two, w_qkv_t, preferred_element_type=jnp.float32
    )
    grad_shift_two = jnp.sum(grad_act_two, axis=(0, 1))
    grad_scale_two = jnp.sum(grad_act_two * normed_two, axis=(0, 1))
    grad_state_one = (
        grad_state_two + standard_back(normed_two, inverse_two, grad_act_two * (1.0 + scale_two))
    ).astype(jnp.bfloat16)
    frames_out, frames_grad = (
        lax.all_to_all(result, "seq", split_axis=0, concat_axis=1, tiled=True),
        lax.all_to_all(grad_state_one, "seq", split_axis=0, concat_axis=1, tiled=True),
    )
    grad_frames = frames_grad.astype(jnp.float32)
    grad_gate_one = jnp.sum(grad_frames * spatial_out, axis=(0, 1))
    grad_spatial = (gate_one * grad_frames).astype(jnp.bfloat16)
    grad_b_out_s = jnp.sum(grad_spatial.astype(jnp.float32), axis=(0, 1))
    grad_w_out_s = jnp.einsum(
        "fpd,fpe->de", flat_one, grad_spatial, preferred_element_type=jnp.float32
    )
    grad_mixed_one = (
        jnp.einsum("fpe,de->fpd", grad_spatial, w_out_s, preferred_element_type=jnp.float32)
        .astype(jnp.bfloat16)
        .reshape(frame_part, cell_total, HEADS, HEAD)
    )
    grad_triple_one = (
        attend_back(triple_one, probs_one, low_one, grad_mixed_one, space_forms)
        .reshape(frame_part, cell_total, 3 * D)
        .astype(jnp.bfloat16)
    )
    grad_w_qkv_s = jnp.einsum(
        "fpd,fpe->de", act_one, grad_triple_one, preferred_element_type=jnp.float32
    )
    grad_act_one = jnp.einsum(
        "fpe,de->fpd", grad_triple_one, w_qkv_s, preferred_element_type=jnp.float32
    )
    grad_shift_one = jnp.sum(grad_act_one, axis=(0, 1))
    grad_scale_one = jnp.sum(grad_act_one * normed_one, axis=(0, 1))
    grad_input = (
        grad_frames + standard_back(normed_one, inverse_one, grad_act_one * (1.0 + scale_one))
    ).astype(jnp.bfloat16)
    home_out, home_grad = (
        lax.all_to_all(frames_out[None], "dp", split_axis=2, concat_axis=0, tiled=True),
        lax.all_to_all(grad_input[None], "dp", split_axis=2, concat_axis=0, tiled=True),
    )
    layer_out = jnp.einsum(
        "jc,jfbd->cfbd", routing, home_out, preferred_element_type=jnp.float32
    ).astype(jnp.bfloat16)
    grad_tokens = jnp.einsum(
        "jc,jfbd->cfbd", routing, home_grad, preferred_element_type=jnp.float32
    ).astype(jnp.bfloat16)
    grad_mod = jnp.concatenate(
        [
            grad_shift_one,
            grad_scale_one,
            grad_gate_one,
            grad_shift_two,
            grad_scale_two,
            grad_gate_two,
            grad_shift_three,
            grad_scale_three,
            grad_gate_three,
        ]
    )
    ada_term = cond_low.astype(jnp.float32)[:, None] * grad_mod[None, :]
    partials = (
        lax.psum_scatter(
            ada_term.astype(jnp.bfloat16), "seq", scatter_dimension=0, tiled=True
        ).astype(jnp.float32),
        lax.psum_scatter(
            grad_mod.astype(jnp.bfloat16), "seq", scatter_dimension=0, tiled=True
        ).astype(jnp.float32),
        lax.psum_scatter(
            grad_w_qkv_s.astype(jnp.bfloat16), "seq", scatter_dimension=0, tiled=True
        ).astype(jnp.float32),
        lax.psum_scatter(
            grad_w_out_s.astype(jnp.bfloat16), "seq", scatter_dimension=0, tiled=True
        ).astype(jnp.float32),
        lax.psum_scatter(
            grad_b_out_s.astype(jnp.bfloat16), "seq", scatter_dimension=0, tiled=True
        ).astype(jnp.float32),
        lax.psum_scatter(
            grad_w_qkv_t.astype(jnp.bfloat16), "seq", scatter_dimension=0, tiled=True
        ).astype(jnp.float32),
        lax.psum_scatter(
            grad_w_out_t.astype(jnp.bfloat16), "seq", scatter_dimension=0, tiled=True
        ).astype(jnp.float32),
        lax.psum_scatter(
            grad_b_out_t.astype(jnp.bfloat16), "seq", scatter_dimension=0, tiled=True
        ).astype(jnp.float32),
        lax.psum_scatter(
            grad_w_up.astype(jnp.bfloat16), "seq", scatter_dimension=0, tiled=True
        ).astype(jnp.float32),
        lax.psum_scatter(
            grad_b_up.astype(jnp.bfloat16), "seq", scatter_dimension=0, tiled=True
        ).astype(jnp.float32),
        lax.psum_scatter(
            grad_w_down.astype(jnp.bfloat16), "seq", scatter_dimension=0, tiled=True
        ).astype(jnp.float32),
        lax.psum_scatter(
            grad_b_down.astype(jnp.bfloat16), "seq", scatter_dimension=0, tiled=True
        ).astype(jnp.float32),
    )
    totals = lax.psum(
        (
            partials[0],
            partials[1],
            partials[2],
            partials[3],
            partials[4],
            partials[5],
            partials[6],
            partials[7],
            partials[8],
            partials[9],
            partials[10],
            partials[11],
        ),
        "dp",
    )
    ada_grad = totals[0]
    ada_bias = totals[1]
    rest = totals[2:]
    return (
        layer_out,
        grad_tokens,
        ada_grad,
        ada_bias,
        rest[0],
        rest[1],
        rest[2],
        rest[3],
        rest[4],
        rest[5],
        rest[6],
        rest[7],
        rest[8],
        rest[9],
    )


MESH = pl.DeviceIdType.MESH
ANY = pl.BlockSpec(memory_space=pl.ANY)
VMEM = pl.BlockSpec(memory_space=pltpu.VMEM)
NEG = -1e30
CLIPS = 8
RANKS = 4
FRAME_PART = 4
CELLS = 256
CELL_HOME = CELLS // CLIPS
CELL_PART = CELLS // RANKS


def f32(value):
    return value.astype(jnp.float32)


def bf16(value):
    return value.astype(jnp.bfloat16)


def dot(left, right):
    return lax.dot_general(left, right, (((1,), (0,)), ((), ())), preferred_element_type=jnp.float32)


def dot_nt(left, right):
    return lax.dot_general(left, right, (((1,), (1,)), ((), ())), preferred_element_type=jnp.float32)


def dot_tn(left, right):
    return lax.dot_general(left, right, (((0,), (0,)), ((), ())), preferred_element_type=jnp.float32)


def head_halves(rows):
    lane = lax.broadcasted_iota(jnp.int32, (1, 2 * HEAD), 1) < HEAD
    zero = jnp.bfloat16(0)
    return jnp.where(lane, rows, zero), jnp.where(lane, zero, rows)


def column_probs(keys, queries, valid):
    scores = jnp.where(valid, dot_nt(keys, queries), NEG)
    exponent = jnp.exp(scores - jnp.max(scores, axis=0, keepdims=True))
    return exponent * (1.0 / jnp.sum(exponent, axis=0, keepdims=True))


def heads_forward(qkv, mixed, valid, blocks, probs=None):
    for pair in range(HEADS // 2):
        places = [pl.ds(part * D + pair * 2 * HEAD, 2 * HEAD) for part in range(3)]
        queries = qkv[:, places[0]] * jnp.bfloat16(0.125)
        keys = head_halves(qkv[:, places[1]])
        turned = qkv[:, places[2]].T
        for spot, (ours, theirs) in enumerate(blocks):
            parts = []
            for half in range(2):
                full = column_probs(keys[half][theirs], queries[ours], valid)
                if probs is not None:
                    probs[2 * pair + half, spot] = full
                parts.append(dot(turned[half * HEAD : (half + 1) * HEAD, theirs], bf16(full)))
            mixed[ours, places[0]] = bf16(jnp.concatenate(parts, axis=0)).T


def heads_backward(qkv, grad_mixed, grad_qkv, valid, blocks, shared, probs=None, pairs=range(HEADS // 2)):
    lane = lax.broadcasted_iota(jnp.int32, (1, 2 * HEAD), 1) < HEAD
    for pair in pairs:
        places = [pl.ds(part * D + pair * 2 * HEAD, 2 * HEAD) for part in range(3)]
        queries = qkv[:, places[0]] * jnp.bfloat16(0.125)
        keys = qkv[:, places[1]]
        turned = keys.T
        keys = head_halves(keys)
        values = head_halves(qkv[:, places[2]])
        grads = grad_mixed[:, places[0]]
        sums = None
        for spot, (ours, theirs) in enumerate(blocks):
            across, downs = [], []
            for half in range(2):
                if probs is None:
                    full = column_probs(keys[half][theirs], queries[ours], valid)
                else:
                    full = probs[2 * pair + half, spot]
                weighted = full * dot_nt(values[half][theirs], grads[ours])
                grad_scores = bf16(weighted - full * jnp.sum(weighted, axis=0, keepdims=True))
                across.append(dot(turned[half * HEAD : (half + 1) * HEAD, theirs], grad_scores))
                downs.append((dot(grad_scores, queries[ours]), dot(bf16(full), grads[ours])))
            grad_qkv[ours, places[0]] = bf16(jnp.concatenate(across, axis=0) * 0.125).T
            downs = [jnp.where(lane, downs[0][part], downs[1][part]) for part in range(2)]
            if shared:
                sums = downs if sums is None else [sums[part] + downs[part] for part in range(2)]
            else:
                for part in range(2):
                    grad_qkv[theirs, places[1 + part]] = bf16(downs[part])
        if shared:
            for part in range(2):
                grad_qkv[:, places[1 + part]] = bf16(sums[part])


BLOCK = 256
SPACE_BLOCKS = [(slice(spot, spot + BLOCK), slice(0, CELLS)) for spot in range(0, CELLS, BLOCK)]


def space_forward_body(
    tokens,
    loss_grad,
    cond,
    valid,
    w_ada,
    b_ada,
    w_qkv,
    w_out,
    b_out,
    arrived,
    qkv_all,
    mixed_all,
    state_cells,
    grad_cells,
    modulation,
    x_scr,
    ada_scr,
    wqkv_scr,
    wout_scr,
    qkv_scr,
    mixed_scr,
    state_scr,
    local_sem,
    in_send,
    in_recv,
    grad_send,
    grad_recv,
    out_send,
    out_recv,
    save_sem,
):
    slot = lax.axis_index("dp")
    rank = lax.axis_index("seq")

    def arrival(frame, hop):
        peer = lax.rem(slot + hop, CLIPS)
        rows = pl.ds(pl.multiple_of(slot * CELL_HOME, CELL_HOME), CELL_HOME)
        return pltpu.make_async_remote_copy(
            src_ref=tokens.at[peer, frame],
            dst_ref=x_scr.at[frame, rows],
            send_sem=in_send.at[frame, hop],
            recv_sem=in_recv.at[frame, hop],
            device_id=(peer, rank),
            device_id_type=MESH,
        )

    def loss_route(hop):
        peer = lax.rem(slot + hop, CLIPS)
        target = slot // 2
        rows = pl.ds(pl.multiple_of(lax.rem(slot, 2) * CELL_HOME, CELL_HOME), CELL_HOME)
        place = grad_cells.at[pl.ds(rank * FRAME_PART, FRAME_PART), rows]
        spot = lax.rem(slot, 2) * RANKS + rank
        return peer, target, place, spot

    def loss_send(hop):
        peer, target, place, spot = loss_route(hop)
        return pltpu.make_async_remote_copy(
            src_ref=loss_grad.at[peer],
            dst_ref=place,
            send_sem=grad_send.at[hop],
            recv_sem=grad_recv.at[spot],
            device_id=(peer, target),
            device_id_type=MESH,
        )

    def loss_keep():
        peer, target, place, spot = loss_route(0)
        return pltpu.make_async_copy(loss_grad.at[peer], place, grad_recv.at[spot])

    def leave(frame, hop):
        peer = lax.rem(rank + hop, RANKS)
        rows = pl.ds(pl.multiple_of(peer * CELL_PART, CELL_PART), CELL_PART)
        return pltpu.make_async_remote_copy(
            src_ref=state_scr.at[frame, rows],
            dst_ref=state_cells.at[rank * FRAME_PART + frame],
            send_sem=out_send.at[frame, hop],
            recv_sem=out_recv.at[frame, hop],
            device_id=(slot, peer),
            device_id_type=MESH,
        )

    def keep(frame):
        rows = pl.ds(pl.multiple_of(rank * CELL_PART, CELL_PART), CELL_PART)
        return pltpu.make_async_copy(
            state_scr.at[frame, rows], state_cells.at[rank * FRAME_PART + frame], out_recv.at[frame, 0]
        )

    def saves(frame):
        return (
            pltpu.make_async_copy(x_scr.at[frame], arrived.at[frame], save_sem.at[frame, 0]),
            pltpu.make_async_copy(qkv_scr.at[frame], qkv_all.at[frame], save_sem.at[frame, 1]),
            pltpu.make_async_copy(mixed_scr.at[frame], mixed_all.at[frame], save_sem.at[frame, 2]),
        )

    own_rows = pl.ds(pl.multiple_of(slot * CELL_HOME, CELL_HOME), CELL_HOME)
    own_copy = pltpu.make_async_copy(tokens.at[slot], x_scr.at[:, own_rows], local_sem.at[0])
    ada_copy = pltpu.make_async_copy(w_ada, ada_scr, local_sem.at[1])
    qkv_copy = pltpu.make_async_copy(w_qkv, wqkv_scr, local_sem.at[2])
    out_copy = pltpu.make_async_copy(w_out, wout_scr, local_sem.at[3])
    for hop in range(1, CLIPS):
        arrival(0, hop).start()
    own_copy.start()
    ada_copy.start()
    for frame in range(1, FRAME_PART):
        for hop in range(1, CLIPS):
            arrival(frame, hop).start()
    qkv_copy.start()
    out_copy.start()
    self_loss = slot // 2 == rank

    ada_copy.wait()
    for piece in range(9):
        row = dot(cond[...], ada_scr[:, pl.ds(piece * D, D)])[0:1]
        modulation[pl.ds(piece, 1)] = row + b_ada[pl.ds(piece, 1)]
    own_copy.wait()
    qkv_copy.wait()
    out_copy.wait()

    def frame_step(frame, carry):
        for hop in range(1, CLIPS):
            arrival(frame, hop).wait_recv()
        for extra in range(2):
            hop = 2 * frame + extra
            alone = jnp.logical_and(self_loss, hop == 0)

            @pl.when(alone)
            def _():
                loss_keep().start()

            @pl.when(jnp.logical_not(alone))
            def _():
                loss_send(hop).start()

        x = f32(x_scr[frame])
        centred = x - jnp.mean(x, axis=-1, keepdims=True)
        normed = centred * lax.rsqrt(jnp.mean(centred * centred, axis=-1, keepdims=True) + 1e-06)
        act = bf16(normed * (1.0 + modulation[1:2]) + modulation[0:1])
        qkv_scr[frame] = bf16(dot(act, wqkv_scr[...]))
        heads_forward(qkv_scr.at[frame], mixed_scr.at[frame], valid[...] > 0.5, SPACE_BLOCKS)
        spatial = dot(mixed_scr[frame], wout_scr[...]) + b_out[...]
        state_scr[frame] = bf16(f32(x_scr[frame]) + modulation[2:3] * spatial)
        for hop in range(1, RANKS):
            leave(frame, hop).start()
        keep(frame).start()
        for save in saves(frame):
            save.start()
        return carry

    lax.fori_loop(0, FRAME_PART, frame_step, 0)

    def frame_end(frame, carry):
        for hop in range(1, CLIPS):
            arrival(frame, hop).wait_send()
        for hop in range(1, RANKS):
            leave(frame, hop).wait()
        keep(frame).wait()
        for save in saves(frame):
            save.wait()
        return carry

    lax.fori_loop(0, FRAME_PART, frame_end, 0)

    @pl.when(jnp.logical_not(self_loss))
    def _():
        loss_send(0).wait_send()

    for hop in range(1, CLIPS):
        loss_send(hop).wait_send()
    for spot in range(2 * RANKS):
        rows = pl.ds((spot // RANKS) * CELL_HOME, CELL_HOME)
        place = grad_cells.at[pl.ds((spot % RANKS) * FRAME_PART, FRAME_PART), rows]
        pltpu.make_async_copy(loss_grad.at[0], place, grad_recv.at[spot]).wait()


def space_forward(tokens, loss_grad, cond, valid, w_ada, b_ada, w_qkv, w_out, b_out):
    low = jnp.bfloat16
    return pl.pallas_call(
        space_forward_body,
        out_shape=(
            jax.ShapeDtypeStruct((FRAME_PART, CELLS, D), low),
            jax.ShapeDtypeStruct((FRAME_PART, CELLS, 3 * D), low),
            jax.ShapeDtypeStruct((FRAME_PART, CELLS, D), low),
            jax.ShapeDtypeStruct((FRAME_PART * RANKS, CELL_PART, D), low),
            jax.ShapeDtypeStruct((FRAME_PART * RANKS, CELL_PART, D), low),
            jax.ShapeDtypeStruct((16, D), jnp.float32),
        ),
        in_specs=[ANY, ANY, VMEM, VMEM, ANY, VMEM, ANY, ANY, VMEM],
        out_specs=(ANY, ANY, ANY, ANY, ANY, VMEM),
        scratch_shapes=[
            pltpu.VMEM((FRAME_PART, CELLS, D), low),
            pltpu.VMEM((D, 9 * D), low),
            pltpu.VMEM((D, 3 * D), low),
            pltpu.VMEM((D, D), low),
            pltpu.VMEM((FRAME_PART, CELLS, 3 * D), low),
            pltpu.VMEM((FRAME_PART, CELLS, D), low),
            pltpu.VMEM((FRAME_PART, CELLS, D), low),
            pltpu.SemaphoreType.DMA((4,)),
            pltpu.SemaphoreType.DMA((FRAME_PART, CLIPS)),
            pltpu.SemaphoreType.DMA((FRAME_PART, CLIPS)),
            pltpu.SemaphoreType.DMA((CLIPS,)),
            pltpu.SemaphoreType.DMA((2 * RANKS,)),
            pltpu.SemaphoreType.DMA((FRAME_PART, RANKS)),
            pltpu.SemaphoreType.DMA((FRAME_PART, RANKS)),
            pltpu.SemaphoreType.DMA((FRAME_PART, 3)),
        ],
        compiler_params=pltpu.CompilerParams(has_side_effects=True, vmem_limit_bytes=48 * 1024 * 1024),
        cost_estimate=pl.CostEstimate(flops=8 * 10**9, bytes_accessed=40 * 10**6, transcendentals=3 * 10**6),
        name="space_forward",
    )(tokens, loss_grad, cond, valid, w_ada, b_ada, w_qkv, w_out, b_out)


def standardise(field):
    centred = field - jnp.mean(field, axis=-1, keepdims=True)
    inverse = lax.rsqrt(jnp.mean(centred * centred, axis=-1, keepdims=True) + 1e-06)
    return centred * inverse, inverse


def column_sum(field):
    return jnp.sum(field, axis=0, keepdims=True)


def row_heads_forward(qkv, mixed, valid, probs=None):
    lane = lax.broadcasted_iota(jnp.int32, (1, 2 * HEAD), 1) < HEAD
    for pair in range(HEADS // 2):
        lanes = pl.ds(pair * 2 * HEAD, 2 * HEAD)
        queries = qkv[:, pl.ds(pair * 2 * HEAD, 2 * HEAD)] * jnp.bfloat16(0.125)
        keys = qkv[:, pl.ds(D + pair * 2 * HEAD, 2 * HEAD)]
        values = qkv[:, pl.ds(2 * D + pair * 2 * HEAD, 2 * HEAD)]
        parts = []
        for half in range(2):
            mine = lane if half == 0 else jnp.logical_not(lane)
            scores = dot_nt(jnp.where(mine, queries, jnp.bfloat16(0)), keys)
            scores = jnp.where(valid, scores, NEG)
            exponent = jnp.exp(scores - jnp.max(scores, axis=-1, keepdims=True))
            full = exponent * (1.0 / jnp.sum(exponent, axis=-1, keepdims=True))
            if probs is not None:
                probs[2 * pair + half] = full
            parts.append(dot(bf16(full), values))
        mixed[:, lanes] = bf16(jnp.where(lane, parts[0], parts[1]))


def head_probs(queries, keys, mine, valid):
    scores = dot_nt(jnp.where(mine, queries, jnp.bfloat16(0)), keys)
    scores = jnp.where(valid, scores, NEG)
    exponent = jnp.exp(scores - jnp.max(scores, axis=-1, keepdims=True))
    return exponent * (1.0 / jnp.sum(exponent, axis=-1, keepdims=True))


def row_heads_backward(qkv, grad_mixed, grad_qkv, valid, probs=None):
    lane = lax.broadcasted_iota(jnp.int32, (1, 2 * HEAD), 1) < HEAD
    for pair in range(HEADS // 2):
        places = [pl.ds(part * D + pair * 2 * HEAD, 2 * HEAD) for part in range(3)]
        queries = qkv[:, places[0]] * jnp.bfloat16(0.125)
        keys = qkv[:, places[1]]
        values = qkv[:, places[2]]
        grads = grad_mixed[:, places[0]]
        parts = []
        for half in range(2):
            mine = lane if half == 0 else jnp.logical_not(lane)
            if probs is None:
                full = head_probs(queries, keys, mine, valid)
            else:
                full = probs[2 * pair + half]
            grad_probs = dot_nt(jnp.where(mine, grads, jnp.bfloat16(0)), values)
            weighted = full * grad_probs
            grad_scores = bf16(weighted - full * jnp.sum(weighted, axis=-1, keepdims=True))
            parts.append((dot(grad_scores, keys), dot_tn(grad_scores, queries), dot_tn(bf16(full), grads)))
        grad_qkv[:, places[0]] = bf16(jnp.where(lane, parts[0][0], parts[1][0]) * 0.125)
        grad_qkv[:, places[1]] = bf16(jnp.where(lane, parts[0][1], parts[1][1]))
        grad_qkv[:, places[2]] = bf16(jnp.where(lane, parts[0][2], parts[1][2]))


FF = 3072
TOKENS = 256
CHUNK_CELLS = TOKENS // (FRAME_PART * RANKS)
CHUNKS = CELL_PART // CHUNK_CELLS


def time_body(
    state_in,
    loss_in,
    mask_in,
    modulation,
    w_qkv,
    w_out,
    b_out,
    w_up,
    b_up,
    w_down,
    b_down,
    layer_out,
    grad_state,
    act_two,
    grad_qkv,
    mixed,
    grad_temporal,
    act_three,
    grad_lifted,
    hidden,
    grad_branch,
    sums,
    probs,
    qkv,
    slopes,
    grad_mixed,
):
    def flat(ref):
        return ref[...].reshape(TOKENS, ref.shape[-1])

    def piece(index):
        return modulation[index : index + 1]

    @pl.when(pl.program_id(0) == 0)
    def _():
        sums[...] = jnp.zeros_like(sums)

    def add(row, value):
        sums[pl.ds(row, 1)] += value

    frames = FRAME_PART * RANKS
    state = f32(flat(state_in))
    normed_two, inverse_two = standardise(state)
    act_two[0] = bf16(normed_two * (1.0 + piece(4)) + piece(3))
    qkv[...] = bf16(dot(act_two[0], w_qkv[...]))
    row_cell = lax.rem(lax.broadcasted_iota(jnp.int32, (TOKENS, TOKENS), 0), CHUNK_CELLS)
    column_cell = lax.rem(lax.broadcasted_iota(jnp.int32, (TOKENS, TOKENS), 1), CHUNK_CELLS)
    valid = row_cell == column_cell
    row_heads_forward(qkv, mixed.at[0], valid, probs)
    temporal = dot(mixed[0], w_out[...]) + b_out[...]
    state_two = state + piece(5) * temporal
    normed_three, inverse_three = standardise(state_two)
    act_three[0] = bf16(normed_three * (1.0 + piece(7)) + piece(6))
    branch = jnp.zeros((TOKENS, D), jnp.float32) + b_down[...]
    for block in range(FF // D):
        lanes = pl.ds(block * D, D)
        lifted = dot(act_three[0], w_up[:, lanes]) + b_up[block : block + 1]
        square = lifted * lifted
        curve = jnp.tanh(0.7978845608028654 * lifted * (1.0 + 0.044715 * square))
        half = 0.5 * (1.0 + curve)
        hidden[0, :, lanes] = bf16(lifted * half)
        slopes[:, lanes] = half + 0.5 * lifted * (1.0 - curve * curve) * (
            0.7978845608028654 * (1.0 + 3.0 * 0.044715 * square)
        )
        branch += dot(hidden[0, :, lanes], w_down[lanes, :])
    layer_out[...] = bf16(state_two + piece(8) * branch).reshape(frames, CHUNK_CELLS, D)
    seed = f32(flat(loss_in)) * flat(mask_in)
    add(8, column_sum(seed * branch))
    low_branch = bf16(piece(8) * seed)
    grad_branch[0] = low_branch
    add(13, column_sum(f32(low_branch)))
    grad_act = jnp.zeros((TOKENS, D), jnp.float32)
    for block in range(FF // D):
        lanes = pl.ds(block * D, D)
        low_lifted = bf16(dot_nt(grad_branch[0], w_down[lanes, :]) * slopes[:, lanes])
        grad_lifted[0, :, lanes] = low_lifted
        add(9 + block, column_sum(f32(low_lifted)))
        grad_act += dot_nt(grad_lifted[0, :, lanes], w_up[:, lanes])
    add(6, column_sum(grad_act))
    add(7, column_sum(grad_act * normed_three))
    grad_state_two = seed + standard_back(normed_three, inverse_three, grad_act * (1.0 + piece(7)))
    add(5, column_sum(grad_state_two * temporal))
    low_temporal = bf16(piece(5) * grad_state_two)
    grad_temporal[0] = low_temporal
    add(14, column_sum(f32(low_temporal)))
    grad_mixed[...] = bf16(dot_nt(low_temporal, w_out[...]))
    row_heads_backward(qkv, grad_mixed, grad_qkv.at[0], valid, probs)
    grad_act_two = dot_nt(grad_qkv[0], w_qkv[...])
    add(3, column_sum(grad_act_two))
    add(4, column_sum(grad_act_two * normed_two))
    grad_state[...] = bf16(
        grad_state_two + standard_back(normed_two, inverse_two, grad_act_two * (1.0 + piece(4)))
    ).reshape(frames, CHUNK_CELLS, D)


def time_section(state, loss_grad, mask, modulation, w_qkv, w_out, b_out, w_up, b_up, w_down, b_down):
    low = jnp.bfloat16
    frames = FRAME_PART * RANKS

    def whole(array):
        return pl.BlockSpec(array.shape, lambda i: (0,) * array.ndim, pipeline_mode=pl.Buffered(1))

    def cells(width):
        return pl.BlockSpec((frames, CHUNK_CELLS, width), lambda i: (0, i, 0))

    def rows(width):
        return pl.BlockSpec((1, TOKENS, width), lambda i: (i, 0, 0))

    widths = (D, 3 * D, D, D, D, FF, FF, D)
    return pl.pallas_call(
        time_body,
        grid=(CHUNKS,),
        out_shape=(
            jax.ShapeDtypeStruct((frames, CELL_PART, D), low),
            jax.ShapeDtypeStruct((frames, CELL_PART, D), low),
        )
        + tuple(jax.ShapeDtypeStruct((CHUNKS, TOKENS, width), low) for width in widths)
        + (jax.ShapeDtypeStruct((16, D), jnp.float32),),
        in_specs=[cells(D), cells(D), cells(1)]
        + [whole(array) for array in (modulation, w_qkv, w_out, b_out, w_up, b_up, w_down, b_down)],
        out_specs=(cells(D), cells(D))
        + tuple(rows(width) for width in widths)
        + (pl.BlockSpec((16, D), lambda i: (0, 0)),),
        scratch_shapes=[
            pltpu.VMEM((HEADS, TOKENS, TOKENS), jnp.float32),
            pltpu.VMEM((TOKENS, 3 * D), low),
            pltpu.VMEM((TOKENS, FF), jnp.float32),
            pltpu.VMEM((TOKENS, D), low),
        ],
        compiler_params=pltpu.CompilerParams(vmem_limit_bytes=56 * 1024 * 1024),
        cost_estimate=pl.CostEstimate(flops=40 * 10**9, bytes_accessed=50 * 10**6, transcendentals=6 * 10**6),
        name="time_section",
    )(state, loss_grad, mask, modulation, w_qkv, w_out, b_out, w_up, b_up, w_down, b_down)


UNITS = 16
ROWS = D // RANKS
LOOSE = 8
RING = 4


def tail_body(
    arrived,
    grad_in,
    qkv,
    mixed,
    act_two,
    grad_qkv_two,
    mixed_two,
    grad_temporal,
    act_three,
    grad_lifted,
    hidden,
    grad_branch,
    valid,
    modulation,
    sums_in,
    w_qkv,
    w_out,
    b_out,
    grad_home,
    totals,
    gathered,
    x_scr,
    state_scr,
    qkv_scr,
    mixed_scr,
    spatial_scr,
    home_scr,
    wqkv_scr,
    wout_scr,
    hidden_scr,
    branch_scr,
    left_scr,
    right_scr,
    grad_mixed,
    own,
    total,
    core_in,
    x_in,
    y_in,
    edge_in,
    middle_in,
    sums,
    sums_in_scr,
    load_sem,
    frame_sem,
    side_sem,
    home_send,
    home_recv,
    unit_send,
    unit_recv,
    sum_send,
    sum_recv,
):
    slot = lax.axis_index("dp")
    rank = lax.axis_index("seq")
    core = lax.rem(rank, 2)
    over_x = rank // 2
    over_y = lax.rem(slot, 2)
    over_z = slot // 2
    at_edge = jnp.logical_or(over_z == 0, over_z == 3)
    low_side = over_z < 2
    core_peer = (slot, rank + 1 - 2 * core)
    x_peer = (slot, lax.rem(rank + 2, RANKS))
    y_peer = (slot + 1 - 2 * over_y, rank)
    inner_peer = (jnp.where(low_side, 2, 4) + over_y, rank)
    middle_peer = (jnp.where(low_side, 4, 2) + over_y, rank)
    outer_peer = (jnp.where(low_side, 0, 6) + over_y, rank)

    def piece(index):
        return modulation[index : index + 1]

    def remote(source, target, send, recv, peer):
        return pltpu.make_async_remote_copy(
            src_ref=source, dst_ref=target, send_sem=send, recv_sem=recv, device_id=peer, device_id_type=MESH
        )

    def half_rows(which):
        return pl.ds(pl.multiple_of(which * (ROWS // 2), ROWS // 2), ROWS // 2)


    def core_copy(unit):
        spot, place = lax.rem(unit, LOOSE), lax.rem(unit, RING)
        return remote(own.at[spot, 1 - core], core_in.at[place], unit_send.at[0, spot], unit_recv.at[0, spot], core_peer)

    def x_copy(unit):
        spot, place = lax.rem(unit, LOOSE), lax.rem(unit, RING)
        return remote(
            own.at[spot, core, 1 - over_x], x_in.at[place], unit_send.at[1, spot], unit_recv.at[1, spot], x_peer
        )

    def y_copy(unit):
        spot, place = lax.rem(unit, LOOSE), lax.rem(unit, RING)
        return remote(
            own.at[spot, core, over_x, half_rows(1 - over_y)],
            y_in.at[place],
            unit_send.at[2, spot],
            unit_recv.at[2, spot],
            y_peer,
        )

    def edge_copy(unit):
        spot, place = lax.rem(unit, LOOSE), lax.rem(unit, RING)
        return remote(
            own.at[spot, core, over_x, half_rows(over_y)],
            edge_in.at[place],
            unit_send.at[3, spot],
            unit_recv.at[3, spot],
            inner_peer,
        )

    def middle_copy(unit):
        spot, place = lax.rem(unit, LOOSE), lax.rem(unit, RING)
        return remote(
            own.at[spot, core, over_x, half_rows(over_y)],
            middle_in.at[place],
            unit_send.at[3, spot],
            unit_recv.at[4, spot],
            middle_peer,
        )

    def outer_copy(unit):
        spot, place = lax.rem(unit, LOOSE), lax.rem(unit, RING)
        return remote(
            total.at[spot], middle_in.at[place], unit_send.at[4, spot], unit_recv.at[4, spot], outer_peer
        )

    def share_copy(unit, source):
        spot = lax.rem(unit, LOOSE)
        return remote(
            source, totals.at[unit, half_rows(over_y)], unit_send.at[5, spot], unit_recv.at[5, spot], y_peer
        )

    def keep_copy(unit, source):
        spot = lax.rem(unit, LOOSE)
        return pltpu.make_async_copy(source, totals.at[unit, half_rows(over_y)], unit_send.at[6, spot])

    def stage_one(unit):
        spot, place = lax.rem(unit, LOOSE), lax.rem(unit, RING)
        core_copy(unit).wait_recv()
        own[spot, core] = bf16(f32(own[spot, core]) + f32(core_in[place]))
        x_copy(unit).start()

    def stage_two(unit):
        spot, place = lax.rem(unit, LOOSE), lax.rem(unit, RING)
        x_copy(unit).wait_recv()
        own[spot, core, over_x] = bf16(f32(own[spot, core, over_x]) + f32(x_in[place]))
        y_copy(unit).start()

    def stage_three(unit):
        spot, place = lax.rem(unit, LOOSE), lax.rem(unit, RING)
        y_copy(unit).wait_recv()
        rows = half_rows(over_y)
        own[spot, core, over_x, rows] = bf16(f32(own[spot, core, over_x, rows]) + f32(y_in[place]))

        @pl.when(at_edge)
        def _():
            edge_copy(unit).start()

    def stage_four(unit):
        spot, place = lax.rem(unit, LOOSE), lax.rem(unit, RING)

        @pl.when(jnp.logical_not(at_edge))
        def _():
            edge_copy(unit).wait_recv()
            rows = half_rows(over_y)
            own[spot, core, over_x, rows] = bf16(f32(own[spot, core, over_x, rows]) + f32(edge_in[place]))
            middle_copy(unit).start()

    def stage_five(unit):
        spot, place = lax.rem(unit, LOOSE), lax.rem(unit, RING)

        @pl.when(jnp.logical_not(at_edge))
        def _():
            middle_copy(unit).wait_recv()
            rows = half_rows(over_y)
            total[spot] = bf16(f32(own[spot, core, over_x, rows]) + f32(middle_in[place]))
            outer_copy(unit).start()
            share_copy(unit, total.at[spot]).start()
            keep_copy(unit, total.at[spot]).start()

    def stage_six(unit):
        place = lax.rem(unit, RING)

        @pl.when(at_edge)
        def _():
            middle_copy(unit).wait_recv()
            share_copy(unit, middle_in.at[place]).start()
            keep_copy(unit, middle_in.at[place]).start()

    def stage_seven(unit):
        spot = lax.rem(unit, LOOSE)
        core_copy(unit).wait_send()
        x_copy(unit).wait_send()
        y_copy(unit).wait_send()
        middle_copy(unit).wait_send()

        @pl.when(jnp.logical_not(at_edge))
        def _():
            outer_copy(unit).wait_send()

        share_copy(unit, total.at[spot]).wait()
        keep_copy(unit, total.at[spot]).wait()

    stages = (
        lambda unit: core_copy(unit).start(),
        stage_one,
        stage_two,
        stage_three,
        stage_four,
        stage_five,
        stage_six,
        stage_seven,
    )

    def advance(time):
        for lag in reversed(range(len(stages))):
            unit = time - lag

            @pl.when(jnp.logical_and(unit >= 0, unit < UNITS))
            def _():
                stages[lag](unit)


    def put_unit(unit, block):
        spot = lax.rem(unit, LOOSE)
        for quarter in range(RANKS):
            own[spot, quarter % 2, quarter // 2] = bf16(block[quarter * ROWS : (quarter + 1) * ROWS])

    def unit_loads(unit, action):
        spot = lax.rem(unit, 2)

        def pull(left, right, column):
            lanes = pl.ds(pl.multiple_of(column * D, D), D)
            action(pltpu.make_async_copy(left, left_scr.at[spot], load_sem.at[0, spot]))
            action(pltpu.make_async_copy(right.at[:, lanes], right_scr.at[spot], load_sem.at[1, spot]))

        @pl.when(unit < 8)
        def _():
            pull(act_three, grad_lifted, unit - 4)

        @pl.when(jnp.logical_and(unit >= 8, unit < 11))
        def _():
            pull(act_two, grad_qkv_two, unit - 8)

        @pl.when(unit == 11)
        def _():
            pull(mixed_two, grad_temporal, 0)

    def unit_early(unit):
        spot = lax.rem(unit, 2)
        unit_loads(unit, lambda copy: copy.wait())

        @pl.when(unit < 11)
        def _():
            unit_loads(unit + 1, lambda copy: copy.start())

        put_unit(unit, dot_tn(left_scr[spot], right_scr[spot]))


    def add(row, value):
        sums[pl.ds(row, 1)] += value

    def frame_loads(frame):
        return (
            pltpu.make_async_copy(arrived.at[frame], x_scr.at[frame], frame_sem.at[0, frame]),
            pltpu.make_async_copy(grad_in.at[frame], state_scr.at[frame], frame_sem.at[1, frame]),
            pltpu.make_async_copy(qkv.at[frame], qkv_scr.at[frame], frame_sem.at[2, frame]),
            pltpu.make_async_copy(mixed.at[frame], mixed_scr.at[frame], frame_sem.at[3, frame]),
        )

    def home_copy(frame, hop):
        peer = lax.rem(slot + hop, CLIPS)
        rows = pl.ds(pl.multiple_of(peer * CELL_HOME, CELL_HOME), CELL_HOME)
        return remote(
            home_scr.at[frame, rows],
            grad_home.at[slot, frame],
            home_send.at[frame, hop],
            home_recv.at[frame, hop],
            (peer, rank),
        )

    def home_keep(frame):
        rows = pl.ds(pl.multiple_of(slot * CELL_HOME, CELL_HOME), CELL_HOME)
        return pltpu.make_async_copy(home_scr.at[frame, rows], grad_home.at[slot, frame], home_recv.at[frame, 0])

    def frame_first(frame):
        for load in frame_loads(frame):
            load.wait()
        grad_state = f32(state_scr[frame])
        spatial = dot(mixed_scr[frame], wout_scr[...]) + b_out[...]
        add(2, column_sum(grad_state * spatial))
        low_spatial = bf16(piece(2) * grad_state)
        spatial_scr[frame] = low_spatial
        add(15, column_sum(f32(low_spatial)))
        grad_mixed[...] = bf16(dot_nt(low_spatial, wout_scr[...]))
        pairs = range(HEADS // 4)
        heads_backward(
            qkv_scr.at[frame], grad_mixed, qkv_scr.at[frame], valid[...] > 0.5, SPACE_BLOCKS, True, pairs=pairs
        )

    def frame_second(frame):
        pairs = range(HEADS // 4, HEADS // 2)
        heads_backward(
            qkv_scr.at[frame], grad_mixed, qkv_scr.at[frame], valid[...] > 0.5, SPACE_BLOCKS, True, pairs=pairs
        )
        grad_act = dot_nt(qkv_scr[frame], wqkv_scr[...])
        normed, inverse = standardise(f32(x_scr[frame]))
        x_scr[frame] = bf16(normed * (1.0 + piece(1)) + piece(0))
        add(0, column_sum(grad_act))
        add(1, column_sum(grad_act * normed))
        home_scr[frame] = bf16(
            f32(state_scr[frame]) + standard_back(normed, inverse, grad_act * (1.0 + piece(1)))
        )
        for hop in range(1, CLIPS):
            home_copy(frame, hop).start()
        home_keep(frame).start()


    def sum_exchange(step):
        peer = core_peer if step == 0 else x_peer
        return remote(sums, sums_in_scr.at[step], sum_send.at[step], sum_recv.at[step], peer)

    def sum_add(step):
        sum_exchange(step).wait()
        sums[...] = sums[...] + sums_in_scr[step]

    def sum_spread(hop):
        peer = lax.rem(slot + hop, CLIPS)
        return remote(sums, gathered.at[slot], sum_send.at[1 + hop], sum_recv.at[1 + hop], (peer, rank))

    def sum_keep():
        return pltpu.make_async_copy(sums, gathered.at[slot], sum_send.at[9])


    weights = (
        pltpu.make_async_copy(hidden, hidden_scr, side_sem.at[0]),
        pltpu.make_async_copy(grad_branch, branch_scr, side_sem.at[1]),
        pltpu.make_async_copy(w_qkv, wqkv_scr, side_sem.at[2]),
        pltpu.make_async_copy(w_out, wout_scr, side_sem.at[3]),
    )
    for copy in weights:
        copy.start()
    for load in frame_loads(0):
        load.start()
    unit_loads(4, lambda copy: copy.start())
    for frame in range(1, FRAME_PART):
        for load in frame_loads(frame):
            load.start()
    sums[...] = sums_in[...]
    weights[0].wait()
    weights[1].wait()
    for double in range(2):
        columns = dot_tn(branch_scr[:, pl.ds(double * 2 * ROWS, 2 * ROWS)], hidden_scr[...])
        for part in range(2):
            unit = 2 * double + part
            for quarter in range(RANKS):
                own[unit, quarter % 2, quarter // 2] = bf16(
                    columns[part * ROWS : (part + 1) * ROWS, quarter * D : (quarter + 1) * D]
                )
        advance(2 * double)
        advance(2 * double + 1)
    weights[2].wait()
    weights[3].wait()

    def frame_step(frame, carry):
        unit = 4 + 2 * frame
        frame_first(frame)
        unit_early(unit)
        advance(unit)
        frame_second(frame)
        unit_early(unit + 1)
        advance(unit + 1)
        return carry

    lax.fori_loop(0, FRAME_PART, frame_step, 0)
    sum_exchange(0).start()

    def late_step(column, carry):
        lanes = pl.ds(pl.multiple_of(column * D, D), D)
        left = x_scr[...].reshape(FRAME_PART * CELLS, D)
        right = qkv_scr[:, :, lanes].reshape(FRAME_PART * CELLS, D)
        put_unit(12 + column, dot_tn(left, right))
        advance(12 + column)
        return carry

    lax.fori_loop(0, 3, late_step, 0)
    put_unit(
        15,
        dot_tn(
            mixed_scr[...].reshape(FRAME_PART * CELLS, D), spatial_scr[...].reshape(FRAME_PART * CELLS, D)
        ),
    )
    advance(15)
    sum_add(0)
    sum_exchange(1).start()
    advance(16)
    sum_add(1)
    for hop in range(1, CLIPS):
        sum_spread(hop).start()
    sum_keep().start()

    def drain(time, carry):
        advance(time)
        return carry

    lax.fori_loop(17, UNITS + len(stages) - 1, drain, 0)
    for hop in range(1, CLIPS):
        sum_spread(hop).wait()
    sum_keep().wait()

    def frame_end(frame, carry):
        for hop in range(1, CLIPS):
            home_copy(frame, hop).wait()
        home_keep(frame).wait()
        return carry

    lax.fori_loop(0, FRAME_PART, frame_end, 0)


def tail_section(saved, valid, modulation, sums, w_qkv, w_out, b_out):
    low = jnp.bfloat16
    tokens = FRAME_PART * CELLS
    return pl.pallas_call(
        tail_body,
        out_shape=(
            jax.ShapeDtypeStruct((CLIPS, FRAME_PART, CELL_HOME, D), low),
            jax.ShapeDtypeStruct((UNITS, ROWS, D), low),
            jax.ShapeDtypeStruct((CLIPS, 16, D), jnp.float32),
        ),
        in_specs=[ANY] * 12 + [VMEM] * 3 + [ANY] * 2 + [VMEM],
        out_specs=(ANY, ANY, ANY),
        scratch_shapes=[
            pltpu.VMEM((FRAME_PART, CELLS, D), low),
            pltpu.VMEM((FRAME_PART, CELLS, D), low),
            pltpu.VMEM((FRAME_PART, CELLS, 3 * D), low),
            pltpu.VMEM((FRAME_PART, CELLS, D), low),
            pltpu.VMEM((FRAME_PART, CELLS, D), low),
            pltpu.VMEM((FRAME_PART, CELLS, D), low),
            pltpu.VMEM((D, 3 * D), low),
            pltpu.VMEM((D, D), low),
            pltpu.VMEM((tokens, FF), low),
            pltpu.VMEM((tokens, D), low),
            pltpu.VMEM((2, tokens, D), low),
            pltpu.VMEM((2, tokens, D), low),
            pltpu.VMEM((CELLS, D), low),
            pltpu.VMEM((LOOSE, 2, 2, ROWS, D), low),
            pltpu.VMEM((LOOSE, ROWS // 2, D), low),
            pltpu.VMEM((RING, 2, ROWS, D), low),
            pltpu.VMEM((RING, ROWS, D), low),
            pltpu.VMEM((RING, ROWS // 2, D), low),
            pltpu.VMEM((RING, ROWS // 2, D), low),
            pltpu.VMEM((RING, ROWS // 2, D), low),
            pltpu.VMEM((16, D), jnp.float32),
            pltpu.VMEM((2, 16, D), jnp.float32),
            pltpu.SemaphoreType.DMA((2, 2)),
            pltpu.SemaphoreType.DMA((4, FRAME_PART)),
            pltpu.SemaphoreType.DMA((4,)),
            pltpu.SemaphoreType.DMA((FRAME_PART, CLIPS)),
            pltpu.SemaphoreType.DMA((FRAME_PART, CLIPS)),
            pltpu.SemaphoreType.DMA((7, LOOSE)),
            pltpu.SemaphoreType.DMA((6, LOOSE)),
            pltpu.SemaphoreType.DMA((10,)),
            pltpu.SemaphoreType.DMA((9,)),
        ],
        compiler_params=pltpu.CompilerParams(has_side_effects=True, vmem_limit_bytes=60 * 1024 * 1024),
        cost_estimate=pl.CostEstimate(flops=30 * 10**9, bytes_accessed=60 * 10**6, transcendentals=3 * 10**6),
        name="tail_section",
    )(*saved, valid, modulation, sums, w_qkv, w_out, b_out)


def per_device_fast(
    tokens,
    condition,
    loss_grad,
    cell_counts,
    frame_tasks,
    destinations,
    w_ada,
    b_ada,
    w_qkv_s,
    w_out_s,
    b_out_s,
    w_qkv_t,
    w_out_t,
    b_out_t,
    w_up,
    b_up,
    w_down,
    b_down,
):
    slot = lax.axis_index("dp")
    rank = lax.axis_index("seq")

    def own(array):
        return lax.dynamic_index_in_dim(array, slot, 0, keepdims=False)

    own_count = own(cell_counts)
    cond_low = bf16(jax.nn.silu(f32(jnp.take(condition, destinations, axis=0))))
    cell_range = jnp.arange(CELLS, dtype=jnp.int32)
    valid = f32(cell_range < own_count)[:, None]
    cell_ids = rank * CELL_PART + jnp.arange(CELL_PART, dtype=jnp.int32)
    mask = f32(jnp.logical_and(own(frame_tasks)[:, None] == 1, cell_ids[None, :] < own_count))[:, :, None]
    arrived, qkv_one, mixed_one, cells_in, cells_grad, modulation = space_forward(
        tokens,
        loss_grad,
        jnp.broadcast_to(own(cond_low)[None], (16, D)),
        valid,
        w_ada,
        f32(b_ada).reshape(9, D),
        w_qkv_s,
        w_out_s,
        f32(b_out_s)[None],
    )
    parts = time_section(
        cells_in,
        cells_grad,
        mask,
        modulation,
        w_qkv_t,
        w_out_t,
        f32(b_out_t)[None],
        w_up,
        f32(b_up).reshape(FF // D, D),
        w_down,
        f32(b_down)[None],
    )
    result, grad_state, sums = parts[0], parts[1], parts[-1]
    grad_frames = lax.all_to_all(grad_state, "seq", split_axis=0, concat_axis=1, tiled=True)
    frames_out = lax.all_to_all(result, "seq", split_axis=0, concat_axis=1, tiled=True)
    layer_out = lax.all_to_all(frames_out[None], "dp", split_axis=2, concat_axis=0, tiled=True)
    saved = [arrived, grad_frames, qkv_one, mixed_one]
    saved += [part.reshape(CHUNKS * TOKENS, part.shape[-1]) for part in parts[2:-1]]
    grad_tokens, totals, gathered = tail_section(saved, valid, modulation, sums, w_qkv_s, w_out_s, f32(b_out_s)[None])
    wide = f32(totals)

    def side(first, count):
        return jnp.concatenate([wide[first + part] for part in range(count)], axis=1)

    grad_w_down = wide[0:4].reshape(D, D).T
    grad_mod = gathered[:, :9].reshape(CLIPS, 9 * D)
    own_cond = lax.dynamic_slice_in_dim(cond_low, rank * ROWS, ROWS, axis=1)
    grad_w_ada = lax.dot_general(
        f32(own_cond), grad_mod, (((0,), (0,)), ((), ())), preferred_element_type=jnp.float32
    )
    sums_all = jnp.sum(gathered, axis=0)
    grad_b_ada = lax.dynamic_slice_in_dim(sums_all[:9].reshape(9 * D), rank * 9 * ROWS, 9 * ROWS)
    grad_b_up = lax.dynamic_index_in_dim(sums_all[9:13], rank, 0, keepdims=False)

    def quarter(row):
        return lax.dynamic_slice_in_dim(sums_all[row], rank * ROWS, ROWS)

    return (
        layer_out,
        grad_tokens,
        grad_w_ada,
        grad_b_ada,
        side(12, 3),
        wide[15],
        quarter(15),
        side(8, 3),
        wide[11],
        quarter(14),
        side(4, 4),
        grad_b_up,
        grad_w_down,
        quarter(13),
    )


def solution(mesh):
    placed = (
        P(None, "seq", "dp", None),
        P(),
        P(None, "seq", "dp", None),
        P(),
        P(),
        P(),
        P(),
        P(),
        P(),
        P(),
        P(),
        P(),
        P(),
        P(),
        P(),
        P(),
        P(),
        P(),
    )
    fast = mesh.shape["dp"] == 8 and mesh.shape["seq"] == 4
    return jax.shard_map(
        per_device_fast if fast else per_device_general,
        mesh=mesh,
        in_specs=placed,
        out_specs=(
            P(None, "seq", "dp", None),
            P(None, "seq", "dp", None),
            P("seq", None),
            P("seq"),
            P("seq", None),
            P("seq", None),
            P("seq"),
            P("seq", None),
            P("seq", None),
            P("seq"),
            P("seq", None),
            P("seq"),
            P("seq", None),
            P("seq"),
        ),
        check_vma=False,
    )
```

```python
import jax
import jax.numpy as jnp
from jax import lax
from jax.experimental import pallas as pl
from jax.experimental.pallas import tpu as pltpu
from jax.sharding import PartitionSpec as P

D = 768
HEADS = 12
HEAD = 64


def standard(field):
    centred = field - jnp.mean(field, axis=-1, keepdims=True)
    inverse = lax.rsqrt(jnp.mean(centred * centred, axis=-1, keepdims=True) + 1e-06)
    return (centred * inverse, inverse)


def standard_back(normed, inverse, grad_normed):
    return inverse * (
        grad_normed
        - jnp.mean(grad_normed, axis=-1, keepdims=True)
        - normed * jnp.mean(grad_normed * normed, axis=-1, keepdims=True)
    )


def gelu_back(lifted, grad_hidden):
    return jax.vjp(lambda inner: jax.nn.gelu(inner, approximate=True), lifted)[1](grad_hidden)[0]


def attend(triple, key_valid, einsum_forms):
    queries = triple[:, :, 0]
    key_rows = triple[:, :, 1]
    value_rows = triple[:, :, 2]
    scores = (
        jnp.einsum(einsum_forms[0], queries, key_rows, preferred_element_type=jnp.float32) * 0.125
    )
    scores = jnp.where(key_valid, scores, -1e30)
    row_top = jnp.max(scores, axis=-1, keepdims=True)
    exponent = jnp.exp(scores - row_top)
    probs_full = exponent / jnp.sum(exponent, axis=-1, keepdims=True)
    probs_low = probs_full.astype(jnp.bfloat16)
    mixed_out = jnp.einsum(
        einsum_forms[1], probs_low, value_rows, preferred_element_type=jnp.float32
    ).astype(jnp.bfloat16)
    return (mixed_out, probs_full, probs_low)


def attend_back(triple, probs_full, probs_low, grad_mixed, einsum_forms):
    queries = triple[:, :, 0]
    key_rows = triple[:, :, 1]
    value_rows = triple[:, :, 2]
    grad_probs = jnp.einsum(
        einsum_forms[0], grad_mixed, value_rows, preferred_element_type=jnp.float32
    )
    row_delta = jnp.sum(probs_full * grad_probs, axis=-1, keepdims=True)
    grad_scores = (probs_full * (grad_probs - row_delta)).astype(jnp.bfloat16)
    grad_values = jnp.einsum(
        einsum_forms[2], probs_low, grad_mixed, preferred_element_type=jnp.float32
    )
    grad_queries = (
        jnp.einsum(einsum_forms[1], grad_scores, key_rows, preferred_element_type=jnp.float32)
        * 0.125
    )
    grad_keys = (
        jnp.einsum(einsum_forms[2], grad_scores, queries, preferred_element_type=jnp.float32)
        * 0.125
    )
    return jnp.stack([grad_queries, grad_keys, grad_values], axis=2)


def per_device_general(
    tokens,
    condition,
    loss_grad,
    cell_counts,
    frame_tasks,
    destinations,
    w_ada,
    b_ada,
    w_qkv_s,
    w_out_s,
    b_out_s,
    w_qkv_t,
    w_out_t,
    b_out_t,
    w_up,
    b_up,
    w_down,
    b_down,
):
    groups = lax.axis_size("dp")
    ranks = lax.axis_size("seq")
    own_slot = lax.axis_index("dp")
    own_rank = lax.axis_index("seq")
    frame_part = tokens.shape[1]
    cell_total = tokens.shape[2] * groups
    cell_part = cell_total // ranks
    frame_total = frame_part * ranks
    slot_ids = jnp.arange(groups, dtype=jnp.int32)
    routing = (destinations[None, :] == slot_ids[:, None]).astype(jnp.bfloat16)
    outgoing = jnp.einsum(
        "jc,cfbd->jfbd", routing, tokens, preferred_element_type=jnp.float32
    ).astype(jnp.bfloat16)
    outgoing_grad = jnp.einsum(
        "jc,cfbd->jfbd", routing, loss_grad, preferred_element_type=jnp.float32
    ).astype(jnp.bfloat16)
    arrived, arrived_grad = (
        lax.all_to_all(outgoing, "dp", split_axis=0, concat_axis=2, tiled=True),
        lax.all_to_all(outgoing_grad, "dp", split_axis=0, concat_axis=2, tiled=True),
    )
    own_clip = jnp.sum(jnp.where(destinations == own_slot, slot_ids, 0))
    own_count = jnp.sum(jnp.where(slot_ids == own_clip, cell_counts, 0))
    own_tasks = lax.dynamic_index_in_dim(frame_tasks, own_clip, 0, keepdims=False)
    cond_row = lax.dynamic_index_in_dim(condition, own_slot, 0, keepdims=False)
    cond_low = jax.nn.silu(cond_row.astype(jnp.float32)).astype(jnp.bfloat16)
    modulation = jnp.dot(cond_low[None, :], w_ada, preferred_element_type=jnp.float32)[
        0
    ] + b_ada.astype(jnp.float32)
    pieces = [modulation[piece_index * D : (piece_index + 1) * D] for piece_index in range(9)]
    (
        shift_one,
        scale_one,
        gate_one,
        shift_two,
        scale_two,
        gate_two,
        shift_three,
        scale_three,
        gate_three,
    ) = pieces
    space_forms = ("fphe,fqhe->fhpq", "fhpq,fqhe->fphe", "fhpq,fphe->fqhe")
    frames_in = arrived[0].astype(jnp.float32)
    normed_one, inverse_one = standard(frames_in)
    act_one = (normed_one * (1.0 + scale_one) + shift_one).astype(jnp.bfloat16)
    triple_one = (
        jnp.einsum("fpd,de->fpe", act_one, w_qkv_s, preferred_element_type=jnp.float32)
        .astype(jnp.bfloat16)
        .reshape(frame_part, cell_total, 3, HEADS, HEAD)
    )
    key_valid = (jnp.arange(cell_total, dtype=jnp.int32) < own_count)[None, None, None, :]
    mixed_one, probs_one, low_one = attend(triple_one, key_valid, space_forms)
    flat_one = mixed_one.reshape(frame_part, cell_total, D)
    spatial_out = jnp.einsum(
        "fpd,de->fpe", flat_one, w_out_s, preferred_element_type=jnp.float32
    ) + b_out_s.astype(jnp.float32)
    state_one = (frames_in + gate_one * spatial_out).astype(jnp.bfloat16)
    cells_in, cells_grad = (
        lax.all_to_all(state_one, "seq", split_axis=1, concat_axis=0, tiled=True),
        lax.all_to_all(arrived_grad[0], "seq", split_axis=1, concat_axis=0, tiled=True),
    )
    time_forms = ("fqhe,gqhe->qhfg", "qhfg,gqhe->fqhe", "qhfg,fqhe->gqhe")
    state_cells = cells_in.astype(jnp.float32)
    normed_two, inverse_two = standard(state_cells)
    act_two = (normed_two * (1.0 + scale_two) + shift_two).astype(jnp.bfloat16)
    triple_two = (
        jnp.einsum("fqd,de->fqe", act_two, w_qkv_t, preferred_element_type=jnp.float32)
        .astype(jnp.bfloat16)
        .reshape(frame_total, cell_part, 3, HEADS, HEAD)
    )
    mixed_two, probs_two, low_two = attend(triple_two, True, time_forms)
    flat_two = mixed_two.reshape(frame_total, cell_part, D)
    temporal_out = jnp.einsum(
        "fqd,de->fqe", flat_two, w_out_t, preferred_element_type=jnp.float32
    ) + b_out_t.astype(jnp.float32)
    state_two = state_cells + gate_two * temporal_out
    normed_three, inverse_three = standard(state_two)
    act_three = (normed_three * (1.0 + scale_three) + shift_three).astype(jnp.bfloat16)
    lifted = jnp.einsum(
        "fqd,dk->fqk", act_three, w_up, preferred_element_type=jnp.float32
    ) + b_up.astype(jnp.float32)
    hidden = jax.nn.gelu(lifted, approximate=True).astype(jnp.bfloat16)
    branch_out = jnp.einsum(
        "fqk,kd->fqd", hidden, w_down, preferred_element_type=jnp.float32
    ) + b_down.astype(jnp.float32)
    result = (state_two + gate_three * branch_out).astype(jnp.bfloat16)
    cell_ids = own_rank * cell_part + jnp.arange(cell_part, dtype=jnp.int32)
    loss_mask = jnp.logical_and(own_tasks[:, None] == 1, cell_ids[None, :] < own_count)
    out_grad = cells_grad.astype(jnp.float32) * loss_mask[:, :, None].astype(jnp.float32)
    grad_gate_three = jnp.sum(out_grad * branch_out, axis=(0, 1))
    grad_branch = (gate_three * out_grad).astype(jnp.bfloat16)
    grad_b_down = jnp.sum(grad_branch.astype(jnp.float32), axis=(0, 1))
    grad_w_down = jnp.einsum("fqk,fqd->kd", hidden, grad_branch, preferred_element_type=jnp.float32)
    grad_hidden = jnp.einsum("fqd,kd->fqk", grad_branch, w_down, preferred_element_type=jnp.float32)
    grad_lifted = gelu_back(lifted, grad_hidden).astype(jnp.bfloat16)
    grad_b_up = jnp.sum(grad_lifted.astype(jnp.float32), axis=(0, 1))
    grad_w_up = jnp.einsum(
        "fqd,fqk->dk", act_three, grad_lifted, preferred_element_type=jnp.float32
    )
    grad_act_three = jnp.einsum(
        "fqk,dk->fqd", grad_lifted, w_up, preferred_element_type=jnp.float32
    )
    grad_shift_three = jnp.sum(grad_act_three, axis=(0, 1))
    grad_scale_three = jnp.sum(grad_act_three * normed_three, axis=(0, 1))
    grad_state_two = out_grad + standard_back(
        normed_three, inverse_three, grad_act_three * (1.0 + scale_three)
    )
    grad_gate_two = jnp.sum(grad_state_two * temporal_out, axis=(0, 1))
    grad_temporal = (gate_two * grad_state_two).astype(jnp.bfloat16)
    grad_b_out_t = jnp.sum(grad_temporal.astype(jnp.float32), axis=(0, 1))
    grad_w_out_t = jnp.einsum(
        "fqd,fqe->de", flat_two, grad_temporal, preferred_element_type=jnp.float32
    )
    grad_mixed_two = (
        jnp.einsum("fqe,de->fqd", grad_temporal, w_out_t, preferred_element_type=jnp.float32)
        .astype(jnp.bfloat16)
        .reshape(frame_total, cell_part, HEADS, HEAD)
    )
    grad_triple_two = (
        attend_back(triple_two, probs_two, low_two, grad_mixed_two, time_forms)
        .reshape(frame_total, cell_part, 3 * D)
        .astype(jnp.bfloat16)
    )
    grad_w_qkv_t = jnp.einsum(
        "fqd,fqe->de", act_two, grad_triple_two, preferred_element_type=jnp.float32
    )
    grad_act_two = jnp.einsum(
        "fqe,de->fqd", grad_triple_two, w_qkv_t, preferred_element_type=jnp.float32
    )
    grad_shift_two = jnp.sum(grad_act_two, axis=(0, 1))
    grad_scale_two = jnp.sum(grad_act_two * normed_two, axis=(0, 1))
    grad_state_one = (
        grad_state_two + standard_back(normed_two, inverse_two, grad_act_two * (1.0 + scale_two))
    ).astype(jnp.bfloat16)
    frames_out, frames_grad = (
        lax.all_to_all(result, "seq", split_axis=0, concat_axis=1, tiled=True),
        lax.all_to_all(grad_state_one, "seq", split_axis=0, concat_axis=1, tiled=True),
    )
    grad_frames = frames_grad.astype(jnp.float32)
    grad_gate_one = jnp.sum(grad_frames * spatial_out, axis=(0, 1))
    grad_spatial = (gate_one * grad_frames).astype(jnp.bfloat16)
    grad_b_out_s = jnp.sum(grad_spatial.astype(jnp.float32), axis=(0, 1))
    grad_w_out_s = jnp.einsum(
        "fpd,fpe->de", flat_one, grad_spatial, preferred_element_type=jnp.float32
    )
    grad_mixed_one = (
        jnp.einsum("fpe,de->fpd", grad_spatial, w_out_s, preferred_element_type=jnp.float32)
        .astype(jnp.bfloat16)
        .reshape(frame_part, cell_total, HEADS, HEAD)
    )
    grad_triple_one = (
        attend_back(triple_one, probs_one, low_one, grad_mixed_one, space_forms)
        .reshape(frame_part, cell_total, 3 * D)
        .astype(jnp.bfloat16)
    )
    grad_w_qkv_s = jnp.einsum(
        "fpd,fpe->de", act_one, grad_triple_one, preferred_element_type=jnp.float32
    )
    grad_act_one = jnp.einsum(
        "fpe,de->fpd", grad_triple_one, w_qkv_s, preferred_element_type=jnp.float32
    )
    grad_shift_one = jnp.sum(grad_act_one, axis=(0, 1))
    grad_scale_one = jnp.sum(grad_act_one * normed_one, axis=(0, 1))
    grad_input = (
        grad_frames + standard_back(normed_one, inverse_one, grad_act_one * (1.0 + scale_one))
    ).astype(jnp.bfloat16)
    home_out, home_grad = (
        lax.all_to_all(frames_out[None], "dp", split_axis=2, concat_axis=0, tiled=True),
        lax.all_to_all(grad_input[None], "dp", split_axis=2, concat_axis=0, tiled=True),
    )
    layer_out = jnp.einsum(
        "jc,jfbd->cfbd", routing, home_out, preferred_element_type=jnp.float32
    ).astype(jnp.bfloat16)
    grad_tokens = jnp.einsum(
        "jc,jfbd->cfbd", routing, home_grad, preferred_element_type=jnp.float32
    ).astype(jnp.bfloat16)
    grad_mod = jnp.concatenate(
        [
            grad_shift_one,
            grad_scale_one,
            grad_gate_one,
            grad_shift_two,
            grad_scale_two,
            grad_gate_two,
            grad_shift_three,
            grad_scale_three,
            grad_gate_three,
        ]
    )
    ada_term = cond_low.astype(jnp.float32)[:, None] * grad_mod[None, :]
    partials = (
        lax.psum_scatter(
            ada_term.astype(jnp.bfloat16), "seq", scatter_dimension=0, tiled=True
        ).astype(jnp.float32),
        lax.psum_scatter(
            grad_mod.astype(jnp.bfloat16), "seq", scatter_dimension=0, tiled=True
        ).astype(jnp.float32),
        lax.psum_scatter(
            grad_w_qkv_s.astype(jnp.bfloat16), "seq", scatter_dimension=0, tiled=True
        ).astype(jnp.float32),
        lax.psum_scatter(
            grad_w_out_s.astype(jnp.bfloat16), "seq", scatter_dimension=0, tiled=True
        ).astype(jnp.float32),
        lax.psum_scatter(
            grad_b_out_s.astype(jnp.bfloat16), "seq", scatter_dimension=0, tiled=True
        ).astype(jnp.float32),
        lax.psum_scatter(
            grad_w_qkv_t.astype(jnp.bfloat16), "seq", scatter_dimension=0, tiled=True
        ).astype(jnp.float32),
        lax.psum_scatter(
            grad_w_out_t.astype(jnp.bfloat16), "seq", scatter_dimension=0, tiled=True
        ).astype(jnp.float32),
        lax.psum_scatter(
            grad_b_out_t.astype(jnp.bfloat16), "seq", scatter_dimension=0, tiled=True
        ).astype(jnp.float32),
        lax.psum_scatter(
            grad_w_up.astype(jnp.bfloat16), "seq", scatter_dimension=0, tiled=True
        ).astype(jnp.float32),
        lax.psum_scatter(
            grad_b_up.astype(jnp.bfloat16), "seq", scatter_dimension=0, tiled=True
        ).astype(jnp.float32),
        lax.psum_scatter(
            grad_w_down.astype(jnp.bfloat16), "seq", scatter_dimension=0, tiled=True
        ).astype(jnp.float32),
        lax.psum_scatter(
            grad_b_down.astype(jnp.bfloat16), "seq", scatter_dimension=0, tiled=True
        ).astype(jnp.float32),
    )
    totals = lax.psum(
        (
            partials[0],
            partials[1],
            partials[2],
            partials[3],
            partials[4],
            partials[5],
            partials[6],
            partials[7],
            partials[8],
            partials[9],
            partials[10],
            partials[11],
        ),
        "dp",
    )
    ada_grad = totals[0]
    ada_bias = totals[1]
    rest = totals[2:]
    return (
        layer_out,
        grad_tokens,
        ada_grad,
        ada_bias,
        rest[0],
        rest[1],
        rest[2],
        rest[3],
        rest[4],
        rest[5],
        rest[6],
        rest[7],
        rest[8],
        rest[9],
    )


MESH = pl.DeviceIdType.MESH
ANY = pl.BlockSpec(memory_space=pl.ANY)
VMEM = pl.BlockSpec(memory_space=pltpu.VMEM)
SMEM = pl.BlockSpec(memory_space=pltpu.SMEM)
NEG = -1e30
CLIPS = 8
RANKS = 4
FRAME_PART = 4
CELLS = 256
CELL_HOME = CELLS // CLIPS
CELL_PART = CELLS // RANKS
FF = 3072
TOKENS = 256
CHUNK_CELLS = TOKENS // (FRAME_PART * RANKS)
CHUNKS = CELL_PART // CHUNK_CELLS


def f32(value):
    return value.astype(jnp.float32)


def bf16(value):
    return value.astype(jnp.bfloat16)


def dot(left, right):
    return lax.dot_general(left, right, (((1,), (0,)), ((), ())), preferred_element_type=jnp.float32)


def dot_nt(left, right):
    return lax.dot_general(left, right, (((1,), (1,)), ((), ())), preferred_element_type=jnp.float32)


def dot_tn(left, right):
    return lax.dot_general(left, right, (((0,), (0,)), ((), ())), preferred_element_type=jnp.float32)


def standardise(field):
    centred = field - jnp.mean(field, axis=-1, keepdims=True)
    inverse = lax.rsqrt(jnp.mean(centred * centred, axis=-1, keepdims=True) + 1e-06)
    return centred * inverse, inverse


def column_sum(field):
    return jnp.sum(field, axis=0, keepdims=True)


def row_heads_forward(qkv, mixed, valid, probs=None):
    lane = lax.broadcasted_iota(jnp.int32, (1, 2 * HEAD), 1) < HEAD
    for pair in range(HEADS // 2):
        lanes = pl.ds(pair * 2 * HEAD, 2 * HEAD)
        queries = qkv[:, pl.ds(pair * 2 * HEAD, 2 * HEAD)] * jnp.bfloat16(0.125)
        keys = qkv[:, pl.ds(D + pair * 2 * HEAD, 2 * HEAD)]
        values = qkv[:, pl.ds(2 * D + pair * 2 * HEAD, 2 * HEAD)]
        parts = []
        for half in range(2):
            mine = lane if half == 0 else jnp.logical_not(lane)
            scores = dot_nt(jnp.where(mine, queries, jnp.bfloat16(0)), keys)
            scores = jnp.where(valid, scores, NEG)
            exponent = jnp.exp(scores - jnp.max(scores, axis=-1, keepdims=True))
            full = exponent * (1.0 / jnp.sum(exponent, axis=-1, keepdims=True))
            if probs is not None:
                probs[2 * pair + half] = full
            parts.append(dot(bf16(full), values))
        mixed[:, lanes] = bf16(jnp.where(lane, parts[0], parts[1]))


def head_probs(queries, keys, mine, valid):
    scores = dot_nt(jnp.where(mine, queries, jnp.bfloat16(0)), keys)
    scores = jnp.where(valid, scores, NEG)
    exponent = jnp.exp(scores - jnp.max(scores, axis=-1, keepdims=True))
    return exponent * (1.0 / jnp.sum(exponent, axis=-1, keepdims=True))


def row_heads_backward(qkv, grad_mixed, grad_qkv, valid, probs=None):
    lane = lax.broadcasted_iota(jnp.int32, (1, 2 * HEAD), 1) < HEAD
    for pair in range(HEADS // 2):
        places = [pl.ds(part * D + pair * 2 * HEAD, 2 * HEAD) for part in range(3)]
        queries = qkv[:, places[0]] * jnp.bfloat16(0.125)
        keys = qkv[:, places[1]]
        values = qkv[:, places[2]]
        grads = grad_mixed[:, places[0]]
        parts = []
        for half in range(2):
            mine = lane if half == 0 else jnp.logical_not(lane)
            if probs is None:
                full = head_probs(queries, keys, mine, valid)
            else:
                full = probs[2 * pair + half]
            grad_probs = dot_nt(jnp.where(mine, grads, jnp.bfloat16(0)), values)
            weighted = full * grad_probs
            grad_scores = bf16(weighted - full * jnp.sum(weighted, axis=-1, keepdims=True))
            parts.append((dot(grad_scores, keys), dot_tn(grad_scores, queries), dot_tn(bf16(full), grads)))
        grad_qkv[:, places[0]] = bf16(jnp.where(lane, parts[0][0], parts[1][0]) * 0.125)
        grad_qkv[:, places[1]] = bf16(jnp.where(lane, parts[0][1], parts[1][1]))
        grad_qkv[:, places[2]] = bf16(jnp.where(lane, parts[0][2], parts[1][2]))


def head_halves(rows):
    lane = lax.broadcasted_iota(jnp.int32, (1, 2 * HEAD), 1) < HEAD
    zero = jnp.bfloat16(0)
    return jnp.where(lane, rows, zero), jnp.where(lane, zero, rows)


def column_probs(keys, queries, valid):
    scores = jnp.where(valid, dot_nt(keys, queries), NEG)
    exponent = jnp.exp(scores - jnp.max(scores, axis=0, keepdims=True))
    return exponent * (1.0 / jnp.sum(exponent, axis=0, keepdims=True))


def heads_forward(qkv, mixed, valid, blocks, probs=None):
    for pair in range(HEADS // 2):
        places = [pl.ds(part * D + pair * 2 * HEAD, 2 * HEAD) for part in range(3)]
        queries = qkv[:, places[0]] * jnp.bfloat16(0.125)
        keys = head_halves(qkv[:, places[1]])
        turned = qkv[:, places[2]].T
        for spot, (ours, theirs) in enumerate(blocks):
            parts = []
            for half in range(2):
                full = column_probs(keys[half][theirs], queries[ours], valid)
                if probs is not None:
                    probs[2 * pair + half, spot] = full
                parts.append(dot(turned[half * HEAD : (half + 1) * HEAD, theirs], bf16(full)))
            mixed[ours, places[0]] = bf16(jnp.concatenate(parts, axis=0)).T


def heads_backward(qkv, grad_mixed, grad_qkv, valid, blocks, shared, probs=None, pairs=range(HEADS // 2)):
    lane = lax.broadcasted_iota(jnp.int32, (1, 2 * HEAD), 1) < HEAD
    for pair in pairs:
        places = [pl.ds(part * D + pair * 2 * HEAD, 2 * HEAD) for part in range(3)]
        queries = qkv[:, places[0]] * jnp.bfloat16(0.125)
        keys = qkv[:, places[1]]
        turned = keys.T
        keys = head_halves(keys)
        values = head_halves(qkv[:, places[2]])
        grads = grad_mixed[:, places[0]]
        sums = None
        for spot, (ours, theirs) in enumerate(blocks):
            across, downs = [], []
            for half in range(2):
                if probs is None:
                    full = column_probs(keys[half][theirs], queries[ours], valid)
                else:
                    full = probs[2 * pair + half, spot]
                weighted = full * dot_nt(values[half][theirs], grads[ours])
                grad_scores = bf16(weighted - full * jnp.sum(weighted, axis=0, keepdims=True))
                across.append(dot(turned[half * HEAD : (half + 1) * HEAD, theirs], grad_scores))
                downs.append((dot(grad_scores, queries[ours]), dot(bf16(full), grads[ours])))
            grad_qkv[ours, places[0]] = bf16(jnp.concatenate(across, axis=0) * 0.125).T
            downs = [jnp.where(lane, downs[0][part], downs[1][part]) for part in range(2)]
            if shared:
                sums = downs if sums is None else [sums[part] + downs[part] for part in range(2)]
            else:
                for part in range(2):
                    grad_qkv[theirs, places[1 + part]] = bf16(downs[part])
        if shared:
            for part in range(2):
                grad_qkv[:, places[1 + part]] = bf16(sums[part])


BLOCK = 256
SPACE_BLOCKS = [(slice(spot, spot + BLOCK), slice(0, CELLS)) for spot in range(0, CELLS, BLOCK)]


def space_forward_body(
    destinations,
    cell_counts,
    tokens,
    loss_grad,
    condition,
    biases,
    w_ada,
    w_qkv,
    w_out,
    arrived,
    qkv_all,
    mixed_all,
    state_cells,
    loss_early,
    modulation,
    x_scr,
    ada_scr,
    wqkv_scr,
    wout_scr,
    qkv_scr,
    mixed_scr,
    state_scr,
    local_sem,
    in_send,
    in_recv,
    grad_send,
    grad_recv,
    out_send,
    out_recv,
    save_sem,
):
    slot = lax.axis_index("dp")
    rank = lax.axis_index("seq")

    def arrival(frame, hop):
        peer = lax.rem(slot + hop, CLIPS)
        rows = pl.ds(pl.multiple_of(slot * CELL_HOME, CELL_HOME), CELL_HOME)
        return pltpu.make_async_remote_copy(
            src_ref=tokens.at[peer, frame],
            dst_ref=x_scr.at[frame, rows],
            send_sem=in_send.at[frame, hop],
            recv_sem=in_recv.at[frame, hop],
            device_id=(peer, rank),
            device_id_type=MESH,
        )

    def loss_place():
        return loss_early.at[lax.rem(slot, 2), pl.ds(rank * FRAME_PART, FRAME_PART)]

    def loss_source(hop):
        return loss_grad.at[lax.rem(slot + hop, CLIPS), :, pl.ds(0, CHUNK_CELLS)]

    def loss_spot():
        return grad_recv.at[lax.rem(slot, 2) * RANKS + rank]

    def loss_send(hop):
        return pltpu.make_async_remote_copy(
            src_ref=loss_source(hop),
            dst_ref=loss_place(),
            send_sem=grad_send.at[hop],
            recv_sem=loss_spot(),
            device_id=(lax.rem(slot + hop, CLIPS), slot // 2),
            device_id_type=MESH,
        )

    def loss_keep():
        return pltpu.make_async_copy(loss_source(0), loss_place(), loss_spot())

    def leave(frame, hop):
        peer = lax.rem(rank + hop, RANKS)
        rows = pl.ds(pl.multiple_of(peer * CELL_PART, CELL_PART), CELL_PART)
        return pltpu.make_async_remote_copy(
            src_ref=state_scr.at[frame, rows],
            dst_ref=state_cells.at[rank * FRAME_PART + frame],
            send_sem=out_send.at[frame, hop],
            recv_sem=out_recv.at[frame, hop],
            device_id=(slot, peer),
            device_id_type=MESH,
        )

    def keep(frame):
        rows = pl.ds(pl.multiple_of(rank * CELL_PART, CELL_PART), CELL_PART)
        return pltpu.make_async_copy(
            state_scr.at[frame, rows], state_cells.at[rank * FRAME_PART + frame], out_recv.at[frame, 0]
        )

    def saves(frame):
        return (
            pltpu.make_async_copy(x_scr.at[frame], arrived.at[frame], save_sem.at[frame, 0]),
            pltpu.make_async_copy(qkv_scr.at[frame], qkv_all.at[frame], save_sem.at[frame, 1]),
            pltpu.make_async_copy(mixed_scr.at[frame], mixed_all.at[frame], save_sem.at[frame, 2]),
        )

    own_rows = pl.ds(pl.multiple_of(slot * CELL_HOME, CELL_HOME), CELL_HOME)
    own_copy = pltpu.make_async_copy(tokens.at[slot], x_scr.at[:, own_rows], local_sem.at[0])
    ada_copy = pltpu.make_async_copy(w_ada, ada_scr, local_sem.at[1])
    qkv_copy = pltpu.make_async_copy(w_qkv, wqkv_scr, local_sem.at[2])
    out_copy = pltpu.make_async_copy(w_out, wout_scr, local_sem.at[3])
    for hop in range(1, CLIPS):
        arrival(0, hop).start()
    own_copy.start()
    ada_copy.start()
    for frame in range(1, FRAME_PART):
        for hop in range(1, CLIPS):
            arrival(frame, hop).start()
    qkv_copy.start()
    out_copy.start()
    self_loss = slot // 2 == rank

    row_ids = lax.broadcasted_iota(jnp.int32, (CLIPS, 1), 0)
    cond = column_sum(jnp.where(row_ids == destinations[slot], f32(condition[...]), 0.0))
    cond = jnp.broadcast_to(bf16(cond / (1.0 + jnp.exp(-cond))), (16, D))
    bias_rows = f32(biases[...])
    valid = lax.broadcasted_iota(jnp.int32, (CELLS, 1), 0) < cell_counts[slot]
    ada_copy.wait()
    for piece in range(9):
        row = dot(cond, ada_scr[:, pl.ds(piece * D, D)])[0:1]
        modulation[pl.ds(piece, 1)] = row + bias_rows[piece : piece + 1]
    own_copy.wait()
    qkv_copy.wait()
    out_copy.wait()

    def frame_step(frame, carry):
        for hop in range(1, CLIPS):
            arrival(frame, hop).wait_recv()

        @pl.when(frame == 2)
        def _():
            @pl.when(self_loss)
            def _():
                loss_keep().start()

            @pl.when(jnp.logical_not(self_loss))
            def _():
                loss_send(0).start()

            for hop in range(1, CLIPS):
                loss_send(hop).start()

        x = f32(x_scr[frame])
        centred = x - jnp.mean(x, axis=-1, keepdims=True)
        normed = centred * lax.rsqrt(jnp.mean(centred * centred, axis=-1, keepdims=True) + 1e-06)
        act = bf16(normed * (1.0 + modulation[1:2]) + modulation[0:1])
        qkv_scr[frame] = bf16(dot(act, wqkv_scr[...]))
        heads_forward(qkv_scr.at[frame], mixed_scr.at[frame], valid, SPACE_BLOCKS)
        spatial = dot(mixed_scr[frame], wout_scr[...]) + bias_rows[9:10]
        state_scr[frame] = bf16(f32(x_scr[frame]) + modulation[2:3] * spatial)
        for hop in range(1, RANKS):
            leave(frame, hop).start()
        keep(frame).start()
        for save in saves(frame):
            save.start()
        return carry

    lax.fori_loop(0, FRAME_PART, frame_step, 0)

    def frame_end(frame, carry):
        for hop in range(1, CLIPS):
            arrival(frame, hop).wait_send()
        for hop in range(1, RANKS):
            leave(frame, hop).wait()
        keep(frame).wait()
        for save in saves(frame):
            save.wait()
        return carry

    lax.fori_loop(0, FRAME_PART, frame_end, 0)

    @pl.when(jnp.logical_not(self_loss))
    def _():
        loss_send(0).wait_send()

    for hop in range(1, CLIPS):
        loss_send(hop).wait_send()
    for spot in range(2 * RANKS):
        place = loss_early.at[spot // RANKS, pl.ds((spot % RANKS) * FRAME_PART, FRAME_PART)]
        pltpu.make_async_copy(loss_grad.at[0, :, pl.ds(0, CHUNK_CELLS)], place, grad_recv.at[spot]).wait()


def space_forward(destinations, cell_counts, tokens, loss_grad, condition, biases, w_ada, w_qkv, w_out):
    low = jnp.bfloat16
    return pl.pallas_call(
        space_forward_body,
        out_shape=(
            jax.ShapeDtypeStruct((FRAME_PART, CELLS, D), low),
            jax.ShapeDtypeStruct((FRAME_PART, CELLS, 3 * D), low),
            jax.ShapeDtypeStruct((FRAME_PART, CELLS, D), low),
            jax.ShapeDtypeStruct((FRAME_PART * RANKS, CELL_PART, D), low),
            jax.ShapeDtypeStruct((2, FRAME_PART * RANKS, CHUNK_CELLS, D), low),
            jax.ShapeDtypeStruct((16, D), jnp.float32),
        ),
        in_specs=[SMEM, SMEM, ANY, ANY, VMEM, VMEM, ANY, ANY, ANY],
        out_specs=(ANY, ANY, ANY, ANY, ANY, VMEM),
        scratch_shapes=[
            pltpu.VMEM((FRAME_PART, CELLS, D), low),
            pltpu.VMEM((D, 9 * D), low),
            pltpu.VMEM((D, 3 * D), low),
            pltpu.VMEM((D, D), low),
            pltpu.VMEM((FRAME_PART, CELLS, 3 * D), low),
            pltpu.VMEM((FRAME_PART, CELLS, D), low),
            pltpu.VMEM((FRAME_PART, CELLS, D), low),
            pltpu.SemaphoreType.DMA((4,)),
            pltpu.SemaphoreType.DMA((FRAME_PART, CLIPS)),
            pltpu.SemaphoreType.DMA((FRAME_PART, CLIPS)),
            pltpu.SemaphoreType.DMA((CLIPS,)),
            pltpu.SemaphoreType.DMA((2 * RANKS,)),
            pltpu.SemaphoreType.DMA((FRAME_PART, RANKS)),
            pltpu.SemaphoreType.DMA((FRAME_PART, RANKS)),
            pltpu.SemaphoreType.DMA((FRAME_PART, 3)),
        ],
        compiler_params=pltpu.CompilerParams(has_side_effects=True, vmem_limit_bytes=48 * 1024 * 1024),
        cost_estimate=pl.CostEstimate(flops=8 * 10**9, bytes_accessed=40 * 10**6, transcendentals=3 * 10**6),
        name="space_forward",
    )(destinations, cell_counts, tokens, loss_grad, condition, biases, w_ada, w_qkv, w_out)


def chunk_of(order):
    return 2 * lax.rem(order, 2) + order // 2


def cell_match():
    row_cell = lax.rem(lax.broadcasted_iota(jnp.int32, (TOKENS, TOKENS), 0), CHUNK_CELLS)
    column_cell = lax.rem(lax.broadcasted_iota(jnp.int32, (TOKENS, TOKENS), 1), CHUNK_CELLS)
    return row_cell == column_cell


SAVED_WIDTHS = (D, 3 * D, D, D, D, FF, FF, D)


def time_forward_body(
    cell_counts,
    frame_tasks,
    state_cells,
    loss_grad,
    loss_early,
    modulation,
    biases,
    w_qkv,
    w_out,
    w_up,
    w_down,
    layer_home,
    act_two_all,
    qkv_all,
    mixed_all,
    grad_temporal_all,
    act_three_all,
    grad_lifted_all,
    hidden_all,
    grad_branch_all,
    grad_state_all,
    sums,
    state_scr,
    loss_scr,
    wqkv_scr,
    wout_scr,
    wup_scr,
    wdown_scr,
    slopes,
    layer_scr,
    act_two,
    qkv,
    mixed,
    grad_temporal,
    act_three,
    grad_lifted,
    hidden,
    grad_branch,
    grad_state,
    load_sem,
    loss_send_sem,
    loss_recv_sem,
    layer_send,
    layer_recv,
    save_sem,
):
    slot = lax.axis_index("dp")
    rank = lax.axis_index("seq")
    frames = FRAME_PART * RANKS

    def loss_place():
        return loss_scr.at[2 + lax.rem(slot, 2), pl.ds(rank * FRAME_PART, FRAME_PART)]

    def loss_source(hop):
        return loss_grad.at[lax.rem(slot + hop, CLIPS), :, pl.ds(CHUNK_CELLS, CHUNK_CELLS)]

    def loss_spot():
        return loss_recv_sem.at[lax.rem(slot, 2), rank]

    def loss_send(hop):
        return pltpu.make_async_remote_copy(
            src_ref=loss_source(hop),
            dst_ref=loss_place(),
            send_sem=loss_send_sem.at[hop],
            recv_sem=loss_spot(),
            device_id=(lax.rem(slot + hop, CLIPS), slot // 2),
            device_id_type=MESH,
        )

    def loss_keep():
        return pltpu.make_async_copy(loss_source(0), loss_place(), loss_spot())

    def loss_arrival(half, source):
        place = loss_scr.at[2 + half, pl.ds(source * FRAME_PART, FRAME_PART)]
        return pltpu.make_async_copy(
            loss_grad.at[0, :, pl.ds(CHUNK_CELLS, CHUNK_CELLS)], place, loss_recv_sem.at[half, source]
        )

    def layer_place(chunk):
        return layer_home.at[slot, :, pl.ds(pl.multiple_of(lax.rem(chunk, 2) * CHUNK_CELLS, CHUNK_CELLS), CHUNK_CELLS)]

    def layer_send_copy(order, chunk, target):
        return pltpu.make_async_remote_copy(
            src_ref=layer_scr.at[order, pl.ds(target * FRAME_PART, FRAME_PART)],
            dst_ref=layer_place(chunk),
            send_sem=layer_send.at[order, target],
            recv_sem=layer_recv.at[slot, lax.rem(chunk, 2)],
            device_id=(2 * rank + chunk // 2, target),
            device_id_type=MESH,
        )

    def layer_keep_copy(order, chunk, target):
        return pltpu.make_async_copy(
            layer_scr.at[order, pl.ds(target * FRAME_PART, FRAME_PART)],
            layer_place(chunk),
            layer_recv.at[slot, lax.rem(chunk, 2)],
        )

    def layer_self(chunk, target):
        return jnp.logical_and(2 * rank + chunk // 2 == slot, rank == target)

    stages = (act_two, qkv, mixed, grad_temporal, act_three, grad_lifted, hidden, grad_branch, grad_state)
    homes = (
        act_two_all,
        qkv_all,
        mixed_all,
        grad_temporal_all,
        act_three_all,
        grad_lifted_all,
        hidden_all,
        grad_branch_all,
        grad_state_all,
    )

    def save(which, order):
        spot = lax.rem(order, 2)
        return pltpu.make_async_copy(stages[which].at[spot], homes[which].at[order], save_sem.at[which, spot])

    loads = (
        pltpu.make_async_copy(state_cells, state_scr, load_sem.at[0]),
        pltpu.make_async_copy(w_qkv, wqkv_scr, load_sem.at[1]),
        pltpu.make_async_copy(w_out, wout_scr, load_sem.at[2]),
        pltpu.make_async_copy(w_up, wup_scr, load_sem.at[3]),
        pltpu.make_async_copy(w_down, wdown_scr, load_sem.at[4]),
        pltpu.make_async_copy(loss_early, loss_scr.at[pl.ds(0, 2)], load_sem.at[5]),
    )
    self_loss = slot // 2 == rank
    for load in loads:
        load.start()

    @pl.when(self_loss)
    def _():
        loss_keep().start()

    @pl.when(jnp.logical_not(self_loss))
    def _():
        loss_send(0).start()

    for hop in range(1, CLIPS):
        loss_send(hop).start()

    sums[...] = jnp.zeros_like(sums)
    bias_rows = f32(biases[...])
    valid = cell_match()
    count = cell_counts[slot]

    def piece(index):
        return modulation[index : index + 1]

    def add(row, value):
        sums[pl.ds(row, 1)] += value

    def chunk_step(order, carry):
        chunk = chunk_of(order)
        spot = lax.rem(order, 2)
        first = order == 0

        def once(*which):
            @pl.when(first)
            def _():
                for load in which:
                    loads[load].wait()

        @pl.when(order >= 2)
        def _():
            for which in range(len(stages)):
                save(which, order - 2).wait()

        once(0)
        cells = pl.ds(pl.multiple_of(chunk * CHUNK_CELLS, CHUNK_CELLS), CHUNK_CELLS)
        state = f32(state_scr[:, cells]).reshape(TOKENS, D)
        normed_two, _ = standardise(state)
        act_two[spot] = bf16(normed_two * (1.0 + piece(4)) + piece(3))
        once(1)
        qkv[spot] = bf16(dot(act_two[spot], wqkv_scr[...]))
        row_heads_forward(qkv.at[spot], mixed.at[spot], valid)
        for which in range(3):
            save(which, order).start()
        once(2)
        temporal = dot(mixed[spot], wout_scr[...]) + bias_rows[10:11]
        state_two = state + piece(5) * temporal
        normed_three, inverse_three = standardise(state_two)
        act_three[spot] = bf16(normed_three * (1.0 + piece(7)) + piece(6))
        save(4, order).start()
        once(3, 4)
        branch = jnp.zeros((TOKENS, D), jnp.float32) + bias_rows[15:16]
        for block in range(FF // D):
            lanes = pl.ds(block * D, D)
            lifted = dot(act_three[spot], wup_scr[:, lanes]) + bias_rows[11 + block : 12 + block]
            square = lifted * lifted
            curve = jnp.tanh(0.7978845608028654 * lifted * (1.0 + 0.044715 * square))
            half = 0.5 * (1.0 + curve)
            hidden[spot, :, lanes] = bf16(lifted * half)
            slopes[:, lanes] = half + 0.5 * lifted * (1.0 - curve * curve) * (
                0.7978845608028654 * (1.0 + 3.0 * 0.044715 * square)
            )
            branch += dot(hidden[spot, :, lanes], wdown_scr[lanes, :])
        save(6, order).start()
        layer_scr[order] = bf16(state_two + piece(8) * branch).reshape(frames, CHUNK_CELLS, D)
        for target in range(RANKS):

            @pl.when(layer_self(chunk, target))
            def _():
                layer_keep_copy(order, chunk, target).start()

            @pl.when(jnp.logical_not(layer_self(chunk, target)))
            def _():
                layer_send_copy(order, chunk, target).start()

        once(5)

        @pl.when(order >= 2)
        def _():
            for source in range(RANKS):
                loss_arrival(order - 2, source).wait()

        token = lax.broadcasted_iota(jnp.int32, (TOKENS, 1), 0)
        frame, cell = token // CHUNK_CELLS, lax.rem(token, CHUNK_CELLS)
        mask = jnp.zeros((TOKENS, 1), jnp.int32)
        for which in range(frames):
            mask = jnp.where(frame == which, frame_tasks[slot, which], mask)
        mask = jnp.where(rank * CELL_PART + chunk * CHUNK_CELLS + cell < count, mask, 0)
        seed = f32(loss_scr[order]).reshape(TOKENS, D) * f32(mask)
        add(8, column_sum(seed * branch))
        low_branch = bf16(piece(8) * seed)
        grad_branch[spot] = low_branch
        save(7, order).start()
        add(13, column_sum(f32(low_branch)))
        grad_act = jnp.zeros((TOKENS, D), jnp.float32)
        for block in range(FF // D):
            lanes = pl.ds(block * D, D)
            low_lifted = bf16(dot_nt(grad_branch[spot], wdown_scr[lanes, :]) * slopes[:, lanes])
            grad_lifted[spot, :, lanes] = low_lifted
            add(9 + block, column_sum(f32(low_lifted)))
            grad_act += dot_nt(grad_lifted[spot, :, lanes], wup_scr[:, lanes])
        save(5, order).start()
        add(6, column_sum(grad_act))
        add(7, column_sum(grad_act * normed_three))
        grad_state_two = seed + standard_back(normed_three, inverse_three, grad_act * (1.0 + piece(7)))
        grad_state[spot] = grad_state_two
        save(8, order).start()
        add(5, column_sum(grad_state_two * temporal))
        low_temporal = bf16(piece(5) * grad_state_two)
        grad_temporal[spot] = low_temporal
        save(3, order).start()
        add(14, column_sum(f32(low_temporal)))
        return carry

    lax.fori_loop(0, CHUNKS, chunk_step, 0)
    for order in (CHUNKS - 2, CHUNKS - 1):
        for which in range(len(stages)):
            save(which, order).wait()

    @pl.when(jnp.logical_not(self_loss))
    def _():
        loss_send(0).wait_send()

    for hop in range(1, CLIPS):
        loss_send(hop).wait_send()

    def layer_end(order, carry):
        chunk = chunk_of(order)
        for target in range(RANKS):

            @pl.when(jnp.logical_not(layer_self(chunk, target)))
            def _():
                layer_send_copy(order, chunk, target).wait_send()

        return carry

    lax.fori_loop(0, CHUNKS, layer_end, 0)
    for clip in range(CLIPS):
        for half in range(2):
            place = layer_home.at[clip, :, pl.ds(half * CHUNK_CELLS, CHUNK_CELLS)]
            pltpu.make_async_copy(
                layer_scr.at[0, pl.ds(0, FRAME_PART)], place, layer_recv.at[clip, half]
            ).wait()


def time_forward(
    cell_counts, frame_tasks, state_cells, loss_grad, loss_early, modulation, biases, w_qkv, w_out, w_up, w_down
):
    low = jnp.bfloat16
    frames = FRAME_PART * RANKS
    kinds = [(width, low) for width in SAVED_WIDTHS] + [(D, jnp.float32)]
    return pl.pallas_call(
        time_forward_body,
        out_shape=(jax.ShapeDtypeStruct((CLIPS, FRAME_PART, CELL_HOME, D), low),)
        + tuple(jax.ShapeDtypeStruct((CHUNKS, TOKENS, width), kind) for width, kind in kinds)
        + (jax.ShapeDtypeStruct((16, D), jnp.float32),),
        in_specs=[SMEM, SMEM, ANY, ANY, ANY, VMEM, VMEM, ANY, ANY, ANY, ANY],
        out_specs=(ANY,) * 10 + (VMEM,),
        scratch_shapes=[
            pltpu.VMEM((frames, CELL_PART, D), low),
            pltpu.VMEM((CHUNKS, frames, CHUNK_CELLS, D), low),
            pltpu.VMEM((D, 3 * D), low),
            pltpu.VMEM((D, D), low),
            pltpu.VMEM((D, FF), low),
            pltpu.VMEM((FF, D), low),
            pltpu.VMEM((TOKENS, FF), jnp.float32),
            pltpu.VMEM((CHUNKS, frames, CHUNK_CELLS, D), low),
        ]
        + [pltpu.VMEM((2, TOKENS, width), kind) for width, kind in kinds]
        + [
            pltpu.SemaphoreType.DMA((6,)),
            pltpu.SemaphoreType.DMA((CLIPS,)),
            pltpu.SemaphoreType.DMA((2, RANKS)),
            pltpu.SemaphoreType.DMA((CHUNKS, RANKS)),
            pltpu.SemaphoreType.DMA((CLIPS, 2)),
            pltpu.SemaphoreType.DMA((9, 2)),
        ],
        compiler_params=pltpu.CompilerParams(has_side_effects=True, vmem_limit_bytes=58 * 1024 * 1024),
        cost_estimate=pl.CostEstimate(flops=40 * 10**9, bytes_accessed=50 * 10**6, transcendentals=6 * 10**6),
        name="time_forward",
    )(cell_counts, frame_tasks, state_cells, loss_grad, loss_early, modulation, biases, w_qkv, w_out, w_up, w_down)


UNITS = 16
ROWS = D // RANKS
LOOSE = 8
RING = 4


def tail_body(
    cell_counts,
    arrived,
    qkv,
    mixed,
    state_cells,
    act_two,
    qkv_two,
    mixed_two,
    grad_temporal,
    act_three,
    grad_lifted,
    hidden,
    grad_branch,
    grad_state_two,
    modulation,
    biases,
    sums_in,
    w_qkv_t,
    w_out_t,
    w_qkv,
    w_out,
    grad_home,
    totals,
    gathered,
    x_scr,
    state_scr,
    qkv_scr,
    mixed_scr,
    spatial_scr,
    time_scr,
    wqkv_scr,
    wout_scr,
    left_scr,
    right_scr,
    grad_mixed,
    chunk_state,
    chunk_grad,
    chunk_temporal,
    own,
    total,
    core_in,
    x_in,
    y_in,
    edge_in,
    middle_in,
    sums,
    sums_in_scr,
    load_sem,
    frame_sem,
    side_sem,
    chunk_sem,
    cell_send,
    cell_recv,
    home_send,
    home_recv,
    unit_send,
    unit_recv,
    sum_send,
    sum_recv,
):
    slot = lax.axis_index("dp")
    rank = lax.axis_index("seq")
    core = lax.rem(rank, 2)
    over_x = rank // 2
    over_y = lax.rem(slot, 2)
    over_z = slot // 2
    at_edge = jnp.logical_or(over_z == 0, over_z == 3)
    low_side = over_z < 2
    core_peer = (slot, rank + 1 - 2 * core)
    x_peer = (slot, lax.rem(rank + 2, RANKS))
    y_peer = (slot + 1 - 2 * over_y, rank)
    inner_peer = (jnp.where(low_side, 2, 4) + over_y, rank)
    middle_peer = (jnp.where(low_side, 4, 2) + over_y, rank)
    outer_peer = (jnp.where(low_side, 0, 6) + over_y, rank)

    def piece(index):
        return modulation[index : index + 1]

    def remote(source, target, send, recv, peer):
        return pltpu.make_async_remote_copy(
            src_ref=source, dst_ref=target, send_sem=send, recv_sem=recv, device_id=peer, device_id_type=MESH
        )

    def half_rows(which):
        return pl.ds(pl.multiple_of(which * (ROWS // 2), ROWS // 2), ROWS // 2)


    def core_copy(unit):
        spot, place = lax.rem(unit, LOOSE), lax.rem(unit, RING)
        return remote(own.at[spot, 1 - core], core_in.at[place], unit_send.at[0, spot], unit_recv.at[0, spot], core_peer)

    def x_copy(unit):
        spot, place = lax.rem(unit, LOOSE), lax.rem(unit, RING)
        return remote(
            own.at[spot, core, 1 - over_x], x_in.at[place], unit_send.at[1, spot], unit_recv.at[1, spot], x_peer
        )

    def y_copy(unit):
        spot, place = lax.rem(unit, LOOSE), lax.rem(unit, RING)
        return remote(
            own.at[spot, core, over_x, half_rows(1 - over_y)],
            y_in.at[place],
            unit_send.at[2, spot],
            unit_recv.at[2, spot],
            y_peer,
        )

    def edge_copy(unit):
        spot, place = lax.rem(unit, LOOSE), lax.rem(unit, RING)
        return remote(
            own.at[spot, core, over_x, half_rows(over_y)],
            edge_in.at[place],
            unit_send.at[3, spot],
            unit_recv.at[3, spot],
            inner_peer,
        )

    def middle_copy(unit):
        spot, place = lax.rem(unit, LOOSE), lax.rem(unit, RING)
        return remote(
            own.at[spot, core, over_x, half_rows(over_y)],
            middle_in.at[place],
            unit_send.at[3, spot],
            unit_recv.at[4, spot],
            middle_peer,
        )

    def outer_copy(unit):
        spot, place = lax.rem(unit, LOOSE), lax.rem(unit, RING)
        return remote(
            total.at[spot], middle_in.at[place], unit_send.at[4, spot], unit_recv.at[4, spot], outer_peer
        )

    def share_copy(unit, source):
        spot = lax.rem(unit, LOOSE)
        return remote(
            source, totals.at[unit, half_rows(over_y)], unit_send.at[5, spot], unit_recv.at[5, spot], y_peer
        )

    def keep_copy(unit, source):
        spot = lax.rem(unit, LOOSE)
        return pltpu.make_async_copy(source, totals.at[unit, half_rows(over_y)], unit_send.at[6, spot])

    def stage_one(unit):
        spot, place = lax.rem(unit, LOOSE), lax.rem(unit, RING)
        core_copy(unit).wait_recv()
        own[spot, core] = bf16(f32(own[spot, core]) + f32(core_in[place]))
        x_copy(unit).start()

    def stage_two(unit):
        spot, place = lax.rem(unit, LOOSE), lax.rem(unit, RING)
        x_copy(unit).wait_recv()
        own[spot, core, over_x] = bf16(f32(own[spot, core, over_x]) + f32(x_in[place]))
        y_copy(unit).start()

    def stage_three(unit):
        spot, place = lax.rem(unit, LOOSE), lax.rem(unit, RING)
        y_copy(unit).wait_recv()
        rows = half_rows(over_y)
        own[spot, core, over_x, rows] = bf16(f32(own[spot, core, over_x, rows]) + f32(y_in[place]))

        @pl.when(at_edge)
        def _():
            edge_copy(unit).start()

    def stage_four(unit):
        spot, place = lax.rem(unit, LOOSE), lax.rem(unit, RING)

        @pl.when(jnp.logical_not(at_edge))
        def _():
            edge_copy(unit).wait_recv()
            rows = half_rows(over_y)
            own[spot, core, over_x, rows] = bf16(f32(own[spot, core, over_x, rows]) + f32(edge_in[place]))
            middle_copy(unit).start()

    def stage_five(unit):
        spot, place = lax.rem(unit, LOOSE), lax.rem(unit, RING)

        @pl.when(jnp.logical_not(at_edge))
        def _():
            middle_copy(unit).wait_recv()
            rows = half_rows(over_y)
            total[spot] = bf16(f32(own[spot, core, over_x, rows]) + f32(middle_in[place]))
            outer_copy(unit).start()
            share_copy(unit, total.at[spot]).start()
            keep_copy(unit, total.at[spot]).start()

    def stage_six(unit):
        place = lax.rem(unit, RING)

        @pl.when(at_edge)
        def _():
            middle_copy(unit).wait_recv()
            share_copy(unit, middle_in.at[place]).start()
            keep_copy(unit, middle_in.at[place]).start()

    def stage_seven(unit):
        spot = lax.rem(unit, LOOSE)
        core_copy(unit).wait_send()
        x_copy(unit).wait_send()
        y_copy(unit).wait_send()
        middle_copy(unit).wait_send()

        @pl.when(jnp.logical_not(at_edge))
        def _():
            outer_copy(unit).wait_send()

        share_copy(unit, total.at[spot]).wait()
        keep_copy(unit, total.at[spot]).wait()

    stages = (
        lambda unit: core_copy(unit).start(),
        stage_one,
        stage_two,
        stage_three,
        stage_four,
        stage_five,
        stage_six,
        stage_seven,
    )

    def advance(time):
        for lag in reversed(range(len(stages))):
            unit = time - lag

            @pl.when(jnp.logical_and(unit >= 0, unit < UNITS))
            def _():
                stages[lag](unit)


    def put_unit(unit, block):
        spot = lax.rem(unit, LOOSE)
        for quarter in range(RANKS):
            own[spot, quarter % 2, quarter // 2] = bf16(block[quarter * ROWS : (quarter + 1) * ROWS])

    def flat(block):
        return block.reshape(CHUNKS * TOKENS, block.shape[-1])

    def unit_loads(unit, action):
        spot = lax.rem(unit, 2)

        def pull(left, right, column):
            lanes = pl.ds(pl.multiple_of(column * D, D), D)
            action(pltpu.make_async_copy(left, left_scr.at[spot], load_sem.at[0, spot]))
            action(pltpu.make_async_copy(right.at[:, :, lanes], right_scr.at[spot], load_sem.at[1, spot]))

        @pl.when(unit < 8)
        def _():
            pull(act_three, grad_lifted, unit - 4)

        @pl.when(jnp.logical_and(unit >= 8, unit < 11))
        def _():
            pull(act_two, time_scr, unit - 8)

        @pl.when(unit == 11)
        def _():
            pull(mixed_two, grad_temporal, 0)

    def unit_early(unit):
        spot = lax.rem(unit, 2)
        unit_loads(unit, lambda copy: copy.wait())

        @pl.when(unit < 11)
        def _():
            unit_loads(unit + 1, lambda copy: copy.start())

        put_unit(unit, dot_tn(flat(left_scr[spot]), flat(right_scr[spot])))

    def hidden_load(block):
        spot = block % 2
        lanes = pl.ds(block % RANKS * D, D)
        return pltpu.make_async_copy(hidden.at[:, :, lanes], right_scr.at[spot], load_sem.at[1, spot])

    def double_unit(double):
        lanes = pl.ds(pl.multiple_of(double * 2 * ROWS, 2 * ROWS), 2 * ROWS)
        for block in range(RANKS):
            hidden_load(block).wait()
            columns = dot_tn(flat(left_scr[0, :, :, lanes]), flat(right_scr[block % 2]))
            if block + 2 < RANKS:
                hidden_load(block + 2).start()
            else:

                @pl.when(double == 0)
                def _():
                    hidden_load(block + 2).start()

            for part in range(2):
                own[2 * double + part, block % 2, block // 2] = bf16(columns[part * ROWS : (part + 1) * ROWS])


    def chunk_loads(order):
        spot = lax.rem(order, 2)
        cells = pl.ds(pl.multiple_of(chunk_of(order) * CHUNK_CELLS, CHUNK_CELLS), CHUNK_CELLS)
        return (
            pltpu.make_async_copy(state_cells.at[:, cells], chunk_state.at[spot], chunk_sem.at[0, spot]),
            pltpu.make_async_copy(grad_state_two.at[order], chunk_grad.at[spot], chunk_sem.at[1, spot]),
            pltpu.make_async_copy(grad_temporal.at[order], chunk_temporal.at[spot], chunk_sem.at[2, spot]),
            pltpu.make_async_copy(qkv_two.at[order], time_scr.at[order], chunk_sem.at[3, spot]),
        )

    def cell_place(order, frame):
        start = rank * CELL_PART + chunk_of(order) * CHUNK_CELLS
        return state_scr.at[frame, pl.ds(pl.multiple_of(start, CHUNK_CELLS), CHUNK_CELLS)]

    def cell_rows(order, target, frame):
        start = (target * FRAME_PART + frame) * CHUNK_CELLS
        return spatial_scr.at[order, pl.ds(pl.multiple_of(start, CHUNK_CELLS), CHUNK_CELLS)]

    def cell_copy(order, hop, frame):
        target = lax.rem(rank + hop, RANKS)
        return remote(
            cell_rows(order, target, frame),
            cell_place(order, frame),
            cell_send.at[order, hop, frame],
            cell_recv.at[order, hop, frame],
            (slot, target),
        )

    def cell_keep(order, frame):
        return pltpu.make_async_copy(
            cell_rows(order, rank, frame), cell_place(order, frame), cell_recv.at[order, 0, frame]
        )

    def time_backward(order):
        spot = lax.rem(order, 2)
        for load in chunk_loads(order):
            load.wait()

        @pl.when(order < CHUNKS - 1)
        def _():
            for load in chunk_loads(order + 1):
                load.start()

        grad_mixed[...] = bf16(dot_nt(chunk_temporal[spot], wout_scr[...]))
        heads_backward(
            time_scr.at[order], grad_mixed, time_scr.at[order], cell_match(), SPACE_BLOCKS, True
        )
        grad_act = dot_nt(time_scr[order], wqkv_scr[...])
        normed, inverse = standardise(f32(chunk_state[spot]).reshape(TOKENS, D))
        add(3, column_sum(grad_act))
        add(4, column_sum(grad_act * normed))
        spatial_scr[order] = bf16(
            chunk_grad[spot] + standard_back(normed, inverse, grad_act * (1.0 + piece(4)))
        )
        for frame in range(FRAME_PART):
            for hop in range(1, RANKS):
                cell_copy(order, hop, frame).start()
            cell_keep(order, frame).start()


    def add(row, value):
        sums[pl.ds(row, 1)] += value

    def frame_loads(frame):
        return (
            pltpu.make_async_copy(arrived.at[frame], x_scr.at[frame], frame_sem.at[0, frame]),
            pltpu.make_async_copy(qkv.at[frame], qkv_scr.at[frame], frame_sem.at[1, frame]),
            pltpu.make_async_copy(mixed.at[frame], mixed_scr.at[frame], frame_sem.at[2, frame]),
        )

    def home_copy(frame, hop):
        peer = lax.rem(slot + hop, CLIPS)
        rows = pl.ds(pl.multiple_of(peer * CELL_HOME, CELL_HOME), CELL_HOME)
        return remote(
            state_scr.at[frame, rows],
            grad_home.at[slot, frame],
            home_send.at[frame, hop],
            home_recv.at[frame, hop],
            (peer, rank),
        )

    def home_keep(frame):
        rows = pl.ds(pl.multiple_of(slot * CELL_HOME, CELL_HOME), CELL_HOME)
        return pltpu.make_async_copy(state_scr.at[frame, rows], grad_home.at[slot, frame], home_recv.at[frame, 0])

    def frame_first(frame):
        for load in frame_loads(frame):
            load.wait()
        for order in range(CHUNKS):
            for hop in range(1, RANKS):
                cell_copy(order, hop, frame).wait_recv()
        grad_state = f32(state_scr[frame])
        spatial = dot(mixed_scr[frame], wout_scr[...]) + bias_rows[9:10]
        add(2, column_sum(grad_state * spatial))
        low_spatial = bf16(piece(2) * grad_state)
        spatial_scr[frame] = low_spatial
        add(15, column_sum(f32(low_spatial)))
        grad_mixed[...] = bf16(dot_nt(low_spatial, wout_scr[...]))
        pairs = range(HEADS // 4)
        heads_backward(
            qkv_scr.at[frame], grad_mixed, qkv_scr.at[frame], valid, SPACE_BLOCKS, True, pairs=pairs
        )

    def frame_second(frame):
        pairs = range(HEADS // 4, HEADS // 2)
        heads_backward(
            qkv_scr.at[frame], grad_mixed, qkv_scr.at[frame], valid, SPACE_BLOCKS, True, pairs=pairs
        )
        grad_act = dot_nt(qkv_scr[frame], wqkv_scr[...])
        normed, inverse = standardise(f32(x_scr[frame]))
        x_scr[frame] = bf16(normed * (1.0 + piece(1)) + piece(0))
        add(0, column_sum(grad_act))
        add(1, column_sum(grad_act * normed))
        state_scr[frame] = bf16(
            f32(state_scr[frame]) + standard_back(normed, inverse, grad_act * (1.0 + piece(1)))
        )
        for hop in range(1, CLIPS):
            home_copy(frame, hop).start()
        home_keep(frame).start()


    def sum_exchange(step):
        peer = core_peer if step == 0 else x_peer
        return remote(sums, sums_in_scr.at[step], sum_send.at[step], sum_recv.at[step], peer)

    def sum_add(step):
        sum_exchange(step).wait()
        sums[...] = sums[...] + sums_in_scr[step]

    def sum_spread(hop):
        peer = lax.rem(slot + hop, CLIPS)
        return remote(sums, gathered.at[slot], sum_send.at[1 + hop], sum_recv.at[1 + hop], (peer, rank))

    def sum_keep():
        return pltpu.make_async_copy(sums, gathered.at[slot], sum_send.at[9])


    time_weights = (
        pltpu.make_async_copy(w_qkv_t, wqkv_scr, side_sem.at[0]),
        pltpu.make_async_copy(w_out_t, wout_scr, side_sem.at[1]),
    )
    space_weights = (
        pltpu.make_async_copy(w_qkv, wqkv_scr, side_sem.at[0]),
        pltpu.make_async_copy(w_out, wout_scr, side_sem.at[1]),
    )
    branch_load = pltpu.make_async_copy(grad_branch, left_scr.at[0], load_sem.at[0, 0])
    branch_load.start()
    hidden_load(0).start()
    hidden_load(1).start()
    for load in chunk_loads(0):
        load.start()
    for load in time_weights:
        load.start()
    for frame in range(FRAME_PART):
        for load in frame_loads(frame):
            load.start()
    sums[...] = sums_in[...]
    bias_rows = f32(biases[...])
    valid = lax.broadcasted_iota(jnp.int32, (CELLS, 1), 0) < cell_counts[slot]
    branch_load.wait()

    def double_step(double, carry):
        double_unit(double)
        advance(2 * double)

        @pl.when(double == 0)
        def _():
            for load in time_weights:
                load.wait()

        @pl.when(double == 1)
        def _():
            unit_loads(4, lambda copy: copy.start())

        time_backward(2 * double)
        advance(2 * double + 1)
        time_backward(2 * double + 1)
        return carry

    lax.fori_loop(0, 2, double_step, 0)
    for load in space_weights:
        load.start()

    def cells_sent(order, carry):
        for frame in range(FRAME_PART):
            for hop in range(1, RANKS):
                cell_copy(order, hop, frame).wait_send()
            cell_keep(order, frame).wait()
        return carry

    lax.fori_loop(0, CHUNKS, cells_sent, 0)
    for load in space_weights:
        load.wait()

    def frame_step(frame, carry):
        unit = 4 + 2 * frame
        frame_first(frame)
        unit_early(unit)
        advance(unit)
        frame_second(frame)
        unit_early(unit + 1)
        advance(unit + 1)
        return carry

    lax.fori_loop(0, FRAME_PART, frame_step, 0)
    sum_exchange(0).start()

    def late_step(column, carry):
        lanes = pl.ds(pl.multiple_of(column * D, D), D)
        left = x_scr[...].reshape(FRAME_PART * CELLS, D)
        right = qkv_scr[:, :, lanes].reshape(FRAME_PART * CELLS, D)
        put_unit(12 + column, dot_tn(left, right))
        advance(12 + column)
        return carry

    lax.fori_loop(0, 3, late_step, 0)
    put_unit(
        15,
        dot_tn(
            mixed_scr[...].reshape(FRAME_PART * CELLS, D), spatial_scr[...].reshape(FRAME_PART * CELLS, D)
        ),
    )
    advance(15)
    sum_add(0)
    sum_exchange(1).start()
    advance(16)
    sum_add(1)
    for hop in range(1, CLIPS):
        sum_spread(hop).start()
    sum_keep().start()

    def drain(time, carry):
        advance(time)
        return carry

    lax.fori_loop(17, UNITS + len(stages) - 1, drain, 0)
    for hop in range(1, CLIPS):
        sum_spread(hop).wait()
    sum_keep().wait()

    def frame_end(frame, carry):
        for hop in range(1, CLIPS):
            home_copy(frame, hop).wait()
        home_keep(frame).wait()
        return carry

    lax.fori_loop(0, FRAME_PART, frame_end, 0)


def tail_section(cell_counts, saved, modulation, biases, sums, w_qkv_t, w_out_t, w_qkv, w_out):
    low = jnp.bfloat16
    return pl.pallas_call(
        tail_body,
        out_shape=(
            jax.ShapeDtypeStruct((CLIPS, FRAME_PART, CELL_HOME, D), low),
            jax.ShapeDtypeStruct((UNITS, ROWS, D), low),
            jax.ShapeDtypeStruct((CLIPS, 16, D), jnp.float32),
        ),
        in_specs=[SMEM] + [ANY] * 13 + [VMEM] * 3 + [ANY] * 4,
        out_specs=(ANY, ANY, ANY),
        scratch_shapes=[
            pltpu.VMEM((FRAME_PART, CELLS, D), low),
            pltpu.VMEM((FRAME_PART, CELLS, D), low),
            pltpu.VMEM((FRAME_PART, CELLS, 3 * D), low),
            pltpu.VMEM((FRAME_PART, CELLS, D), low),
            pltpu.VMEM((FRAME_PART, CELLS, D), low),
            pltpu.VMEM((CHUNKS, TOKENS, 3 * D), low),
            pltpu.VMEM((D, 3 * D), low),
            pltpu.VMEM((D, D), low),
            pltpu.VMEM((2, CHUNKS, TOKENS, D), low),
            pltpu.VMEM((2, CHUNKS, TOKENS, D), low),
            pltpu.VMEM((CELLS, D), low),
            pltpu.VMEM((2, FRAME_PART * RANKS, CHUNK_CELLS, D), low),
            pltpu.VMEM((2, TOKENS, D), jnp.float32),
            pltpu.VMEM((2, TOKENS, D), low),
            pltpu.VMEM((LOOSE, 2, 2, ROWS, D), low),
            pltpu.VMEM((LOOSE, ROWS // 2, D), low),
            pltpu.VMEM((RING, 2, ROWS, D), low),
            pltpu.VMEM((RING, ROWS, D), low),
            pltpu.VMEM((RING, ROWS // 2, D), low),
            pltpu.VMEM((RING, ROWS // 2, D), low),
            pltpu.VMEM((RING, ROWS // 2, D), low),
            pltpu.VMEM((16, D), jnp.float32),
            pltpu.VMEM((2, 16, D), jnp.float32),
            pltpu.SemaphoreType.DMA((2, 2)),
            pltpu.SemaphoreType.DMA((3, FRAME_PART)),
            pltpu.SemaphoreType.DMA((2,)),
            pltpu.SemaphoreType.DMA((4, 2)),
            pltpu.SemaphoreType.DMA((CHUNKS, RANKS, FRAME_PART)),
            pltpu.SemaphoreType.DMA((CHUNKS, RANKS, FRAME_PART)),
            pltpu.SemaphoreType.DMA((FRAME_PART, CLIPS)),
            pltpu.SemaphoreType.DMA((FRAME_PART, CLIPS)),
            pltpu.SemaphoreType.DMA((7, LOOSE)),
            pltpu.SemaphoreType.DMA((6, LOOSE)),
            pltpu.SemaphoreType.DMA((10,)),
            pltpu.SemaphoreType.DMA((9,)),
        ],
        compiler_params=pltpu.CompilerParams(has_side_effects=True, vmem_limit_bytes=60 * 1024 * 1024),
        cost_estimate=pl.CostEstimate(flops=30 * 10**9, bytes_accessed=60 * 10**6, transcendentals=3 * 10**6),
        name="tail_section",
    )(cell_counts, *saved, modulation, biases, sums, w_qkv_t, w_out_t, w_qkv, w_out)


def per_device_fast(
    tokens,
    condition,
    loss_grad,
    cell_counts,
    frame_tasks,
    destinations,
    w_ada,
    b_ada,
    w_qkv_s,
    w_out_s,
    b_out_s,
    w_qkv_t,
    w_out_t,
    b_out_t,
    w_up,
    b_up,
    w_down,
    b_down,
):
    rank = lax.axis_index("seq")
    cond_low = bf16(jax.nn.silu(f32(jnp.take(condition, destinations, axis=0))))
    biases = jnp.concatenate([b_ada, b_out_s, b_out_t, b_up, b_down]).reshape(16, D)
    arrived, qkv_one, mixed_one, cells_in, loss_early, modulation = space_forward(
        destinations, cell_counts, tokens, loss_grad, condition, biases, w_ada, w_qkv_s, w_out_s
    )
    parts = time_forward(
        cell_counts,
        frame_tasks,
        cells_in,
        loss_grad,
        loss_early,
        modulation,
        biases,
        w_qkv_t,
        w_out_t,
        w_up,
        w_down,
    )
    layer_out, saved, sums = parts[0], parts[1:-1], parts[-1]
    grad_tokens, totals, gathered = tail_section(
        cell_counts,
        (arrived, qkv_one, mixed_one, cells_in) + tuple(saved),
        modulation,
        biases,
        sums,
        w_qkv_t,
        w_out_t,
        w_qkv_s,
        w_out_s,
    )
    wide = f32(totals)

    def side(first, count):
        return jnp.concatenate([wide[first + part] for part in range(count)], axis=1)

    grad_w_down = wide[0:4].reshape(D, D).T
    grad_mod = gathered[:, :9].reshape(CLIPS, 9 * D)
    own_cond = lax.dynamic_slice_in_dim(cond_low, rank * ROWS, ROWS, axis=1)
    grad_w_ada = lax.dot_general(
        f32(own_cond), grad_mod, (((0,), (0,)), ((), ())), preferred_element_type=jnp.float32
    )
    sums_all = jnp.sum(gathered, axis=0)
    grad_b_ada = lax.dynamic_slice_in_dim(sums_all[:9].reshape(9 * D), rank * 9 * ROWS, 9 * ROWS)
    grad_b_up = lax.dynamic_index_in_dim(sums_all[9:13], rank, 0, keepdims=False)

    def quarter(row):
        return lax.dynamic_slice_in_dim(sums_all[row], rank * ROWS, ROWS)

    return (
        layer_out,
        grad_tokens,
        grad_w_ada,
        grad_b_ada,
        side(12, 3),
        wide[15],
        quarter(15),
        side(8, 3),
        wide[11],
        quarter(14),
        side(4, 4),
        grad_b_up,
        grad_w_down,
        quarter(13),
    )


def solution(mesh):
    placed = (
        P(None, "seq", "dp", None),
        P(),
        P(None, "seq", "dp", None),
        P(),
        P(),
        P(),
        P(),
        P(),
        P(),
        P(),
        P(),
        P(),
        P(),
        P(),
        P(),
        P(),
        P(),
        P(),
    )
    fast = mesh.shape["dp"] == 8 and mesh.shape["seq"] == 4
    return jax.shard_map(
        per_device_fast if fast else per_device_general,
        mesh=mesh,
        in_specs=placed,
        out_specs=(
            P(None, "seq", "dp", None),
            P(None, "seq", "dp", None),
            P("seq", None),
            P("seq"),
            P("seq", None),
            P("seq", None),
            P("seq"),
            P("seq", None),
            P("seq", None),
            P("seq"),
            P("seq", None),
            P("seq"),
            P("seq", None),
            P("seq"),
        ),
        check_vma=False,
    )
```

```python
import jax
import jax.numpy as jnp
from jax import lax
from jax.experimental import pallas as pl
from jax.experimental.pallas import tpu as pltpu
from jax.sharding import PartitionSpec as P

D = 768
HEADS = 12
HEAD = 64


def standard(field):
    centred = field - jnp.mean(field, axis=-1, keepdims=True)
    inverse = lax.rsqrt(jnp.mean(centred * centred, axis=-1, keepdims=True) + 1e-06)
    return (centred * inverse, inverse)


def standard_back(normed, inverse, grad_normed):
    return inverse * (
        grad_normed
        - jnp.mean(grad_normed, axis=-1, keepdims=True)
        - normed * jnp.mean(grad_normed * normed, axis=-1, keepdims=True)
    )


def gelu_back(lifted, grad_hidden):
    return jax.vjp(lambda inner: jax.nn.gelu(inner, approximate=True), lifted)[1](grad_hidden)[0]


def attend(triple, key_valid, einsum_forms):
    queries = triple[:, :, 0]
    key_rows = triple[:, :, 1]
    value_rows = triple[:, :, 2]
    scores = (
        jnp.einsum(einsum_forms[0], queries, key_rows, preferred_element_type=jnp.float32) * 0.125
    )
    scores = jnp.where(key_valid, scores, -1e30)
    row_top = jnp.max(scores, axis=-1, keepdims=True)
    exponent = jnp.exp(scores - row_top)
    probs_full = exponent / jnp.sum(exponent, axis=-1, keepdims=True)
    probs_low = probs_full.astype(jnp.bfloat16)
    mixed_out = jnp.einsum(
        einsum_forms[1], probs_low, value_rows, preferred_element_type=jnp.float32
    ).astype(jnp.bfloat16)
    return (mixed_out, probs_full, probs_low)


def attend_back(triple, probs_full, probs_low, grad_mixed, einsum_forms):
    queries = triple[:, :, 0]
    key_rows = triple[:, :, 1]
    value_rows = triple[:, :, 2]
    grad_probs = jnp.einsum(
        einsum_forms[0], grad_mixed, value_rows, preferred_element_type=jnp.float32
    )
    row_delta = jnp.sum(probs_full * grad_probs, axis=-1, keepdims=True)
    grad_scores = (probs_full * (grad_probs - row_delta)).astype(jnp.bfloat16)
    grad_values = jnp.einsum(
        einsum_forms[2], probs_low, grad_mixed, preferred_element_type=jnp.float32
    )
    grad_queries = (
        jnp.einsum(einsum_forms[1], grad_scores, key_rows, preferred_element_type=jnp.float32)
        * 0.125
    )
    grad_keys = (
        jnp.einsum(einsum_forms[2], grad_scores, queries, preferred_element_type=jnp.float32)
        * 0.125
    )
    return jnp.stack([grad_queries, grad_keys, grad_values], axis=2)


def per_device_general(
    tokens,
    condition,
    loss_grad,
    cell_counts,
    frame_tasks,
    destinations,
    w_ada,
    b_ada,
    w_qkv_s,
    w_out_s,
    b_out_s,
    w_qkv_t,
    w_out_t,
    b_out_t,
    w_up,
    b_up,
    w_down,
    b_down,
):
    groups = lax.axis_size("dp")
    ranks = lax.axis_size("seq")
    own_slot = lax.axis_index("dp")
    own_rank = lax.axis_index("seq")
    frame_part = tokens.shape[1]
    cell_total = tokens.shape[2] * groups
    cell_part = cell_total // ranks
    frame_total = frame_part * ranks
    slot_ids = jnp.arange(groups, dtype=jnp.int32)
    routing = (destinations[None, :] == slot_ids[:, None]).astype(jnp.bfloat16)
    outgoing = jnp.einsum(
        "jc,cfbd->jfbd", routing, tokens, preferred_element_type=jnp.float32
    ).astype(jnp.bfloat16)
    outgoing_grad = jnp.einsum(
        "jc,cfbd->jfbd", routing, loss_grad, preferred_element_type=jnp.float32
    ).astype(jnp.bfloat16)
    arrived, arrived_grad = (
        lax.all_to_all(outgoing, "dp", split_axis=0, concat_axis=2, tiled=True),
        lax.all_to_all(outgoing_grad, "dp", split_axis=0, concat_axis=2, tiled=True),
    )
    own_clip = jnp.sum(jnp.where(destinations == own_slot, slot_ids, 0))
    own_count = jnp.sum(jnp.where(slot_ids == own_clip, cell_counts, 0))
    own_tasks = lax.dynamic_index_in_dim(frame_tasks, own_clip, 0, keepdims=False)
    cond_row = lax.dynamic_index_in_dim(condition, own_slot, 0, keepdims=False)
    cond_low = jax.nn.silu(cond_row.astype(jnp.float32)).astype(jnp.bfloat16)
    modulation = jnp.dot(cond_low[None, :], w_ada, preferred_element_type=jnp.float32)[
        0
    ] + b_ada.astype(jnp.float32)
    pieces = [modulation[piece_index * D : (piece_index + 1) * D] for piece_index in range(9)]
    (
        shift_one,
        scale_one,
        gate_one,
        shift_two,
        scale_two,
        gate_two,
        shift_three,
        scale_three,
        gate_three,
    ) = pieces
    space_forms = ("fphe,fqhe->fhpq", "fhpq,fqhe->fphe", "fhpq,fphe->fqhe")
    frames_in = arrived[0].astype(jnp.float32)
    normed_one, inverse_one = standard(frames_in)
    act_one = (normed_one * (1.0 + scale_one) + shift_one).astype(jnp.bfloat16)
    triple_one = (
        jnp.einsum("fpd,de->fpe", act_one, w_qkv_s, preferred_element_type=jnp.float32)
        .astype(jnp.bfloat16)
        .reshape(frame_part, cell_total, 3, HEADS, HEAD)
    )
    key_valid = (jnp.arange(cell_total, dtype=jnp.int32) < own_count)[None, None, None, :]
    mixed_one, probs_one, low_one = attend(triple_one, key_valid, space_forms)
    flat_one = mixed_one.reshape(frame_part, cell_total, D)
    spatial_out = jnp.einsum(
        "fpd,de->fpe", flat_one, w_out_s, preferred_element_type=jnp.float32
    ) + b_out_s.astype(jnp.float32)
    state_one = (frames_in + gate_one * spatial_out).astype(jnp.bfloat16)
    cells_in, cells_grad = (
        lax.all_to_all(state_one, "seq", split_axis=1, concat_axis=0, tiled=True),
        lax.all_to_all(arrived_grad[0], "seq", split_axis=1, concat_axis=0, tiled=True),
    )
    time_forms = ("fqhe,gqhe->qhfg", "qhfg,gqhe->fqhe", "qhfg,fqhe->gqhe")
    state_cells = cells_in.astype(jnp.float32)
    normed_two, inverse_two = standard(state_cells)
    act_two = (normed_two * (1.0 + scale_two) + shift_two).astype(jnp.bfloat16)
    triple_two = (
        jnp.einsum("fqd,de->fqe", act_two, w_qkv_t, preferred_element_type=jnp.float32)
        .astype(jnp.bfloat16)
        .reshape(frame_total, cell_part, 3, HEADS, HEAD)
    )
    mixed_two, probs_two, low_two = attend(triple_two, True, time_forms)
    flat_two = mixed_two.reshape(frame_total, cell_part, D)
    temporal_out = jnp.einsum(
        "fqd,de->fqe", flat_two, w_out_t, preferred_element_type=jnp.float32
    ) + b_out_t.astype(jnp.float32)
    state_two = state_cells + gate_two * temporal_out
    normed_three, inverse_three = standard(state_two)
    act_three = (normed_three * (1.0 + scale_three) + shift_three).astype(jnp.bfloat16)
    lifted = jnp.einsum(
        "fqd,dk->fqk", act_three, w_up, preferred_element_type=jnp.float32
    ) + b_up.astype(jnp.float32)
    hidden = jax.nn.gelu(lifted, approximate=True).astype(jnp.bfloat16)
    branch_out = jnp.einsum(
        "fqk,kd->fqd", hidden, w_down, preferred_element_type=jnp.float32
    ) + b_down.astype(jnp.float32)
    result = (state_two + gate_three * branch_out).astype(jnp.bfloat16)
    cell_ids = own_rank * cell_part + jnp.arange(cell_part, dtype=jnp.int32)
    loss_mask = jnp.logical_and(own_tasks[:, None] == 1, cell_ids[None, :] < own_count)
    out_grad = cells_grad.astype(jnp.float32) * loss_mask[:, :, None].astype(jnp.float32)
    grad_gate_three = jnp.sum(out_grad * branch_out, axis=(0, 1))
    grad_branch = (gate_three * out_grad).astype(jnp.bfloat16)
    grad_b_down = jnp.sum(grad_branch.astype(jnp.float32), axis=(0, 1))
    grad_w_down = jnp.einsum("fqk,fqd->kd", hidden, grad_branch, preferred_element_type=jnp.float32)
    grad_hidden = jnp.einsum("fqd,kd->fqk", grad_branch, w_down, preferred_element_type=jnp.float32)
    grad_lifted = gelu_back(lifted, grad_hidden).astype(jnp.bfloat16)
    grad_b_up = jnp.sum(grad_lifted.astype(jnp.float32), axis=(0, 1))
    grad_w_up = jnp.einsum(
        "fqd,fqk->dk", act_three, grad_lifted, preferred_element_type=jnp.float32
    )
    grad_act_three = jnp.einsum(
        "fqk,dk->fqd", grad_lifted, w_up, preferred_element_type=jnp.float32
    )
    grad_shift_three = jnp.sum(grad_act_three, axis=(0, 1))
    grad_scale_three = jnp.sum(grad_act_three * normed_three, axis=(0, 1))
    grad_state_two = out_grad + standard_back(
        normed_three, inverse_three, grad_act_three * (1.0 + scale_three)
    )
    grad_gate_two = jnp.sum(grad_state_two * temporal_out, axis=(0, 1))
    grad_temporal = (gate_two * grad_state_two).astype(jnp.bfloat16)
    grad_b_out_t = jnp.sum(grad_temporal.astype(jnp.float32), axis=(0, 1))
    grad_w_out_t = jnp.einsum(
        "fqd,fqe->de", flat_two, grad_temporal, preferred_element_type=jnp.float32
    )
    grad_mixed_two = (
        jnp.einsum("fqe,de->fqd", grad_temporal, w_out_t, preferred_element_type=jnp.float32)
        .astype(jnp.bfloat16)
        .reshape(frame_total, cell_part, HEADS, HEAD)
    )
    grad_triple_two = (
        attend_back(triple_two, probs_two, low_two, grad_mixed_two, time_forms)
        .reshape(frame_total, cell_part, 3 * D)
        .astype(jnp.bfloat16)
    )
    grad_w_qkv_t = jnp.einsum(
        "fqd,fqe->de", act_two, grad_triple_two, preferred_element_type=jnp.float32
    )
    grad_act_two = jnp.einsum(
        "fqe,de->fqd", grad_triple_two, w_qkv_t, preferred_element_type=jnp.float32
    )
    grad_shift_two = jnp.sum(grad_act_two, axis=(0, 1))
    grad_scale_two = jnp.sum(grad_act_two * normed_two, axis=(0, 1))
    grad_state_one = (
        grad_state_two + standard_back(normed_two, inverse_two, grad_act_two * (1.0 + scale_two))
    ).astype(jnp.bfloat16)
    frames_out, frames_grad = (
        lax.all_to_all(result, "seq", split_axis=0, concat_axis=1, tiled=True),
        lax.all_to_all(grad_state_one, "seq", split_axis=0, concat_axis=1, tiled=True),
    )
    grad_frames = frames_grad.astype(jnp.float32)
    grad_gate_one = jnp.sum(grad_frames * spatial_out, axis=(0, 1))
    grad_spatial = (gate_one * grad_frames).astype(jnp.bfloat16)
    grad_b_out_s = jnp.sum(grad_spatial.astype(jnp.float32), axis=(0, 1))
    grad_w_out_s = jnp.einsum(
        "fpd,fpe->de", flat_one, grad_spatial, preferred_element_type=jnp.float32
    )
    grad_mixed_one = (
        jnp.einsum("fpe,de->fpd", grad_spatial, w_out_s, preferred_element_type=jnp.float32)
        .astype(jnp.bfloat16)
        .reshape(frame_part, cell_total, HEADS, HEAD)
    )
    grad_triple_one = (
        attend_back(triple_one, probs_one, low_one, grad_mixed_one, space_forms)
        .reshape(frame_part, cell_total, 3 * D)
        .astype(jnp.bfloat16)
    )
    grad_w_qkv_s = jnp.einsum(
        "fpd,fpe->de", act_one, grad_triple_one, preferred_element_type=jnp.float32
    )
    grad_act_one = jnp.einsum(
        "fpe,de->fpd", grad_triple_one, w_qkv_s, preferred_element_type=jnp.float32
    )
    grad_shift_one = jnp.sum(grad_act_one, axis=(0, 1))
    grad_scale_one = jnp.sum(grad_act_one * normed_one, axis=(0, 1))
    grad_input = (
        grad_frames + standard_back(normed_one, inverse_one, grad_act_one * (1.0 + scale_one))
    ).astype(jnp.bfloat16)
    home_out, home_grad = (
        lax.all_to_all(frames_out[None], "dp", split_axis=2, concat_axis=0, tiled=True),
        lax.all_to_all(grad_input[None], "dp", split_axis=2, concat_axis=0, tiled=True),
    )
    layer_out = jnp.einsum(
        "jc,jfbd->cfbd", routing, home_out, preferred_element_type=jnp.float32
    ).astype(jnp.bfloat16)
    grad_tokens = jnp.einsum(
        "jc,jfbd->cfbd", routing, home_grad, preferred_element_type=jnp.float32
    ).astype(jnp.bfloat16)
    grad_mod = jnp.concatenate(
        [
            grad_shift_one,
            grad_scale_one,
            grad_gate_one,
            grad_shift_two,
            grad_scale_two,
            grad_gate_two,
            grad_shift_three,
            grad_scale_three,
            grad_gate_three,
        ]
    )
    ada_term = cond_low.astype(jnp.float32)[:, None] * grad_mod[None, :]
    partials = (
        lax.psum_scatter(
            ada_term.astype(jnp.bfloat16), "seq", scatter_dimension=0, tiled=True
        ).astype(jnp.float32),
        lax.psum_scatter(
            grad_mod.astype(jnp.bfloat16), "seq", scatter_dimension=0, tiled=True
        ).astype(jnp.float32),
        lax.psum_scatter(
            grad_w_qkv_s.astype(jnp.bfloat16), "seq", scatter_dimension=0, tiled=True
        ).astype(jnp.float32),
        lax.psum_scatter(
            grad_w_out_s.astype(jnp.bfloat16), "seq", scatter_dimension=0, tiled=True
        ).astype(jnp.float32),
        lax.psum_scatter(
            grad_b_out_s.astype(jnp.bfloat16), "seq", scatter_dimension=0, tiled=True
        ).astype(jnp.float32),
        lax.psum_scatter(
            grad_w_qkv_t.astype(jnp.bfloat16), "seq", scatter_dimension=0, tiled=True
        ).astype(jnp.float32),
        lax.psum_scatter(
            grad_w_out_t.astype(jnp.bfloat16), "seq", scatter_dimension=0, tiled=True
        ).astype(jnp.float32),
        lax.psum_scatter(
            grad_b_out_t.astype(jnp.bfloat16), "seq", scatter_dimension=0, tiled=True
        ).astype(jnp.float32),
        lax.psum_scatter(
            grad_w_up.astype(jnp.bfloat16), "seq", scatter_dimension=0, tiled=True
        ).astype(jnp.float32),
        lax.psum_scatter(
            grad_b_up.astype(jnp.bfloat16), "seq", scatter_dimension=0, tiled=True
        ).astype(jnp.float32),
        lax.psum_scatter(
            grad_w_down.astype(jnp.bfloat16), "seq", scatter_dimension=0, tiled=True
        ).astype(jnp.float32),
        lax.psum_scatter(
            grad_b_down.astype(jnp.bfloat16), "seq", scatter_dimension=0, tiled=True
        ).astype(jnp.float32),
    )
    totals = lax.psum(
        (
            partials[0],
            partials[1],
            partials[2],
            partials[3],
            partials[4],
            partials[5],
            partials[6],
            partials[7],
            partials[8],
            partials[9],
            partials[10],
            partials[11],
        ),
        "dp",
    )
    ada_grad = totals[0]
    ada_bias = totals[1]
    rest = totals[2:]
    return (
        layer_out,
        grad_tokens,
        ada_grad,
        ada_bias,
        rest[0],
        rest[1],
        rest[2],
        rest[3],
        rest[4],
        rest[5],
        rest[6],
        rest[7],
        rest[8],
        rest[9],
    )


MESH = pl.DeviceIdType.MESH
ANY = pl.BlockSpec(memory_space=pl.ANY)
VMEM = pl.BlockSpec(memory_space=pltpu.VMEM)
SMEM = pl.BlockSpec(memory_space=pltpu.SMEM)
NEG = -1e30
CLIPS = 8
RANKS = 4
FRAME_PART = 4
CELLS = 256
CELL_HOME = CELLS // CLIPS
CELL_PART = CELLS // RANKS
FF = 3072
TOKENS = 256
CHUNK_CELLS = TOKENS // (FRAME_PART * RANKS)
CHUNKS = CELL_PART // CHUNK_CELLS


def turn_of(rank):
    return 2 * lax.rem(rank, 2) + rank // 2


def chunk_of(order, rank):
    return lax.rem(order + turn_of(rank), CHUNKS)


def order_of(chunk, rank):
    return lax.rem(chunk - turn_of(rank) + CHUNKS, CHUNKS)


def share_of(chunk, rank):
    return lax.rem(rank - chunk + RANKS, RANKS)


def chunk_cells(order, rank):
    chunk = chunk_of(order, rank)
    start = chunk * CELL_PART + share_of(chunk, rank) * CHUNK_CELLS
    return pl.ds(pl.multiple_of(start, CHUNK_CELLS), CHUNK_CELLS)


def loss_target(slot, half):
    chunk = slot // 2
    target = lax.rem(2 * lax.rem(slot, 2) + half + chunk, RANKS)
    return target, order_of(chunk, target)


def f32(value):
    return value.astype(jnp.float32)


def bf16(value):
    return value.astype(jnp.bfloat16)


def dot(left, right):
    return lax.dot_general(left, right, (((1,), (0,)), ((), ())), preferred_element_type=jnp.float32)


def dot_nt(left, right):
    return lax.dot_general(left, right, (((1,), (1,)), ((), ())), preferred_element_type=jnp.float32)


def dot_tn(left, right):
    return lax.dot_general(left, right, (((0,), (0,)), ((), ())), preferred_element_type=jnp.float32)


def standardise(field):
    centred = field - jnp.mean(field, axis=-1, keepdims=True)
    inverse = lax.rsqrt(jnp.mean(centred * centred, axis=-1, keepdims=True) + 1e-06)
    return centred * inverse, inverse


def column_sum(field):
    return jnp.sum(field, axis=0, keepdims=True)


def head_halves(rows):
    lane = lax.broadcasted_iota(jnp.int32, (1, 2 * HEAD), 1) < HEAD
    zero = jnp.bfloat16(0)
    return jnp.where(lane, rows, zero), jnp.where(lane, zero, rows)


def pair_lanes(pair, part):
    return pl.ds(part * D + pair * 2 * HEAD, 2 * HEAD)


def heads_forward(qkv, mixed, probs, valid):
    lane = lax.broadcasted_iota(jnp.int32, (1, 2 * HEAD), 1) < HEAD
    scores = []
    for pair in range(HEADS // 2):
        queries = head_halves(qkv[:, pair_lanes(pair, 0)] * jnp.bfloat16(0.125))
        keys = qkv[:, pair_lanes(pair, 1)]
        scores += [dot_nt(queries[half], keys) for half in range(2)]
    low = []
    for head in range(HEADS):
        masked = jnp.where(valid, scores[head], NEG)
        exponent = jnp.exp(masked - jnp.max(masked, axis=-1, keepdims=True))
        low.append(bf16(exponent * (1.0 / jnp.sum(exponent, axis=-1, keepdims=True))))
        probs[head] = low[head]
    for pair in range(HEADS // 2):
        values = qkv[:, pair_lanes(pair, 2)]
        parts = [dot(low[2 * pair + half], values) for half in range(2)]
        mixed[:, pair_lanes(pair, 0)] = bf16(jnp.where(lane, parts[0], parts[1]))


def heads_backward(qkv, grad_mixed, probs, pairs):
    lane = lax.broadcasted_iota(jnp.int32, (1, 2 * HEAD), 1) < HEAD
    heads = [(pair, half) for pair in pairs for half in range(2)]
    operands = {pair: [qkv[:, pair_lanes(pair, part)] for part in range(3)] for pair in pairs}
    grads = {pair: grad_mixed[:, pair_lanes(pair, 0)] for pair in pairs}
    halves = {pair: head_halves(grads[pair]) for pair in pairs}
    low = {head: probs[2 * head[0] + head[1]] for head in heads}
    grad_probs = {head: dot_nt(halves[head[0]][head[1]], operands[head[0]][2]) for head in heads}
    grad_values = {head: dot_tn(low[head], grads[head[0]]) for head in heads}
    grad_scores = {}
    for head in heads:
        full = f32(low[head])
        weighted = full * grad_probs[head]
        grad_scores[head] = bf16(weighted - full * jnp.sum(weighted, axis=-1, keepdims=True))
    grad_keys = {head: dot_tn(grad_scores[head], operands[head[0]][0]) for head in heads}
    grad_queries = {head: dot(grad_scores[head], operands[head[0]][1]) for head in heads}
    for pair in pairs:
        first, second = (pair, 0), (pair, 1)
        qkv[:, pair_lanes(pair, 0)] = bf16(jnp.where(lane, grad_queries[first], grad_queries[second]) * 0.125)
        qkv[:, pair_lanes(pair, 1)] = bf16(jnp.where(lane, grad_keys[first], grad_keys[second]) * 0.125)
        qkv[:, pair_lanes(pair, 2)] = bf16(jnp.where(lane, grad_values[first], grad_values[second]))


def space_forward_body(
    destinations,
    cell_counts,
    tokens,
    loss_grad,
    condition,
    biases,
    w_ada,
    w_qkv,
    w_out,
    arrived,
    qkv_all,
    mixed_all,
    probs_all,
    state_cells,
    loss_early,
    modulation,
    x_scr,
    ada_scr,
    wqkv_scr,
    wout_scr,
    qkv_scr,
    mixed_scr,
    probs_scr,
    state_scr,
    local_sem,
    in_send,
    in_recv,
    grad_send,
    grad_recv,
    out_send,
    out_recv,
    save_sem,
):
    slot = lax.axis_index("dp")
    rank = lax.axis_index("seq")

    def arrival(frame, hop):
        peer = lax.rem(slot + hop, CLIPS)
        rows = pl.ds(pl.multiple_of(slot * CELL_HOME, CELL_HOME), CELL_HOME)
        return pltpu.make_async_remote_copy(
            src_ref=tokens.at[peer, frame],
            dst_ref=x_scr.at[frame, rows],
            send_sem=in_send.at[frame, hop],
            recv_sem=in_recv.at[frame, hop],
            device_id=(peer, rank),
            device_id_type=MESH,
        )

    def loss_source(half, hop):
        return loss_grad.at[lax.rem(slot + hop, CLIPS), :, pl.ds(half * CHUNK_CELLS, CHUNK_CELLS)]

    def loss_place(order):
        return loss_early.at[lax.rem(order, 2), pl.ds(rank * FRAME_PART, FRAME_PART)]

    def loss_send(half, hop):
        target, order = loss_target(slot, half)
        return pltpu.make_async_remote_copy(
            src_ref=loss_source(half, hop),
            dst_ref=loss_place(order),
            send_sem=grad_send.at[half, hop],
            recv_sem=grad_recv.at[lax.rem(order, 2), rank],
            device_id=(lax.rem(slot + hop, CLIPS), target),
            device_id_type=MESH,
        )

    def loss_keep(half):
        _, order = loss_target(slot, half)
        return pltpu.make_async_copy(loss_source(half, 0), loss_place(order), grad_recv.at[lax.rem(order, 2), rank])

    def loss_each(remote, local):
        for half in range(2):
            target, order = loss_target(slot, half)

            @pl.when(order < 2)
            def _():
                @pl.when(target == rank)
                def _():
                    local(half)

                @pl.when(target != rank)
                def _():
                    remote(half, 0)

                for hop in range(1, CLIPS):
                    remote(half, hop)

    def leave(frame, hop, order):
        peer = lax.rem(rank + hop, RANKS)
        return pltpu.make_async_remote_copy(
            src_ref=state_scr.at[frame, chunk_cells(order, peer)],
            dst_ref=state_cells.at[order, rank * FRAME_PART + frame],
            send_sem=out_send.at[frame, hop, order],
            recv_sem=out_recv.at[frame, hop, order],
            device_id=(slot, peer),
            device_id_type=MESH,
        )

    def keep(frame, order):
        return pltpu.make_async_copy(
            state_scr.at[frame, chunk_cells(order, rank)],
            state_cells.at[order, rank * FRAME_PART + frame],
            out_recv.at[frame, 0, order],
        )

    def saves(frame):
        return (
            pltpu.make_async_copy(x_scr.at[frame], arrived.at[frame], save_sem.at[frame, 0]),
            pltpu.make_async_copy(qkv_scr.at[frame], qkv_all.at[frame], save_sem.at[frame, 1]),
            pltpu.make_async_copy(mixed_scr.at[frame], mixed_all.at[frame], save_sem.at[frame, 2]),
        )

    def save_probs(frame):
        return pltpu.make_async_copy(probs_scr.at[lax.rem(frame, 2)], probs_all.at[frame], save_sem.at[frame, 3])

    own_rows = pl.ds(pl.multiple_of(slot * CELL_HOME, CELL_HOME), CELL_HOME)
    own_copy = pltpu.make_async_copy(tokens.at[slot], x_scr.at[:, own_rows], local_sem.at[0])
    ada_copy = pltpu.make_async_copy(w_ada, ada_scr, local_sem.at[1])
    qkv_copy = pltpu.make_async_copy(w_qkv, wqkv_scr, local_sem.at[2])
    out_copy = pltpu.make_async_copy(w_out, wout_scr, local_sem.at[3])
    for hop in range(1, CLIPS):
        arrival(0, hop).start()
    own_copy.start()
    ada_copy.start()
    for frame in range(1, FRAME_PART):
        for hop in range(1, CLIPS):
            arrival(frame, hop).start()
    qkv_copy.start()
    out_copy.start()

    row_ids = lax.broadcasted_iota(jnp.int32, (CLIPS, 1), 0)
    cond = column_sum(jnp.where(row_ids == destinations[slot], f32(condition[...]), 0.0))
    cond = jnp.broadcast_to(bf16(cond / (1.0 + jnp.exp(-cond))), (16, D))
    bias_rows = f32(biases[...])
    valid = lax.broadcasted_iota(jnp.int32, (1, CELLS), 1) < cell_counts[slot]
    ada_copy.wait()
    for piece in range(9):
        row = dot(cond, ada_scr[:, pl.ds(piece * D, D)])[0:1]
        modulation[pl.ds(piece, 1)] = row + bias_rows[piece : piece + 1]
    own_copy.wait()
    qkv_copy.wait()
    out_copy.wait()

    def frame_step(frame, carry):
        for hop in range(1, CLIPS):
            arrival(frame, hop).wait_recv()

        @pl.when(frame == 2)
        def _():
            loss_each(lambda half, hop: loss_send(half, hop).start(), lambda half: loss_keep(half).start())

        x = f32(x_scr[frame])
        centred = x - jnp.mean(x, axis=-1, keepdims=True)
        normed = centred * lax.rsqrt(jnp.mean(centred * centred, axis=-1, keepdims=True) + 1e-06)
        act = bf16(normed * (1.0 + modulation[1:2]) + modulation[0:1])
        qkv_scr[frame] = bf16(dot(act, wqkv_scr[...]))

        @pl.when(frame >= 2)
        def _():
            save_probs(frame - 2).wait()

        heads_forward(qkv_scr.at[frame], mixed_scr.at[frame], probs_scr.at[lax.rem(frame, 2)], valid)
        save_probs(frame).start()
        spatial = dot(mixed_scr[frame], wout_scr[...]) + bias_rows[9:10]
        state_scr[frame] = bf16(f32(x_scr[frame]) + modulation[2:3] * spatial)
        for order in range(CHUNKS):
            for hop in range(1, RANKS):
                leave(frame, hop, order).start()
            keep(frame, order).start()
        for save in saves(frame):
            save.start()
        return carry

    lax.fori_loop(0, FRAME_PART, frame_step, 0)

    def frame_end(frame, carry):
        for hop in range(1, CLIPS):
            arrival(frame, hop).wait_send()
        for order in range(CHUNKS):
            for hop in range(1, RANKS):
                leave(frame, hop, order).wait()
            keep(frame, order).wait()
        for save in saves(frame):
            save.wait()
        return carry

    lax.fori_loop(0, FRAME_PART, frame_end, 0)
    for frame in range(FRAME_PART - 2, FRAME_PART):
        save_probs(frame).wait()

    loss_each(lambda half, hop: loss_send(half, hop).wait_send(), lambda half: None)
    for order in range(2):
        for source in range(RANKS):
            place = loss_early.at[order, pl.ds(source * FRAME_PART, FRAME_PART)]
            pltpu.make_async_copy(
                loss_grad.at[0, :, pl.ds(0, CHUNK_CELLS)], place, grad_recv.at[order, source]
            ).wait()


def space_forward(destinations, cell_counts, tokens, loss_grad, condition, biases, w_ada, w_qkv, w_out):
    low = jnp.bfloat16
    return pl.pallas_call(
        space_forward_body,
        out_shape=(
            jax.ShapeDtypeStruct((FRAME_PART, CELLS, D), low),
            jax.ShapeDtypeStruct((FRAME_PART, CELLS, 3 * D), low),
            jax.ShapeDtypeStruct((FRAME_PART, CELLS, D), low),
            jax.ShapeDtypeStruct((FRAME_PART, HEADS, CELLS, CELLS), low),
            jax.ShapeDtypeStruct((CHUNKS, FRAME_PART * RANKS, CHUNK_CELLS, D), low),
            jax.ShapeDtypeStruct((2, FRAME_PART * RANKS, CHUNK_CELLS, D), low),
            jax.ShapeDtypeStruct((16, D), jnp.float32),
        ),
        in_specs=[SMEM, SMEM, ANY, ANY, VMEM, VMEM, ANY, ANY, ANY],
        out_specs=(ANY, ANY, ANY, ANY, ANY, ANY, VMEM),
        scratch_shapes=[
            pltpu.VMEM((FRAME_PART, CELLS, D), low),
            pltpu.VMEM((D, 9 * D), low),
            pltpu.VMEM((D, 3 * D), low),
            pltpu.VMEM((D, D), low),
            pltpu.VMEM((FRAME_PART, CELLS, 3 * D), low),
            pltpu.VMEM((FRAME_PART, CELLS, D), low),
            pltpu.VMEM((2, HEADS, CELLS, CELLS), low),
            pltpu.VMEM((FRAME_PART, CELLS, D), low),
            pltpu.SemaphoreType.DMA((4,)),
            pltpu.SemaphoreType.DMA((FRAME_PART, CLIPS)),
            pltpu.SemaphoreType.DMA((FRAME_PART, CLIPS)),
            pltpu.SemaphoreType.DMA((2, CLIPS)),
            pltpu.SemaphoreType.DMA((2, RANKS)),
            pltpu.SemaphoreType.DMA((FRAME_PART, RANKS, CHUNKS)),
            pltpu.SemaphoreType.DMA((FRAME_PART, RANKS, CHUNKS)),
            pltpu.SemaphoreType.DMA((FRAME_PART, 4)),
        ],
        compiler_params=pltpu.CompilerParams(has_side_effects=True, vmem_limit_bytes=48 * 1024 * 1024),
        cost_estimate=pl.CostEstimate(flops=8 * 10**9, bytes_accessed=40 * 10**6, transcendentals=3 * 10**6),
        name="space_forward",
    )(destinations, cell_counts, tokens, loss_grad, condition, biases, w_ada, w_qkv, w_out)


def cell_match():
    row_cell = lax.rem(lax.broadcasted_iota(jnp.int32, (TOKENS, TOKENS), 0), CHUNK_CELLS)
    column_cell = lax.rem(lax.broadcasted_iota(jnp.int32, (TOKENS, TOKENS), 1), CHUNK_CELLS)
    return row_cell == column_cell


SAVED_WIDTHS = (D, 3 * D, D, D, D, FF, FF, D)


def time_forward_body(
    cell_counts,
    frame_tasks,
    state_cells,
    loss_grad,
    loss_early,
    modulation,
    biases,
    w_qkv,
    w_out,
    w_up,
    w_down,
    layer_home,
    act_two_all,
    qkv_all,
    mixed_all,
    grad_temporal_all,
    act_three_all,
    grad_lifted_all,
    hidden_all,
    grad_branch_all,
    grad_state_all,
    probs_all,
    sums,
    state_scr,
    loss_scr,
    wqkv_scr,
    wout_scr,
    wup_scr,
    wdown_scr,
    slopes,
    layer_scr,
    act_two,
    qkv,
    mixed,
    grad_temporal,
    act_three,
    grad_lifted,
    hidden,
    grad_branch,
    grad_state,
    probs,
    load_sem,
    loss_send_sem,
    loss_recv_sem,
    layer_send,
    layer_recv,
    save_sem,
):
    slot = lax.axis_index("dp")
    rank = lax.axis_index("seq")
    frames = FRAME_PART * RANKS

    def loss_source(half, hop):
        return loss_grad.at[lax.rem(slot + hop, CLIPS), :, pl.ds(half * CHUNK_CELLS, CHUNK_CELLS)]

    def loss_place(order):
        return loss_scr.at[2 + lax.rem(order, 2), pl.ds(rank * FRAME_PART, FRAME_PART)]

    def loss_send(half, hop):
        target, order = loss_target(slot, half)
        return pltpu.make_async_remote_copy(
            src_ref=loss_source(half, hop),
            dst_ref=loss_place(order),
            send_sem=loss_send_sem.at[half, hop],
            recv_sem=loss_recv_sem.at[lax.rem(order, 2), rank],
            device_id=(lax.rem(slot + hop, CLIPS), target),
            device_id_type=MESH,
        )

    def loss_keep(half):
        _, order = loss_target(slot, half)
        return pltpu.make_async_copy(
            loss_source(half, 0), loss_place(order), loss_recv_sem.at[lax.rem(order, 2), rank]
        )

    def loss_each(remote, local):
        for half in range(2):
            target, order = loss_target(slot, half)

            @pl.when(order >= 2)
            def _():
                @pl.when(target == rank)
                def _():
                    local(half)

                @pl.when(target != rank)
                def _():
                    remote(half, 0)

                for hop in range(1, CLIPS):
                    remote(half, hop)

    def loss_arrival(order, source):
        place = loss_scr.at[order, pl.ds(source * FRAME_PART, FRAME_PART)]
        return pltpu.make_async_copy(
            loss_grad.at[0, :, pl.ds(0, CHUNK_CELLS)], place, loss_recv_sem.at[order - 2, source]
        )

    def layer_home_of(order):
        chunk = chunk_of(order, rank)
        share = share_of(chunk, rank)
        return 2 * chunk + share // 2, lax.rem(share, 2)

    def layer_place(half):
        return layer_home.at[slot, :, pl.ds(pl.multiple_of(half * CHUNK_CELLS, CHUNK_CELLS), CHUNK_CELLS)]

    def layer_send_copy(order, target):
        home, half = layer_home_of(order)
        return pltpu.make_async_remote_copy(
            src_ref=layer_scr.at[order, pl.ds(target * FRAME_PART, FRAME_PART)],
            dst_ref=layer_place(half),
            send_sem=layer_send.at[order, target],
            recv_sem=layer_recv.at[slot, half],
            device_id=(home, target),
            device_id_type=MESH,
        )

    def layer_keep_copy(order, target):
        _, half = layer_home_of(order)
        return pltpu.make_async_copy(
            layer_scr.at[order, pl.ds(target * FRAME_PART, FRAME_PART)], layer_place(half), layer_recv.at[slot, half]
        )

    def layer_self(order, target):
        return jnp.logical_and(layer_home_of(order)[0] == slot, rank == target)

    stages = (act_two, qkv, mixed, grad_temporal, act_three, grad_lifted, hidden, grad_branch, grad_state, probs)
    homes = (
        act_two_all,
        qkv_all,
        mixed_all,
        grad_temporal_all,
        act_three_all,
        grad_lifted_all,
        hidden_all,
        grad_branch_all,
        grad_state_all,
        probs_all,
    )

    def save(which, order):
        spot = lax.rem(order, 2)
        return pltpu.make_async_copy(stages[which].at[spot], homes[which].at[order], save_sem.at[which, spot])

    loads = (
        pltpu.make_async_copy(state_cells, state_scr, load_sem.at[0]),
        pltpu.make_async_copy(w_qkv, wqkv_scr, load_sem.at[1]),
        pltpu.make_async_copy(w_out, wout_scr, load_sem.at[2]),
        pltpu.make_async_copy(w_up, wup_scr, load_sem.at[3]),
        pltpu.make_async_copy(w_down, wdown_scr, load_sem.at[4]),
        pltpu.make_async_copy(loss_early, loss_scr.at[pl.ds(0, 2)], load_sem.at[5]),
    )
    for load in loads:
        load.start()
    loss_each(lambda half, hop: loss_send(half, hop).start(), lambda half: loss_keep(half).start())
    sums[...] = jnp.zeros_like(sums)
    bias_rows = f32(biases[...])
    valid = cell_match()
    count = cell_counts[slot]

    def piece(index):
        return modulation[index : index + 1]

    def add(row, value):
        sums[pl.ds(row, 1)] += value

    def chunk_step(order, carry):
        spot = lax.rem(order, 2)
        first = order == 0

        def once(*which):
            @pl.when(first)
            def _():
                for load in which:
                    loads[load].wait()

        @pl.when(order >= 2)
        def _():
            for which in range(len(stages)):
                save(which, order - 2).wait()

        once(0)
        state = f32(state_scr[order]).reshape(TOKENS, D)
        normed_two, _ = standardise(state)
        act_two[spot] = bf16(normed_two * (1.0 + piece(4)) + piece(3))
        once(1)
        qkv[spot] = bf16(dot(act_two[spot], wqkv_scr[...]))
        heads_forward(qkv.at[spot], mixed.at[spot], probs.at[spot], valid)
        for which in (0, 1, 2, 9):
            save(which, order).start()
        once(2)
        temporal = dot(mixed[spot], wout_scr[...]) + bias_rows[10:11]
        state_two = state + piece(5) * temporal
        normed_three, inverse_three = standardise(state_two)
        act_three[spot] = bf16(normed_three * (1.0 + piece(7)) + piece(6))
        save(4, order).start()
        once(3, 4)
        branch = jnp.zeros((TOKENS, D), jnp.float32) + bias_rows[15:16]
        for block in range(FF // D):
            lanes = pl.ds(block * D, D)
            lifted = dot(act_three[spot], wup_scr[:, lanes]) + bias_rows[11 + block : 12 + block]
            square = lifted * lifted
            curve = jnp.tanh(0.7978845608028654 * lifted * (1.0 + 0.044715 * square))
            half = 0.5 * (1.0 + curve)
            hidden[spot, :, lanes] = bf16(lifted * half)
            slopes[:, lanes] = half + 0.5 * lifted * (1.0 - curve * curve) * (
                0.7978845608028654 * (1.0 + 3.0 * 0.044715 * square)
            )
            branch += dot(hidden[spot, :, lanes], wdown_scr[lanes, :])
        save(6, order).start()
        layer_scr[order] = bf16(state_two + piece(8) * branch).reshape(frames, CHUNK_CELLS, D)
        for target in range(RANKS):

            @pl.when(layer_self(order, target))
            def _():
                layer_keep_copy(order, target).start()

            @pl.when(jnp.logical_not(layer_self(order, target)))
            def _():
                layer_send_copy(order, target).start()

        once(5)

        @pl.when(order >= 2)
        def _():
            for source in range(RANKS):
                loss_arrival(order, source).wait()

        chunk = chunk_of(order, rank)
        first_cell = chunk * CELL_PART + share_of(chunk, rank) * CHUNK_CELLS
        token = lax.broadcasted_iota(jnp.int32, (TOKENS, 1), 0)
        frame, cell = token // CHUNK_CELLS, lax.rem(token, CHUNK_CELLS)
        mask = jnp.zeros((TOKENS, 1), jnp.int32)
        for which in range(frames):
            mask = jnp.where(frame == which, frame_tasks[slot, which], mask)
        mask = jnp.where(first_cell + cell < count, mask, 0)
        seed = f32(loss_scr[order]).reshape(TOKENS, D) * f32(mask)
        add(8, column_sum(seed * branch))
        low_branch = bf16(piece(8) * seed)
        grad_branch[spot] = low_branch
        save(7, order).start()
        add(13, column_sum(f32(low_branch)))
        grad_act = jnp.zeros((TOKENS, D), jnp.float32)
        for block in range(FF // D):
            lanes = pl.ds(block * D, D)
            low_lifted = bf16(dot_nt(grad_branch[spot], wdown_scr[lanes, :]) * slopes[:, lanes])
            grad_lifted[spot, :, lanes] = low_lifted
            add(9 + block, column_sum(f32(low_lifted)))
            grad_act += dot_nt(grad_lifted[spot, :, lanes], wup_scr[:, lanes])
        save(5, order).start()
        add(6, column_sum(grad_act))
        add(7, column_sum(grad_act * normed_three))
        grad_state_two = seed + standard_back(normed_three, inverse_three, grad_act * (1.0 + piece(7)))
        grad_state[spot] = grad_state_two
        save(8, order).start()
        add(5, column_sum(grad_state_two * temporal))
        low_temporal = bf16(piece(5) * grad_state_two)
        grad_temporal[spot] = low_temporal
        save(3, order).start()
        add(14, column_sum(f32(low_temporal)))
        return carry

    lax.fori_loop(0, CHUNKS, chunk_step, 0)
    for order in (CHUNKS - 2, CHUNKS - 1):
        for which in range(len(stages)):
            save(which, order).wait()

    loss_each(lambda half, hop: loss_send(half, hop).wait_send(), lambda half: None)

    def layer_end(order, carry):
        for target in range(RANKS):

            @pl.when(jnp.logical_not(layer_self(order, target)))
            def _():
                layer_send_copy(order, target).wait_send()

        return carry

    lax.fori_loop(0, CHUNKS, layer_end, 0)
    for clip in range(CLIPS):
        for half in range(2):
            place = layer_home.at[clip, :, pl.ds(half * CHUNK_CELLS, CHUNK_CELLS)]
            pltpu.make_async_copy(
                layer_scr.at[0, pl.ds(0, FRAME_PART)], place, layer_recv.at[clip, half]
            ).wait()


def time_forward(
    cell_counts, frame_tasks, state_cells, loss_grad, loss_early, modulation, biases, w_qkv, w_out, w_up, w_down
):
    low = jnp.bfloat16
    frames = FRAME_PART * RANKS
    kinds = [(width, low) for width in SAVED_WIDTHS] + [(D, jnp.float32)]
    return pl.pallas_call(
        time_forward_body,
        out_shape=(jax.ShapeDtypeStruct((CLIPS, FRAME_PART, CELL_HOME, D), low),)
        + tuple(jax.ShapeDtypeStruct((CHUNKS, TOKENS, width), kind) for width, kind in kinds)
        + (jax.ShapeDtypeStruct((CHUNKS, HEADS, TOKENS, TOKENS), low),)
        + (jax.ShapeDtypeStruct((16, D), jnp.float32),),
        in_specs=[SMEM, SMEM, ANY, ANY, ANY, VMEM, VMEM, ANY, ANY, ANY, ANY],
        out_specs=(ANY,) * 11 + (VMEM,),
        scratch_shapes=[
            pltpu.VMEM((CHUNKS, frames, CHUNK_CELLS, D), low),
            pltpu.VMEM((CHUNKS, frames, CHUNK_CELLS, D), low),
            pltpu.VMEM((D, 3 * D), low),
            pltpu.VMEM((D, D), low),
            pltpu.VMEM((D, FF), low),
            pltpu.VMEM((FF, D), low),
            pltpu.VMEM((TOKENS, FF), jnp.float32),
            pltpu.VMEM((CHUNKS, frames, CHUNK_CELLS, D), low),
        ]
        + [pltpu.VMEM((2, TOKENS, width), kind) for width, kind in kinds]
        + [
            pltpu.VMEM((2, HEADS, TOKENS, TOKENS), low),
            pltpu.SemaphoreType.DMA((6,)),
            pltpu.SemaphoreType.DMA((2, CLIPS)),
            pltpu.SemaphoreType.DMA((2, RANKS)),
            pltpu.SemaphoreType.DMA((CHUNKS, RANKS)),
            pltpu.SemaphoreType.DMA((CLIPS, 2)),
            pltpu.SemaphoreType.DMA((10, 2)),
        ],
        compiler_params=pltpu.CompilerParams(has_side_effects=True, vmem_limit_bytes=58 * 1024 * 1024),
        cost_estimate=pl.CostEstimate(flops=40 * 10**9, bytes_accessed=50 * 10**6, transcendentals=6 * 10**6),
        name="time_forward",
    )(cell_counts, frame_tasks, state_cells, loss_grad, loss_early, modulation, biases, w_qkv, w_out, w_up, w_down)


UNITS = 16
ROWS = D // RANKS
HALF_ROWS = ROWS // 2
KINDS = "PSSSSPPPPMPPPPMP"
SCHEDULE = (
    ("double", 0), (0, 0), (0, 1), ("chunk", 0), (1, 0), ("chunk", 1), (1, 1), ("double", 1), (0, 2), (0, 3),
    ("chunk", 2), (1, 2), ("chunk", 3), (2, 0), (2, 1), (1, 3), ("unit", 4), (0, 4), ("unit", 5), (0, 5), (2, 2),
    ("unit", 6), (0, 6), (1, 4), (3, 0), ("unit", 7), (0, 7), (1, 5), (3, 1), (1, 6), ("first", 0), (2, 3), (4, 0),
    (3, 2), (1, 7), ("second", 0), (4, 1), ("first", 1), (5, 0), (4, 2), (2, 4), (2, 5), ("second", 1),
    ("unit", 8), (0, 8), (2, 6), ("first", 2), (3, 5), ("second", 2), (6, 0), (3, 3), (1, 8), (5, 1), ("unit", 9),
    (0, 9), ("first", 3), (5, 2), (4, 5), (3, 6), (2, 7), ("second", 3), (3, 4), (1, 9), ("unit", 10), (0, 10),
    (7, 0), ("unit", 11), (0, 11), (6, 1), (4, 3), (3, 7), (2, 8), ("sums", 0), ("unit", 12), (0, 12), (6, 2),
    (4, 6), (1, 10), (1, 11), ("unit", 13), (0, 13), (2, 9), (7, 1), (1, 12), ("sums", 1), ("unit", 14), (0, 14),
    (5, 5), (3, 8), (1, 13), (4, 4), ("unit", 15), (0, 15), (7, 2), (2, 10), (4, 7), (1, 14), (6, 5), (1, 15),
    (2, 11), (5, 3), (3, 9), (3, 10), (5, 6), (4, 8), (7, 5), (6, 3), (2, 12), (4, 10), (3, 11), (6, 6), (7, 3),
    (5, 4), (4, 11), (2, 13), (3, 12), (5, 7), (6, 4), (7, 6), (4, 9), (4, 12), (2, 14), (6, 7), (3, 13), (5, 8),
    (7, 4), (5, 10), (2, 15), (6, 8), (5, 9), (5, 11), (3, 14), (6, 10), (7, 7), (5, 12), (4, 13), (3, 15), (6, 9),
    (6, 11), (7, 8), (4, 14), (4, 15), (6, 12), (7, 10), (5, 13), (7, 9), (7, 11), (5, 15), (6, 13), (5, 14),
    (6, 15), (7, 12), (6, 14), (7, 13), (7, 15), (7, 14),
)


def tail_body(
    arrived,
    qkv,
    mixed,
    probs,
    state_cells,
    act_two,
    qkv_two,
    mixed_two,
    grad_temporal,
    act_three,
    grad_lifted,
    hidden,
    grad_branch,
    grad_state_two,
    probs_two,
    modulation,
    biases,
    sums_in,
    w_qkv_t,
    w_out_t,
    w_qkv,
    w_out,
    grad_home,
    totals,
    gathered,
    x_scr,
    state_scr,
    qkv_scr,
    mixed_scr,
    spatial_scr,
    time_scr,
    wqkv_scr,
    wout_scr,
    left_scr,
    right_scr,
    grad_mixed,
    chunk_state,
    chunk_grad,
    chunk_temporal,
    probs_scr,
    own,
    first_out,
    kept,
    core_in,
    first_in,
    second_in,
    edge_in,
    middle_in,
    sums,
    sums_in_scr,
    load_sem,
    frame_sem,
    probs_sem,
    side_sem,
    chunk_sem,
    cell_send,
    cell_recv,
    home_send,
    home_recv,
    unit_send,
    unit_recv,
    sum_send,
    sum_recv,
):
    slot = lax.axis_index("dp")
    rank = lax.axis_index("seq")
    core = lax.rem(rank, 2)
    over_x = rank // 2
    over_y = lax.rem(slot, 2)
    over_z = slot // 2
    at_edge = jnp.logical_or(over_z == 0, over_z == 3)
    low_side = over_z < 2
    core_peer = (slot, rank + 1 - 2 * core)
    x_peer = (slot, lax.rem(rank + 2, RANKS))
    y_peer = (slot + 1 - 2 * over_y, rank)
    inner_peer = (jnp.where(low_side, 2, 4) + over_y, rank)
    middle_peer = (jnp.where(low_side, 4, 2) + over_y, rank)
    outer_peer = (jnp.where(low_side, 0, 6) + over_y, rank)

    def piece(index):
        return modulation[index : index + 1]

    def remote(source, target, send, recv, peer):
        return pltpu.make_async_remote_copy(
            src_ref=source, dst_ref=target, send_sem=send, recv_sem=recv, device_id=peer, device_id_type=MESH
        )


    turned = over_z // 2

    def spots(unit):
        mine = {"P": over_y, "S": over_x, "M": turned}[KINDS[unit]]
        return mine, 1 - mine

    def half_rows(which):
        return pl.ds(pl.multiple_of(which * HALF_ROWS, HALF_ROWS), HALF_ROWS)

    def send(kind, unit, source, target, peer, landing=None):
        landing = kind if landing is None else landing
        return remote(source, target, unit_send.at[kind, unit], unit_recv.at[landing, unit], peer)

    def core_copy(unit):
        return send(0, unit, own.at[unit % 4, 1 - core], core_in.at[unit % 6], core_peer)

    def first_copy(unit):
        peer = y_peer if KINDS[unit] == "S" else x_peer
        return send(1, unit, first_out.at[unit % 8], first_in.at[unit % 10], peer)

    def second_copy(unit):
        mine, other = spots(unit)
        if KINDS[unit] == "M":
            return send(2, unit, kept.at[unit, mine], second_in.at[unit % 10], y_peer)
        peer = x_peer if KINDS[unit] == "S" else y_peer
        return send(2, unit, kept.at[unit, other], second_in.at[unit % 10], peer)

    def edge_copy(unit):
        if KINDS[unit] == "M":
            return send(3, unit, kept.at[unit], edge_in.at[unit % 8], inner_peer)
        mine, _ = spots(unit)
        return send(3, unit, kept.at[unit, mine], edge_in.at[unit % 8, 0], inner_peer)

    def middle_copy(unit):
        mine, other = spots(unit)
        source = kept.at[unit, other if KINDS[unit] == "M" else mine]
        return send(4, unit, source, middle_in.at[unit % 10], middle_peer)

    def outer_copy(unit):
        _, other = spots(unit)
        return send(5, unit, kept.at[unit, other], middle_in.at[unit % 10], outer_peer, 4)

    def share_copy(unit, source):
        return send(6, unit, source, totals.at[unit, half_rows(over_y)], y_peer)

    def keep_copy(unit, source, which):
        return pltpu.make_async_copy(source, totals.at[unit, half_rows(which)], unit_send.at[7, unit])

    def cross_copy(unit):
        mine, other = spots(unit)
        return send(6, unit, kept.at[unit, other], totals.at[unit, half_rows(mine)], middle_peer)

    def near_copy(unit):
        mine, other = spots(unit)
        return send(5, unit, kept.at[unit, other], totals.at[unit, half_rows(mine)], outer_peer)

    def far_copy(unit):
        _, other = spots(unit)
        place = totals.at[unit, half_rows(other)]
        return send(8, unit, place, place, outer_peer)

    def plus(left, right):
        return bf16(f32(left) + f32(right))

    def stage_one(unit):
        core_copy(unit).wait()
        held, came = own.at[unit % 4, core], core_in.at[unit % 6]
        if KINDS[unit] == "S":
            for part in range(2):
                first_out[unit % 8, part] = plus(held[part, 1 - over_y], came[part, 1 - over_y])
            first_copy(unit).start()
            for part in range(2):
                kept[unit, part] = plus(held[part, over_y], came[part, over_y])
        else:
            first_out[unit % 8] = plus(held[1 - over_x], came[1 - over_x])
            first_copy(unit).start()
            kept[unit] = plus(held[over_x], came[over_x])

    def stage_two(unit):
        first_copy(unit).wait()
        mine, other = spots(unit)
        if KINDS[unit] == "M":
            kept[unit] = plus(kept[unit], first_in[unit % 10])

            @pl.when(at_edge)
            def _():
                edge_copy(unit).start()

        else:
            kept[unit, other] = plus(kept[unit, other], first_in[unit % 10, other])
            second_copy(unit).start()
            kept[unit, mine] = plus(kept[unit, mine], first_in[unit % 10, mine])

    def stage_three(unit):
        mine, _ = spots(unit)
        if KINDS[unit] == "M":

            @pl.when(jnp.logical_not(at_edge))
            def _():
                edge_copy(unit).wait_recv()
                kept[unit] = plus(kept[unit], edge_in[unit % 8])
                middle_copy(unit).start()

        else:
            second_copy(unit).wait()
            kept[unit, mine] = plus(kept[unit, mine], second_in[unit % 10])

            @pl.when(at_edge)
            def _():
                edge_copy(unit).start()

    def stage_four(unit):
        mine, _ = spots(unit)

        @pl.when(jnp.logical_not(at_edge))
        def _():
            if KINDS[unit] == "M":
                middle_copy(unit).wait()
                kept[unit, mine] = plus(kept[unit, mine], middle_in[unit % 10])
                second_copy(unit).start()
            else:
                edge_copy(unit).wait_recv()
                kept[unit, mine] = plus(kept[unit, mine], edge_in[unit % 8, 0])
                middle_copy(unit).start()

    def stage_five(unit):
        mine, other = spots(unit)

        @pl.when(jnp.logical_not(at_edge))
        def _():
            if KINDS[unit] == "M":
                second_copy(unit).wait()
                kept[unit, other] = plus(kept[unit, mine], second_in[unit % 10])
                cross_copy(unit).start()
                near_copy(unit).start()
                keep_copy(unit, kept.at[unit, other], mine).start()
            else:
                middle_copy(unit).wait()
                kept[unit, other] = plus(kept[unit, mine], middle_in[unit % 10])
                share_copy(unit, kept.at[unit, other]).start()
                outer_copy(unit).start()
                keep_copy(unit, kept.at[unit, other], over_y).start()

    def stage_six(unit):
        if KINDS[unit] == "M":

            @pl.when(jnp.logical_not(at_edge))
            def _():
                cross_copy(unit).wait_recv()
                far_copy(unit).start()

        else:

            @pl.when(at_edge)
            def _():
                outer_copy(unit).wait_recv()
                share_copy(unit, middle_in.at[unit % 10]).start()
                keep_copy(unit, middle_in.at[unit % 10], over_y).start()

    def stage_seven(unit):
        mine, other = spots(unit)
        source = kept.at[unit, other]
        if KINDS[unit] == "M":

            @pl.when(at_edge)
            def _():
                edge_copy(unit).wait_send()
                near_copy(unit).wait_recv()
                far_copy(unit).wait_recv()

            @pl.when(jnp.logical_not(at_edge))
            def _():
                cross_copy(unit).wait_send()
                near_copy(unit).wait_send()
                far_copy(unit).wait_send()
                keep_copy(unit, source, mine).wait()

        else:

            @pl.when(at_edge)
            def _():
                edge_copy(unit).wait_send()

            @pl.when(jnp.logical_not(at_edge))
            def _():
                outer_copy(unit).wait_send()

            share_copy(unit, source).wait()
            keep_copy(unit, source, over_y).wait()

    stages = (
        lambda unit: core_copy(unit).start(),
        stage_one,
        stage_two,
        stage_three,
        stage_four,
        stage_five,
        stage_six,
        stage_seven,
    )


    def put_quarter(unit, quarter, rows):
        own[unit % 4, quarter % 2, quarter // 2] = bf16(rows).reshape(2, HALF_ROWS, D)

    def put_unit(unit, block):
        for quarter in range(RANKS):
            put_quarter(unit, quarter, block[quarter * ROWS : (quarter + 1) * ROWS])

    def flat(block):
        return block.reshape(CHUNKS * TOKENS, block.shape[-1])

    def unit_loads(unit):
        if unit < 8:
            left, right, column = act_three, grad_lifted, unit - 4
        elif unit < 11:
            left, right, column = act_two, time_scr, unit - 8
        else:
            left, right, column = mixed_two, grad_temporal, 0
        return (
            pltpu.make_async_copy(left, left_scr.at[unit % 2], load_sem.at[0, unit % 2]),
            pltpu.make_async_copy(
                right.at[:, :, pl.ds(column * D, D)], right_scr.at[unit % 2], load_sem.at[1, unit % 2]
            ),
        )

    def make_unit(unit):
        if unit < 12:
            for load in unit_loads(unit):
                load.wait()
            left, right = left_scr[unit % 2], right_scr[unit % 2]
        elif unit < 15:
            left, right = x_scr[...], qkv_scr[:, :, pl.ds((unit - 12) * D, D)]
        else:
            left, right = mixed_scr[...], spatial_scr[...]
        put_unit(unit, dot_tn(flat(left), flat(right)))
        if 4 <= unit < 10:
            for load in unit_loads(unit + 2):
                load.start()

    def hidden_load(block):
        spot = block % 2
        lanes = pl.ds(block % RANKS * D, D)
        return pltpu.make_async_copy(hidden.at[:, :, lanes], right_scr.at[spot], load_sem.at[1, spot])

    def double_unit(double):
        for block in range(RANKS):
            hidden_load(block).wait()
            left = left_scr[0, :, :, pl.ds(double * 2 * ROWS, 2 * ROWS)]
            columns = dot_tn(flat(left), flat(right_scr[block % 2]))
            if block + 2 < RANKS or double == 0:
                hidden_load(block + 2).start()
            for part in range(2):
                put_quarter(2 * double + part, block, columns[part * ROWS : (part + 1) * ROWS])
        if double == 1:
            for unit in (4, 5):
                for load in unit_loads(unit):
                    load.start()


    def chunk_loads(order):
        spot = order % 2
        return (
            pltpu.make_async_copy(state_cells.at[order], chunk_state.at[spot], chunk_sem.at[0, spot]),
            pltpu.make_async_copy(grad_state_two.at[order], chunk_grad.at[spot], chunk_sem.at[1, spot]),
            pltpu.make_async_copy(grad_temporal.at[order], chunk_temporal.at[spot], chunk_sem.at[2, spot]),
            pltpu.make_async_copy(qkv_two.at[order], time_scr.at[order], chunk_sem.at[3, spot]),
        )

    def cell_place(order, frame):
        return state_scr.at[frame, chunk_cells(order, rank)]

    def cell_rows(order, target, frame):
        start = (target * FRAME_PART + frame) * CHUNK_CELLS
        return spatial_scr.at[order, pl.ds(pl.multiple_of(start, CHUNK_CELLS), CHUNK_CELLS)]

    def cell_copy(order, hop, frame):
        target = lax.rem(rank + hop, RANKS)
        return remote(
            cell_rows(order, target, frame),
            cell_place(order, frame),
            cell_send.at[order, hop, frame],
            cell_recv.at[order, hop, frame],
            (slot, target),
        )

    def cell_keep(order, frame):
        return pltpu.make_async_copy(
            cell_rows(order, rank, frame), cell_place(order, frame), cell_recv.at[order, 0, frame]
        )

    def probs_load(step):
        source = probs_two.at[step] if step < CHUNKS else probs.at[step - CHUNKS]
        return pltpu.make_async_copy(source, probs_scr, probs_sem.at[0])

    def probs_next(step):
        if step < CHUNKS + FRAME_PART:
            probs_load(step).start()

    def time_backward(order):
        spot = order % 2
        for load in chunk_loads(order):
            load.wait()
        probs_load(order).wait()
        if order < CHUNKS - 1:
            for load in chunk_loads(order + 1):
                load.start()

        grad_mixed[...] = bf16(dot_nt(chunk_temporal[spot], wout_scr[...]))
        heads_backward(time_scr.at[order], grad_mixed, probs_scr, range(HEADS // 2))
        probs_next(order + 1)
        grad_act = dot_nt(time_scr[order], wqkv_scr[...])
        normed, inverse = standardise(f32(chunk_state[spot]).reshape(TOKENS, D))
        add(3, column_sum(grad_act))
        add(4, column_sum(grad_act * normed))
        spatial_scr[order] = bf16(
            chunk_grad[spot] + standard_back(normed, inverse, grad_act * (1.0 + piece(4)))
        )
        for frame in range(FRAME_PART):
            for hop in range(1, RANKS):
                cell_copy(order, hop, frame).start()
            cell_keep(order, frame).start()


    def add(row, value):
        sums[pl.ds(row, 1)] += value

    def frame_loads(frame):
        return (
            pltpu.make_async_copy(arrived.at[frame], x_scr.at[frame], frame_sem.at[0, frame]),
            pltpu.make_async_copy(qkv.at[frame], qkv_scr.at[frame], frame_sem.at[1, frame]),
            pltpu.make_async_copy(mixed.at[frame], mixed_scr.at[frame], frame_sem.at[2, frame]),
        )

    def home_copy(frame, hop):
        peer = lax.rem(slot + hop, CLIPS)
        rows = pl.ds(pl.multiple_of(peer * CELL_HOME, CELL_HOME), CELL_HOME)
        return remote(
            state_scr.at[frame, rows],
            grad_home.at[slot, frame],
            home_send.at[frame, hop],
            home_recv.at[frame, hop],
            (peer, rank),
        )

    def home_keep(frame):
        rows = pl.ds(pl.multiple_of(slot * CELL_HOME, CELL_HOME), CELL_HOME)
        return pltpu.make_async_copy(state_scr.at[frame, rows], grad_home.at[slot, frame], home_recv.at[frame, 0])

    def frame_first(frame):
        for load in frame_loads(frame):
            load.wait()
        for order in range(CHUNKS):
            for hop in range(1, RANKS):
                cell_copy(order, hop, frame).wait_recv()
        grad_state = f32(state_scr[frame])
        spatial = dot(mixed_scr[frame], wout_scr[...]) + bias_rows[9:10]
        add(2, column_sum(grad_state * spatial))
        low_spatial = bf16(piece(2) * grad_state)
        spatial_scr[frame] = low_spatial
        add(15, column_sum(f32(low_spatial)))
        grad_mixed[...] = bf16(dot_nt(low_spatial, wout_scr[...]))
        probs_load(CHUNKS + frame).wait()
        heads_backward(qkv_scr.at[frame], grad_mixed, probs_scr, range(HEADS // 4))

    def frame_second(frame):
        heads_backward(qkv_scr.at[frame], grad_mixed, probs_scr, range(HEADS // 4, HEADS // 2))
        probs_next(CHUNKS + frame + 1)
        grad_act = dot_nt(qkv_scr[frame], wqkv_scr[...])
        normed, inverse = standardise(f32(x_scr[frame]))
        x_scr[frame] = bf16(normed * (1.0 + piece(1)) + piece(0))
        add(0, column_sum(grad_act))
        add(1, column_sum(grad_act * normed))
        state_scr[frame] = bf16(
            f32(state_scr[frame]) + standard_back(normed, inverse, grad_act * (1.0 + piece(1)))
        )
        for hop in range(1, CLIPS):
            home_copy(frame, hop).start()
        home_keep(frame).start()


    def sum_exchange(step):
        peer = core_peer if step == 0 else x_peer
        return remote(sums, sums_in_scr.at[step], sum_send.at[step], sum_recv.at[step], peer)

    def sum_add(step):
        sum_exchange(step).wait()
        sums[...] = sums[...] + sums_in_scr[step]

    def sum_spread(hop):
        peer = lax.rem(slot + hop, CLIPS)
        return remote(sums, gathered.at[slot], sum_send.at[1 + hop], sum_recv.at[1 + hop], (peer, rank))

    def sum_keep():
        return pltpu.make_async_copy(sums, gathered.at[slot], sum_send.at[9])


    time_weights = (
        pltpu.make_async_copy(w_qkv_t, wqkv_scr, side_sem.at[0]),
        pltpu.make_async_copy(w_out_t, wout_scr, side_sem.at[1]),
    )
    space_weights = (
        pltpu.make_async_copy(w_qkv, wqkv_scr, side_sem.at[0]),
        pltpu.make_async_copy(w_out, wout_scr, side_sem.at[1]),
    )
    branch_load = pltpu.make_async_copy(grad_branch, left_scr.at[0], load_sem.at[0, 0])
    branch_load.start()
    hidden_load(0).start()
    hidden_load(1).start()
    for load in chunk_loads(0):
        load.start()
    probs_load(0).start()
    for load in time_weights:
        load.start()
    sums[...] = sums_in[...]
    bias_rows = f32(biases[...])
    branch_load.wait()

    def first_of_frames():
        for load in space_weights:
            load.start()
        for order in range(CHUNKS):
            for frame in range(FRAME_PART):
                for hop in range(1, RANKS):
                    cell_copy(order, hop, frame).wait_send()
                cell_keep(order, frame).wait()
        for load in space_weights:
            load.wait()

    for action, index in SCHEDULE:
        if action == "double":
            double_unit(index)
        elif action == "chunk":
            if index == 0:
                for load in time_weights:
                    load.wait()
            if index == 2:
                for frame in range(FRAME_PART):
                    for load in frame_loads(frame):
                        load.start()
            time_backward(index)
        elif action == "first":
            if index == 0:
                first_of_frames()
            frame_first(index)
        elif action == "second":
            frame_second(index)
            if index == FRAME_PART - 1:
                sum_exchange(0).start()
        elif action == "unit":
            make_unit(index)
        elif action == "sums":
            sum_add(index)
            if index == 0:
                sum_exchange(1).start()
            else:
                for hop in range(1, CLIPS):
                    sum_spread(hop).start()
                sum_keep().start()
        else:
            stages[action](index)

    for hop in range(1, CLIPS):
        sum_spread(hop).wait()
    sum_keep().wait()

    def frame_end(frame, carry):
        for hop in range(1, CLIPS):
            home_copy(frame, hop).wait()
        home_keep(frame).wait()
        return carry

    lax.fori_loop(0, FRAME_PART, frame_end, 0)


def tail_section(saved, modulation, biases, sums, w_qkv_t, w_out_t, w_qkv, w_out):
    low = jnp.bfloat16
    return pl.pallas_call(
        tail_body,
        out_shape=(
            jax.ShapeDtypeStruct((CLIPS, FRAME_PART, CELL_HOME, D), low),
            jax.ShapeDtypeStruct((UNITS, ROWS, D), low),
            jax.ShapeDtypeStruct((CLIPS, 16, D), jnp.float32),
        ),
        in_specs=[ANY] * 15 + [VMEM] * 3 + [ANY] * 4,
        out_specs=(ANY, ANY, ANY),
        scratch_shapes=[
            pltpu.VMEM((FRAME_PART, CELLS, D), low),
            pltpu.VMEM((FRAME_PART, CELLS, D), low),
            pltpu.VMEM((FRAME_PART, CELLS, 3 * D), low),
            pltpu.VMEM((FRAME_PART, CELLS, D), low),
            pltpu.VMEM((FRAME_PART, CELLS, D), low),
            pltpu.VMEM((CHUNKS, TOKENS, 3 * D), low),
            pltpu.VMEM((D, 3 * D), low),
            pltpu.VMEM((D, D), low),
            pltpu.VMEM((2, CHUNKS, TOKENS, D), low),
            pltpu.VMEM((2, CHUNKS, TOKENS, D), low),
            pltpu.VMEM((CELLS, D), low),
            pltpu.VMEM((2, FRAME_PART * RANKS, CHUNK_CELLS, D), low),
            pltpu.VMEM((2, TOKENS, D), jnp.float32),
            pltpu.VMEM((2, TOKENS, D), low),
            pltpu.VMEM((HEADS, TOKENS, TOKENS), low),
            pltpu.VMEM((4, 2, 2, 2, HALF_ROWS, D), low),
            pltpu.VMEM((8, 2, HALF_ROWS, D), low),
            pltpu.VMEM((UNITS, 2, HALF_ROWS, D), low),
            pltpu.VMEM((6, 2, 2, HALF_ROWS, D), low),
            pltpu.VMEM((10, 2, HALF_ROWS, D), low),
            pltpu.VMEM((10, HALF_ROWS, D), low),
            pltpu.VMEM((8, 2, HALF_ROWS, D), low),
            pltpu.VMEM((10, HALF_ROWS, D), low),
            pltpu.VMEM((16, D), jnp.float32),
            pltpu.VMEM((2, 16, D), jnp.float32),
            pltpu.SemaphoreType.DMA((2, 2)),
            pltpu.SemaphoreType.DMA((3, FRAME_PART)),
            pltpu.SemaphoreType.DMA((2,)),
            pltpu.SemaphoreType.DMA((2,)),
            pltpu.SemaphoreType.DMA((4, 2)),
            pltpu.SemaphoreType.DMA((CHUNKS, RANKS, FRAME_PART)),
            pltpu.SemaphoreType.DMA((CHUNKS, RANKS, FRAME_PART)),
            pltpu.SemaphoreType.DMA((FRAME_PART, CLIPS)),
            pltpu.SemaphoreType.DMA((FRAME_PART, CLIPS)),
            pltpu.SemaphoreType.DMA((9, UNITS)),
            pltpu.SemaphoreType.DMA((9, UNITS)),
            pltpu.SemaphoreType.DMA((10,)),
            pltpu.SemaphoreType.DMA((9,)),
        ],
        compiler_params=pltpu.CompilerParams(has_side_effects=True, vmem_limit_bytes=62 * 1024 * 1024),
        cost_estimate=pl.CostEstimate(flops=30 * 10**9, bytes_accessed=60 * 10**6, transcendentals=3 * 10**6),
        name="tail_section",
    )(*saved, modulation, biases, sums, w_qkv_t, w_out_t, w_qkv, w_out)


def per_device_fast(
    tokens,
    condition,
    loss_grad,
    cell_counts,
    frame_tasks,
    destinations,
    w_ada,
    b_ada,
    w_qkv_s,
    w_out_s,
    b_out_s,
    w_qkv_t,
    w_out_t,
    b_out_t,
    w_up,
    b_up,
    w_down,
    b_down,
):
    rank = lax.axis_index("seq")
    cond_low = bf16(jax.nn.silu(f32(jnp.take(condition, destinations, axis=0))))
    biases = jnp.concatenate([b_ada, b_out_s, b_out_t, b_up, b_down]).reshape(16, D)
    arrived, qkv_one, mixed_one, probs_one, cells_in, loss_early, modulation = space_forward(
        destinations, cell_counts, tokens, loss_grad, condition, biases, w_ada, w_qkv_s, w_out_s
    )
    parts = time_forward(
        cell_counts,
        frame_tasks,
        cells_in,
        loss_grad,
        loss_early,
        modulation,
        biases,
        w_qkv_t,
        w_out_t,
        w_up,
        w_down,
    )
    layer_out, saved, sums = parts[0], parts[1:-1], parts[-1]
    grad_tokens, totals, gathered = tail_section(
        (arrived, qkv_one, mixed_one, probs_one, cells_in) + tuple(saved),
        modulation,
        biases,
        sums,
        w_qkv_t,
        w_out_t,
        w_qkv_s,
        w_out_s,
    )
    wide = f32(totals)

    def side(first, count):
        return jnp.concatenate([wide[first + part] for part in range(count)], axis=1)

    grad_w_down = wide[0:4].reshape(D, D).T
    grad_mod = gathered[:, :9].reshape(CLIPS, 9 * D)
    own_cond = lax.dynamic_slice_in_dim(cond_low, rank * ROWS, ROWS, axis=1)
    grad_w_ada = lax.dot_general(
        f32(own_cond), grad_mod, (((0,), (0,)), ((), ())), preferred_element_type=jnp.float32
    )
    sums_all = jnp.sum(gathered, axis=0)
    grad_b_ada = lax.dynamic_slice_in_dim(sums_all[:9].reshape(9 * D), rank * 9 * ROWS, 9 * ROWS)
    grad_b_up = lax.dynamic_index_in_dim(sums_all[9:13], rank, 0, keepdims=False)

    def quarter(row):
        return lax.dynamic_slice_in_dim(sums_all[row], rank * ROWS, ROWS)

    return (
        layer_out,
        grad_tokens,
        grad_w_ada,
        grad_b_ada,
        side(12, 3),
        wide[15],
        quarter(15),
        side(8, 3),
        wide[11],
        quarter(14),
        side(4, 4),
        grad_b_up,
        grad_w_down,
        quarter(13),
    )


def solution(mesh):
    placed = (
        P(None, "seq", "dp", None),
        P(),
        P(None, "seq", "dp", None),
        P(),
        P(),
        P(),
        P(),
        P(),
        P(),
        P(),
        P(),
        P(),
        P(),
        P(),
        P(),
        P(),
        P(),
        P(),
    )
    fast = mesh.shape["dp"] == 8 and mesh.shape["seq"] == 4
    return jax.shard_map(
        per_device_fast if fast else per_device_general,
        mesh=mesh,
        in_specs=placed,
        out_specs=(
            P(None, "seq", "dp", None),
            P(None, "seq", "dp", None),
            P("seq", None),
            P("seq"),
            P("seq", None),
            P("seq", None),
            P("seq"),
            P("seq", None),
            P("seq", None),
            P("seq"),
            P("seq", None),
            P("seq"),
            P("seq", None),
            P("seq"),
        ),
        check_vma=False,
    )
```

```python
import functools

import jax
import jax.numpy as jnp
from jax import lax
from jax.experimental import pallas as pl
from jax.experimental.pallas import tpu as pltpu
from jax.sharding import PartitionSpec as P

D = 768
HEADS = 12
HEAD = 64


def standard(field):
    centred = field - jnp.mean(field, axis=-1, keepdims=True)
    inverse = lax.rsqrt(jnp.mean(centred * centred, axis=-1, keepdims=True) + 1e-06)
    return (centred * inverse, inverse)


def standard_back(normed, inverse, grad_normed):
    return inverse * (
        grad_normed
        - jnp.mean(grad_normed, axis=-1, keepdims=True)
        - normed * jnp.mean(grad_normed * normed, axis=-1, keepdims=True)
    )


def gelu_back(lifted, grad_hidden):
    return jax.vjp(lambda inner: jax.nn.gelu(inner, approximate=True), lifted)[1](grad_hidden)[0]


def attend(triple, key_valid, einsum_forms):
    queries = triple[:, :, 0]
    key_rows = triple[:, :, 1]
    value_rows = triple[:, :, 2]
    scores = (
        jnp.einsum(einsum_forms[0], queries, key_rows, preferred_element_type=jnp.float32) * 0.125
    )
    scores = jnp.where(key_valid, scores, -1e30)
    row_top = jnp.max(scores, axis=-1, keepdims=True)
    exponent = jnp.exp(scores - row_top)
    probs_full = exponent / jnp.sum(exponent, axis=-1, keepdims=True)
    probs_low = probs_full.astype(jnp.bfloat16)
    mixed_out = jnp.einsum(
        einsum_forms[1], probs_low, value_rows, preferred_element_type=jnp.float32
    ).astype(jnp.bfloat16)
    return (mixed_out, probs_full, probs_low)


def attend_back(triple, probs_full, probs_low, grad_mixed, einsum_forms):
    queries = triple[:, :, 0]
    key_rows = triple[:, :, 1]
    value_rows = triple[:, :, 2]
    grad_probs = jnp.einsum(
        einsum_forms[0], grad_mixed, value_rows, preferred_element_type=jnp.float32
    )
    row_delta = jnp.sum(probs_full * grad_probs, axis=-1, keepdims=True)
    grad_scores = (probs_full * (grad_probs - row_delta)).astype(jnp.bfloat16)
    grad_values = jnp.einsum(
        einsum_forms[2], probs_low, grad_mixed, preferred_element_type=jnp.float32
    )
    grad_queries = (
        jnp.einsum(einsum_forms[1], grad_scores, key_rows, preferred_element_type=jnp.float32)
        * 0.125
    )
    grad_keys = (
        jnp.einsum(einsum_forms[2], grad_scores, queries, preferred_element_type=jnp.float32)
        * 0.125
    )
    return jnp.stack([grad_queries, grad_keys, grad_values], axis=2)


def per_device_general(
    tokens,
    condition,
    loss_grad,
    cell_counts,
    frame_tasks,
    destinations,
    w_ada,
    b_ada,
    w_qkv_s,
    w_out_s,
    b_out_s,
    w_qkv_t,
    w_out_t,
    b_out_t,
    w_up,
    b_up,
    w_down,
    b_down,
):
    groups = lax.axis_size("dp")
    ranks = lax.axis_size("seq")
    own_slot = lax.axis_index("dp")
    own_rank = lax.axis_index("seq")
    frame_part = tokens.shape[1]
    cell_total = tokens.shape[2] * groups
    cell_part = cell_total // ranks
    frame_total = frame_part * ranks
    slot_ids = jnp.arange(groups, dtype=jnp.int32)
    routing = (destinations[None, :] == slot_ids[:, None]).astype(jnp.bfloat16)
    outgoing = jnp.einsum(
        "jc,cfbd->jfbd", routing, tokens, preferred_element_type=jnp.float32
    ).astype(jnp.bfloat16)
    outgoing_grad = jnp.einsum(
        "jc,cfbd->jfbd", routing, loss_grad, preferred_element_type=jnp.float32
    ).astype(jnp.bfloat16)
    arrived, arrived_grad = (
        lax.all_to_all(outgoing, "dp", split_axis=0, concat_axis=2, tiled=True),
        lax.all_to_all(outgoing_grad, "dp", split_axis=0, concat_axis=2, tiled=True),
    )
    own_clip = jnp.sum(jnp.where(destinations == own_slot, slot_ids, 0))
    own_count = jnp.sum(jnp.where(slot_ids == own_clip, cell_counts, 0))
    own_tasks = lax.dynamic_index_in_dim(frame_tasks, own_clip, 0, keepdims=False)
    cond_row = lax.dynamic_index_in_dim(condition, own_slot, 0, keepdims=False)
    cond_low = jax.nn.silu(cond_row.astype(jnp.float32)).astype(jnp.bfloat16)
    modulation = jnp.dot(cond_low[None, :], w_ada, preferred_element_type=jnp.float32)[
        0
    ] + b_ada.astype(jnp.float32)
    pieces = [modulation[piece_index * D : (piece_index + 1) * D] for piece_index in range(9)]
    (
        shift_one,
        scale_one,
        gate_one,
        shift_two,
        scale_two,
        gate_two,
        shift_three,
        scale_three,
        gate_three,
    ) = pieces
    space_forms = ("fphe,fqhe->fhpq", "fhpq,fqhe->fphe", "fhpq,fphe->fqhe")
    frames_in = arrived[0].astype(jnp.float32)
    normed_one, inverse_one = standard(frames_in)
    act_one = (normed_one * (1.0 + scale_one) + shift_one).astype(jnp.bfloat16)
    triple_one = (
        jnp.einsum("fpd,de->fpe", act_one, w_qkv_s, preferred_element_type=jnp.float32)
        .astype(jnp.bfloat16)
        .reshape(frame_part, cell_total, 3, HEADS, HEAD)
    )
    key_valid = (jnp.arange(cell_total, dtype=jnp.int32) < own_count)[None, None, None, :]
    mixed_one, probs_one, low_one = attend(triple_one, key_valid, space_forms)
    flat_one = mixed_one.reshape(frame_part, cell_total, D)
    spatial_out = jnp.einsum(
        "fpd,de->fpe", flat_one, w_out_s, preferred_element_type=jnp.float32
    ) + b_out_s.astype(jnp.float32)
    state_one = (frames_in + gate_one * spatial_out).astype(jnp.bfloat16)
    cells_in, cells_grad = (
        lax.all_to_all(state_one, "seq", split_axis=1, concat_axis=0, tiled=True),
        lax.all_to_all(arrived_grad[0], "seq", split_axis=1, concat_axis=0, tiled=True),
    )
    time_forms = ("fqhe,gqhe->qhfg", "qhfg,gqhe->fqhe", "qhfg,fqhe->gqhe")
    state_cells = cells_in.astype(jnp.float32)
    normed_two, inverse_two = standard(state_cells)
    act_two = (normed_two * (1.0 + scale_two) + shift_two).astype(jnp.bfloat16)
    triple_two = (
        jnp.einsum("fqd,de->fqe", act_two, w_qkv_t, preferred_element_type=jnp.float32)
        .astype(jnp.bfloat16)
        .reshape(frame_total, cell_part, 3, HEADS, HEAD)
    )
    mixed_two, probs_two, low_two = attend(triple_two, True, time_forms)
    flat_two = mixed_two.reshape(frame_total, cell_part, D)
    temporal_out = jnp.einsum(
        "fqd,de->fqe", flat_two, w_out_t, preferred_element_type=jnp.float32
    ) + b_out_t.astype(jnp.float32)
    state_two = state_cells + gate_two * temporal_out
    normed_three, inverse_three = standard(state_two)
    act_three = (normed_three * (1.0 + scale_three) + shift_three).astype(jnp.bfloat16)
    lifted = jnp.einsum(
        "fqd,dk->fqk", act_three, w_up, preferred_element_type=jnp.float32
    ) + b_up.astype(jnp.float32)
    hidden = jax.nn.gelu(lifted, approximate=True).astype(jnp.bfloat16)
    branch_out = jnp.einsum(
        "fqk,kd->fqd", hidden, w_down, preferred_element_type=jnp.float32
    ) + b_down.astype(jnp.float32)
    result = (state_two + gate_three * branch_out).astype(jnp.bfloat16)
    cell_ids = own_rank * cell_part + jnp.arange(cell_part, dtype=jnp.int32)
    loss_mask = jnp.logical_and(own_tasks[:, None] == 1, cell_ids[None, :] < own_count)
    out_grad = cells_grad.astype(jnp.float32) * loss_mask[:, :, None].astype(jnp.float32)
    grad_gate_three = jnp.sum(out_grad * branch_out, axis=(0, 1))
    grad_branch = (gate_three * out_grad).astype(jnp.bfloat16)
    grad_b_down = jnp.sum(grad_branch.astype(jnp.float32), axis=(0, 1))
    grad_w_down = jnp.einsum("fqk,fqd->kd", hidden, grad_branch, preferred_element_type=jnp.float32)
    grad_hidden = jnp.einsum("fqd,kd->fqk", grad_branch, w_down, preferred_element_type=jnp.float32)
    grad_lifted = gelu_back(lifted, grad_hidden).astype(jnp.bfloat16)
    grad_b_up = jnp.sum(grad_lifted.astype(jnp.float32), axis=(0, 1))
    grad_w_up = jnp.einsum(
        "fqd,fqk->dk", act_three, grad_lifted, preferred_element_type=jnp.float32
    )
    grad_act_three = jnp.einsum(
        "fqk,dk->fqd", grad_lifted, w_up, preferred_element_type=jnp.float32
    )
    grad_shift_three = jnp.sum(grad_act_three, axis=(0, 1))
    grad_scale_three = jnp.sum(grad_act_three * normed_three, axis=(0, 1))
    grad_state_two = out_grad + standard_back(
        normed_three, inverse_three, grad_act_three * (1.0 + scale_three)
    )
    grad_gate_two = jnp.sum(grad_state_two * temporal_out, axis=(0, 1))
    grad_temporal = (gate_two * grad_state_two).astype(jnp.bfloat16)
    grad_b_out_t = jnp.sum(grad_temporal.astype(jnp.float32), axis=(0, 1))
    grad_w_out_t = jnp.einsum(
        "fqd,fqe->de", flat_two, grad_temporal, preferred_element_type=jnp.float32
    )
    grad_mixed_two = (
        jnp.einsum("fqe,de->fqd", grad_temporal, w_out_t, preferred_element_type=jnp.float32)
        .astype(jnp.bfloat16)
        .reshape(frame_total, cell_part, HEADS, HEAD)
    )
    grad_triple_two = (
        attend_back(triple_two, probs_two, low_two, grad_mixed_two, time_forms)
        .reshape(frame_total, cell_part, 3 * D)
        .astype(jnp.bfloat16)
    )
    grad_w_qkv_t = jnp.einsum(
        "fqd,fqe->de", act_two, grad_triple_two, preferred_element_type=jnp.float32
    )
    grad_act_two = jnp.einsum(
        "fqe,de->fqd", grad_triple_two, w_qkv_t, preferred_element_type=jnp.float32
    )
    grad_shift_two = jnp.sum(grad_act_two, axis=(0, 1))
    grad_scale_two = jnp.sum(grad_act_two * normed_two, axis=(0, 1))
    grad_state_one = (
        grad_state_two + standard_back(normed_two, inverse_two, grad_act_two * (1.0 + scale_two))
    ).astype(jnp.bfloat16)
    frames_out, frames_grad = (
        lax.all_to_all(result, "seq", split_axis=0, concat_axis=1, tiled=True),
        lax.all_to_all(grad_state_one, "seq", split_axis=0, concat_axis=1, tiled=True),
    )
    grad_frames = frames_grad.astype(jnp.float32)
    grad_gate_one = jnp.sum(grad_frames * spatial_out, axis=(0, 1))
    grad_spatial = (gate_one * grad_frames).astype(jnp.bfloat16)
    grad_b_out_s = jnp.sum(grad_spatial.astype(jnp.float32), axis=(0, 1))
    grad_w_out_s = jnp.einsum(
        "fpd,fpe->de", flat_one, grad_spatial, preferred_element_type=jnp.float32
    )
    grad_mixed_one = (
        jnp.einsum("fpe,de->fpd", grad_spatial, w_out_s, preferred_element_type=jnp.float32)
        .astype(jnp.bfloat16)
        .reshape(frame_part, cell_total, HEADS, HEAD)
    )
    grad_triple_one = (
        attend_back(triple_one, probs_one, low_one, grad_mixed_one, space_forms)
        .reshape(frame_part, cell_total, 3 * D)
        .astype(jnp.bfloat16)
    )
    grad_w_qkv_s = jnp.einsum(
        "fpd,fpe->de", act_one, grad_triple_one, preferred_element_type=jnp.float32
    )
    grad_act_one = jnp.einsum(
        "fpe,de->fpd", grad_triple_one, w_qkv_s, preferred_element_type=jnp.float32
    )
    grad_shift_one = jnp.sum(grad_act_one, axis=(0, 1))
    grad_scale_one = jnp.sum(grad_act_one * normed_one, axis=(0, 1))
    grad_input = (
        grad_frames + standard_back(normed_one, inverse_one, grad_act_one * (1.0 + scale_one))
    ).astype(jnp.bfloat16)
    home_out, home_grad = (
        lax.all_to_all(frames_out[None], "dp", split_axis=2, concat_axis=0, tiled=True),
        lax.all_to_all(grad_input[None], "dp", split_axis=2, concat_axis=0, tiled=True),
    )
    layer_out = jnp.einsum(
        "jc,jfbd->cfbd", routing, home_out, preferred_element_type=jnp.float32
    ).astype(jnp.bfloat16)
    grad_tokens = jnp.einsum(
        "jc,jfbd->cfbd", routing, home_grad, preferred_element_type=jnp.float32
    ).astype(jnp.bfloat16)
    grad_mod = jnp.concatenate(
        [
            grad_shift_one,
            grad_scale_one,
            grad_gate_one,
            grad_shift_two,
            grad_scale_two,
            grad_gate_two,
            grad_shift_three,
            grad_scale_three,
            grad_gate_three,
        ]
    )
    ada_term = cond_low.astype(jnp.float32)[:, None] * grad_mod[None, :]
    partials = (
        lax.psum_scatter(
            ada_term.astype(jnp.bfloat16), "seq", scatter_dimension=0, tiled=True
        ).astype(jnp.float32),
        lax.psum_scatter(
            grad_mod.astype(jnp.bfloat16), "seq", scatter_dimension=0, tiled=True
        ).astype(jnp.float32),
        lax.psum_scatter(
            grad_w_qkv_s.astype(jnp.bfloat16), "seq", scatter_dimension=0, tiled=True
        ).astype(jnp.float32),
        lax.psum_scatter(
            grad_w_out_s.astype(jnp.bfloat16), "seq", scatter_dimension=0, tiled=True
        ).astype(jnp.float32),
        lax.psum_scatter(
            grad_b_out_s.astype(jnp.bfloat16), "seq", scatter_dimension=0, tiled=True
        ).astype(jnp.float32),
        lax.psum_scatter(
            grad_w_qkv_t.astype(jnp.bfloat16), "seq", scatter_dimension=0, tiled=True
        ).astype(jnp.float32),
        lax.psum_scatter(
            grad_w_out_t.astype(jnp.bfloat16), "seq", scatter_dimension=0, tiled=True
        ).astype(jnp.float32),
        lax.psum_scatter(
            grad_b_out_t.astype(jnp.bfloat16), "seq", scatter_dimension=0, tiled=True
        ).astype(jnp.float32),
        lax.psum_scatter(
            grad_w_up.astype(jnp.bfloat16), "seq", scatter_dimension=0, tiled=True
        ).astype(jnp.float32),
        lax.psum_scatter(
            grad_b_up.astype(jnp.bfloat16), "seq", scatter_dimension=0, tiled=True
        ).astype(jnp.float32),
        lax.psum_scatter(
            grad_w_down.astype(jnp.bfloat16), "seq", scatter_dimension=0, tiled=True
        ).astype(jnp.float32),
        lax.psum_scatter(
            grad_b_down.astype(jnp.bfloat16), "seq", scatter_dimension=0, tiled=True
        ).astype(jnp.float32),
    )
    totals = lax.psum(
        (
            partials[0],
            partials[1],
            partials[2],
            partials[3],
            partials[4],
            partials[5],
            partials[6],
            partials[7],
            partials[8],
            partials[9],
            partials[10],
            partials[11],
        ),
        "dp",
    )
    ada_grad = totals[0]
    ada_bias = totals[1]
    rest = totals[2:]
    return (
        layer_out,
        grad_tokens,
        ada_grad,
        ada_bias,
        rest[0],
        rest[1],
        rest[2],
        rest[3],
        rest[4],
        rest[5],
        rest[6],
        rest[7],
        rest[8],
        rest[9],
    )


MESH = pl.DeviceIdType.MESH
ANY = pl.BlockSpec(memory_space=pl.ANY)
VMEM = pl.BlockSpec(memory_space=pltpu.VMEM)
SMEM = pl.BlockSpec(memory_space=pltpu.SMEM)
NEG = -1e30
CLIPS = 8
RANKS = 4
FRAME_PART = 4
CELLS = 256
CELL_HOME = CELLS // CLIPS
CELL_PART = CELLS // RANKS
FF = 3072
TOKENS = 256
CHUNK_CELLS = TOKENS // (FRAME_PART * RANKS)
CHUNKS = CELL_PART // CHUNK_CELLS


def turn_of(rank):
    return 2 * lax.rem(rank, 2) + rank // 2


def chunk_of(order, rank):
    return lax.rem(order + turn_of(rank), CHUNKS)


def order_of(chunk, rank):
    return lax.rem(chunk - turn_of(rank) + CHUNKS, CHUNKS)


def share_of(chunk, rank):
    return lax.rem(rank - chunk + RANKS, RANKS)


def chunk_cells(order, rank):
    chunk = chunk_of(order, rank)
    start = chunk * CELL_PART + share_of(chunk, rank) * CHUNK_CELLS
    return pl.ds(pl.multiple_of(start, CHUNK_CELLS), CHUNK_CELLS)


def loss_target(slot, half):
    chunk = slot // 2
    target = lax.rem(2 * lax.rem(slot, 2) + half + chunk, RANKS)
    return target, order_of(chunk, target)


def f32(value):
    return value.astype(jnp.float32)


def bf16(value):
    return value.astype(jnp.bfloat16)


def dot(left, right):
    return lax.dot_general(left, right, (((1,), (0,)), ((), ())), preferred_element_type=jnp.float32)


def dot_nt(left, right):
    return lax.dot_general(left, right, (((1,), (1,)), ((), ())), preferred_element_type=jnp.float32)


def dot_tn(left, right):
    return lax.dot_general(left, right, (((0,), (0,)), ((), ())), preferred_element_type=jnp.float32)


def standardise(field):
    centred = field - jnp.mean(field, axis=-1, keepdims=True)
    inverse = lax.rsqrt(jnp.mean(centred * centred, axis=-1, keepdims=True) + 1e-06)
    return centred * inverse, inverse


def column_sum(field):
    return jnp.sum(field, axis=0, keepdims=True)


def head_halves(rows):
    lane = lax.broadcasted_iota(jnp.int32, (1, 2 * HEAD), 1) < HEAD
    zero = jnp.bfloat16(0)
    return jnp.where(lane, rows, zero), jnp.where(lane, zero, rows)


def pair_lanes(pair, part):
    return pl.ds(part * D + pair * 2 * HEAD, 2 * HEAD)


def heads_forward(qkv, mixed, probs, valid):
    lane = lax.broadcasted_iota(jnp.int32, (1, 2 * HEAD), 1) < HEAD
    scores = []
    for pair in range(HEADS // 2):
        queries = head_halves(qkv[:, pair_lanes(pair, 0)] * jnp.bfloat16(0.125))
        keys = qkv[:, pair_lanes(pair, 1)]
        scores += [dot_nt(queries[half], keys) for half in range(2)]
    low = []
    for head in range(HEADS):
        masked = jnp.where(valid, scores[head], NEG)
        exponent = jnp.exp(masked - jnp.max(masked, axis=-1, keepdims=True))
        low.append(bf16(exponent * (1.0 / jnp.sum(exponent, axis=-1, keepdims=True))))
        probs[head] = low[head]
    for pair in range(HEADS // 2):
        values = qkv[:, pair_lanes(pair, 2)]
        parts = [dot(low[2 * pair + half], values) for half in range(2)]
        mixed[:, pair_lanes(pair, 0)] = bf16(jnp.where(lane, parts[0], parts[1]))


def heads_backward(qkv, grad_mixed, probs, pairs):
    lane = lax.broadcasted_iota(jnp.int32, (1, 2 * HEAD), 1) < HEAD
    heads = [(pair, half) for pair in pairs for half in range(2)]
    operands = {pair: [qkv[:, pair_lanes(pair, part)] for part in range(3)] for pair in pairs}
    grads = {pair: grad_mixed[:, pair_lanes(pair, 0)] for pair in pairs}
    halves = {pair: head_halves(grads[pair]) for pair in pairs}
    low = {head: probs[2 * head[0] + head[1]] for head in heads}
    grad_probs = {head: dot_nt(halves[head[0]][head[1]], operands[head[0]][2]) for head in heads}
    grad_values = {head: dot_tn(low[head], grads[head[0]]) for head in heads}
    grad_scores = {}
    for head in heads:
        full = f32(low[head])
        weighted = full * grad_probs[head]
        grad_scores[head] = bf16(weighted - full * jnp.sum(weighted, axis=-1, keepdims=True))
    grad_keys = {head: dot_tn(grad_scores[head], operands[head[0]][0]) for head in heads}
    grad_queries = {head: dot(grad_scores[head], operands[head[0]][1]) for head in heads}
    for pair in pairs:
        first, second = (pair, 0), (pair, 1)
        qkv[:, pair_lanes(pair, 0)] = bf16(jnp.where(lane, grad_queries[first], grad_queries[second]) * 0.125)
        qkv[:, pair_lanes(pair, 1)] = bf16(jnp.where(lane, grad_keys[first], grad_keys[second]) * 0.125)
        qkv[:, pair_lanes(pair, 2)] = bf16(jnp.where(lane, grad_values[first], grad_values[second]))


def space_forward_body(
    destinations,
    cell_counts,
    tokens,
    condition,
    biases,
    w_ada,
    w_qkv,
    w_out,
    qkv_all,
    mixed_all,
    probs_all,
    state_cells,
    modulation,
    x_scr,
    ada_scr,
    wqkv_scr,
    wout_scr,
    qkv_scr,
    mixed_scr,
    probs_scr,
    state_scr,
    local_sem,
    in_send,
    in_recv,
    out_send,
    out_recv,
    save_sem,
    load_later,
    send_loss,
):
    slot = lax.axis_index("dp")
    rank = lax.axis_index("seq")

    def arrival(frame, hop):
        peer = lax.rem(slot + hop, CLIPS)
        rows = pl.ds(pl.multiple_of(slot * CELL_HOME, CELL_HOME), CELL_HOME)
        return pltpu.make_async_remote_copy(
            src_ref=tokens.at[peer, frame],
            dst_ref=x_scr.at[frame, rows],
            send_sem=in_send.at[frame, hop],
            recv_sem=in_recv.at[frame, hop],
            device_id=(peer, rank),
            device_id_type=MESH,
        )

    def leave(frame, hop, order):
        peer = lax.rem(rank + hop, RANKS)
        return pltpu.make_async_remote_copy(
            src_ref=state_scr.at[frame, chunk_cells(order, peer)],
            dst_ref=state_cells.at[order, rank * FRAME_PART + frame],
            send_sem=out_send.at[frame, hop, order],
            recv_sem=out_recv.at[frame, hop, order],
            device_id=(slot, peer),
            device_id_type=MESH,
        )

    def keep(frame, order):
        return pltpu.make_async_copy(
            state_scr.at[frame, chunk_cells(order, rank)],
            state_cells.at[order, rank * FRAME_PART + frame],
            out_recv.at[frame, 0, order],
        )

    def saves(frame):
        return (
            pltpu.make_async_copy(qkv_scr.at[frame], qkv_all.at[frame], save_sem.at[frame, 1]),
            pltpu.make_async_copy(mixed_scr.at[frame], mixed_all.at[frame], save_sem.at[frame, 2]),
        )

    def save_probs(frame):
        return pltpu.make_async_copy(probs_scr.at[lax.rem(frame, 2)], probs_all.at[frame], save_sem.at[frame, 3])

    own_rows = pl.ds(pl.multiple_of(slot * CELL_HOME, CELL_HOME), CELL_HOME)
    own_copy = pltpu.make_async_copy(tokens.at[slot], x_scr.at[:, own_rows], local_sem.at[0])
    ada_copy = pltpu.make_async_copy(w_ada, ada_scr, local_sem.at[1])
    qkv_copy = pltpu.make_async_copy(w_qkv, wqkv_scr, local_sem.at[2])
    out_copy = pltpu.make_async_copy(w_out, wout_scr, local_sem.at[3])
    for hop in range(1, CLIPS):
        arrival(0, hop).start()
    own_copy.start()
    ada_copy.start()
    for frame in range(1, FRAME_PART):
        for hop in range(1, CLIPS):
            arrival(frame, hop).start()
    qkv_copy.start()
    out_copy.start()

    row_ids = lax.broadcasted_iota(jnp.int32, (CLIPS, 1), 0)
    cond = column_sum(jnp.where(row_ids == destinations[slot], f32(condition[...]), 0.0))
    cond = jnp.broadcast_to(bf16(cond / (1.0 + jnp.exp(-cond))), (16, D))
    bias_rows = f32(biases[...])
    valid = lax.broadcasted_iota(jnp.int32, (1, CELLS), 1) < cell_counts[slot]
    ada_copy.wait()
    for piece in range(9):
        row = dot(cond, ada_scr[:, pl.ds(piece * D, D)])[0:1]
        modulation[pl.ds(piece, 1)] = row + bias_rows[piece : piece + 1]
    own_copy.wait()
    qkv_copy.wait()
    out_copy.wait()

    def frame_step(frame, carry):
        for hop in range(1, CLIPS):
            arrival(frame, hop).wait_recv()

        @pl.when(frame == 0)
        def _():
            load_later()

        x = f32(x_scr[frame])
        centred = x - jnp.mean(x, axis=-1, keepdims=True)
        normed = centred * lax.rsqrt(jnp.mean(centred * centred, axis=-1, keepdims=True) + 1e-06)
        act = bf16(normed * (1.0 + modulation[1:2]) + modulation[0:1])
        qkv_scr[frame] = bf16(dot(act, wqkv_scr[...]))

        @pl.when(frame >= 2)
        def _():
            save_probs(frame - 2).wait()

        heads_forward(qkv_scr.at[frame], mixed_scr.at[frame], probs_scr.at[lax.rem(frame, 2)], valid)
        save_probs(frame).start()
        spatial = dot(mixed_scr[frame], wout_scr[...]) + bias_rows[9:10]
        state_scr[frame] = bf16(f32(x_scr[frame]) + modulation[2:3] * spatial)
        for order in range(CHUNKS):
            for hop in range(1, RANKS):
                leave(frame, hop, order).start()
            keep(frame, order).start()

        @pl.when(frame == FRAME_PART - 1)
        def _():
            send_loss(True)

        for save in saves(frame):
            save.start()
        return carry

    lax.fori_loop(0, FRAME_PART, frame_step, 0)

    def frame_end(frame, carry):
        for hop in range(1, CLIPS):
            arrival(frame, hop).wait_send()
        for order in range(CHUNKS):
            for hop in range(1, RANKS):
                leave(frame, hop, order).wait_send()
            keep(frame, order).wait()
        for save in saves(frame):
            save.wait()
        return carry

    lax.fori_loop(0, FRAME_PART, frame_end, 0)
    for frame in range(FRAME_PART - 2, FRAME_PART):
        save_probs(frame).wait()


def cell_match():
    row_cell = lax.rem(lax.broadcasted_iota(jnp.int32, (TOKENS, TOKENS), 0), CHUNK_CELLS)
    column_cell = lax.rem(lax.broadcasted_iota(jnp.int32, (TOKENS, TOKENS), 1), CHUNK_CELLS)
    return row_cell == column_cell


SAVED_WIDTHS = (D, 3 * D, D, D, D, FF, FF, D)


def time_forward_body(
    cell_counts,
    frame_tasks,
    state_cells,
    loss_cells,
    layer_cells,
    modulation,
    biases,
    homes,
    sums,
    wqkv_scr,
    wout_scr,
    wup_scr,
    wdown_scr,
    slopes,
    state_scr,
    loss_scr,
    layer_scr,
    act_two,
    qkv,
    mixed,
    grad_temporal,
    act_three,
    grad_lifted,
    hidden,
    grad_branch,
    grad_state,
    probs,
    stage_sem,
    save_sem,
    weight_loads,
    cells_arrive,
    loss_arrive,
    send_layer,
):
    slot = lax.axis_index("dp")
    rank = lax.axis_index("seq")
    frames = FRAME_PART * RANKS

    stages = (act_two, qkv, mixed, grad_temporal, act_three, grad_lifted, hidden, grad_branch, grad_state, probs)
    def save(which, order):
        spot = lax.rem(order, 2)
        return pltpu.make_async_copy(stages[which].at[spot], homes[which].at[order], save_sem.at[which, spot])

    def state_load(order):
        spot = lax.rem(order, 2)
        return pltpu.make_async_copy(state_cells.at[order], state_scr.at[spot], stage_sem.at[0])

    def loss_load(order):
        return pltpu.make_async_copy(loss_cells.at[order], loss_scr, stage_sem.at[1])

    def layer_save(order):
        return pltpu.make_async_copy(layer_scr, layer_cells.at[order], stage_sem.at[2])

    sums[...] = jnp.zeros_like(sums)
    bias_rows = f32(biases[...])
    valid = cell_match()
    count = cell_counts[slot]

    def piece(index):
        return modulation[index : index + 1]

    def add(row, value):
        sums[pl.ds(row, 1)] += value

    def chunk_step(order, carry):
        spot = lax.rem(order, 2)
        first = order == 0

        def once(*which):
            @pl.when(first)
            def _():
                for load in which:
                    weight_loads[load].wait()

        @pl.when(order >= 2)
        def _():
            for which in range(len(stages)):
                save(which, order - 2).wait()

        state_load(order).wait()
        state = f32(state_scr[spot]).reshape(TOKENS, D)
        normed_two, _ = standardise(state)
        act_two[spot] = bf16(normed_two * (1.0 + piece(4)) + piece(3))
        once(0)
        qkv[spot] = bf16(dot(act_two[spot], wqkv_scr[...]))
        heads_forward(qkv.at[spot], mixed.at[spot], probs.at[spot], valid)
        for which in (0, 1, 2, 9):
            save(which, order).start()
        once(1)
        temporal = dot(mixed[spot], wout_scr[...]) + bias_rows[10:11]
        state_two = state + piece(5) * temporal
        normed_three, inverse_three = standardise(state_two)
        act_three[spot] = bf16(normed_three * (1.0 + piece(7)) + piece(6))
        save(4, order).start()
        once(2, 3)
        branch = jnp.zeros((TOKENS, D), jnp.float32) + bias_rows[15:16]
        for block in range(FF // D):
            lanes = pl.ds(block * D, D)
            lifted = dot(act_three[spot], wup_scr[:, lanes]) + bias_rows[11 + block : 12 + block]
            square = lifted * lifted
            curve = jnp.tanh(0.7978845608028654 * lifted * (1.0 + 0.044715 * square))
            half = 0.5 * (1.0 + curve)
            hidden[spot, :, lanes] = bf16(lifted * half)
            slopes[:, lanes] = half + 0.5 * lifted * (1.0 - curve * curve) * (
                0.7978845608028654 * (1.0 + 3.0 * 0.044715 * square)
            )
            branch += dot(hidden[spot, :, lanes], wdown_scr[lanes, :])
        save(6, order).start()
        loss_arrive(order)
        loss_load(order).start()
        layer_scr[...] = bf16(state_two + piece(8) * branch).reshape(frames, CHUNK_CELLS, D)
        layer_save(order).start()
        chunk = chunk_of(order, rank)
        first_cell = chunk * CELL_PART + share_of(chunk, rank) * CHUNK_CELLS
        token = lax.broadcasted_iota(jnp.int32, (TOKENS, 1), 0)
        frame, cell = token // CHUNK_CELLS, lax.rem(token, CHUNK_CELLS)
        mask = jnp.zeros((TOKENS, 1), jnp.int32)
        for which in range(frames):
            mask = jnp.where(frame == which, frame_tasks[slot, which], mask)
        mask = jnp.where(first_cell + cell < count, mask, 0)
        loss_load(order).wait()
        seed = f32(loss_scr[...]).reshape(TOKENS, D) * f32(mask)
        add(8, column_sum(seed * branch))
        low_branch = bf16(piece(8) * seed)
        grad_branch[spot] = low_branch
        save(7, order).start()
        add(13, column_sum(f32(low_branch)))
        grad_act = jnp.zeros((TOKENS, D), jnp.float32)
        for block in range(FF // D):
            lanes = pl.ds(block * D, D)
            low_lifted = bf16(dot_nt(grad_branch[spot], wdown_scr[lanes, :]) * slopes[:, lanes])
            grad_lifted[spot, :, lanes] = low_lifted
            add(9 + block, column_sum(f32(low_lifted)))
            grad_act += dot_nt(grad_lifted[spot, :, lanes], wup_scr[:, lanes])
        save(5, order).start()
        layer_save(order).wait()
        send_layer(order)

        @pl.when(order < CHUNKS - 1)
        def _():
            cells_arrive(order + 1)
            state_load(order + 1).start()

        add(6, column_sum(grad_act))
        add(7, column_sum(grad_act * normed_three))
        grad_state_two = seed + standard_back(normed_three, inverse_three, grad_act * (1.0 + piece(7)))
        grad_state[spot] = grad_state_two
        save(8, order).start()
        add(5, column_sum(grad_state_two * temporal))
        low_temporal = bf16(piece(5) * grad_state_two)
        grad_temporal[spot] = low_temporal
        save(3, order).start()
        add(14, column_sum(f32(low_temporal)))
        return carry

    cells_arrive(0)
    state_load(0).start()
    lax.fori_loop(0, CHUNKS, chunk_step, 0)
    for order in (CHUNKS - 2, CHUNKS - 1):
        for which in range(len(stages)):
            save(which, order).wait()


UNITS = 16
ROWS = D // RANKS
HALF_ROWS = ROWS // 2
KINDS = "PSSSSPPPPMPPPPMP"
SCHEDULE = (
    ("double", 0), (0, 0), (0, 1), ("chunk", 0), (1, 0), ("chunk", 1), (1, 1), ("double", 1), (0, 2), (0, 3),
    ("chunk", 2), (1, 2), ("chunk", 3), (2, 0), (2, 1), (1, 3), ("unit", 4), (0, 4), ("unit", 5), (0, 5), (2, 2),
    ("unit", 6), (0, 6), (1, 4), (3, 0), ("unit", 7), (0, 7), (1, 5), (3, 1), (1, 6), ("first", 0), (2, 3), (4, 0),
    (3, 2), (1, 7), ("second", 0), (4, 1), ("first", 1), (5, 0), (4, 2), (2, 4), (2, 5), ("second", 1),
    ("unit", 8), (0, 8), (2, 6), ("first", 2), (3, 5), ("second", 2), (6, 0), (3, 3), (1, 8), (5, 1), ("unit", 9),
    (0, 9), ("first", 3), (5, 2), (4, 5), (3, 6), (2, 7), ("second", 3), (3, 4), (1, 9), ("unit", 10), (0, 10),
    (7, 0), ("unit", 11), (0, 11), (6, 1), (4, 3), (3, 7), (2, 8), ("sums", 0), ("unit", 12), (0, 12), (6, 2),
    (4, 6), (1, 10), (1, 11), ("unit", 13), (0, 13), (2, 9), (7, 1), (1, 12), ("sums", 1), ("unit", 14), (0, 14),
    (5, 5), (3, 8), (1, 13), (4, 4), ("unit", 15), (0, 15), (7, 2), (2, 10), (4, 7), (1, 14), (6, 5), (1, 15),
    (2, 11), (5, 3), (3, 9), (3, 10), (5, 6), (4, 8), (7, 5), (6, 3), (2, 12), (4, 10), (3, 11), (6, 6), (7, 3),
    (5, 4), (4, 11), (2, 13), (3, 12), (5, 7), (6, 4), (7, 6), (4, 9), (4, 12), (2, 14), (6, 7), (3, 13), (5, 8),
    (7, 4), (5, 10), (2, 15), (6, 8), (5, 9), (5, 11), (3, 14), (6, 10), (7, 7), (5, 12), (4, 13), (3, 15), (6, 9),
    (6, 11), (7, 8), (4, 14), (4, 15), (6, 12), (7, 10), (5, 13), (7, 9), (7, 11), (5, 15), (6, 13), (5, 14),
    (6, 15), (7, 12), (6, 14), (7, 13), (7, 15), (7, 14),
)


def tail_body(
    qkv,
    mixed,
    probs,
    state_cells,
    act_two,
    qkv_two,
    mixed_two,
    grad_temporal,
    act_three,
    grad_lifted,
    hidden,
    grad_branch,
    grad_state_two,
    probs_two,
    modulation,
    biases,
    w_qkv_t,
    w_out_t,
    w_qkv,
    w_out,
    grad_home,
    totals,
    gathered,
    x_scr,
    state_scr,
    sums,
    sums_in_scr,
    core_in,
    first_in,
    second_in,
    edge_in,
    middle_in,
    qkv_scr,
    mixed_scr,
    spatial_scr,
    time_scr,
    wqkv_scr,
    wout_scr,
    left_scr,
    right_scr,
    grad_mixed,
    chunk_state,
    chunk_grad,
    chunk_temporal,
    probs_scr,
    own,
    first_out,
    kept,
    load_sem,
    frame_sem,
    probs_sem,
    side_sem,
    chunk_sem,
    cell_send,
    cell_recv,
    home_send,
    home_recv,
    unit_send,
    unit_recv,
    sum_send,
    sum_recv,
):
    slot = lax.axis_index("dp")
    rank = lax.axis_index("seq")
    core = lax.rem(rank, 2)
    over_x = rank // 2
    over_y = lax.rem(slot, 2)
    over_z = slot // 2
    at_edge = jnp.logical_or(over_z == 0, over_z == 3)
    low_side = over_z < 2
    core_peer = (slot, rank + 1 - 2 * core)
    x_peer = (slot, lax.rem(rank + 2, RANKS))
    y_peer = (slot + 1 - 2 * over_y, rank)
    inner_peer = (jnp.where(low_side, 2, 4) + over_y, rank)
    middle_peer = (jnp.where(low_side, 4, 2) + over_y, rank)
    outer_peer = (jnp.where(low_side, 0, 6) + over_y, rank)

    def piece(index):
        return modulation[index : index + 1]

    def remote(source, target, send, recv, peer):
        return pltpu.make_async_remote_copy(
            src_ref=source, dst_ref=target, send_sem=send, recv_sem=recv, device_id=peer, device_id_type=MESH
        )


    turned = over_z // 2

    def spots(unit):
        mine = {"P": over_y, "S": over_x, "M": turned}[KINDS[unit]]
        return mine, 1 - mine

    def half_rows(which):
        return pl.ds(pl.multiple_of(which * HALF_ROWS, HALF_ROWS), HALF_ROWS)

    def send(kind, unit, source, target, peer, landing=None):
        landing = kind if landing is None else landing
        return remote(source, target, unit_send.at[kind, unit], unit_recv.at[landing, unit], peer)

    def core_copy(unit):
        return send(0, unit, own.at[unit % 4, 1 - core], core_in.at[unit % 6], core_peer)

    def first_copy(unit):
        peer = y_peer if KINDS[unit] == "S" else x_peer
        return send(1, unit, first_out.at[unit % 8], first_in.at[unit % 10], peer)

    def second_copy(unit):
        mine, other = spots(unit)
        if KINDS[unit] == "M":
            return send(2, unit, kept.at[unit, mine], second_in.at[unit % 10], y_peer)
        peer = x_peer if KINDS[unit] == "S" else y_peer
        return send(2, unit, kept.at[unit, other], second_in.at[unit % 10], peer)

    def edge_copy(unit):
        if KINDS[unit] == "M":
            return send(3, unit, kept.at[unit], edge_in.at[unit % 8], inner_peer)
        mine, _ = spots(unit)
        return send(3, unit, kept.at[unit, mine], edge_in.at[unit % 8, 0], inner_peer)

    def middle_copy(unit):
        mine, other = spots(unit)
        source = kept.at[unit, other if KINDS[unit] == "M" else mine]
        return send(4, unit, source, middle_in.at[unit % 10], middle_peer)

    def outer_copy(unit):
        _, other = spots(unit)
        return send(5, unit, kept.at[unit, other], middle_in.at[unit % 10], outer_peer, 4)

    def share_copy(unit, source):
        return send(6, unit, source, totals.at[unit, half_rows(over_y)], y_peer)

    def keep_copy(unit, source, which):
        return pltpu.make_async_copy(source, totals.at[unit, half_rows(which)], unit_send.at[7, unit])

    def cross_copy(unit):
        mine, other = spots(unit)
        return send(6, unit, kept.at[unit, other], totals.at[unit, half_rows(mine)], middle_peer)

    def near_copy(unit):
        mine, other = spots(unit)
        return send(5, unit, kept.at[unit, other], totals.at[unit, half_rows(mine)], outer_peer)

    def far_copy(unit):
        _, other = spots(unit)
        place = totals.at[unit, half_rows(other)]
        return send(8, unit, place, place, outer_peer)

    def plus(left, right):
        return bf16(f32(left) + f32(right))

    def stage_one(unit):
        core_copy(unit).wait()
        held, came = own.at[unit % 4, core], core_in.at[unit % 6]
        if KINDS[unit] == "S":
            for part in range(2):
                first_out[unit % 8, part] = plus(held[part, 1 - over_y], came[part, 1 - over_y])
            first_copy(unit).start()
            for part in range(2):
                kept[unit, part] = plus(held[part, over_y], came[part, over_y])
        else:
            first_out[unit % 8] = plus(held[1 - over_x], came[1 - over_x])
            first_copy(unit).start()
            kept[unit] = plus(held[over_x], came[over_x])

    def stage_two(unit):
        first_copy(unit).wait()
        mine, other = spots(unit)
        if KINDS[unit] == "M":
            kept[unit] = plus(kept[unit], first_in[unit % 10])

            @pl.when(at_edge)
            def _():
                edge_copy(unit).start()

        else:
            kept[unit, other] = plus(kept[unit, other], first_in[unit % 10, other])
            second_copy(unit).start()
            kept[unit, mine] = plus(kept[unit, mine], first_in[unit % 10, mine])

    def stage_three(unit):
        mine, _ = spots(unit)
        if KINDS[unit] == "M":

            @pl.when(jnp.logical_not(at_edge))
            def _():
                edge_copy(unit).wait_recv()
                kept[unit] = plus(kept[unit], edge_in[unit % 8])
                middle_copy(unit).start()

        else:
            second_copy(unit).wait()
            kept[unit, mine] = plus(kept[unit, mine], second_in[unit % 10])

            @pl.when(at_edge)
            def _():
                edge_copy(unit).start()

    def stage_four(unit):
        mine, _ = spots(unit)

        @pl.when(jnp.logical_not(at_edge))
        def _():
            if KINDS[unit] == "M":
                middle_copy(unit).wait()
                kept[unit, mine] = plus(kept[unit, mine], middle_in[unit % 10])
                second_copy(unit).start()
            else:
                edge_copy(unit).wait_recv()
                kept[unit, mine] = plus(kept[unit, mine], edge_in[unit % 8, 0])
                middle_copy(unit).start()

    def stage_five(unit):
        mine, other = spots(unit)

        @pl.when(jnp.logical_not(at_edge))
        def _():
            if KINDS[unit] == "M":
                second_copy(unit).wait()
                kept[unit, other] = plus(kept[unit, mine], second_in[unit % 10])
                cross_copy(unit).start()
                near_copy(unit).start()
                keep_copy(unit, kept.at[unit, other], mine).start()
            else:
                middle_copy(unit).wait()
                kept[unit, other] = plus(kept[unit, mine], middle_in[unit % 10])
                share_copy(unit, kept.at[unit, other]).start()
                outer_copy(unit).start()
                keep_copy(unit, kept.at[unit, other], over_y).start()

    def stage_six(unit):
        if KINDS[unit] == "M":

            @pl.when(jnp.logical_not(at_edge))
            def _():
                cross_copy(unit).wait_recv()
                far_copy(unit).start()

        else:

            @pl.when(at_edge)
            def _():
                outer_copy(unit).wait_recv()
                share_copy(unit, middle_in.at[unit % 10]).start()
                keep_copy(unit, middle_in.at[unit % 10], over_y).start()

    def stage_seven(unit):
        mine, other = spots(unit)
        source = kept.at[unit, other]
        if KINDS[unit] == "M":

            @pl.when(at_edge)
            def _():
                edge_copy(unit).wait_send()
                near_copy(unit).wait_recv()
                far_copy(unit).wait_recv()

            @pl.when(jnp.logical_not(at_edge))
            def _():
                cross_copy(unit).wait_send()
                near_copy(unit).wait_send()
                far_copy(unit).wait_send()
                keep_copy(unit, source, mine).wait()

        else:

            @pl.when(at_edge)
            def _():
                edge_copy(unit).wait_send()

            @pl.when(jnp.logical_not(at_edge))
            def _():
                outer_copy(unit).wait_send()

            share_copy(unit, source).wait()
            keep_copy(unit, source, over_y).wait()

    stages = (
        lambda unit: core_copy(unit).start(),
        stage_one,
        stage_two,
        stage_three,
        stage_four,
        stage_five,
        stage_six,
        stage_seven,
    )


    def put_quarter(unit, quarter, rows):
        own[unit % 4, quarter % 2, quarter // 2] = bf16(rows).reshape(2, HALF_ROWS, D)

    def put_unit(unit, block):
        for quarter in range(RANKS):
            put_quarter(unit, quarter, block[quarter * ROWS : (quarter + 1) * ROWS])

    def flat(block):
        return block.reshape(CHUNKS * TOKENS, block.shape[-1])

    def unit_loads(unit):
        if unit < 8:
            left, right, column = act_three, grad_lifted, unit - 4
        elif unit < 11:
            left, right, column = act_two, time_scr, unit - 8
        else:
            left, right, column = mixed_two, grad_temporal, 0
        return (
            pltpu.make_async_copy(left, left_scr.at[unit % 2], load_sem.at[0, unit % 2]),
            pltpu.make_async_copy(
                right.at[:, :, pl.ds(column * D, D)], right_scr.at[unit % 2], load_sem.at[1, unit % 2]
            ),
        )

    def make_unit(unit):
        if unit < 12:
            for load in unit_loads(unit):
                load.wait()
            left, right = left_scr[unit % 2], right_scr[unit % 2]
        elif unit < 15:
            left, right = x_scr[...], qkv_scr[:, :, pl.ds((unit - 12) * D, D)]
        else:
            left, right = mixed_scr[...], spatial_scr[...]
        put_unit(unit, dot_tn(flat(left), flat(right)))
        if 4 <= unit < 10:
            for load in unit_loads(unit + 2):
                load.start()

    def hidden_load(block):
        spot = block % 2
        lanes = pl.ds(block % RANKS * D, D)
        return pltpu.make_async_copy(hidden.at[:, :, lanes], right_scr.at[spot], load_sem.at[1, spot])

    def double_unit(double):
        for block in range(RANKS):
            hidden_load(block).wait()
            left = left_scr[0, :, :, pl.ds(double * 2 * ROWS, 2 * ROWS)]
            columns = dot_tn(flat(left), flat(right_scr[block % 2]))
            if block + 2 < RANKS or double == 0:
                hidden_load(block + 2).start()
            for part in range(2):
                put_quarter(2 * double + part, block, columns[part * ROWS : (part + 1) * ROWS])
        if double == 1:
            for unit in (4, 5):
                for load in unit_loads(unit):
                    load.start()


    def chunk_loads(order):
        spot = order % 2
        return (
            pltpu.make_async_copy(state_cells.at[order], chunk_state.at[spot], chunk_sem.at[0, spot]),
            pltpu.make_async_copy(grad_state_two.at[order], chunk_grad.at[spot], chunk_sem.at[1, spot]),
            pltpu.make_async_copy(grad_temporal.at[order], chunk_temporal.at[spot], chunk_sem.at[2, spot]),
            pltpu.make_async_copy(qkv_two.at[order], time_scr.at[order], chunk_sem.at[3, spot]),
        )

    def cell_place(order, frame):
        return state_scr.at[frame, chunk_cells(order, rank)]

    def cell_rows(order, target, frame):
        start = (target * FRAME_PART + frame) * CHUNK_CELLS
        return spatial_scr.at[order, pl.ds(pl.multiple_of(start, CHUNK_CELLS), CHUNK_CELLS)]

    def cell_copy(order, hop, frame):
        target = lax.rem(rank + hop, RANKS)
        return remote(
            cell_rows(order, target, frame),
            cell_place(order, frame),
            cell_send.at[order, hop, frame],
            cell_recv.at[order, hop, frame],
            (slot, target),
        )

    def cell_keep(order, frame):
        return pltpu.make_async_copy(
            cell_rows(order, rank, frame), cell_place(order, frame), cell_recv.at[order, 0, frame]
        )

    def probs_load(step):
        source = probs_two.at[step] if step < CHUNKS else probs.at[step - CHUNKS]
        return pltpu.make_async_copy(source, probs_scr, probs_sem.at[0])

    def probs_next(step):
        if step < CHUNKS + FRAME_PART:
            probs_load(step).start()

    def time_backward(order):
        spot = order % 2
        for load in chunk_loads(order):
            load.wait()
        probs_load(order).wait()
        if order < CHUNKS - 1:
            for load in chunk_loads(order + 1):
                load.start()

        grad_mixed[...] = bf16(dot_nt(chunk_temporal[spot], wout_scr[...]))
        heads_backward(time_scr.at[order], grad_mixed, probs_scr, range(HEADS // 2))
        probs_next(order + 1)
        grad_act = dot_nt(time_scr[order], wqkv_scr[...])
        normed, inverse = standardise(f32(chunk_state[spot]).reshape(TOKENS, D))
        add(3, column_sum(grad_act))
        add(4, column_sum(grad_act * normed))
        spatial_scr[order] = bf16(
            chunk_grad[spot] + standard_back(normed, inverse, grad_act * (1.0 + piece(4)))
        )
        for frame in range(FRAME_PART):
            for hop in range(1, RANKS):
                cell_copy(order, hop, frame).start()
            cell_keep(order, frame).start()


    def add(row, value):
        sums[pl.ds(row, 1)] += value

    def frame_loads(frame):
        return (
            pltpu.make_async_copy(qkv.at[frame], qkv_scr.at[frame], frame_sem.at[0, frame]),
            pltpu.make_async_copy(mixed.at[frame], mixed_scr.at[frame], frame_sem.at[1, frame]),
        )

    def home_copy(frame, hop):
        peer = lax.rem(slot + hop, CLIPS)
        rows = pl.ds(pl.multiple_of(peer * CELL_HOME, CELL_HOME), CELL_HOME)
        return remote(
            state_scr.at[frame, rows],
            grad_home.at[slot, frame],
            home_send.at[frame, hop],
            home_recv.at[frame, hop],
            (peer, rank),
        )

    def home_keep(frame):
        rows = pl.ds(pl.multiple_of(slot * CELL_HOME, CELL_HOME), CELL_HOME)
        return pltpu.make_async_copy(state_scr.at[frame, rows], grad_home.at[slot, frame], home_recv.at[frame, 0])

    def frame_first(frame):
        for load in frame_loads(frame):
            load.wait()
        for order in range(CHUNKS):
            for hop in range(1, RANKS):
                cell_copy(order, hop, frame).wait_recv()
        grad_state = f32(state_scr[frame])
        spatial = dot(mixed_scr[frame], wout_scr[...]) + bias_rows[9:10]
        add(2, column_sum(grad_state * spatial))
        low_spatial = bf16(piece(2) * grad_state)
        spatial_scr[frame] = low_spatial
        add(15, column_sum(f32(low_spatial)))
        grad_mixed[...] = bf16(dot_nt(low_spatial, wout_scr[...]))
        probs_load(CHUNKS + frame).wait()
        heads_backward(qkv_scr.at[frame], grad_mixed, probs_scr, range(HEADS // 4))

    def frame_second(frame):
        heads_backward(qkv_scr.at[frame], grad_mixed, probs_scr, range(HEADS // 4, HEADS // 2))
        probs_next(CHUNKS + frame + 1)
        grad_act = dot_nt(qkv_scr[frame], wqkv_scr[...])
        normed, inverse = standardise(f32(x_scr[frame]))
        x_scr[frame] = bf16(normed * (1.0 + piece(1)) + piece(0))
        add(0, column_sum(grad_act))
        add(1, column_sum(grad_act * normed))
        state_scr[frame] = bf16(
            f32(state_scr[frame]) + standard_back(normed, inverse, grad_act * (1.0 + piece(1)))
        )
        for hop in range(1, CLIPS):
            home_copy(frame, hop).start()
        home_keep(frame).start()


    def sum_exchange(step):
        peer = core_peer if step == 0 else x_peer
        return remote(sums, sums_in_scr.at[step], sum_send.at[step], sum_recv.at[step], peer)

    def sum_add(step):
        sum_exchange(step).wait()
        sums[...] = sums[...] + sums_in_scr[step]

    def sum_spread(hop):
        peer = lax.rem(slot + hop, CLIPS)
        return remote(sums, gathered.at[slot], sum_send.at[1 + hop], sum_recv.at[1 + hop], (peer, rank))

    def sum_keep():
        return pltpu.make_async_copy(sums, gathered.at[slot], sum_send.at[9])


    time_weights = (
        pltpu.make_async_copy(w_qkv_t, wqkv_scr, side_sem.at[0]),
        pltpu.make_async_copy(w_out_t, wout_scr, side_sem.at[1]),
    )
    space_weights = (
        pltpu.make_async_copy(w_qkv, wqkv_scr, side_sem.at[0]),
        pltpu.make_async_copy(w_out, wout_scr, side_sem.at[1]),
    )
    branch_load = pltpu.make_async_copy(grad_branch, left_scr.at[0], load_sem.at[0, 0])
    branch_load.start()
    hidden_load(0).start()
    hidden_load(1).start()
    for load in chunk_loads(0):
        load.start()
    probs_load(0).start()
    for load in time_weights:
        load.start()
    bias_rows = f32(biases[...])
    branch_load.wait()

    def first_of_frames():
        for load in space_weights:
            load.start()
        for order in range(CHUNKS):
            for frame in range(FRAME_PART):
                for hop in range(1, RANKS):
                    cell_copy(order, hop, frame).wait_send()
                cell_keep(order, frame).wait()
        for load in space_weights:
            load.wait()

    for action, index in SCHEDULE:
        if action == "double":
            double_unit(index)
        elif action == "chunk":
            if index == 0:
                for load in time_weights:
                    load.wait()
            if index == 2:
                for frame in range(FRAME_PART):
                    for load in frame_loads(frame):
                        load.start()
            time_backward(index)
        elif action == "first":
            if index == 0:
                first_of_frames()
            frame_first(index)
        elif action == "second":
            frame_second(index)
            if index == FRAME_PART - 1:
                sum_exchange(0).start()
        elif action == "unit":
            make_unit(index)
        elif action == "sums":
            sum_add(index)
            if index == 0:
                sum_exchange(1).start()
            else:
                for hop in range(1, CLIPS):
                    sum_spread(hop).start()
                sum_keep().start()
        else:
            stages[action](index)

    for hop in range(1, CLIPS):
        sum_spread(hop).wait()
    sum_keep().wait()

    def frame_end(frame, carry):
        for hop in range(1, CLIPS):
            home_copy(frame, hop).wait()
        home_keep(frame).wait()
        return carry

    lax.fori_loop(0, FRAME_PART, frame_end, 0)


def block_body(
    destinations,
    cell_counts,
    frame_tasks,
    tokens,
    loss_grad,
    condition,
    biases,
    w_ada,
    w_qkv_s,
    w_out_s,
    w_qkv_t,
    w_out_t,
    w_up,
    w_down,
    layer_home,
    grad_home,
    totals,
    gathered,
    qkv_one,
    mixed_one,
    probs_one,
    state_cells,
    loss_cells,
    layer_cells,
    act_two,
    qkv_two,
    mixed_two,
    grad_temporal,
    act_three,
    grad_lifted,
    hidden,
    grad_branch,
    grad_state_two,
    probs_two,
    modulation,
    sums,
    sums_in,
    x_scr,
    state_scr,
    core_in,
    first_in,
    second_in,
    edge_in,
    middle_in,
    local_sem,
    in_send,
    in_recv,
    out_send,
    out_recv,
    save_one_sem,
    loss_send_sem,
    loss_recv_sem,
    weight_sem,
    stage_sem,
    save_two_sem,
    layer_send_sem,
    layer_recv_sem,
    *tail_sems,
):
    slot = lax.axis_index("dp")
    rank = lax.axis_index("seq")
    low = jnp.bfloat16
    frames = FRAME_PART * RANKS


    def loss_source(half, hop):
        return loss_grad.at[lax.rem(slot + hop, CLIPS), :, pl.ds(half * CHUNK_CELLS, CHUNK_CELLS)]

    def loss_place(order):
        return loss_cells.at[order, pl.ds(rank * FRAME_PART, FRAME_PART)]

    def loss_send(half, hop):
        target, order = loss_target(slot, half)
        return pltpu.make_async_remote_copy(
            src_ref=loss_source(half, hop),
            dst_ref=loss_place(order),
            send_sem=loss_send_sem.at[half, hop],
            recv_sem=loss_recv_sem.at[order, rank],
            device_id=(lax.rem(slot + hop, CLIPS), target),
            device_id_type=MESH,
        )

    def loss_keep(half):
        _, order = loss_target(slot, half)
        return pltpu.make_async_copy(loss_source(half, 0), loss_place(order), loss_recv_sem.at[order, rank])

    def send_loss(early):
        for half in range(2):
            target, order = loss_target(slot, half)

            @pl.when((order < 2) if early else (order >= 2))
            def _():
                @pl.when(target == rank)
                def _():
                    loss_keep(half).start()

                @pl.when(target != rank)
                def _():
                    loss_send(half, 0).start()

                for hop in range(1, CLIPS):
                    loss_send(half, hop).start()

    def loss_sent():
        for half in range(2):
            target, _ = loss_target(slot, half)

            @pl.when(target != rank)
            def _():
                loss_send(half, 0).wait_send()

            for hop in range(1, CLIPS):
                loss_send(half, hop).wait_send()

    def loss_arrive(order):
        for source in range(RANKS):
            place = loss_cells.at[order, pl.ds(source * FRAME_PART, FRAME_PART)]
            pltpu.make_async_copy(
                loss_grad.at[0, :, pl.ds(0, CHUNK_CELLS)], place, loss_recv_sem.at[order, source]
            ).wait()


    def cells_arrive(order):
        for frame in range(FRAME_PART):
            for hop in range(1, RANKS):
                place = state_cells.at[order, frame]
                pltpu.make_async_copy(place, place, out_recv.at[frame, hop, order]).wait()


    def layer_home_of(order):
        chunk = chunk_of(order, rank)
        share = share_of(chunk, rank)
        return 2 * chunk + share // 2, lax.rem(share, 2)

    def layer_copies(order, target):
        home, half = layer_home_of(order)
        source = layer_cells.at[order, pl.ds(target * FRAME_PART, FRAME_PART)]
        place = layer_home.at[slot, :, pl.ds(pl.multiple_of(half * CHUNK_CELLS, CHUNK_CELLS), CHUNK_CELLS)]
        arrival = layer_recv_sem.at[slot, half]
        local = jnp.logical_and(home == slot, rank == target)
        keep = functools.partial(pltpu.make_async_copy, source, place, arrival)
        leave = functools.partial(
            pltpu.make_async_remote_copy,
            src_ref=source,
            dst_ref=place,
            send_sem=layer_send_sem.at[order, target],
            recv_sem=arrival,
            device_id=(home, target),
            device_id_type=MESH,
        )
        return local, keep, leave

    def send_layer(order):
        for target in range(RANKS):
            local, keep, leave = layer_copies(order, target)

            @pl.when(local)
            def _():
                keep().start()

            @pl.when(jnp.logical_not(local))
            def _():
                leave().start()

    def layer_sent(order, carry):
        for target in range(RANKS):
            local, _, leave = layer_copies(order, target)

            @pl.when(jnp.logical_not(local))
            def _():
                leave().wait_send()

        return carry

    def layer_arrive():
        for clip in range(CLIPS):
            for half in range(2):
                place = layer_home.at[clip, :, pl.ds(half * CHUNK_CELLS, CHUNK_CELLS)]
                pltpu.make_async_copy(place, place, layer_recv_sem.at[clip, half]).wait()


    def front(wqkv_scr, wout_scr, wup_scr, wdown_scr):
        sources = (w_qkv_t, w_out_t, w_up, w_down)
        places = (wqkv_scr, wout_scr, wup_scr, wdown_scr)
        weight_loads = [
            pltpu.make_async_copy(source, place, weight_sem.at[which])
            for which, (source, place) in enumerate(zip(sources, places))
        ]

        def load_later():
            for load in weight_loads:
                load.start()

        def space(*scoped):
            space_forward_body(
                destinations,
                cell_counts,
                tokens,
                condition,
                biases,
                w_ada,
                w_qkv_s,
                w_out_s,
                qkv_one,
                mixed_one,
                probs_one,
                state_cells,
                modulation,
                x_scr,
                *scoped,
                local_sem,
                in_send,
                in_recv,
                out_send,
                out_recv,
                save_one_sem,
                load_later,
                send_loss,
            )

        pl.run_scoped(
            space,
            pltpu.VMEM((D, 9 * D), low),
            pltpu.VMEM((D, 3 * D), low),
            pltpu.VMEM((D, D), low),
            pltpu.VMEM((FRAME_PART, CELLS, 3 * D), low),
            pltpu.VMEM((FRAME_PART, CELLS, D), low),
            pltpu.VMEM((2, HEADS, CELLS, CELLS), low),
            pltpu.VMEM((FRAME_PART, CELLS, D), low),
        )
        send_loss(False)

        def time(*scoped):
            time_forward_body(
                cell_counts,
                frame_tasks,
                state_cells,
                loss_cells,
                layer_cells,
                modulation,
                biases,
                (
                    act_two,
                    qkv_two,
                    mixed_two,
                    grad_temporal,
                    act_three,
                    grad_lifted,
                    hidden,
                    grad_branch,
                    grad_state_two,
                    probs_two,
                ),
                sums,
                wqkv_scr,
                wout_scr,
                wup_scr,
                wdown_scr,
                *scoped,
                stage_sem,
                save_two_sem,
                weight_loads,
                cells_arrive,
                loss_arrive,
                send_layer,
            )

        pl.run_scoped(
            time,
            pltpu.VMEM((TOKENS, FF), jnp.float32),
            pltpu.VMEM((2, frames, CHUNK_CELLS, D), low),
            pltpu.VMEM((frames, CHUNK_CELLS, D), low),
            pltpu.VMEM((frames, CHUNK_CELLS, D), low),
            *[pltpu.VMEM((2, TOKENS, width), low) for width in SAVED_WIDTHS],
            pltpu.VMEM((2, TOKENS, D), jnp.float32),
            pltpu.VMEM((2, HEADS, TOKENS, TOKENS), low),
        )

    pl.run_scoped(
        front,
        pltpu.VMEM((D, 3 * D), low),
        pltpu.VMEM((D, D), low),
        pltpu.VMEM((D, FF), low),
        pltpu.VMEM((FF, D), low),
    )

    def tail(*scoped):
        tail_body(
            qkv_one,
            mixed_one,
            probs_one,
            state_cells,
            act_two,
            qkv_two,
            mixed_two,
            grad_temporal,
            act_three,
            grad_lifted,
            hidden,
            grad_branch,
            grad_state_two,
            probs_two,
            modulation,
            biases,
            w_qkv_t,
            w_out_t,
            w_qkv_s,
            w_out_s,
            grad_home,
            totals,
            gathered,
            x_scr,
            state_scr,
            sums,
            sums_in,
            core_in,
            first_in,
            second_in,
            edge_in,
            middle_in,
            *scoped,
            *tail_sems,
        )

    pl.run_scoped(
        tail,
        pltpu.VMEM((FRAME_PART, CELLS, 3 * D), low),
        pltpu.VMEM((FRAME_PART, CELLS, D), low),
        pltpu.VMEM((FRAME_PART, CELLS, D), low),
        pltpu.VMEM((CHUNKS, TOKENS, 3 * D), low),
        pltpu.VMEM((D, 3 * D), low),
        pltpu.VMEM((D, D), low),
        pltpu.VMEM((2, CHUNKS, TOKENS, D), low),
        pltpu.VMEM((2, CHUNKS, TOKENS, D), low),
        pltpu.VMEM((CELLS, D), low),
        pltpu.VMEM((2, frames, CHUNK_CELLS, D), low),
        pltpu.VMEM((2, TOKENS, D), jnp.float32),
        pltpu.VMEM((2, TOKENS, D), low),
        pltpu.VMEM((HEADS, TOKENS, TOKENS), low),
        pltpu.VMEM((4, 2, 2, 2, HALF_ROWS, D), low),
        pltpu.VMEM((8, 2, HALF_ROWS, D), low),
        pltpu.VMEM((UNITS, 2, HALF_ROWS, D), low),
    )
    loss_sent()
    lax.fori_loop(0, CHUNKS, layer_sent, 0)
    layer_arrive()


def block(destinations, cell_counts, frame_tasks, tokens, loss_grad, condition, biases, *weights):
    low = jnp.bfloat16
    frames = FRAME_PART * RANKS
    dma = pltpu.SemaphoreType.DMA

    def cells():
        return jax.ShapeDtypeStruct((CHUNKS, frames, CHUNK_CELLS, D), low)

    def home():
        return jax.ShapeDtypeStruct((CLIPS, FRAME_PART, CELL_HOME, D), low)

    def probs():
        return jax.ShapeDtypeStruct((CHUNKS, HEADS, TOKENS, TOKENS), low)

    out_shape = (
        home(),
        home(),
        jax.ShapeDtypeStruct((UNITS, ROWS, D), low),
        jax.ShapeDtypeStruct((CLIPS, 16, D), jnp.float32),
        jax.ShapeDtypeStruct((FRAME_PART, CELLS, 3 * D), low),
        jax.ShapeDtypeStruct((FRAME_PART, CELLS, D), low),
        probs(),
        cells(),
        cells(),
        cells(),
        *[jax.ShapeDtypeStruct((CHUNKS, TOKENS, width), low) for width in SAVED_WIDTHS],
        jax.ShapeDtypeStruct((CHUNKS, TOKENS, D), jnp.float32),
        probs(),
    )
    return pl.pallas_call(
        block_body,
        out_shape=out_shape,
        in_specs=[SMEM, SMEM, SMEM, ANY, ANY, VMEM, VMEM] + [ANY] * 7,
        out_specs=(ANY,) * len(out_shape),
        scratch_shapes=[
            pltpu.VMEM((16, D), jnp.float32),
            pltpu.VMEM((16, D), jnp.float32),
            pltpu.VMEM((2, 16, D), jnp.float32),
            pltpu.VMEM((FRAME_PART, CELLS, D), low),
            pltpu.VMEM((FRAME_PART, CELLS, D), low),
            pltpu.VMEM((6, 2, 2, HALF_ROWS, D), low),
            pltpu.VMEM((10, 2, HALF_ROWS, D), low),
            pltpu.VMEM((10, HALF_ROWS, D), low),
            pltpu.VMEM((8, 2, HALF_ROWS, D), low),
            pltpu.VMEM((10, HALF_ROWS, D), low),
            dma((4,)),
            dma((FRAME_PART, CLIPS)),
            dma((FRAME_PART, CLIPS)),
            dma((FRAME_PART, RANKS, CHUNKS)),
            dma((FRAME_PART, RANKS, CHUNKS)),
            dma((FRAME_PART, 4)),
            dma((2, CLIPS)),
            dma((CHUNKS, RANKS)),
            dma((4,)),
            dma((3,)),
            dma((10, 2)),
            dma((CHUNKS, RANKS)),
            dma((CLIPS, 2)),
            dma((2, 2)),
            dma((2, FRAME_PART)),
            dma((1,)),
            dma((2,)),
            dma((4, 2)),
            dma((CHUNKS, RANKS, FRAME_PART)),
            dma((CHUNKS, RANKS, FRAME_PART)),
            dma((FRAME_PART, CLIPS)),
            dma((FRAME_PART, CLIPS)),
            dma((9, UNITS)),
            dma((9, UNITS)),
            dma((10,)),
            dma((9,)),
        ],
        compiler_params=pltpu.CompilerParams(has_side_effects=True, vmem_limit_bytes=62 * 1024 * 1024),
        cost_estimate=pl.CostEstimate(flops=70 * 10**9, bytes_accessed=150 * 10**6, transcendentals=10**7),
        name="block",
    )(destinations, cell_counts, frame_tasks, tokens, loss_grad, condition, biases, *weights)


def finish_body(
    destinations,
    condition,
    gathered,
    totals,
    layer_home,
    grad_home,
    layer_out,
    grad_tokens,
    grad_w_ada,
    grad_w_qkv_s,
    grad_w_out_s,
    grad_w_qkv_t,
    grad_w_out_t,
    grad_w_up,
    grad_w_down,
    sums_all,
    totals_scr,
    ada_scr,
    wide_scr,
    cond_scr,
    sem,
    ada_sem,
    wide_sem,
):
    rank = lax.axis_index("seq")
    moves = (
        pltpu.make_async_copy(layer_home, layer_out, sem.at[0]),
        pltpu.make_async_copy(grad_home, grad_tokens, sem.at[1]),
    )
    load = pltpu.make_async_copy(totals, totals_scr, sem.at[2])
    load.start()
    for move in moves:
        move.start()
    clips = lax.broadcasted_iota(jnp.int32, (CLIPS, 1), 0)
    rows = f32(condition[...])
    cond = jnp.zeros((CLIPS, D), jnp.float32)
    for clip in range(CLIPS):
        row = column_sum(jnp.where(clips == destinations[clip], rows, 0.0))
        cond = jnp.where(clips == clip, row, cond)
    cond = cond / (1.0 + jnp.exp(-cond))
    for which in range(RANKS):

        @pl.when(rank == which)
        def _():
            cond_scr[...] = cond[:, which * ROWS : (which + 1) * ROWS]

    own_cond = bf16(jnp.concatenate([cond_scr[...]] * 2, axis=0))
    pieces = []
    for piece in range(9):
        grads = jnp.concatenate([gathered[clip, piece : piece + 1] for clip in range(CLIPS)], axis=0)
        high = bf16(grads)
        both = jnp.concatenate([f32(high), grads - f32(high)], axis=0)
        lanes = pl.ds(piece * D, D)
        ada_scr[:, lanes] = dot_tn(own_cond, bf16(both))
        pieces.append(pltpu.make_async_copy(ada_scr.at[:, lanes], grad_w_ada.at[:, lanes], ada_sem.at[piece]))
        pieces[-1].start()
    total = gathered[0]
    for clip in range(1, CLIPS):
        total = total + gathered[clip]
    sums_all[...] = total
    load.wait()
    places = [(grad_w_up, part) for part in range(4)] + [(grad_w_qkv_t, part) for part in range(3)]
    places += [(grad_w_out_t, 0)] + [(grad_w_qkv_s, part) for part in range(3)] + [(grad_w_out_s, 0)]
    for unit, (target, part) in enumerate(places, start=4):
        wide_scr[unit - 4] = f32(totals_scr[unit])
        pieces.append(
            pltpu.make_async_copy(wide_scr.at[unit - 4], target.at[:, pl.ds(part * D, D)], wide_sem.at[unit - 4])
        )
        pieces[-1].start()
    for unit in range(4):
        spot = UNITS - 4 + unit
        lanes = pl.ds(unit * ROWS, ROWS)
        wide_scr[spot] = f32(totals_scr[unit])
    turned = jnp.concatenate([wide_scr[UNITS - 4 + unit] for unit in range(4)], axis=0).T
    for unit in range(4):
        spot = UNITS - 4 + unit
        wide_scr[spot] = turned[unit * ROWS : (unit + 1) * ROWS]
        pieces.append(
            pltpu.make_async_copy(wide_scr.at[spot], grad_w_down.at[pl.ds(unit * ROWS, ROWS)], wide_sem.at[spot])
        )
        pieces[-1].start()
    for move in moves:
        move.wait()
    for copy in pieces:
        copy.wait()


def finish(destinations, condition, gathered, totals, layer_home, grad_home):
    shapes = [(ROWS, 9 * D), (ROWS, 3 * D), (ROWS, D), (ROWS, 3 * D), (ROWS, D), (ROWS, FF), (D, D)]
    dma = pltpu.SemaphoreType.DMA
    return pl.pallas_call(
        finish_body,
        out_shape=(
            jax.ShapeDtypeStruct(layer_home.shape, layer_home.dtype),
            jax.ShapeDtypeStruct(grad_home.shape, grad_home.dtype),
            *[jax.ShapeDtypeStruct(shape, jnp.float32) for shape in shapes],
            jax.ShapeDtypeStruct((16, D), jnp.float32),
        ),
        in_specs=[SMEM, VMEM, VMEM, ANY, ANY, ANY],
        out_specs=(ANY,) * 9 + (VMEM,),
        scratch_shapes=[
            pltpu.VMEM((UNITS, ROWS, D), jnp.bfloat16),
            pltpu.VMEM((ROWS, 9 * D), jnp.float32),
            pltpu.VMEM((UNITS, ROWS, D), jnp.float32),
            pltpu.VMEM((CLIPS, ROWS), jnp.float32),
            dma((3,)),
            dma((9,)),
            dma((UNITS,)),
        ],
        compiler_params=pltpu.CompilerParams(vmem_limit_bytes=40 * 1024 * 1024),
        cost_estimate=pl.CostEstimate(flops=10**8, bytes_accessed=30 * 10**6, transcendentals=0),
        name="finish",
    )(destinations, condition, gathered, totals, layer_home, grad_home)


def per_device_fast(
    tokens,
    condition,
    loss_grad,
    cell_counts,
    frame_tasks,
    destinations,
    w_ada,
    b_ada,
    w_qkv_s,
    w_out_s,
    b_out_s,
    w_qkv_t,
    w_out_t,
    b_out_t,
    w_up,
    b_up,
    w_down,
    b_down,
):
    rank = lax.axis_index("seq")
    biases = jnp.concatenate([b_ada, b_out_s, b_out_t, b_up, b_down]).reshape(16, D)
    layer_home, grad_home, totals, gathered = block(
        destinations,
        cell_counts,
        frame_tasks,
        tokens,
        loss_grad,
        condition,
        biases,
        w_ada,
        w_qkv_s,
        w_out_s,
        w_qkv_t,
        w_out_t,
        w_up,
        w_down,
    )[:4]
    results = finish(destinations, condition, gathered, totals, layer_home, grad_home)
    layer_out, grad_tokens, grad_w_ada, grad_w_qkv_s, grad_w_out_s, grad_w_qkv_t, grad_w_out_t = results[:7]
    grad_w_up, grad_w_down, sums = results[7:]
    grad_b_ada = lax.dynamic_slice_in_dim(sums[:9].reshape(9 * D), rank * 9 * ROWS, 9 * ROWS)
    grad_b_up = lax.dynamic_index_in_dim(sums[9:13], rank, 0, keepdims=False)
    quarters = lax.dynamic_slice_in_dim(sums, rank * ROWS, ROWS, axis=1)
    return (
        layer_out,
        grad_tokens,
        grad_w_ada,
        grad_b_ada,
        grad_w_qkv_s,
        grad_w_out_s,
        quarters[15],
        grad_w_qkv_t,
        grad_w_out_t,
        quarters[14],
        grad_w_up,
        grad_b_up,
        grad_w_down,
        quarters[13],
    )


def solution(mesh):
    placed = (
        P(None, "seq", "dp", None),
        P(),
        P(None, "seq", "dp", None),
        P(),
        P(),
        P(),
        P(),
        P(),
        P(),
        P(),
        P(),
        P(),
        P(),
        P(),
        P(),
        P(),
        P(),
        P(),
    )
    fast = mesh.shape["dp"] == 8 and mesh.shape["seq"] == 4
    return jax.shard_map(
        per_device_fast if fast else per_device_general,
        mesh=mesh,
        in_specs=placed,
        out_specs=(
            P(None, "seq", "dp", None),
            P(None, "seq", "dp", None),
            P("seq", None),
            P("seq"),
            P("seq", None),
            P("seq", None),
            P("seq"),
            P("seq", None),
            P("seq", None),
            P("seq"),
            P("seq", None),
            P("seq"),
            P("seq", None),
            P("seq"),
        ),
        check_vma=False,
    )
```

```python
import functools

import jax
import jax.numpy as jnp
from jax import lax
from jax.experimental import pallas as pl
from jax.experimental.pallas import tpu as pltpu
from jax.sharding import PartitionSpec as P

D = 768
HEADS = 12
HEAD = 64


def standard(field):
    centred = field - jnp.mean(field, axis=-1, keepdims=True)
    inverse = lax.rsqrt(jnp.mean(centred * centred, axis=-1, keepdims=True) + 1e-06)
    return (centred * inverse, inverse)


def standard_back(normed, inverse, grad_normed):
    return inverse * (
        grad_normed
        - jnp.mean(grad_normed, axis=-1, keepdims=True)
        - normed * jnp.mean(grad_normed * normed, axis=-1, keepdims=True)
    )


def gelu_back(lifted, grad_hidden):
    return jax.vjp(lambda inner: jax.nn.gelu(inner, approximate=True), lifted)[1](grad_hidden)[0]


def attend(triple, key_valid, einsum_forms):
    queries = triple[:, :, 0]
    key_rows = triple[:, :, 1]
    value_rows = triple[:, :, 2]
    scores = (
        jnp.einsum(einsum_forms[0], queries, key_rows, preferred_element_type=jnp.float32) * 0.125
    )
    scores = jnp.where(key_valid, scores, -1e30)
    row_top = jnp.max(scores, axis=-1, keepdims=True)
    exponent = jnp.exp(scores - row_top)
    probs_full = exponent / jnp.sum(exponent, axis=-1, keepdims=True)
    probs_low = probs_full.astype(jnp.bfloat16)
    mixed_out = jnp.einsum(
        einsum_forms[1], probs_low, value_rows, preferred_element_type=jnp.float32
    ).astype(jnp.bfloat16)
    return (mixed_out, probs_full, probs_low)


def attend_back(triple, probs_full, probs_low, grad_mixed, einsum_forms):
    queries = triple[:, :, 0]
    key_rows = triple[:, :, 1]
    value_rows = triple[:, :, 2]
    grad_probs = jnp.einsum(
        einsum_forms[0], grad_mixed, value_rows, preferred_element_type=jnp.float32
    )
    row_delta = jnp.sum(probs_full * grad_probs, axis=-1, keepdims=True)
    grad_scores = (probs_full * (grad_probs - row_delta)).astype(jnp.bfloat16)
    grad_values = jnp.einsum(
        einsum_forms[2], probs_low, grad_mixed, preferred_element_type=jnp.float32
    )
    grad_queries = (
        jnp.einsum(einsum_forms[1], grad_scores, key_rows, preferred_element_type=jnp.float32)
        * 0.125
    )
    grad_keys = (
        jnp.einsum(einsum_forms[2], grad_scores, queries, preferred_element_type=jnp.float32)
        * 0.125
    )
    return jnp.stack([grad_queries, grad_keys, grad_values], axis=2)


def per_device_general(
    tokens,
    condition,
    loss_grad,
    cell_counts,
    frame_tasks,
    destinations,
    w_ada,
    b_ada,
    w_qkv_s,
    w_out_s,
    b_out_s,
    w_qkv_t,
    w_out_t,
    b_out_t,
    w_up,
    b_up,
    w_down,
    b_down,
):
    groups = lax.axis_size("dp")
    ranks = lax.axis_size("seq")
    own_slot = lax.axis_index("dp")
    own_rank = lax.axis_index("seq")
    frame_part = tokens.shape[1]
    cell_total = tokens.shape[2] * groups
    cell_part = cell_total // ranks
    frame_total = frame_part * ranks
    slot_ids = jnp.arange(groups, dtype=jnp.int32)
    routing = (destinations[None, :] == slot_ids[:, None]).astype(jnp.bfloat16)
    outgoing = jnp.einsum(
        "jc,cfbd->jfbd", routing, tokens, preferred_element_type=jnp.float32
    ).astype(jnp.bfloat16)
    outgoing_grad = jnp.einsum(
        "jc,cfbd->jfbd", routing, loss_grad, preferred_element_type=jnp.float32
    ).astype(jnp.bfloat16)
    arrived, arrived_grad = (
        lax.all_to_all(outgoing, "dp", split_axis=0, concat_axis=2, tiled=True),
        lax.all_to_all(outgoing_grad, "dp", split_axis=0, concat_axis=2, tiled=True),
    )
    own_clip = jnp.sum(jnp.where(destinations == own_slot, slot_ids, 0))
    own_count = jnp.sum(jnp.where(slot_ids == own_clip, cell_counts, 0))
    own_tasks = lax.dynamic_index_in_dim(frame_tasks, own_clip, 0, keepdims=False)
    cond_row = lax.dynamic_index_in_dim(condition, own_slot, 0, keepdims=False)
    cond_low = jax.nn.silu(cond_row.astype(jnp.float32)).astype(jnp.bfloat16)
    modulation = jnp.dot(cond_low[None, :], w_ada, preferred_element_type=jnp.float32)[
        0
    ] + b_ada.astype(jnp.float32)
    pieces = [modulation[piece_index * D : (piece_index + 1) * D] for piece_index in range(9)]
    (
        shift_one,
        scale_one,
        gate_one,
        shift_two,
        scale_two,
        gate_two,
        shift_three,
        scale_three,
        gate_three,
    ) = pieces
    space_forms = ("fphe,fqhe->fhpq", "fhpq,fqhe->fphe", "fhpq,fphe->fqhe")
    frames_in = arrived[0].astype(jnp.float32)
    normed_one, inverse_one = standard(frames_in)
    act_one = (normed_one * (1.0 + scale_one) + shift_one).astype(jnp.bfloat16)
    triple_one = (
        jnp.einsum("fpd,de->fpe", act_one, w_qkv_s, preferred_element_type=jnp.float32)
        .astype(jnp.bfloat16)
        .reshape(frame_part, cell_total, 3, HEADS, HEAD)
    )
    key_valid = (jnp.arange(cell_total, dtype=jnp.int32) < own_count)[None, None, None, :]
    mixed_one, probs_one, low_one = attend(triple_one, key_valid, space_forms)
    flat_one = mixed_one.reshape(frame_part, cell_total, D)
    spatial_out = jnp.einsum(
        "fpd,de->fpe", flat_one, w_out_s, preferred_element_type=jnp.float32
    ) + b_out_s.astype(jnp.float32)
    state_one = (frames_in + gate_one * spatial_out).astype(jnp.bfloat16)
    cells_in, cells_grad = (
        lax.all_to_all(state_one, "seq", split_axis=1, concat_axis=0, tiled=True),
        lax.all_to_all(arrived_grad[0], "seq", split_axis=1, concat_axis=0, tiled=True),
    )
    time_forms = ("fqhe,gqhe->qhfg", "qhfg,gqhe->fqhe", "qhfg,fqhe->gqhe")
    state_cells = cells_in.astype(jnp.float32)
    normed_two, inverse_two = standard(state_cells)
    act_two = (normed_two * (1.0 + scale_two) + shift_two).astype(jnp.bfloat16)
    triple_two = (
        jnp.einsum("fqd,de->fqe", act_two, w_qkv_t, preferred_element_type=jnp.float32)
        .astype(jnp.bfloat16)
        .reshape(frame_total, cell_part, 3, HEADS, HEAD)
    )
    mixed_two, probs_two, low_two = attend(triple_two, True, time_forms)
    flat_two = mixed_two.reshape(frame_total, cell_part, D)
    temporal_out = jnp.einsum(
        "fqd,de->fqe", flat_two, w_out_t, preferred_element_type=jnp.float32
    ) + b_out_t.astype(jnp.float32)
    state_two = state_cells + gate_two * temporal_out
    normed_three, inverse_three = standard(state_two)
    act_three = (normed_three * (1.0 + scale_three) + shift_three).astype(jnp.bfloat16)
    lifted = jnp.einsum(
        "fqd,dk->fqk", act_three, w_up, preferred_element_type=jnp.float32
    ) + b_up.astype(jnp.float32)
    hidden = jax.nn.gelu(lifted, approximate=True).astype(jnp.bfloat16)
    branch_out = jnp.einsum(
        "fqk,kd->fqd", hidden, w_down, preferred_element_type=jnp.float32
    ) + b_down.astype(jnp.float32)
    result = (state_two + gate_three * branch_out).astype(jnp.bfloat16)
    cell_ids = own_rank * cell_part + jnp.arange(cell_part, dtype=jnp.int32)
    loss_mask = jnp.logical_and(own_tasks[:, None] == 1, cell_ids[None, :] < own_count)
    out_grad = cells_grad.astype(jnp.float32) * loss_mask[:, :, None].astype(jnp.float32)
    grad_gate_three = jnp.sum(out_grad * branch_out, axis=(0, 1))
    grad_branch = (gate_three * out_grad).astype(jnp.bfloat16)
    grad_b_down = jnp.sum(grad_branch.astype(jnp.float32), axis=(0, 1))
    grad_w_down = jnp.einsum("fqk,fqd->kd", hidden, grad_branch, preferred_element_type=jnp.float32)
    grad_hidden = jnp.einsum("fqd,kd->fqk", grad_branch, w_down, preferred_element_type=jnp.float32)
    grad_lifted = gelu_back(lifted, grad_hidden).astype(jnp.bfloat16)
    grad_b_up = jnp.sum(grad_lifted.astype(jnp.float32), axis=(0, 1))
    grad_w_up = jnp.einsum(
        "fqd,fqk->dk", act_three, grad_lifted, preferred_element_type=jnp.float32
    )
    grad_act_three = jnp.einsum(
        "fqk,dk->fqd", grad_lifted, w_up, preferred_element_type=jnp.float32
    )
    grad_shift_three = jnp.sum(grad_act_three, axis=(0, 1))
    grad_scale_three = jnp.sum(grad_act_three * normed_three, axis=(0, 1))
    grad_state_two = out_grad + standard_back(
        normed_three, inverse_three, grad_act_three * (1.0 + scale_three)
    )
    grad_gate_two = jnp.sum(grad_state_two * temporal_out, axis=(0, 1))
    grad_temporal = (gate_two * grad_state_two).astype(jnp.bfloat16)
    grad_b_out_t = jnp.sum(grad_temporal.astype(jnp.float32), axis=(0, 1))
    grad_w_out_t = jnp.einsum(
        "fqd,fqe->de", flat_two, grad_temporal, preferred_element_type=jnp.float32
    )
    grad_mixed_two = (
        jnp.einsum("fqe,de->fqd", grad_temporal, w_out_t, preferred_element_type=jnp.float32)
        .astype(jnp.bfloat16)
        .reshape(frame_total, cell_part, HEADS, HEAD)
    )
    grad_triple_two = (
        attend_back(triple_two, probs_two, low_two, grad_mixed_two, time_forms)
        .reshape(frame_total, cell_part, 3 * D)
        .astype(jnp.bfloat16)
    )
    grad_w_qkv_t = jnp.einsum(
        "fqd,fqe->de", act_two, grad_triple_two, preferred_element_type=jnp.float32
    )
    grad_act_two = jnp.einsum(
        "fqe,de->fqd", grad_triple_two, w_qkv_t, preferred_element_type=jnp.float32
    )
    grad_shift_two = jnp.sum(grad_act_two, axis=(0, 1))
    grad_scale_two = jnp.sum(grad_act_two * normed_two, axis=(0, 1))
    grad_state_one = (
        grad_state_two + standard_back(normed_two, inverse_two, grad_act_two * (1.0 + scale_two))
    ).astype(jnp.bfloat16)
    frames_out, frames_grad = (
        lax.all_to_all(result, "seq", split_axis=0, concat_axis=1, tiled=True),
        lax.all_to_all(grad_state_one, "seq", split_axis=0, concat_axis=1, tiled=True),
    )
    grad_frames = frames_grad.astype(jnp.float32)
    grad_gate_one = jnp.sum(grad_frames * spatial_out, axis=(0, 1))
    grad_spatial = (gate_one * grad_frames).astype(jnp.bfloat16)
    grad_b_out_s = jnp.sum(grad_spatial.astype(jnp.float32), axis=(0, 1))
    grad_w_out_s = jnp.einsum(
        "fpd,fpe->de", flat_one, grad_spatial, preferred_element_type=jnp.float32
    )
    grad_mixed_one = (
        jnp.einsum("fpe,de->fpd", grad_spatial, w_out_s, preferred_element_type=jnp.float32)
        .astype(jnp.bfloat16)
        .reshape(frame_part, cell_total, HEADS, HEAD)
    )
    grad_triple_one = (
        attend_back(triple_one, probs_one, low_one, grad_mixed_one, space_forms)
        .reshape(frame_part, cell_total, 3 * D)
        .astype(jnp.bfloat16)
    )
    grad_w_qkv_s = jnp.einsum(
        "fpd,fpe->de", act_one, grad_triple_one, preferred_element_type=jnp.float32
    )
    grad_act_one = jnp.einsum(
        "fpe,de->fpd", grad_triple_one, w_qkv_s, preferred_element_type=jnp.float32
    )
    grad_shift_one = jnp.sum(grad_act_one, axis=(0, 1))
    grad_scale_one = jnp.sum(grad_act_one * normed_one, axis=(0, 1))
    grad_input = (
        grad_frames + standard_back(normed_one, inverse_one, grad_act_one * (1.0 + scale_one))
    ).astype(jnp.bfloat16)
    home_out, home_grad = (
        lax.all_to_all(frames_out[None], "dp", split_axis=2, concat_axis=0, tiled=True),
        lax.all_to_all(grad_input[None], "dp", split_axis=2, concat_axis=0, tiled=True),
    )
    layer_out = jnp.einsum(
        "jc,jfbd->cfbd", routing, home_out, preferred_element_type=jnp.float32
    ).astype(jnp.bfloat16)
    grad_tokens = jnp.einsum(
        "jc,jfbd->cfbd", routing, home_grad, preferred_element_type=jnp.float32
    ).astype(jnp.bfloat16)
    grad_mod = jnp.concatenate(
        [
            grad_shift_one,
            grad_scale_one,
            grad_gate_one,
            grad_shift_two,
            grad_scale_two,
            grad_gate_two,
            grad_shift_three,
            grad_scale_three,
            grad_gate_three,
        ]
    )
    ada_term = cond_low.astype(jnp.float32)[:, None] * grad_mod[None, :]
    partials = (
        lax.psum_scatter(
            ada_term.astype(jnp.bfloat16), "seq", scatter_dimension=0, tiled=True
        ).astype(jnp.float32),
        lax.psum_scatter(
            grad_mod.astype(jnp.bfloat16), "seq", scatter_dimension=0, tiled=True
        ).astype(jnp.float32),
        lax.psum_scatter(
            grad_w_qkv_s.astype(jnp.bfloat16), "seq", scatter_dimension=0, tiled=True
        ).astype(jnp.float32),
        lax.psum_scatter(
            grad_w_out_s.astype(jnp.bfloat16), "seq", scatter_dimension=0, tiled=True
        ).astype(jnp.float32),
        lax.psum_scatter(
            grad_b_out_s.astype(jnp.bfloat16), "seq", scatter_dimension=0, tiled=True
        ).astype(jnp.float32),
        lax.psum_scatter(
            grad_w_qkv_t.astype(jnp.bfloat16), "seq", scatter_dimension=0, tiled=True
        ).astype(jnp.float32),
        lax.psum_scatter(
            grad_w_out_t.astype(jnp.bfloat16), "seq", scatter_dimension=0, tiled=True
        ).astype(jnp.float32),
        lax.psum_scatter(
            grad_b_out_t.astype(jnp.bfloat16), "seq", scatter_dimension=0, tiled=True
        ).astype(jnp.float32),
        lax.psum_scatter(
            grad_w_up.astype(jnp.bfloat16), "seq", scatter_dimension=0, tiled=True
        ).astype(jnp.float32),
        lax.psum_scatter(
            grad_b_up.astype(jnp.bfloat16), "seq", scatter_dimension=0, tiled=True
        ).astype(jnp.float32),
        lax.psum_scatter(
            grad_w_down.astype(jnp.bfloat16), "seq", scatter_dimension=0, tiled=True
        ).astype(jnp.float32),
        lax.psum_scatter(
            grad_b_down.astype(jnp.bfloat16), "seq", scatter_dimension=0, tiled=True
        ).astype(jnp.float32),
    )
    totals = lax.psum(
        (
            partials[0],
            partials[1],
            partials[2],
            partials[3],
            partials[4],
            partials[5],
            partials[6],
            partials[7],
            partials[8],
            partials[9],
            partials[10],
            partials[11],
        ),
        "dp",
    )
    ada_grad = totals[0]
    ada_bias = totals[1]
    rest = totals[2:]
    return (
        layer_out,
        grad_tokens,
        ada_grad,
        ada_bias,
        rest[0],
        rest[1],
        rest[2],
        rest[3],
        rest[4],
        rest[5],
        rest[6],
        rest[7],
        rest[8],
        rest[9],
    )


MESH = pl.DeviceIdType.MESH
ANY = pl.BlockSpec(memory_space=pl.ANY)
VMEM = pl.BlockSpec(memory_space=pltpu.VMEM)
SMEM = pl.BlockSpec(memory_space=pltpu.SMEM)
NEG = -1e30
CLIPS = 8
RANKS = 4
FRAME_PART = 4
CELLS = 256
CELL_HOME = CELLS // CLIPS
CELL_PART = CELLS // RANKS
FF = 3072
TOKENS = 256
CHUNK_CELLS = TOKENS // (FRAME_PART * RANKS)
CHUNKS = CELL_PART // CHUNK_CELLS


def turn_of(rank):
    return 2 * lax.rem(rank, 2) + rank // 2


def chunk_of(order, rank):
    return lax.rem(order + turn_of(rank), CHUNKS)


def order_of(chunk, rank):
    return lax.rem(chunk - turn_of(rank) + CHUNKS, CHUNKS)


def share_of(chunk, rank):
    return lax.rem(rank - chunk + RANKS, RANKS)


def chunk_cells(order, rank):
    chunk = chunk_of(order, rank)
    start = chunk * CELL_PART + share_of(chunk, rank) * CHUNK_CELLS
    return pl.ds(pl.multiple_of(start, CHUNK_CELLS), CHUNK_CELLS)


def loss_target(slot, half):
    chunk = slot // 2
    target = lax.rem(2 * lax.rem(slot, 2) + half + chunk, RANKS)
    return target, order_of(chunk, target)


def f32(value):
    return value.astype(jnp.float32)


def bf16(value):
    return value.astype(jnp.bfloat16)


def dot(left, right):
    return lax.dot_general(left, right, (((1,), (0,)), ((), ())), preferred_element_type=jnp.float32)


def dot_nt(left, right):
    return lax.dot_general(left, right, (((1,), (1,)), ((), ())), preferred_element_type=jnp.float32)


def dot_tn(left, right):
    return lax.dot_general(left, right, (((0,), (0,)), ((), ())), preferred_element_type=jnp.float32)


def standardise(field):
    centred = field - jnp.mean(field, axis=-1, keepdims=True)
    inverse = lax.rsqrt(jnp.mean(centred * centred, axis=-1, keepdims=True) + 1e-06)
    return centred * inverse, inverse


def column_sum(field):
    return jnp.sum(field, axis=0, keepdims=True)


def head_halves(rows):
    lane = lax.broadcasted_iota(jnp.int32, (1, 2 * HEAD), 1) < HEAD
    zero = jnp.bfloat16(0)
    return jnp.where(lane, rows, zero), jnp.where(lane, zero, rows)


def pair_lanes(pair, part):
    return pl.ds(part * D + pair * 2 * HEAD, 2 * HEAD)


def heads_forward(qkv, mixed, probs, valid):
    lane = lax.broadcasted_iota(jnp.int32, (1, 2 * HEAD), 1) < HEAD
    scores = []
    for pair in range(HEADS // 2):
        queries = head_halves(qkv[:, pair_lanes(pair, 0)] * jnp.bfloat16(0.125))
        keys = qkv[:, pair_lanes(pair, 1)]
        scores += [dot_nt(queries[half], keys) for half in range(2)]
    low = []
    for head in range(HEADS):
        masked = jnp.where(valid, scores[head], NEG)
        exponent = jnp.exp(masked - jnp.max(masked, axis=-1, keepdims=True))
        low.append(bf16(exponent * (1.0 / jnp.sum(exponent, axis=-1, keepdims=True))))
        probs[head] = low[head]
    for pair in range(HEADS // 2):
        values = qkv[:, pair_lanes(pair, 2)]
        parts = [dot(low[2 * pair + half], values) for half in range(2)]
        mixed[:, pair_lanes(pair, 0)] = bf16(jnp.where(lane, parts[0], parts[1]))


def heads_backward(qkv, grad_mixed, probs, pairs):
    lane = lax.broadcasted_iota(jnp.int32, (1, 2 * HEAD), 1) < HEAD
    heads = [(pair, half) for pair in pairs for half in range(2)]
    operands = {pair: [qkv[:, pair_lanes(pair, part)] for part in range(3)] for pair in pairs}
    grads = {pair: grad_mixed[:, pair_lanes(pair, 0)] for pair in pairs}
    halves = {pair: head_halves(grads[pair]) for pair in pairs}
    low = {head: probs[2 * head[0] + head[1]] for head in heads}
    grad_probs = {head: dot_nt(halves[head[0]][head[1]], operands[head[0]][2]) for head in heads}
    grad_values = {head: dot_tn(low[head], grads[head[0]]) for head in heads}
    grad_scores = {}
    for head in heads:
        full = f32(low[head])
        weighted = full * grad_probs[head]
        grad_scores[head] = bf16(weighted - full * jnp.sum(weighted, axis=-1, keepdims=True))
    grad_keys = {head: dot_tn(grad_scores[head], operands[head[0]][0]) for head in heads}
    grad_queries = {head: dot(grad_scores[head], operands[head[0]][1]) for head in heads}
    for pair in pairs:
        first, second = (pair, 0), (pair, 1)
        qkv[:, pair_lanes(pair, 0)] = bf16(jnp.where(lane, grad_queries[first], grad_queries[second]) * 0.125)
        qkv[:, pair_lanes(pair, 1)] = bf16(jnp.where(lane, grad_keys[first], grad_keys[second]) * 0.125)
        qkv[:, pair_lanes(pair, 2)] = bf16(jnp.where(lane, grad_values[first], grad_values[second]))


def space_forward_body(
    destinations,
    cell_counts,
    tokens,
    condition,
    biases,
    w_ada,
    w_qkv,
    w_out,
    qkv_all,
    mixed_all,
    probs_all,
    state_cells,
    modulation,
    x_scr,
    ada_scr,
    wqkv_scr,
    wout_scr,
    qkv_scr,
    mixed_scr,
    probs_scr,
    state_scr,
    local_sem,
    ada_sem,
    in_send,
    in_recv,
    out_send,
    out_recv,
    save_sem,
    load_later,
    send_loss,
):
    slot = lax.axis_index("dp")
    rank = lax.axis_index("seq")

    def arrival(frame, hop):
        peer = lax.rem(slot + hop, CLIPS)
        rows = pl.ds(pl.multiple_of(slot * CELL_HOME, CELL_HOME), CELL_HOME)
        return pltpu.make_async_remote_copy(
            src_ref=tokens.at[peer, frame],
            dst_ref=x_scr.at[frame, rows],
            send_sem=in_send.at[frame, hop],
            recv_sem=in_recv.at[frame, hop],
            device_id=(peer, rank),
            device_id_type=MESH,
        )

    def leave(frame, hop, order):
        peer = lax.rem(rank + hop, RANKS)
        return pltpu.make_async_remote_copy(
            src_ref=state_scr.at[frame, chunk_cells(order, peer)],
            dst_ref=state_cells.at[order, rank * FRAME_PART + frame],
            send_sem=out_send.at[frame, hop, order],
            recv_sem=out_recv.at[frame, hop, order],
            device_id=(slot, peer),
            device_id_type=MESH,
        )

    def keep(frame, order):
        return pltpu.make_async_copy(
            state_scr.at[frame, chunk_cells(order, rank)],
            state_cells.at[order, rank * FRAME_PART + frame],
            out_recv.at[frame, 0, order],
        )

    def saves(frame):
        return (
            pltpu.make_async_copy(qkv_scr.at[frame], qkv_all.at[frame], save_sem.at[frame, 1]),
            pltpu.make_async_copy(mixed_scr.at[frame], mixed_all.at[frame], save_sem.at[frame, 2]),
        )

    def save_probs(frame):
        return pltpu.make_async_copy(probs_scr.at[lax.rem(frame, 2)], probs_all.at[frame], save_sem.at[frame, 3])

    own_rows = pl.ds(pl.multiple_of(slot * CELL_HOME, CELL_HOME), CELL_HOME)
    own_copy = pltpu.make_async_copy(tokens.at[slot], x_scr.at[:, own_rows], local_sem.at[0])

    def ada_copy(piece):
        return pltpu.make_async_copy(
            w_ada.at[:, pl.ds(piece * D, D)], ada_scr.at[piece % 3], ada_sem.at[piece % 3]
        )

    qkv_copy = pltpu.make_async_copy(w_qkv, wqkv_scr, local_sem.at[2])
    out_copy = pltpu.make_async_copy(w_out, wout_scr, local_sem.at[3])
    barrier = pltpu.get_barrier_semaphore()
    for over_slots in range(CLIPS):
        for over_ranks in range(RANKS):
            if over_slots + over_ranks:
                peer = (lax.rem(slot + over_slots, CLIPS), lax.rem(rank + over_ranks, RANKS))
                pl.semaphore_signal(barrier, inc=1, device_id=peer, device_id_type=MESH)
    pl.semaphore_wait(barrier, CLIPS * RANKS - 1)
    for hop in range(1, CLIPS):
        arrival(0, hop).start()
    own_copy.start()
    for piece in range(3):
        ada_copy(piece).start()
    for frame in range(1, FRAME_PART):
        for hop in range(1, CLIPS):
            arrival(frame, hop).start()
    qkv_copy.start()
    out_copy.start()
    send_loss(True)

    row_ids = lax.broadcasted_iota(jnp.int32, (CLIPS, 1), 0)
    cond = column_sum(jnp.where(row_ids == destinations[slot], f32(condition[...]), 0.0))
    cond = jnp.broadcast_to(bf16(cond / (1.0 + jnp.exp(-cond))), (16, D))
    bias_rows = f32(biases[...])
    valid = lax.broadcasted_iota(jnp.int32, (1, CELLS), 1) < cell_counts[slot]
    for piece in range(9):
        ada_copy(piece).wait()
        row = dot(cond, ada_scr[piece % 3])[0:1]
        if piece + 3 < 9:
            ada_copy(piece + 3).start()
        modulation[pl.ds(piece, 1)] = row + bias_rows[piece : piece + 1]
    own_copy.wait()
    qkv_copy.wait()
    out_copy.wait()

    def frame_step(frame, carry):
        for hop in range(1, CLIPS):
            arrival(frame, hop).wait_recv()

        @pl.when(frame == 0)
        def _():
            load_later()

        x = f32(x_scr[frame])
        centred = x - jnp.mean(x, axis=-1, keepdims=True)
        normed = centred * lax.rsqrt(jnp.mean(centred * centred, axis=-1, keepdims=True) + 1e-06)
        act = bf16(normed * (1.0 + modulation[1:2]) + modulation[0:1])
        qkv_scr[frame] = bf16(dot(act, wqkv_scr[...]))

        @pl.when(frame >= 2)
        def _():
            save_probs(frame - 2).wait()

        heads_forward(qkv_scr.at[frame], mixed_scr.at[frame], probs_scr.at[lax.rem(frame, 2)], valid)
        save_probs(frame).start()
        spatial = dot(mixed_scr[frame], wout_scr[...]) + bias_rows[9:10]
        state_scr[frame] = bf16(f32(x_scr[frame]) + modulation[2:3] * spatial)
        for order in range(CHUNKS):
            for hop in range(1, RANKS):
                leave(frame, hop, order).start()
            keep(frame, order).start()
        for save in saves(frame):
            save.start()
        return carry

    lax.fori_loop(0, FRAME_PART, frame_step, 0)

    def frame_end(frame, carry):
        for hop in range(1, CLIPS):
            arrival(frame, hop).wait_send()
        for order in range(CHUNKS):
            for hop in range(1, RANKS):
                leave(frame, hop, order).wait_send()
            keep(frame, order).wait()
        for save in saves(frame):
            save.wait()
        return carry

    lax.fori_loop(0, FRAME_PART, frame_end, 0)
    for frame in range(FRAME_PART - 2, FRAME_PART):
        save_probs(frame).wait()


def cell_match():
    row_cell = lax.rem(lax.broadcasted_iota(jnp.int32, (TOKENS, TOKENS), 0), CHUNK_CELLS)
    column_cell = lax.rem(lax.broadcasted_iota(jnp.int32, (TOKENS, TOKENS), 1), CHUNK_CELLS)
    return row_cell == column_cell


SAVED_WIDTHS = (D, 3 * D, D, D, D, FF, FF, D)


STEP = 32


def row_blocks():
    return [slice(start, start + STEP) for start in range(0, TOKENS, STEP)]


def fold(field):
    return jnp.sum(field.reshape(-1, 8, field.shape[-1]), axis=0)


def time_forward_body(
    cell_counts,
    frame_tasks,
    state_cells,
    loss_cells,
    layer_cells,
    modulation,
    biases,
    homes,
    sums,
    wqkv_scr,
    wout_scr,
    wup_scr,
    wdown_scr,
    slopes,
    state_scr,
    loss_scr,
    layer_scr,
    act_two,
    qkv,
    mixed,
    grad_temporal,
    act_three,
    grad_lifted,
    hidden,
    grad_branch,
    grad_state,
    probs,
    stage_sem,
    save_sem,
    weight_loads,
    cells_arrive,
    loss_arrive,
    send_layer,
    load_ahead,
):
    slot = lax.axis_index("dp")
    rank = lax.axis_index("seq")
    frames = FRAME_PART * RANKS

    stages = (act_two, qkv, mixed, grad_temporal, act_three, grad_lifted, hidden, grad_branch, grad_state, probs)
    def save(which, order):
        spot = lax.rem(order, 2)
        return pltpu.make_async_copy(stages[which].at[spot], homes[which].at[order], save_sem.at[which, spot])

    def state_load(order):
        spot = lax.rem(order, 2)
        return pltpu.make_async_copy(state_cells.at[order], state_scr.at[spot], stage_sem.at[0])

    def loss_load(order):
        return pltpu.make_async_copy(loss_cells.at[order], loss_scr, stage_sem.at[1])

    def layer_save(order):
        return pltpu.make_async_copy(layer_scr, layer_cells.at[order], stage_sem.at[2])

    sums[...] = jnp.zeros_like(sums)
    bias_rows = f32(biases[...])
    valid = cell_match()
    count = cell_counts[slot]
    frame_cell = (frames, CHUNK_CELLS, 1)
    cell = lax.broadcasted_iota(jnp.int32, frame_cell, 1).reshape(TOKENS, 1)
    frame_ids = lax.broadcasted_iota(jnp.int32, frame_cell, 0)
    tasks = jnp.zeros(frame_cell, jnp.int32)
    for which in range(frames):
        tasks = jnp.where(frame_ids == which, frame_tasks[slot, which], tasks)
    tasks = tasks.reshape(TOKENS, 1)

    def piece(index):
        return modulation[index : index + 1]

    def add(row, value):
        sums[pl.ds(row, 1)] += value

    def chunk_step(order, carry):
        spot = lax.rem(order, 2)
        first = order == 0

        def once(*which):
            @pl.when(first)
            def _():
                for load in which:
                    weight_loads[load].wait()

        @pl.when(order >= 2)
        def _():
            for which in range(len(stages)):
                save(which, order - 2).wait()

        state_load(order).wait()

        def state_rows(rows):
            span = pl.ds(rows.start // CHUNK_CELLS, STEP // CHUNK_CELLS)
            return f32(state_scr[spot, span]).reshape(STEP, D)

        for rows in row_blocks():
            normed, _ = standardise(state_rows(rows))
            act_two[spot, rows] = bf16(normed * (1.0 + piece(4)) + piece(3))
        once(0)
        qkv[spot] = bf16(dot(act_two[spot], wqkv_scr[...]))
        heads_forward(qkv.at[spot], mixed.at[spot], probs.at[spot], valid)
        for which in (0, 1, 2, 9):
            save(which, order).start()
        once(1)
        temporal = dot(mixed[spot], wout_scr[...])
        kept = []
        for rows in row_blocks():
            back = temporal[rows] + bias_rows[10:11]
            state_two = state_rows(rows) + piece(5) * back
            normed, inverse = standardise(state_two)
            act_three[spot, rows] = bf16(normed * (1.0 + piece(7)) + piece(6))
            kept.append((back, state_two, normed, inverse))
        save(4, order).start()
        once(2, 3)
        branch = None
        for block in range(FF // D):
            lanes = pl.ds(block * D, D)
            lifted = dot(act_three[spot], wup_scr[:, lanes])
            for rows in row_blocks():
                up = lifted[rows] + bias_rows[11 + block : 12 + block]
                square = up * up
                curve = jnp.tanh(up * (0.7978845608028654 + 0.7978845608028654 * 0.044715 * square))
                half = 0.5 * curve + 0.5
                whole = up * half
                hidden[spot, rows, lanes] = bf16(whole)
                slopes[rows, lanes] = half + (whole - whole * half) * (
                    2.0 * 0.7978845608028654 + 6.0 * 0.7978845608028654 * 0.044715 * square
                )
            part = dot(hidden[spot, :, lanes], wdown_scr[lanes, :])
            branch = part if branch is None else branch + part
        save(6, order).start()
        loss_arrive(order)
        loss_load(order).start()
        outs = [branch[rows] + bias_rows[15:16] for rows in row_blocks()]
        for rows, out, (_, state_two, _, _) in zip(row_blocks(), outs, kept):
            span = pl.ds(rows.start // CHUNK_CELLS, STEP // CHUNK_CELLS)
            layer = bf16(state_two + piece(8) * out)
            layer_scr[span] = layer.reshape(STEP // CHUNK_CELLS, CHUNK_CELLS, D)
        layer_save(order).start()
        chunk = chunk_of(order, rank)
        first_cell = chunk * CELL_PART + share_of(chunk, rank) * CHUNK_CELLS
        mask = jnp.where(first_cell + cell < count, tasks, 0)
        loss_load(order).wait()
        mask = f32(mask)

        def seed_rows(rows):
            span = pl.ds(rows.start // CHUNK_CELLS, STEP // CHUNK_CELLS)
            return f32(loss_scr[span]).reshape(STEP, D) * mask[rows]

        def add_all(row, parts):
            add(row, column_sum(sum(parts[1:], parts[0])))

        gates, biased = [], []
        for rows, out in zip(row_blocks(), outs):
            seed = seed_rows(rows)
            gates.append(fold(seed * out))
            low = bf16(piece(8) * seed)
            grad_branch[spot, rows] = low
            biased.append(fold(f32(low)))
        add_all(8, gates)
        add_all(13, biased)
        save(7, order).start()
        for block in range(FF // D):
            lanes = pl.ds(block * D, D)
            back = dot_nt(grad_branch[spot], wdown_scr[lanes, :])
            biased = []
            for rows in row_blocks():
                low = bf16(back[rows] * slopes[rows, lanes])
                grad_lifted[spot, rows, lanes] = low
                biased.append(fold(f32(low)))
            add_all(9 + block, biased)
        grad_act = dot_nt(grad_lifted[spot], wup_scr[...])
        save(5, order).start()
        layer_save(order).wait()
        send_layer(order)

        @pl.when(order < CHUNKS - 1)
        def _():
            cells_arrive(order + 1)
            state_load(order + 1).start()


        @pl.when(order == CHUNKS - 1)
        def _():
            for which in (6, 7):
                save(which, CHUNKS - 2).wait()
                save(which, CHUNKS - 1).wait()
            load_ahead()

        parts = [[], [], [], []]
        for rows, (back, _, normed, inverse) in zip(row_blocks(), kept):
            grads = grad_act[rows]
            parts[0].append(fold(grads))
            parts[1].append(fold(grads * normed))
            state_grads = seed_rows(rows) + standard_back(normed, inverse, grads * (1.0 + piece(7)))
            grad_state[spot, rows] = state_grads
            parts[2].append(fold(state_grads * back))
            low = bf16(piece(5) * state_grads)
            grad_temporal[spot, rows] = low
            parts[3].append(fold(f32(low)))
        for row, part in zip((6, 7, 5, 14), parts):
            add_all(row, part)
        save(8, order).start()
        save(3, order).start()
        return carry

    cells_arrive(0)
    state_load(0).start()
    lax.fori_loop(0, CHUNKS, chunk_step, 0)
    for order in (CHUNKS - 2, CHUNKS - 1):
        for which in (0, 1, 2, 3, 4, 5, 8, 9):
            save(which, order).wait()


UNITS = 16
ROWS = D // RANKS
HALF_ROWS = ROWS // 2
KINDS = "SSSSSPSPPPMPPMPP"
SCHEDULE = (
    ("double", 0), (0, 0), (0, 1), ("chunk", 0), (1, 0), ("double", 1), (0, 2), (0, 3), (1, 1), ("chunk", 1),
    (1, 2), (1, 3), (2, 0), ("chunk", 2), (2, 1), ("unit", 4), (0, 4), ("chunk", 3), (1, 4), (2, 2), (3, 0),
    ("unit", 5), (0, 5), ("unit", 6), (0, 6), (2, 3), (3, 1), (1, 5), (4, 0), ("first", 0), (1, 6), ("unit", 7),
    (0, 7), (2, 4), (3, 2), (4, 1), (5, 0), ("second", 0), (1, 7), (3, 3), ("first", 1), (2, 6), (4, 2), (5, 1),
    (6, 0), (2, 5), ("second", 1), (3, 4), ("unit", 8), (0, 8), ("unit", 9), (0, 9), (4, 3), (6, 1), (7, 0),
    ("first", 2), (1, 8), (2, 7), (1, 9), (3, 5), (3, 6), (5, 2), ("second", 2), ("unit", 10), (0, 10), (4, 4),
    (7, 1), ("first", 3), (2, 8), (3, 7), (4, 5), (5, 3), (6, 2), (1, 10), (4, 6), ("second", 3), ("unit", 11),
    (0, 11), (2, 9), (3, 8), (6, 3), ("unit", 12), (0, 12), ("sums", 0), (7, 2), ("unit", 13), (0, 13), (1, 11),
    (2, 10), (4, 7), (5, 4), (1, 12), ("sums", 1), (5, 5), ("unit", 14), (0, 14), (1, 13), (3, 9), (5, 6),
    ("unit", 15), (0, 15), (4, 8), (6, 4), (7, 3), (1, 14), (2, 11), (6, 5), (1, 15), (3, 10), (6, 6), (7, 4),
    (2, 12), (4, 9), (5, 7), (3, 11), (7, 5), (6, 7), (2, 13), (4, 11), (7, 6), (5, 8), (3, 12), (4, 10), (2, 14),
    (6, 8), (7, 7), (3, 13), (5, 9), (5, 10), (4, 12), (5, 11), (2, 15), (6, 9), (3, 14), (4, 13), (7, 8), (6, 10),
    (4, 14), (6, 11), (3, 15), (5, 12), (7, 10), (7, 9), (5, 14), (4, 15), (6, 12), (5, 13), (6, 14), (7, 11),
    (5, 15), (7, 12), (6, 13), (6, 15), (7, 14), (7, 13), (7, 15),
)


def tail_body(
    qkv,
    mixed,
    probs,
    state_cells,
    act_two,
    qkv_two,
    mixed_two,
    grad_temporal,
    act_three,
    grad_lifted,
    hidden,
    grad_branch,
    grad_state_two,
    probs_two,
    modulation,
    biases,
    w_qkv_t,
    w_out_t,
    w_qkv,
    w_out,
    grad_home,
    totals,
    gathered,
    x_scr,
    state_scr,
    sums,
    sums_in_scr,
    core_in,
    first_in,
    second_in,
    edge_in,
    middle_in,
    left_scr,
    right_scr,
    qkv_scr,
    mixed_scr,
    spatial_scr,
    time_scr,
    wqkv_scr,
    wout_scr,
    grad_mixed,
    chunk_state,
    chunk_grad,
    chunk_temporal,
    probs_scr,
    own,
    first_out,
    kept,
    load_sem,
    frame_sem,
    probs_sem,
    side_sem,
    chunk_sem,
    cell_send,
    cell_recv,
    home_send,
    home_recv,
    unit_send,
    unit_recv,
    sum_send,
    sum_recv,
):
    slot = lax.axis_index("dp")
    rank = lax.axis_index("seq")
    core = lax.rem(rank, 2)
    over_x = rank // 2
    over_y = lax.rem(slot, 2)
    over_z = slot // 2
    at_edge = jnp.logical_or(over_z == 0, over_z == 3)
    low_side = over_z < 2
    core_peer = (slot, rank + 1 - 2 * core)
    x_peer = (slot, lax.rem(rank + 2, RANKS))
    y_peer = (slot + 1 - 2 * over_y, rank)
    inner_peer = (jnp.where(low_side, 2, 4) + over_y, rank)
    middle_peer = (jnp.where(low_side, 4, 2) + over_y, rank)
    outer_peer = (jnp.where(low_side, 0, 6) + over_y, rank)

    def piece(index):
        return modulation[index : index + 1]

    def remote(source, target, send, recv, peer):
        return pltpu.make_async_remote_copy(
            src_ref=source, dst_ref=target, send_sem=send, recv_sem=recv, device_id=peer, device_id_type=MESH
        )


    turned = over_z // 2

    def spots(unit):
        mine = {"P": over_y, "S": over_x, "M": turned}[KINDS[unit]]
        return mine, 1 - mine

    def half_rows(which):
        return pl.ds(pl.multiple_of(which * HALF_ROWS, HALF_ROWS), HALF_ROWS)

    def send(kind, unit, source, target, peer, landing=None):
        landing = kind if landing is None else landing
        return remote(source, target, unit_send.at[kind, unit], unit_recv.at[landing, unit], peer)

    def core_copy(unit):
        return send(0, unit, own.at[unit % 4, 1 - core], core_in.at[unit % 6], core_peer)

    def first_copy(unit):
        peer = y_peer if KINDS[unit] == "S" else x_peer
        return send(1, unit, first_out.at[unit % 8], first_in.at[unit % 10], peer)

    def second_copy(unit):
        mine, other = spots(unit)
        if KINDS[unit] == "M":
            return send(2, unit, kept.at[unit, mine], second_in.at[unit % 10], y_peer)
        peer = x_peer if KINDS[unit] == "S" else y_peer
        return send(2, unit, kept.at[unit, other], second_in.at[unit % 10], peer)

    def edge_copy(unit):
        if KINDS[unit] == "M":
            return send(3, unit, kept.at[unit], edge_in.at[unit % 8], inner_peer)
        mine, _ = spots(unit)
        return send(3, unit, kept.at[unit, mine], edge_in.at[unit % 8, 0], inner_peer)

    def middle_copy(unit):
        mine, other = spots(unit)
        source = kept.at[unit, other if KINDS[unit] == "M" else mine]
        return send(4, unit, source, middle_in.at[unit % 10], middle_peer)

    def outer_copy(unit):
        _, other = spots(unit)
        return send(5, unit, kept.at[unit, other], middle_in.at[unit % 10], outer_peer, 4)

    def share_copy(unit, source):
        return send(6, unit, source, totals.at[unit, half_rows(over_y)], y_peer)

    def keep_copy(unit, source, which):
        return pltpu.make_async_copy(source, totals.at[unit, half_rows(which)], unit_send.at[7, unit])

    def cross_copy(unit):
        mine, other = spots(unit)
        return send(6, unit, kept.at[unit, other], totals.at[unit, half_rows(mine)], middle_peer)

    def near_copy(unit):
        mine, other = spots(unit)
        return send(5, unit, kept.at[unit, other], totals.at[unit, half_rows(mine)], outer_peer)

    def far_copy(unit):
        _, other = spots(unit)
        place = totals.at[unit, half_rows(other)]
        return send(8, unit, place, place, outer_peer)

    def plus(left, right):
        return bf16(f32(left) + f32(right))

    def stage_one(unit):
        core_copy(unit).wait()
        held, came = own.at[unit % 4, core], core_in.at[unit % 6]
        if KINDS[unit] == "S":
            for part in range(2):
                first_out[unit % 8, part] = plus(held[part, 1 - over_y], came[part, 1 - over_y])
            first_copy(unit).start()
            for part in range(2):
                kept[unit, part] = plus(held[part, over_y], came[part, over_y])
        else:
            first_out[unit % 8] = plus(held[1 - over_x], came[1 - over_x])
            first_copy(unit).start()
            kept[unit] = plus(held[over_x], came[over_x])

    def stage_two(unit):
        first_copy(unit).wait()
        mine, other = spots(unit)
        if KINDS[unit] == "M":
            kept[unit] = plus(kept[unit], first_in[unit % 10])

            @pl.when(at_edge)
            def _():
                edge_copy(unit).start()

        else:
            kept[unit, other] = plus(kept[unit, other], first_in[unit % 10, other])
            second_copy(unit).start()
            kept[unit, mine] = plus(kept[unit, mine], first_in[unit % 10, mine])

    def stage_three(unit):
        mine, _ = spots(unit)
        if KINDS[unit] == "M":

            @pl.when(jnp.logical_not(at_edge))
            def _():
                edge_copy(unit).wait_recv()
                kept[unit] = plus(kept[unit], edge_in[unit % 8])
                middle_copy(unit).start()

        else:
            second_copy(unit).wait()
            kept[unit, mine] = plus(kept[unit, mine], second_in[unit % 10])

            @pl.when(at_edge)
            def _():
                edge_copy(unit).start()

    def stage_four(unit):
        mine, _ = spots(unit)

        @pl.when(jnp.logical_not(at_edge))
        def _():
            if KINDS[unit] == "M":
                middle_copy(unit).wait()
                kept[unit, mine] = plus(kept[unit, mine], middle_in[unit % 10])
                second_copy(unit).start()
            else:
                edge_copy(unit).wait_recv()
                kept[unit, mine] = plus(kept[unit, mine], edge_in[unit % 8, 0])
                middle_copy(unit).start()

    def stage_five(unit):
        mine, other = spots(unit)

        @pl.when(jnp.logical_not(at_edge))
        def _():
            if KINDS[unit] == "M":
                second_copy(unit).wait()
                kept[unit, other] = plus(kept[unit, mine], second_in[unit % 10])
                cross_copy(unit).start()
                near_copy(unit).start()
                keep_copy(unit, kept.at[unit, other], mine).start()
            else:
                middle_copy(unit).wait()
                kept[unit, other] = plus(kept[unit, mine], middle_in[unit % 10])
                share_copy(unit, kept.at[unit, other]).start()
                outer_copy(unit).start()
                keep_copy(unit, kept.at[unit, other], over_y).start()

    def stage_six(unit):
        if KINDS[unit] == "M":

            @pl.when(jnp.logical_not(at_edge))
            def _():
                cross_copy(unit).wait_recv()
                far_copy(unit).start()

        else:

            @pl.when(at_edge)
            def _():
                outer_copy(unit).wait_recv()
                share_copy(unit, middle_in.at[unit % 10]).start()
                keep_copy(unit, middle_in.at[unit % 10], over_y).start()

    def stage_seven(unit):
        mine, other = spots(unit)
        source = kept.at[unit, other]
        if KINDS[unit] == "M":

            @pl.when(at_edge)
            def _():
                edge_copy(unit).wait_send()
                near_copy(unit).wait_recv()
                far_copy(unit).wait_recv()

            @pl.when(jnp.logical_not(at_edge))
            def _():
                cross_copy(unit).wait_send()
                near_copy(unit).wait_send()
                far_copy(unit).wait_send()
                keep_copy(unit, source, mine).wait()

        else:

            @pl.when(at_edge)
            def _():
                edge_copy(unit).wait_send()

            @pl.when(jnp.logical_not(at_edge))
            def _():
                outer_copy(unit).wait_send()

            share_copy(unit, source).wait()
            keep_copy(unit, source, over_y).wait()

    stages = (
        lambda unit: core_copy(unit).start(),
        stage_one,
        stage_two,
        stage_three,
        stage_four,
        stage_five,
        stage_six,
        stage_seven,
    )


    def put_quarter(unit, quarter, rows):
        own[unit % 4, quarter % 2, quarter // 2] = bf16(rows).reshape(2, HALF_ROWS, D)

    def put_unit(unit, block):
        for quarter in range(RANKS):
            put_quarter(unit, quarter, block[quarter * ROWS : (quarter + 1) * ROWS])

    def flat(block):
        return block.reshape(CHUNKS * TOKENS, block.shape[-1])

    def unit_loads(unit):
        if unit < 8:
            left, right, column = act_three, grad_lifted, unit - 4
        elif unit < 11:
            left, right, column = act_two, time_scr, unit - 8
        else:
            left, right, column = mixed_two, grad_temporal, 0
        return (
            pltpu.make_async_copy(left, left_scr.at[unit % 2], load_sem.at[0, unit % 2]),
            pltpu.make_async_copy(
                right.at[:, :, pl.ds(column * D, D)], right_scr.at[unit % 2], load_sem.at[1, unit % 2]
            ),
        )

    def make_unit(unit):
        if unit < 12:
            for load in unit_loads(unit):
                load.wait()
            left, right = left_scr[unit % 2], right_scr[unit % 2]
        elif unit < 15:
            left, right = x_scr[...], qkv_scr[:, :, pl.ds((unit - 12) * D, D)]
        else:
            left, right = mixed_scr[...], spatial_scr[...]
        put_unit(unit, dot_tn(flat(left), flat(right)))
        if 4 <= unit < 10:
            for load in unit_loads(unit + 2):
                load.start()

    def hidden_load(block):
        spot = block % 2
        lanes = pl.ds(block % RANKS * D, D)
        return pltpu.make_async_copy(hidden.at[:, :, lanes], right_scr.at[spot], load_sem.at[1, spot])

    def double_unit(double):
        for block in range(RANKS):
            hidden_load(block).wait()
            left = left_scr[0, :, :, pl.ds(double * 2 * ROWS, 2 * ROWS)]
            columns = dot_tn(flat(left), flat(right_scr[block % 2]))
            if block + 2 < RANKS or double == 0:
                hidden_load(block + 2).start()
            for part in range(2):
                put_quarter(2 * double + part, block, columns[part * ROWS : (part + 1) * ROWS])
        if double == 1:
            for unit in (4, 5):
                for load in unit_loads(unit):
                    load.start()


    def chunk_loads(order):
        spot = order % 2
        return (
            pltpu.make_async_copy(state_cells.at[order], chunk_state.at[spot], chunk_sem.at[0, spot]),
            pltpu.make_async_copy(grad_state_two.at[order], chunk_grad.at[spot], chunk_sem.at[1, spot]),
            pltpu.make_async_copy(grad_temporal.at[order], chunk_temporal.at[spot], chunk_sem.at[2, spot]),
            pltpu.make_async_copy(qkv_two.at[order], time_scr.at[order], chunk_sem.at[3, spot]),
        )

    def cell_place(order, frame):
        return state_scr.at[frame, chunk_cells(order, rank)]

    def cell_rows(order, target, frame):
        start = (target * FRAME_PART + frame) * CHUNK_CELLS
        return spatial_scr.at[order, pl.ds(pl.multiple_of(start, CHUNK_CELLS), CHUNK_CELLS)]

    def cell_copy(order, hop, frame):
        target = lax.rem(rank + hop, RANKS)
        return remote(
            cell_rows(order, target, frame),
            cell_place(order, frame),
            cell_send.at[order, hop, frame],
            cell_recv.at[order, hop, frame],
            (slot, target),
        )

    def cell_keep(order, frame):
        return pltpu.make_async_copy(
            cell_rows(order, rank, frame), cell_place(order, frame), cell_recv.at[order, 0, frame]
        )

    def probs_load(step):
        source = probs_two.at[step] if step < CHUNKS else probs.at[step - CHUNKS]
        return pltpu.make_async_copy(source, probs_scr, probs_sem.at[0])

    def probs_next(step):
        if step < CHUNKS + FRAME_PART:
            probs_load(step).start()

    def time_backward(order):
        spot = order % 2
        for load in chunk_loads(order):
            load.wait()
        probs_load(order).wait()
        if order < CHUNKS - 1:
            for load in chunk_loads(order + 1):
                load.start()

        grad_mixed[...] = bf16(dot_nt(chunk_temporal[spot], wout_scr[...]))
        heads_backward(time_scr.at[order], grad_mixed, probs_scr, range(HEADS // 2))
        probs_next(order + 1)
        grad_act = dot_nt(time_scr[order], wqkv_scr[...])
        normed, inverse = standardise(f32(chunk_state[spot]).reshape(TOKENS, D))
        add(3, column_sum(grad_act))
        add(4, column_sum(grad_act * normed))
        spatial_scr[order] = bf16(
            chunk_grad[spot] + standard_back(normed, inverse, grad_act * (1.0 + piece(4)))
        )
        for frame in range(FRAME_PART):
            for hop in range(1, RANKS):
                cell_copy(order, hop, frame).start()
            cell_keep(order, frame).start()


    def add(row, value):
        sums[pl.ds(row, 1)] += value

    def frame_loads(frame):
        return (
            pltpu.make_async_copy(qkv.at[frame], qkv_scr.at[frame], frame_sem.at[0, frame]),
            pltpu.make_async_copy(mixed.at[frame], mixed_scr.at[frame], frame_sem.at[1, frame]),
        )

    def home_copy(frame, hop):
        peer = lax.rem(slot + hop, CLIPS)
        rows = pl.ds(pl.multiple_of(peer * CELL_HOME, CELL_HOME), CELL_HOME)
        return remote(
            state_scr.at[frame, rows],
            grad_home.at[slot, frame],
            home_send.at[frame, hop],
            home_recv.at[frame, hop],
            (peer, rank),
        )

    def home_keep(frame):
        rows = pl.ds(pl.multiple_of(slot * CELL_HOME, CELL_HOME), CELL_HOME)
        return pltpu.make_async_copy(state_scr.at[frame, rows], grad_home.at[slot, frame], home_recv.at[frame, 0])

    def frame_first(frame):
        for load in frame_loads(frame):
            load.wait()
        for order in range(CHUNKS):
            for hop in range(1, RANKS):
                cell_copy(order, hop, frame).wait_recv()
        grad_state = f32(state_scr[frame])
        spatial = dot(mixed_scr[frame], wout_scr[...]) + bias_rows[9:10]
        add(2, column_sum(grad_state * spatial))
        low_spatial = bf16(piece(2) * grad_state)
        spatial_scr[frame] = low_spatial
        add(15, column_sum(f32(low_spatial)))
        grad_mixed[...] = bf16(dot_nt(low_spatial, wout_scr[...]))
        probs_load(CHUNKS + frame).wait()
        heads_backward(qkv_scr.at[frame], grad_mixed, probs_scr, range(HEADS // 4))

    def frame_second(frame):
        heads_backward(qkv_scr.at[frame], grad_mixed, probs_scr, range(HEADS // 4, HEADS // 2))
        probs_next(CHUNKS + frame + 1)
        grad_act = dot_nt(qkv_scr[frame], wqkv_scr[...])
        normed, inverse = standardise(f32(x_scr[frame]))
        x_scr[frame] = bf16(normed * (1.0 + piece(1)) + piece(0))
        add(0, column_sum(grad_act))
        add(1, column_sum(grad_act * normed))
        state_scr[frame] = bf16(
            f32(state_scr[frame]) + standard_back(normed, inverse, grad_act * (1.0 + piece(1)))
        )
        for hop in range(1, CLIPS):
            home_copy(frame, hop).start()
        home_keep(frame).start()


    def sum_exchange(step):
        peer = core_peer if step == 0 else x_peer
        return remote(sums, sums_in_scr.at[step], sum_send.at[step], sum_recv.at[step], peer)

    def sum_add(step):
        sum_exchange(step).wait()
        sums[...] = sums[...] + sums_in_scr[step]

    def sum_spread(hop):
        peer = lax.rem(slot + hop, CLIPS)
        return remote(sums, gathered.at[slot], sum_send.at[1 + hop], sum_recv.at[1 + hop], (peer, rank))

    def sum_keep():
        return pltpu.make_async_copy(sums, gathered.at[slot], sum_send.at[9])


    time_weights = (
        pltpu.make_async_copy(w_qkv_t, wqkv_scr, side_sem.at[0]),
        pltpu.make_async_copy(w_out_t, wout_scr, side_sem.at[1]),
    )
    space_weights = (
        pltpu.make_async_copy(w_qkv, wqkv_scr, side_sem.at[0]),
        pltpu.make_async_copy(w_out, wout_scr, side_sem.at[1]),
    )
    branch_load = pltpu.make_async_copy(grad_branch, left_scr.at[0], load_sem.at[0, 0])
    for load in chunk_loads(0):
        load.start()
    probs_load(0).start()
    for load in time_weights:
        load.start()
    bias_rows = f32(biases[...])
    branch_load.wait()

    def first_of_frames():
        for load in space_weights:
            load.start()
        for order in range(CHUNKS):
            for frame in range(FRAME_PART):
                for hop in range(1, RANKS):
                    cell_copy(order, hop, frame).wait_send()
                cell_keep(order, frame).wait()
        for load in space_weights:
            load.wait()

    for action, index in SCHEDULE:
        if action == "double":
            double_unit(index)
        elif action == "chunk":
            if index == 0:
                for load in time_weights:
                    load.wait()
            if index == 2:
                for frame in range(FRAME_PART):
                    for load in frame_loads(frame):
                        load.start()
            time_backward(index)
        elif action == "first":
            if index == 0:
                first_of_frames()
            frame_first(index)
        elif action == "second":
            frame_second(index)
            if index == FRAME_PART - 1:
                sum_exchange(0).start()
        elif action == "unit":
            make_unit(index)
        elif action == "sums":
            sum_add(index)
            if index == 0:
                sum_exchange(1).start()
            else:
                for hop in range(1, CLIPS):
                    sum_spread(hop).start()
                sum_keep().start()
        else:
            stages[action](index)

    for hop in range(1, CLIPS):
        sum_spread(hop).wait()
    sum_keep().wait()

    def frame_end(frame, carry):
        for hop in range(1, CLIPS):
            home_copy(frame, hop).wait()
        home_keep(frame).wait()
        return carry

    lax.fori_loop(0, FRAME_PART, frame_end, 0)


def block_body(
    destinations,
    cell_counts,
    frame_tasks,
    tokens,
    loss_grad,
    condition,
    biases,
    w_ada,
    w_qkv_s,
    w_out_s,
    w_qkv_t,
    w_out_t,
    w_up,
    w_down,
    layer_home,
    grad_home,
    totals,
    gathered,
    qkv_one,
    mixed_one,
    probs_one,
    state_cells,
    loss_cells,
    layer_cells,
    act_two,
    qkv_two,
    mixed_two,
    grad_temporal,
    act_three,
    grad_lifted,
    hidden,
    grad_branch,
    grad_state_two,
    probs_two,
    modulation,
    sums,
    sums_in,
    x_scr,
    state_scr,
    core_in,
    first_in,
    second_in,
    edge_in,
    middle_in,
    left_scr,
    right_scr,
    local_sem,
    ada_sem,
    in_send,
    in_recv,
    out_send,
    out_recv,
    save_one_sem,
    loss_send_sem,
    loss_recv_sem,
    weight_sem,
    stage_sem,
    save_two_sem,
    layer_send_sem,
    layer_recv_sem,
    *tail_sems,
):
    slot = lax.axis_index("dp")
    rank = lax.axis_index("seq")
    low = jnp.bfloat16
    frames = FRAME_PART * RANKS


    def loss_source(half, hop):
        return loss_grad.at[lax.rem(slot + hop, CLIPS), :, pl.ds(half * CHUNK_CELLS, CHUNK_CELLS)]

    def loss_place(order):
        return loss_cells.at[order, pl.ds(rank * FRAME_PART, FRAME_PART)]

    def loss_send(half, hop):
        target, order = loss_target(slot, half)
        return pltpu.make_async_remote_copy(
            src_ref=loss_source(half, hop),
            dst_ref=loss_place(order),
            send_sem=loss_send_sem.at[half, hop],
            recv_sem=loss_recv_sem.at[order, rank],
            device_id=(lax.rem(slot + hop, CLIPS), target),
            device_id_type=MESH,
        )

    def loss_keep(half):
        _, order = loss_target(slot, half)
        return pltpu.make_async_copy(loss_source(half, 0), loss_place(order), loss_recv_sem.at[order, rank])

    def send_loss(early):
        for half in range(2):
            target, order = loss_target(slot, half)

            @pl.when((order < 2) if early else (order >= 2))
            def _():
                @pl.when(target == rank)
                def _():
                    loss_keep(half).start()

                @pl.when(target != rank)
                def _():
                    loss_send(half, 0).start()

                for hop in range(1, CLIPS):
                    loss_send(half, hop).start()

    def loss_sent():
        for half in range(2):
            target, _ = loss_target(slot, half)

            @pl.when(target != rank)
            def _():
                loss_send(half, 0).wait_send()

            for hop in range(1, CLIPS):
                loss_send(half, hop).wait_send()

    def loss_arrive(order):
        for source in range(RANKS):
            place = loss_cells.at[order, pl.ds(source * FRAME_PART, FRAME_PART)]
            pltpu.make_async_copy(
                loss_grad.at[0, :, pl.ds(0, CHUNK_CELLS)], place, loss_recv_sem.at[order, source]
            ).wait()


    def cells_arrive(order):
        for frame in range(FRAME_PART):
            for hop in range(1, RANKS):
                place = state_cells.at[order, frame]
                pltpu.make_async_copy(place, place, out_recv.at[frame, hop, order]).wait()


    def layer_home_of(order):
        chunk = chunk_of(order, rank)
        share = share_of(chunk, rank)
        return 2 * chunk + share // 2, lax.rem(share, 2)

    def layer_copies(order, target):
        home, half = layer_home_of(order)
        source = layer_cells.at[order, pl.ds(target * FRAME_PART, FRAME_PART)]
        place = layer_home.at[slot, :, pl.ds(pl.multiple_of(half * CHUNK_CELLS, CHUNK_CELLS), CHUNK_CELLS)]
        arrival = layer_recv_sem.at[slot, half]
        local = jnp.logical_and(home == slot, rank == target)
        keep = functools.partial(pltpu.make_async_copy, source, place, arrival)
        leave = functools.partial(
            pltpu.make_async_remote_copy,
            src_ref=source,
            dst_ref=place,
            send_sem=layer_send_sem.at[order, target],
            recv_sem=arrival,
            device_id=(home, target),
            device_id_type=MESH,
        )
        return local, keep, leave

    def send_layer(order):
        for target in range(RANKS):
            local, keep, leave = layer_copies(order, target)

            @pl.when(local)
            def _():
                keep().start()

            @pl.when(jnp.logical_not(local))
            def _():
                leave().start()

    def layer_sent(order, carry):
        for target in range(RANKS):
            local, _, leave = layer_copies(order, target)

            @pl.when(jnp.logical_not(local))
            def _():
                leave().wait_send()

        return carry

    def layer_arrive():
        for clip in range(CLIPS):
            for half in range(2):
                place = layer_home.at[clip, :, pl.ds(half * CHUNK_CELLS, CHUNK_CELLS)]
                pltpu.make_async_copy(place, place, layer_recv_sem.at[clip, half]).wait()


    def load_ahead():
        load_sem = tail_sems[0]
        pltpu.make_async_copy(grad_branch, left_scr.at[0], load_sem.at[0, 0]).start()
        for block in range(2):
            lanes = pl.ds(block * D, D)
            pltpu.make_async_copy(hidden.at[:, :, lanes], right_scr.at[block], load_sem.at[1, block]).start()

    def front(wqkv_scr, wout_scr, wup_scr, wdown_scr):
        sources = (w_qkv_t, w_out_t, w_up, w_down)
        places = (wqkv_scr, wout_scr, wup_scr, wdown_scr)
        weight_loads = [
            pltpu.make_async_copy(source, place, weight_sem.at[which])
            for which, (source, place) in enumerate(zip(sources, places))
        ]

        def load_later():
            for load in weight_loads:
                load.start()

        def space(*scoped):
            space_forward_body(
                destinations,
                cell_counts,
                tokens,
                condition,
                biases,
                w_ada,
                w_qkv_s,
                w_out_s,
                qkv_one,
                mixed_one,
                probs_one,
                state_cells,
                modulation,
                x_scr,
                *scoped,
                local_sem,
                ada_sem,
                in_send,
                in_recv,
                out_send,
                out_recv,
                save_one_sem,
                load_later,
                send_loss,
            )

        pl.run_scoped(
            space,
            pltpu.VMEM((3, D, D), low),
            pltpu.VMEM((D, 3 * D), low),
            pltpu.VMEM((D, D), low),
            pltpu.VMEM((FRAME_PART, CELLS, 3 * D), low),
            pltpu.VMEM((FRAME_PART, CELLS, D), low),
            pltpu.VMEM((2, HEADS, CELLS, CELLS), low),
            pltpu.VMEM((FRAME_PART, CELLS, D), low),
        )
        send_loss(False)

        def time(*scoped):
            time_forward_body(
                cell_counts,
                frame_tasks,
                state_cells,
                loss_cells,
                layer_cells,
                modulation,
                biases,
                (
                    act_two,
                    qkv_two,
                    mixed_two,
                    grad_temporal,
                    act_three,
                    grad_lifted,
                    hidden,
                    grad_branch,
                    grad_state_two,
                    probs_two,
                ),
                sums,
                wqkv_scr,
                wout_scr,
                wup_scr,
                wdown_scr,
                *scoped,
                stage_sem,
                save_two_sem,
                weight_loads,
                cells_arrive,
                loss_arrive,
                send_layer,
                load_ahead,
            )

        pl.run_scoped(
            time,
            pltpu.VMEM((TOKENS, FF), jnp.float32),
            pltpu.VMEM((2, frames, CHUNK_CELLS, D), low),
            pltpu.VMEM((frames, CHUNK_CELLS, D), low),
            pltpu.VMEM((frames, CHUNK_CELLS, D), low),
            *[pltpu.VMEM((2, TOKENS, width), low) for width in SAVED_WIDTHS],
            pltpu.VMEM((2, TOKENS, D), jnp.float32),
            pltpu.VMEM((2, HEADS, TOKENS, TOKENS), low),
        )

    pl.run_scoped(
        front,
        pltpu.VMEM((D, 3 * D), low),
        pltpu.VMEM((D, D), low),
        pltpu.VMEM((D, FF), low),
        pltpu.VMEM((FF, D), low),
    )

    def tail(*scoped):
        tail_body(
            qkv_one,
            mixed_one,
            probs_one,
            state_cells,
            act_two,
            qkv_two,
            mixed_two,
            grad_temporal,
            act_three,
            grad_lifted,
            hidden,
            grad_branch,
            grad_state_two,
            probs_two,
            modulation,
            biases,
            w_qkv_t,
            w_out_t,
            w_qkv_s,
            w_out_s,
            grad_home,
            totals,
            gathered,
            x_scr,
            state_scr,
            sums,
            sums_in,
            core_in,
            first_in,
            second_in,
            edge_in,
            middle_in,
            left_scr,
            right_scr,
            *scoped,
            *tail_sems,
        )

    pl.run_scoped(
        tail,
        pltpu.VMEM((FRAME_PART, CELLS, 3 * D), low),
        pltpu.VMEM((FRAME_PART, CELLS, D), low),
        pltpu.VMEM((FRAME_PART, CELLS, D), low),
        pltpu.VMEM((CHUNKS, TOKENS, 3 * D), low),
        pltpu.VMEM((D, 3 * D), low),
        pltpu.VMEM((D, D), low),
        pltpu.VMEM((CELLS, D), low),
        pltpu.VMEM((2, frames, CHUNK_CELLS, D), low),
        pltpu.VMEM((2, TOKENS, D), jnp.float32),
        pltpu.VMEM((2, TOKENS, D), low),
        pltpu.VMEM((HEADS, TOKENS, TOKENS), low),
        pltpu.VMEM((4, 2, 2, 2, HALF_ROWS, D), low),
        pltpu.VMEM((8, 2, HALF_ROWS, D), low),
        pltpu.VMEM((UNITS, 2, HALF_ROWS, D), low),
    )
    loss_sent()
    lax.fori_loop(0, CHUNKS, layer_sent, 0)
    layer_arrive()


def block(destinations, cell_counts, frame_tasks, tokens, loss_grad, condition, biases, *weights):
    low = jnp.bfloat16
    frames = FRAME_PART * RANKS
    dma = pltpu.SemaphoreType.DMA

    def cells():
        return jax.ShapeDtypeStruct((CHUNKS, frames, CHUNK_CELLS, D), low)

    def home():
        return jax.ShapeDtypeStruct((CLIPS, FRAME_PART, CELL_HOME, D), low)

    def probs():
        return jax.ShapeDtypeStruct((CHUNKS, HEADS, TOKENS, TOKENS), low)

    out_shape = (
        home(),
        home(),
        jax.ShapeDtypeStruct((UNITS, ROWS, D), low),
        jax.ShapeDtypeStruct((CLIPS, 16, D), jnp.float32),
        jax.ShapeDtypeStruct((FRAME_PART, CELLS, 3 * D), low),
        jax.ShapeDtypeStruct((FRAME_PART, CELLS, D), low),
        probs(),
        cells(),
        cells(),
        cells(),
        *[jax.ShapeDtypeStruct((CHUNKS, TOKENS, width), low) for width in SAVED_WIDTHS],
        jax.ShapeDtypeStruct((CHUNKS, TOKENS, D), jnp.float32),
        probs(),
    )
    return pl.pallas_call(
        block_body,
        out_shape=out_shape,
        in_specs=[SMEM, SMEM, SMEM, ANY, ANY, VMEM, VMEM] + [ANY] * 7,
        out_specs=(ANY,) * len(out_shape),
        scratch_shapes=[
            pltpu.VMEM((16, D), jnp.float32),
            pltpu.VMEM((16, D), jnp.float32),
            pltpu.VMEM((2, 16, D), jnp.float32),
            pltpu.VMEM((FRAME_PART, CELLS, D), low),
            pltpu.VMEM((FRAME_PART, CELLS, D), low),
            pltpu.VMEM((6, 2, 2, HALF_ROWS, D), low),
            pltpu.VMEM((10, 2, HALF_ROWS, D), low),
            pltpu.VMEM((10, HALF_ROWS, D), low),
            pltpu.VMEM((8, 2, HALF_ROWS, D), low),
            pltpu.VMEM((10, HALF_ROWS, D), low),
            pltpu.VMEM((2, CHUNKS, TOKENS, D), low),
            pltpu.VMEM((2, CHUNKS, TOKENS, D), low),
            dma((4,)),
            dma((3,)),
            dma((FRAME_PART, CLIPS)),
            dma((FRAME_PART, CLIPS)),
            dma((FRAME_PART, RANKS, CHUNKS)),
            dma((FRAME_PART, RANKS, CHUNKS)),
            dma((FRAME_PART, 4)),
            dma((2, CLIPS)),
            dma((CHUNKS, RANKS)),
            dma((4,)),
            dma((3,)),
            dma((10, 2)),
            dma((CHUNKS, RANKS)),
            dma((CLIPS, 2)),
            dma((2, 2)),
            dma((2, FRAME_PART)),
            dma((1,)),
            dma((2,)),
            dma((4, 2)),
            dma((CHUNKS, RANKS, FRAME_PART)),
            dma((CHUNKS, RANKS, FRAME_PART)),
            dma((FRAME_PART, CLIPS)),
            dma((FRAME_PART, CLIPS)),
            dma((9, UNITS)),
            dma((9, UNITS)),
            dma((10,)),
            dma((9,)),
        ],
        compiler_params=pltpu.CompilerParams(
            collective_id=0, has_side_effects=True, vmem_limit_bytes=62 * 1024 * 1024
        ),
        cost_estimate=pl.CostEstimate(flops=70 * 10**9, bytes_accessed=150 * 10**6, transcendentals=10**7),
        name="block",
    )(destinations, cell_counts, frame_tasks, tokens, loss_grad, condition, biases, *weights)


def finish_body(
    destinations,
    condition,
    gathered,
    totals,
    layer_home,
    grad_home,
    layer_out,
    grad_tokens,
    grad_w_ada,
    grad_w_qkv_s,
    grad_w_out_s,
    grad_w_qkv_t,
    grad_w_out_t,
    grad_w_up,
    grad_w_down,
    sums_all,
    gathered_scr,
    home_scr,
    totals_scr,
    ada_scr,
    wide_scr,
    cond_scr,
    sem,
    ada_sem,
    wide_sem,
):
    rank = lax.axis_index("seq")
    brings = (
        pltpu.make_async_copy(layer_home, home_scr.at[0], sem.at[0]),
        pltpu.make_async_copy(grad_home, home_scr.at[1], sem.at[1]),
    )
    moves = (
        pltpu.make_async_copy(home_scr.at[0], layer_out, sem.at[0]),
        pltpu.make_async_copy(home_scr.at[1], grad_tokens, sem.at[1]),
    )
    load = pltpu.make_async_copy(totals, totals_scr, sem.at[2])
    gathered_load = pltpu.make_async_copy(gathered, gathered_scr, sem.at[3])
    gathered_load.start()
    load.start()
    for bring in brings:
        bring.start()
    clips = lax.broadcasted_iota(jnp.int32, (CLIPS, 1), 0)
    rows = f32(condition[...])
    cond = jnp.zeros((CLIPS, D), jnp.float32)
    for clip in range(CLIPS):
        row = column_sum(jnp.where(clips == destinations[clip], rows, 0.0))
        cond = jnp.where(clips == clip, row, cond)
    cond = cond / (1.0 + jnp.exp(-cond))
    for which in range(RANKS):

        @pl.when(rank == which)
        def _():
            cond_scr[...] = cond[:, which * ROWS : (which + 1) * ROWS]

    own_cond = bf16(jnp.concatenate([cond_scr[...]] * 2, axis=0))
    pieces = []
    gathered_load.wait()
    for piece in range(9):
        grads = jnp.concatenate([gathered_scr[clip, piece : piece + 1] for clip in range(CLIPS)], axis=0)
        high = bf16(grads)
        both = jnp.concatenate([f32(high), grads - f32(high)], axis=0)
        lanes = pl.ds(piece * D, D)
        ada_scr[:, lanes] = dot_tn(own_cond, bf16(both))
        pieces.append(pltpu.make_async_copy(ada_scr.at[:, lanes], grad_w_ada.at[:, lanes], ada_sem.at[piece]))
        pieces[-1].start()
    total = gathered_scr[0]
    for clip in range(1, CLIPS):
        total = total + gathered_scr[clip]
    sums_all[...] = total
    for bring, move in zip(brings, moves):
        bring.wait()
        move.start()
    load.wait()
    places = [(grad_w_up, part) for part in range(4)] + [(grad_w_qkv_t, part) for part in range(3)]
    places += [(grad_w_out_t, 0)] + [(grad_w_qkv_s, part) for part in range(3)] + [(grad_w_out_s, 0)]
    for unit, (target, part) in enumerate(places, start=4):
        wide_scr[unit - 4] = f32(totals_scr[unit])
        pieces.append(
            pltpu.make_async_copy(wide_scr.at[unit - 4], target.at[:, pl.ds(part * D, D)], wide_sem.at[unit - 4])
        )
        pieces[-1].start()
    for unit in range(4):
        spot = UNITS - 4 + unit
        lanes = pl.ds(unit * ROWS, ROWS)
        wide_scr[spot] = f32(totals_scr[unit])
    turned = jnp.concatenate([wide_scr[UNITS - 4 + unit] for unit in range(4)], axis=0).T
    for unit in range(4):
        spot = UNITS - 4 + unit
        wide_scr[spot] = turned[unit * ROWS : (unit + 1) * ROWS]
        pieces.append(
            pltpu.make_async_copy(wide_scr.at[spot], grad_w_down.at[pl.ds(unit * ROWS, ROWS)], wide_sem.at[spot])
        )
        pieces[-1].start()
    for move in moves:
        move.wait()
    for copy in pieces:
        copy.wait()


def finish(destinations, condition, gathered, totals, layer_home, grad_home):
    shapes = [(ROWS, 9 * D), (ROWS, 3 * D), (ROWS, D), (ROWS, 3 * D), (ROWS, D), (ROWS, FF), (D, D)]
    dma = pltpu.SemaphoreType.DMA
    return pl.pallas_call(
        finish_body,
        out_shape=(
            jax.ShapeDtypeStruct(layer_home.shape, layer_home.dtype),
            jax.ShapeDtypeStruct(grad_home.shape, grad_home.dtype),
            *[jax.ShapeDtypeStruct(shape, jnp.float32) for shape in shapes],
            jax.ShapeDtypeStruct((16, D), jnp.float32),
        ),
        in_specs=[SMEM, VMEM, ANY, ANY, ANY, ANY],
        out_specs=(ANY,) * 9 + (VMEM,),
        scratch_shapes=[
            pltpu.VMEM((CLIPS, 16, D), jnp.float32),
            pltpu.VMEM((2, *layer_home.shape), layer_home.dtype),
            pltpu.VMEM((UNITS, ROWS, D), jnp.bfloat16),
            pltpu.VMEM((ROWS, 9 * D), jnp.float32),
            pltpu.VMEM((UNITS, ROWS, D), jnp.float32),
            pltpu.VMEM((CLIPS, ROWS), jnp.float32),
            dma((4,)),
            dma((9,)),
            dma((UNITS,)),
        ],
        compiler_params=pltpu.CompilerParams(vmem_limit_bytes=62 * 1024 * 1024),
        cost_estimate=pl.CostEstimate(flops=10**8, bytes_accessed=30 * 10**6, transcendentals=0),
        name="finish",
    )(destinations, condition, gathered, totals, layer_home, grad_home)


def per_device_fast(
    tokens,
    condition,
    loss_grad,
    cell_counts,
    frame_tasks,
    destinations,
    w_ada,
    b_ada,
    w_qkv_s,
    w_out_s,
    b_out_s,
    w_qkv_t,
    w_out_t,
    b_out_t,
    w_up,
    b_up,
    w_down,
    b_down,
):
    rank = lax.axis_index("seq")
    parts = (b_ada, b_out_s, b_out_t, b_up, b_down)
    biases, start = 0.0, 0
    for part in parts:
        biases = biases + jnp.pad(f32(part), (start, 16 * D - start - part.shape[0]))
        start += part.shape[0]
    biases = biases.reshape(16, D)
    layer_home, grad_home, totals, gathered = block(
        destinations,
        cell_counts,
        frame_tasks,
        tokens,
        loss_grad,
        condition,
        biases,
        w_ada,
        w_qkv_s,
        w_out_s,
        w_qkv_t,
        w_out_t,
        w_up,
        w_down,
    )[:4]
    results = finish(destinations, condition, gathered, totals, layer_home, grad_home)
    layer_out, grad_tokens, grad_w_ada, grad_w_qkv_s, grad_w_out_s, grad_w_qkv_t, grad_w_out_t = results[:7]
    grad_w_up, grad_w_down, sums = results[7:]
    grad_b_ada = lax.dynamic_slice_in_dim(sums[:9].reshape(9 * D), rank * 9 * ROWS, 9 * ROWS)
    grad_b_up = lax.dynamic_index_in_dim(sums[9:13], rank, 0, keepdims=False)
    quarters = lax.dynamic_slice_in_dim(sums, rank * ROWS, ROWS, axis=1)
    return (
        layer_out,
        grad_tokens,
        grad_w_ada,
        grad_b_ada,
        grad_w_qkv_s,
        grad_w_out_s,
        quarters[15],
        grad_w_qkv_t,
        grad_w_out_t,
        quarters[14],
        grad_w_up,
        grad_b_up,
        grad_w_down,
        quarters[13],
    )


def solution(mesh):
    placed = (
        P(None, "seq", "dp", None),
        P(),
        P(None, "seq", "dp", None),
        P(),
        P(),
        P(),
        P(),
        P(),
        P(),
        P(),
        P(),
        P(),
        P(),
        P(),
        P(),
        P(),
        P(),
        P(),
    )
    fast = mesh.shape["dp"] == 8 and mesh.shape["seq"] == 4
    return jax.shard_map(
        per_device_fast if fast else per_device_general,
        mesh=mesh,
        in_specs=placed,
        out_specs=(
            P(None, "seq", "dp", None),
            P(None, "seq", "dp", None),
            P("seq", None),
            P("seq"),
            P("seq", None),
            P("seq", None),
            P("seq"),
            P("seq", None),
            P("seq", None),
            P("seq"),
            P("seq", None),
            P("seq"),
            P("seq", None),
            P("seq"),
        ),
        check_vma=False,
    )
```

```python
import functools

import jax
import jax.numpy as jnp
from jax import lax
from jax.experimental import pallas as pl
from jax.experimental.pallas import tpu as pltpu
from jax.sharding import PartitionSpec as P

D = 768
HEADS = 12
HEAD = 64


def standard(field):
    centred = field - jnp.mean(field, axis=-1, keepdims=True)
    inverse = lax.rsqrt(jnp.mean(centred * centred, axis=-1, keepdims=True) + 1e-06)
    return (centred * inverse, inverse)


def standard_back(normed, inverse, grad_normed):
    return inverse * (
        grad_normed
        - jnp.mean(grad_normed, axis=-1, keepdims=True)
        - normed * jnp.mean(grad_normed * normed, axis=-1, keepdims=True)
    )


def gelu_back(lifted, grad_hidden):
    return jax.vjp(lambda inner: jax.nn.gelu(inner, approximate=True), lifted)[1](grad_hidden)[0]


def attend(triple, key_valid, einsum_forms):
    queries = triple[:, :, 0]
    key_rows = triple[:, :, 1]
    value_rows = triple[:, :, 2]
    scores = (
        jnp.einsum(einsum_forms[0], queries, key_rows, preferred_element_type=jnp.float32) * 0.125
    )
    scores = jnp.where(key_valid, scores, -1e30)
    row_top = jnp.max(scores, axis=-1, keepdims=True)
    exponent = jnp.exp(scores - row_top)
    probs_full = exponent / jnp.sum(exponent, axis=-1, keepdims=True)
    probs_low = probs_full.astype(jnp.bfloat16)
    mixed_out = jnp.einsum(
        einsum_forms[1], probs_low, value_rows, preferred_element_type=jnp.float32
    ).astype(jnp.bfloat16)
    return (mixed_out, probs_full, probs_low)


def attend_back(triple, probs_full, probs_low, grad_mixed, einsum_forms):
    queries = triple[:, :, 0]
    key_rows = triple[:, :, 1]
    value_rows = triple[:, :, 2]
    grad_probs = jnp.einsum(
        einsum_forms[0], grad_mixed, value_rows, preferred_element_type=jnp.float32
    )
    row_delta = jnp.sum(probs_full * grad_probs, axis=-1, keepdims=True)
    grad_scores = (probs_full * (grad_probs - row_delta)).astype(jnp.bfloat16)
    grad_values = jnp.einsum(
        einsum_forms[2], probs_low, grad_mixed, preferred_element_type=jnp.float32
    )
    grad_queries = (
        jnp.einsum(einsum_forms[1], grad_scores, key_rows, preferred_element_type=jnp.float32)
        * 0.125
    )
    grad_keys = (
        jnp.einsum(einsum_forms[2], grad_scores, queries, preferred_element_type=jnp.float32)
        * 0.125
    )
    return jnp.stack([grad_queries, grad_keys, grad_values], axis=2)


def per_device_general(
    tokens,
    condition,
    loss_grad,
    cell_counts,
    frame_tasks,
    destinations,
    w_ada,
    b_ada,
    w_qkv_s,
    w_out_s,
    b_out_s,
    w_qkv_t,
    w_out_t,
    b_out_t,
    w_up,
    b_up,
    w_down,
    b_down,
):
    groups = lax.axis_size("dp")
    ranks = lax.axis_size("seq")
    own_slot = lax.axis_index("dp")
    own_rank = lax.axis_index("seq")
    frame_part = tokens.shape[1]
    cell_total = tokens.shape[2] * groups
    cell_part = cell_total // ranks
    frame_total = frame_part * ranks
    slot_ids = jnp.arange(groups, dtype=jnp.int32)
    routing = (destinations[None, :] == slot_ids[:, None]).astype(jnp.bfloat16)
    outgoing = jnp.einsum(
        "jc,cfbd->jfbd", routing, tokens, preferred_element_type=jnp.float32
    ).astype(jnp.bfloat16)
    outgoing_grad = jnp.einsum(
        "jc,cfbd->jfbd", routing, loss_grad, preferred_element_type=jnp.float32
    ).astype(jnp.bfloat16)
    arrived, arrived_grad = (
        lax.all_to_all(outgoing, "dp", split_axis=0, concat_axis=2, tiled=True),
        lax.all_to_all(outgoing_grad, "dp", split_axis=0, concat_axis=2, tiled=True),
    )
    own_clip = jnp.sum(jnp.where(destinations == own_slot, slot_ids, 0))
    own_count = jnp.sum(jnp.where(slot_ids == own_clip, cell_counts, 0))
    own_tasks = lax.dynamic_index_in_dim(frame_tasks, own_clip, 0, keepdims=False)
    cond_row = lax.dynamic_index_in_dim(condition, own_slot, 0, keepdims=False)
    cond_low = jax.nn.silu(cond_row.astype(jnp.float32)).astype(jnp.bfloat16)
    modulation = jnp.dot(cond_low[None, :], w_ada, preferred_element_type=jnp.float32)[
        0
    ] + b_ada.astype(jnp.float32)
    pieces = [modulation[piece_index * D : (piece_index + 1) * D] for piece_index in range(9)]
    (
        shift_one,
        scale_one,
        gate_one,
        shift_two,
        scale_two,
        gate_two,
        shift_three,
        scale_three,
        gate_three,
    ) = pieces
    space_forms = ("fphe,fqhe->fhpq", "fhpq,fqhe->fphe", "fhpq,fphe->fqhe")
    frames_in = arrived[0].astype(jnp.float32)
    normed_one, inverse_one = standard(frames_in)
    act_one = (normed_one * (1.0 + scale_one) + shift_one).astype(jnp.bfloat16)
    triple_one = (
        jnp.einsum("fpd,de->fpe", act_one, w_qkv_s, preferred_element_type=jnp.float32)
        .astype(jnp.bfloat16)
        .reshape(frame_part, cell_total, 3, HEADS, HEAD)
    )
    key_valid = (jnp.arange(cell_total, dtype=jnp.int32) < own_count)[None, None, None, :]
    mixed_one, probs_one, low_one = attend(triple_one, key_valid, space_forms)
    flat_one = mixed_one.reshape(frame_part, cell_total, D)
    spatial_out = jnp.einsum(
        "fpd,de->fpe", flat_one, w_out_s, preferred_element_type=jnp.float32
    ) + b_out_s.astype(jnp.float32)
    state_one = (frames_in + gate_one * spatial_out).astype(jnp.bfloat16)
    cells_in, cells_grad = (
        lax.all_to_all(state_one, "seq", split_axis=1, concat_axis=0, tiled=True),
        lax.all_to_all(arrived_grad[0], "seq", split_axis=1, concat_axis=0, tiled=True),
    )
    time_forms = ("fqhe,gqhe->qhfg", "qhfg,gqhe->fqhe", "qhfg,fqhe->gqhe")
    state_cells = cells_in.astype(jnp.float32)
    normed_two, inverse_two = standard(state_cells)
    act_two = (normed_two * (1.0 + scale_two) + shift_two).astype(jnp.bfloat16)
    triple_two = (
        jnp.einsum("fqd,de->fqe", act_two, w_qkv_t, preferred_element_type=jnp.float32)
        .astype(jnp.bfloat16)
        .reshape(frame_total, cell_part, 3, HEADS, HEAD)
    )
    mixed_two, probs_two, low_two = attend(triple_two, True, time_forms)
    flat_two = mixed_two.reshape(frame_total, cell_part, D)
    temporal_out = jnp.einsum(
        "fqd,de->fqe", flat_two, w_out_t, preferred_element_type=jnp.float32
    ) + b_out_t.astype(jnp.float32)
    state_two = state_cells + gate_two * temporal_out
    normed_three, inverse_three = standard(state_two)
    act_three = (normed_three * (1.0 + scale_three) + shift_three).astype(jnp.bfloat16)
    lifted = jnp.einsum(
        "fqd,dk->fqk", act_three, w_up, preferred_element_type=jnp.float32
    ) + b_up.astype(jnp.float32)
    hidden = jax.nn.gelu(lifted, approximate=True).astype(jnp.bfloat16)
    branch_out = jnp.einsum(
        "fqk,kd->fqd", hidden, w_down, preferred_element_type=jnp.float32
    ) + b_down.astype(jnp.float32)
    result = (state_two + gate_three * branch_out).astype(jnp.bfloat16)
    cell_ids = own_rank * cell_part + jnp.arange(cell_part, dtype=jnp.int32)
    loss_mask = jnp.logical_and(own_tasks[:, None] == 1, cell_ids[None, :] < own_count)
    out_grad = cells_grad.astype(jnp.float32) * loss_mask[:, :, None].astype(jnp.float32)
    grad_gate_three = jnp.sum(out_grad * branch_out, axis=(0, 1))
    grad_branch = (gate_three * out_grad).astype(jnp.bfloat16)
    grad_b_down = jnp.sum(grad_branch.astype(jnp.float32), axis=(0, 1))
    grad_w_down = jnp.einsum("fqk,fqd->kd", hidden, grad_branch, preferred_element_type=jnp.float32)
    grad_hidden = jnp.einsum("fqd,kd->fqk", grad_branch, w_down, preferred_element_type=jnp.float32)
    grad_lifted = gelu_back(lifted, grad_hidden).astype(jnp.bfloat16)
    grad_b_up = jnp.sum(grad_lifted.astype(jnp.float32), axis=(0, 1))
    grad_w_up = jnp.einsum(
        "fqd,fqk->dk", act_three, grad_lifted, preferred_element_type=jnp.float32
    )
    grad_act_three = jnp.einsum(
        "fqk,dk->fqd", grad_lifted, w_up, preferred_element_type=jnp.float32
    )
    grad_shift_three = jnp.sum(grad_act_three, axis=(0, 1))
    grad_scale_three = jnp.sum(grad_act_three * normed_three, axis=(0, 1))
    grad_state_two = out_grad + standard_back(
        normed_three, inverse_three, grad_act_three * (1.0 + scale_three)
    )
    grad_gate_two = jnp.sum(grad_state_two * temporal_out, axis=(0, 1))
    grad_temporal = (gate_two * grad_state_two).astype(jnp.bfloat16)
    grad_b_out_t = jnp.sum(grad_temporal.astype(jnp.float32), axis=(0, 1))
    grad_w_out_t = jnp.einsum(
        "fqd,fqe->de", flat_two, grad_temporal, preferred_element_type=jnp.float32
    )
    grad_mixed_two = (
        jnp.einsum("fqe,de->fqd", grad_temporal, w_out_t, preferred_element_type=jnp.float32)
        .astype(jnp.bfloat16)
        .reshape(frame_total, cell_part, HEADS, HEAD)
    )
    grad_triple_two = (
        attend_back(triple_two, probs_two, low_two, grad_mixed_two, time_forms)
        .reshape(frame_total, cell_part, 3 * D)
        .astype(jnp.bfloat16)
    )
    grad_w_qkv_t = jnp.einsum(
        "fqd,fqe->de", act_two, grad_triple_two, preferred_element_type=jnp.float32
    )
    grad_act_two = jnp.einsum(
        "fqe,de->fqd", grad_triple_two, w_qkv_t, preferred_element_type=jnp.float32
    )
    grad_shift_two = jnp.sum(grad_act_two, axis=(0, 1))
    grad_scale_two = jnp.sum(grad_act_two * normed_two, axis=(0, 1))
    grad_state_one = (
        grad_state_two + standard_back(normed_two, inverse_two, grad_act_two * (1.0 + scale_two))
    ).astype(jnp.bfloat16)
    frames_out, frames_grad = (
        lax.all_to_all(result, "seq", split_axis=0, concat_axis=1, tiled=True),
        lax.all_to_all(grad_state_one, "seq", split_axis=0, concat_axis=1, tiled=True),
    )
    grad_frames = frames_grad.astype(jnp.float32)
    grad_gate_one = jnp.sum(grad_frames * spatial_out, axis=(0, 1))
    grad_spatial = (gate_one * grad_frames).astype(jnp.bfloat16)
    grad_b_out_s = jnp.sum(grad_spatial.astype(jnp.float32), axis=(0, 1))
    grad_w_out_s = jnp.einsum(
        "fpd,fpe->de", flat_one, grad_spatial, preferred_element_type=jnp.float32
    )
    grad_mixed_one = (
        jnp.einsum("fpe,de->fpd", grad_spatial, w_out_s, preferred_element_type=jnp.float32)
        .astype(jnp.bfloat16)
        .reshape(frame_part, cell_total, HEADS, HEAD)
    )
    grad_triple_one = (
        attend_back(triple_one, probs_one, low_one, grad_mixed_one, space_forms)
        .reshape(frame_part, cell_total, 3 * D)
        .astype(jnp.bfloat16)
    )
    grad_w_qkv_s = jnp.einsum(
        "fpd,fpe->de", act_one, grad_triple_one, preferred_element_type=jnp.float32
    )
    grad_act_one = jnp.einsum(
        "fpe,de->fpd", grad_triple_one, w_qkv_s, preferred_element_type=jnp.float32
    )
    grad_shift_one = jnp.sum(grad_act_one, axis=(0, 1))
    grad_scale_one = jnp.sum(grad_act_one * normed_one, axis=(0, 1))
    grad_input = (
        grad_frames + standard_back(normed_one, inverse_one, grad_act_one * (1.0 + scale_one))
    ).astype(jnp.bfloat16)
    home_out, home_grad = (
        lax.all_to_all(frames_out[None], "dp", split_axis=2, concat_axis=0, tiled=True),
        lax.all_to_all(grad_input[None], "dp", split_axis=2, concat_axis=0, tiled=True),
    )
    layer_out = jnp.einsum(
        "jc,jfbd->cfbd", routing, home_out, preferred_element_type=jnp.float32
    ).astype(jnp.bfloat16)
    grad_tokens = jnp.einsum(
        "jc,jfbd->cfbd", routing, home_grad, preferred_element_type=jnp.float32
    ).astype(jnp.bfloat16)
    grad_mod = jnp.concatenate(
        [
            grad_shift_one,
            grad_scale_one,
            grad_gate_one,
            grad_shift_two,
            grad_scale_two,
            grad_gate_two,
            grad_shift_three,
            grad_scale_three,
            grad_gate_three,
        ]
    )
    ada_term = cond_low.astype(jnp.float32)[:, None] * grad_mod[None, :]
    partials = (
        lax.psum_scatter(
            ada_term.astype(jnp.bfloat16), "seq", scatter_dimension=0, tiled=True
        ).astype(jnp.float32),
        lax.psum_scatter(
            grad_mod.astype(jnp.bfloat16), "seq", scatter_dimension=0, tiled=True
        ).astype(jnp.float32),
        lax.psum_scatter(
            grad_w_qkv_s.astype(jnp.bfloat16), "seq", scatter_dimension=0, tiled=True
        ).astype(jnp.float32),
        lax.psum_scatter(
            grad_w_out_s.astype(jnp.bfloat16), "seq", scatter_dimension=0, tiled=True
        ).astype(jnp.float32),
        lax.psum_scatter(
            grad_b_out_s.astype(jnp.bfloat16), "seq", scatter_dimension=0, tiled=True
        ).astype(jnp.float32),
        lax.psum_scatter(
            grad_w_qkv_t.astype(jnp.bfloat16), "seq", scatter_dimension=0, tiled=True
        ).astype(jnp.float32),
        lax.psum_scatter(
            grad_w_out_t.astype(jnp.bfloat16), "seq", scatter_dimension=0, tiled=True
        ).astype(jnp.float32),
        lax.psum_scatter(
            grad_b_out_t.astype(jnp.bfloat16), "seq", scatter_dimension=0, tiled=True
        ).astype(jnp.float32),
        lax.psum_scatter(
            grad_w_up.astype(jnp.bfloat16), "seq", scatter_dimension=0, tiled=True
        ).astype(jnp.float32),
        lax.psum_scatter(
            grad_b_up.astype(jnp.bfloat16), "seq", scatter_dimension=0, tiled=True
        ).astype(jnp.float32),
        lax.psum_scatter(
            grad_w_down.astype(jnp.bfloat16), "seq", scatter_dimension=0, tiled=True
        ).astype(jnp.float32),
        lax.psum_scatter(
            grad_b_down.astype(jnp.bfloat16), "seq", scatter_dimension=0, tiled=True
        ).astype(jnp.float32),
    )
    totals = lax.psum(
        (
            partials[0],
            partials[1],
            partials[2],
            partials[3],
            partials[4],
            partials[5],
            partials[6],
            partials[7],
            partials[8],
            partials[9],
            partials[10],
            partials[11],
        ),
        "dp",
    )
    ada_grad = totals[0]
    ada_bias = totals[1]
    rest = totals[2:]
    return (
        layer_out,
        grad_tokens,
        ada_grad,
        ada_bias,
        rest[0],
        rest[1],
        rest[2],
        rest[3],
        rest[4],
        rest[5],
        rest[6],
        rest[7],
        rest[8],
        rest[9],
    )


MESH = pl.DeviceIdType.MESH
ANY = pl.BlockSpec(memory_space=pl.ANY)
VMEM = pl.BlockSpec(memory_space=pltpu.VMEM)
SMEM = pl.BlockSpec(memory_space=pltpu.SMEM)
NEG = -1e30
CLIPS = 8
RANKS = 4
FRAME_PART = 4
CELLS = 256
CELL_HOME = CELLS // CLIPS
CELL_PART = CELLS // RANKS
FF = 3072
TOKENS = 256
CHUNK_CELLS = TOKENS // (FRAME_PART * RANKS)
CHUNKS = CELL_PART // CHUNK_CELLS


def turn_of(rank):
    return 2 * lax.rem(rank, 2) + rank // 2


def chunk_of(order, rank):
    return lax.rem(order + turn_of(rank), CHUNKS)


def order_of(chunk, rank):
    return lax.rem(chunk - turn_of(rank) + CHUNKS, CHUNKS)


def share_of(chunk, rank):
    return lax.rem(rank - chunk + RANKS, RANKS)


def chunk_cells(order, rank):
    chunk = chunk_of(order, rank)
    start = chunk * CELL_PART + share_of(chunk, rank) * CHUNK_CELLS
    return pl.ds(pl.multiple_of(start, CHUNK_CELLS), CHUNK_CELLS)


def loss_target(slot, half):
    chunk = slot // 2
    target = lax.rem(2 * lax.rem(slot, 2) + half + chunk, RANKS)
    return target, order_of(chunk, target)


def f32(value):
    return value.astype(jnp.float32)


def bf16(value):
    return value.astype(jnp.bfloat16)


def dot(left, right):
    return lax.dot_general(left, right, (((1,), (0,)), ((), ())), preferred_element_type=jnp.float32)


def dot_nt(left, right):
    return lax.dot_general(left, right, (((1,), (1,)), ((), ())), preferred_element_type=jnp.float32)


def dot_tn(left, right):
    return lax.dot_general(left, right, (((0,), (0,)), ((), ())), preferred_element_type=jnp.float32)


def standardise(field):
    centred = field - jnp.mean(field, axis=-1, keepdims=True)
    inverse = lax.rsqrt(jnp.mean(centred * centred, axis=-1, keepdims=True) + 1e-06)
    return centred * inverse, inverse


def column_sum(field):
    return jnp.sum(field, axis=0, keepdims=True)


def head_halves(rows):
    lane = lax.broadcasted_iota(jnp.int32, (1, 2 * HEAD), 1) < HEAD
    zero = jnp.bfloat16(0)
    return jnp.where(lane, rows, zero), jnp.where(lane, zero, rows)


def pair_lanes(pair, part):
    return pl.ds(part * D + pair * 2 * HEAD, 2 * HEAD)


def heads_forward(qkv, mixed, probs, valid):
    lane = lax.broadcasted_iota(jnp.int32, (1, 2 * HEAD), 1) < HEAD
    scores = []
    for pair in range(HEADS // 2):
        queries = head_halves(qkv[:, pair_lanes(pair, 0)] * jnp.bfloat16(0.125))
        keys = qkv[:, pair_lanes(pair, 1)]
        scores += [dot_nt(queries[half], keys) for half in range(2)]
    low = []
    for head in range(HEADS):
        masked = jnp.where(valid, scores[head], NEG)
        exponent = jnp.exp(masked - jnp.max(masked, axis=-1, keepdims=True))
        low.append(bf16(exponent * (1.0 / jnp.sum(exponent, axis=-1, keepdims=True))))
        probs[head] = low[head]
    for pair in range(HEADS // 2):
        values = qkv[:, pair_lanes(pair, 2)]
        parts = [dot(low[2 * pair + half], values) for half in range(2)]
        mixed[:, pair_lanes(pair, 0)] = bf16(jnp.where(lane, parts[0], parts[1]))


def heads_backward(qkv, grad_mixed, probs, pairs):
    lane = lax.broadcasted_iota(jnp.int32, (1, 2 * HEAD), 1) < HEAD
    heads = [(pair, half) for pair in pairs for half in range(2)]
    operands = {pair: [qkv[:, pair_lanes(pair, part)] for part in range(3)] for pair in pairs}
    grads = {pair: grad_mixed[:, pair_lanes(pair, 0)] for pair in pairs}
    halves = {pair: head_halves(grads[pair]) for pair in pairs}
    low = {head: probs[2 * head[0] + head[1]] for head in heads}
    grad_probs = {head: dot_nt(halves[head[0]][head[1]], operands[head[0]][2]) for head in heads}
    grad_values = {head: dot_tn(low[head], grads[head[0]]) for head in heads}
    grad_scores = {}
    for head in heads:
        full = f32(low[head])
        weighted = full * grad_probs[head]
        grad_scores[head] = bf16(weighted - full * jnp.sum(weighted, axis=-1, keepdims=True))
    grad_keys = {head: dot_tn(grad_scores[head], operands[head[0]][0]) for head in heads}
    grad_queries = {head: dot(grad_scores[head], operands[head[0]][1]) for head in heads}
    for pair in pairs:
        first, second = (pair, 0), (pair, 1)
        qkv[:, pair_lanes(pair, 0)] = bf16(jnp.where(lane, grad_queries[first], grad_queries[second]) * 0.125)
        qkv[:, pair_lanes(pair, 1)] = bf16(jnp.where(lane, grad_keys[first], grad_keys[second]) * 0.125)
        qkv[:, pair_lanes(pair, 2)] = bf16(jnp.where(lane, grad_values[first], grad_values[second]))


def space_forward_body(
    destinations,
    cell_counts,
    tokens,
    condition,
    biases,
    w_ada,
    w_qkv,
    w_out,
    qkv_all,
    mixed_all,
    probs_all,
    state_cells,
    modulation,
    x_scr,
    ada_scr,
    wqkv_scr,
    wout_scr,
    qkv_scr,
    mixed_scr,
    probs_scr,
    state_scr,
    local_sem,
    ada_sem,
    in_send,
    in_recv,
    out_send,
    out_recv,
    save_sem,
    load_later,
    send_loss,
):
    slot = lax.axis_index("dp")
    rank = lax.axis_index("seq")

    def arrival(frame, hop):
        peer = lax.rem(slot + hop, CLIPS)
        rows = pl.ds(pl.multiple_of(slot * CELL_HOME, CELL_HOME), CELL_HOME)
        return pltpu.make_async_remote_copy(
            src_ref=tokens.at[peer, frame],
            dst_ref=x_scr.at[frame, rows],
            send_sem=in_send.at[frame, hop],
            recv_sem=in_recv.at[frame, hop],
            device_id=(peer, rank),
            device_id_type=MESH,
        )

    def leave(frame, hop, order):
        peer = lax.rem(rank + hop, RANKS)
        return pltpu.make_async_remote_copy(
            src_ref=state_scr.at[frame, chunk_cells(order, peer)],
            dst_ref=state_cells.at[order, rank * FRAME_PART + frame],
            send_sem=out_send.at[frame, hop, order],
            recv_sem=out_recv.at[frame, hop, order],
            device_id=(slot, peer),
            device_id_type=MESH,
        )

    def keep(frame, order):
        return pltpu.make_async_copy(
            state_scr.at[frame, chunk_cells(order, rank)],
            state_cells.at[order, rank * FRAME_PART + frame],
            out_recv.at[frame, 0, order],
        )

    def saves(frame):
        return (
            pltpu.make_async_copy(qkv_scr.at[frame], qkv_all.at[frame], save_sem.at[frame, 1]),
            pltpu.make_async_copy(mixed_scr.at[frame], mixed_all.at[frame], save_sem.at[frame, 2]),
        )

    def save_probs(frame):
        return pltpu.make_async_copy(probs_scr.at[lax.rem(frame, 2)], probs_all.at[frame], save_sem.at[frame, 3])

    own_rows = pl.ds(pl.multiple_of(slot * CELL_HOME, CELL_HOME), CELL_HOME)
    own_copy = pltpu.make_async_copy(tokens.at[slot], x_scr.at[:, own_rows], local_sem.at[0])

    def ada_copy(piece):
        return pltpu.make_async_copy(
            w_ada.at[:, pl.ds(piece * D, D)], ada_scr.at[piece % 3], ada_sem.at[piece % 3]
        )

    qkv_copy = pltpu.make_async_copy(w_qkv, wqkv_scr, local_sem.at[2])
    out_copy = pltpu.make_async_copy(w_out, wout_scr, local_sem.at[3])
    barrier = pltpu.get_barrier_semaphore()
    for over_slots in range(CLIPS):
        for over_ranks in range(RANKS):
            if over_slots + over_ranks:
                peer = (lax.rem(slot + over_slots, CLIPS), lax.rem(rank + over_ranks, RANKS))
                pl.semaphore_signal(barrier, inc=1, device_id=peer, device_id_type=MESH)
    pl.semaphore_wait(barrier, CLIPS * RANKS - 1)
    for hop in range(1, CLIPS):
        arrival(0, hop).start()
    own_copy.start()
    for piece in range(3):
        ada_copy(piece).start()
    for frame in range(1, FRAME_PART):
        for hop in range(1, CLIPS):
            arrival(frame, hop).start()
    qkv_copy.start()
    out_copy.start()
    send_loss(True)

    row_ids = lax.broadcasted_iota(jnp.int32, (CLIPS, 1), 0)
    cond = column_sum(jnp.where(row_ids == destinations[slot], f32(condition[...]), 0.0))
    cond = jnp.broadcast_to(bf16(cond / (1.0 + jnp.exp(-cond))), (16, D))
    bias_rows = f32(biases[...])
    valid = lax.broadcasted_iota(jnp.int32, (1, CELLS), 1) < cell_counts[slot]
    for piece in range(9):
        ada_copy(piece).wait()
        row = dot(cond, ada_scr[piece % 3])[0:1]
        if piece + 3 < 9:
            ada_copy(piece + 3).start()
        modulation[pl.ds(piece, 1)] = row + bias_rows[piece : piece + 1]
    own_copy.wait()
    qkv_copy.wait()
    out_copy.wait()

    def frame_step(frame, carry):
        for hop in range(1, CLIPS):
            arrival(frame, hop).wait_recv()

        @pl.when(frame == 0)
        def _():
            load_later()

        x = f32(x_scr[frame])
        centred = x - jnp.mean(x, axis=-1, keepdims=True)
        normed = centred * lax.rsqrt(jnp.mean(centred * centred, axis=-1, keepdims=True) + 1e-06)
        act = bf16(normed * (1.0 + modulation[1:2]) + modulation[0:1])
        qkv_scr[frame] = bf16(dot(act, wqkv_scr[...]))

        @pl.when(frame >= 2)
        def _():
            save_probs(frame - 2).wait()

        heads_forward(qkv_scr.at[frame], mixed_scr.at[frame], probs_scr.at[lax.rem(frame, 2)], valid)
        save_probs(frame).start()
        spatial = dot(mixed_scr[frame], wout_scr[...]) + bias_rows[9:10]
        state_scr[frame] = bf16(f32(x_scr[frame]) + modulation[2:3] * spatial)
        for order in range(CHUNKS):
            for hop in range(1, RANKS):
                leave(frame, hop, order).start()
            keep(frame, order).start()
        for save in saves(frame):
            save.start()
        return carry

    lax.fori_loop(0, FRAME_PART, frame_step, 0)

    def frame_end(frame, carry):
        for hop in range(1, CLIPS):
            arrival(frame, hop).wait_send()
        for order in range(CHUNKS):
            for hop in range(1, RANKS):
                leave(frame, hop, order).wait_send()
            keep(frame, order).wait()
        for save in saves(frame):
            save.wait()
        return carry

    lax.fori_loop(0, FRAME_PART, frame_end, 0)
    for frame in range(FRAME_PART - 2, FRAME_PART):
        save_probs(frame).wait()


def cell_match():
    row_cell = lax.rem(lax.broadcasted_iota(jnp.int32, (TOKENS, TOKENS), 0), CHUNK_CELLS)
    column_cell = lax.rem(lax.broadcasted_iota(jnp.int32, (TOKENS, TOKENS), 1), CHUNK_CELLS)
    return row_cell == column_cell


SAVED_WIDTHS = (D, 3 * D, D, D, D, FF, FF, D)


STEP = 32


def row_blocks():
    return [slice(start, start + STEP) for start in range(0, TOKENS, STEP)]


def fold(field):
    return jnp.sum(field.reshape(-1, 8, field.shape[-1]), axis=0)


def time_forward_body(
    cell_counts,
    frame_tasks,
    state_cells,
    loss_cells,
    layer_cells,
    modulation,
    biases,
    homes,
    sums,
    wqkv_scr,
    wout_scr,
    wup_scr,
    wdown_scr,
    slopes,
    state_scr,
    loss_scr,
    layer_scr,
    act_two,
    qkv,
    mixed,
    grad_temporal,
    act_three,
    grad_lifted,
    hidden,
    grad_branch,
    grad_state,
    probs,
    stage_sem,
    save_sem,
    weight_loads,
    cells_arrive,
    loss_arrive,
    send_layer,
    load_ahead,
):
    slot = lax.axis_index("dp")
    rank = lax.axis_index("seq")
    frames = FRAME_PART * RANKS

    stages = (act_two, qkv, mixed, grad_temporal, act_three, grad_lifted, hidden, grad_branch, grad_state, probs)
    def save(which, order):
        spot = lax.rem(order, 2)
        return pltpu.make_async_copy(stages[which].at[spot], homes[which].at[order], save_sem.at[which, spot])

    def state_load(order):
        spot = lax.rem(order, 2)
        return pltpu.make_async_copy(state_cells.at[order], state_scr.at[spot], stage_sem.at[0])

    def loss_load(order):
        return pltpu.make_async_copy(loss_cells.at[order], loss_scr, stage_sem.at[1])

    def layer_save(order):
        return pltpu.make_async_copy(layer_scr, layer_cells.at[order], stage_sem.at[2])

    sums[...] = jnp.zeros_like(sums)
    bias_rows = f32(biases[...])
    valid = cell_match()
    count = cell_counts[slot]
    frame_cell = (frames, CHUNK_CELLS, 1)
    cell = lax.broadcasted_iota(jnp.int32, frame_cell, 1).reshape(TOKENS, 1)
    frame_ids = lax.broadcasted_iota(jnp.int32, frame_cell, 0)
    tasks = jnp.zeros(frame_cell, jnp.int32)
    for which in range(frames):
        tasks = jnp.where(frame_ids == which, frame_tasks[slot, which], tasks)
    tasks = tasks.reshape(TOKENS, 1)

    def piece(index):
        return modulation[index : index + 1]

    def add(row, value):
        sums[pl.ds(row, 1)] += value

    def chunk_step(order, carry):
        spot = lax.rem(order, 2)
        first = order == 0

        def once(*which):
            @pl.when(first)
            def _():
                for load in which:
                    weight_loads[load].wait()

        @pl.when(order >= 2)
        def _():
            for which in range(len(stages)):
                save(which, order - 2).wait()

        state_load(order).wait()

        def state_rows(rows):
            span = pl.ds(rows.start // CHUNK_CELLS, STEP // CHUNK_CELLS)
            return f32(state_scr[spot, span]).reshape(STEP, D)

        for rows in row_blocks():
            normed, _ = standardise(state_rows(rows))
            act_two[spot, rows] = bf16(normed * (1.0 + piece(4)) + piece(3))
        once(0)
        qkv[spot] = bf16(dot(act_two[spot], wqkv_scr[...]))
        heads_forward(qkv.at[spot], mixed.at[spot], probs.at[spot], valid)
        for which in (0, 1, 2, 9):
            save(which, order).start()
        once(1)
        temporal = dot(mixed[spot], wout_scr[...])
        kept = []
        for rows in row_blocks():
            back = temporal[rows] + bias_rows[10:11]
            state_two = state_rows(rows) + piece(5) * back
            normed, inverse = standardise(state_two)
            act_three[spot, rows] = bf16(normed * (1.0 + piece(7)) + piece(6))
            kept.append((back, state_two, normed, inverse))
        save(4, order).start()
        once(2, 3)
        branch = None
        for block in range(FF // D):
            lanes = pl.ds(block * D, D)
            lifted = dot(act_three[spot], wup_scr[:, lanes])
            for rows in row_blocks():
                up = lifted[rows] + bias_rows[11 + block : 12 + block]
                square = up * up
                curve = jnp.tanh(up * (0.7978845608028654 + 0.7978845608028654 * 0.044715 * square))
                half = 0.5 * curve + 0.5
                whole = up * half
                hidden[spot, rows, lanes] = bf16(whole)
                slopes[rows, lanes] = half + (whole - whole * half) * (
                    2.0 * 0.7978845608028654 + 6.0 * 0.7978845608028654 * 0.044715 * square
                )
            part = dot(hidden[spot, :, lanes], wdown_scr[lanes, :])
            branch = part if branch is None else branch + part
        save(6, order).start()
        loss_arrive(order)
        loss_load(order).start()
        outs = [branch[rows] + bias_rows[15:16] for rows in row_blocks()]
        for rows, out, (_, state_two, _, _) in zip(row_blocks(), outs, kept):
            span = pl.ds(rows.start // CHUNK_CELLS, STEP // CHUNK_CELLS)
            layer = bf16(state_two + piece(8) * out)
            layer_scr[span] = layer.reshape(STEP // CHUNK_CELLS, CHUNK_CELLS, D)
        layer_save(order).start()
        chunk = chunk_of(order, rank)
        first_cell = chunk * CELL_PART + share_of(chunk, rank) * CHUNK_CELLS
        mask = jnp.where(first_cell + cell < count, tasks, 0)
        loss_load(order).wait()
        mask = f32(mask)

        def seed_rows(rows):
            span = pl.ds(rows.start // CHUNK_CELLS, STEP // CHUNK_CELLS)
            return f32(loss_scr[span]).reshape(STEP, D) * mask[rows]

        def add_all(row, parts):
            add(row, column_sum(sum(parts[1:], parts[0])))

        gates, biased = [], []
        for rows, out in zip(row_blocks(), outs):
            seed = seed_rows(rows)
            gates.append(fold(seed * out))
            low = bf16(piece(8) * seed)
            grad_branch[spot, rows] = low
            biased.append(fold(f32(low)))
        add_all(8, gates)
        add_all(13, biased)
        save(7, order).start()
        for block in range(FF // D):
            lanes = pl.ds(block * D, D)
            back = dot_nt(grad_branch[spot], wdown_scr[lanes, :])
            biased = []
            for rows in row_blocks():
                low = bf16(back[rows] * slopes[rows, lanes])
                grad_lifted[spot, rows, lanes] = low
                biased.append(fold(f32(low)))
            add_all(9 + block, biased)
        grad_act = dot_nt(grad_lifted[spot], wup_scr[...])
        save(5, order).start()
        layer_save(order).wait()
        send_layer(order)

        @pl.when(order < CHUNKS - 1)
        def _():
            cells_arrive(order + 1)
            state_load(order + 1).start()


        @pl.when(order == CHUNKS - 1)
        def _():
            for which in (6, 7):
                save(which, CHUNKS - 2).wait()
                save(which, CHUNKS - 1).wait()
            load_ahead()

        parts = [[], [], [], []]
        for rows, (back, _, normed, inverse) in zip(row_blocks(), kept):
            grads = grad_act[rows]
            parts[0].append(fold(grads))
            parts[1].append(fold(grads * normed))
            state_grads = seed_rows(rows) + standard_back(normed, inverse, grads * (1.0 + piece(7)))
            grad_state[spot, rows] = state_grads
            parts[2].append(fold(state_grads * back))
            low = bf16(piece(5) * state_grads)
            grad_temporal[spot, rows] = low
            parts[3].append(fold(f32(low)))
        for row, part in zip((6, 7, 5, 14), parts):
            add_all(row, part)
        save(8, order).start()
        save(3, order).start()
        return carry

    cells_arrive(0)
    state_load(0).start()
    lax.fori_loop(0, CHUNKS, chunk_step, 0)
    for order in (CHUNKS - 2, CHUNKS - 1):
        for which in (0, 1, 2, 3, 4, 5, 8, 9):
            save(which, order).wait()


UNITS = 16
ROWS = D // RANKS
HALF_ROWS = ROWS // 2
KINDS = "SSSSSPSPPPMPPMPP"
SCHEDULE = (
    ("double", 0), (0, 0), (0, 1), ("chunk", 0), (1, 0), ("double", 1), (0, 2), (0, 3), (1, 1), ("chunk", 1),
    (1, 2), (1, 3), (2, 0), ("chunk", 2), (2, 1), ("unit", 4), (0, 4), ("chunk", 3), (1, 4), (2, 2), (3, 0),
    ("unit", 5), (0, 5), ("unit", 6), (0, 6), (2, 3), (3, 1), (1, 5), (4, 0), ("first", 0), (1, 6), ("unit", 7),
    (0, 7), (2, 4), (3, 2), (4, 1), (5, 0), ("second", 0), (1, 7), (3, 3), ("first", 1), (2, 6), (4, 2), (5, 1),
    (6, 0), (2, 5), ("second", 1), (3, 4), ("unit", 8), (0, 8), ("unit", 9), (0, 9), (4, 3), (6, 1), (7, 0),
    ("first", 2), (1, 8), (2, 7), (1, 9), (3, 5), (3, 6), (5, 2), ("second", 2), ("unit", 10), (0, 10), (4, 4),
    (7, 1), ("first", 3), (2, 8), (3, 7), (4, 5), (5, 3), (6, 2), (1, 10), (4, 6), ("second", 3), ("unit", 11),
    (0, 11), (2, 9), (3, 8), (6, 3), ("unit", 12), (0, 12), ("sums", 0), (7, 2), ("unit", 13), (0, 13), (1, 11),
    (2, 10), (4, 7), (5, 4), (1, 12), ("sums", 1), (5, 5), ("unit", 14), (0, 14), (1, 13), (3, 9), (5, 6),
    ("unit", 15), (0, 15), (4, 8), (6, 4), (7, 3), (1, 14), (2, 11), (6, 5), (1, 15), (3, 10), (6, 6), (7, 4),
    (2, 12), (4, 9), (5, 7), (3, 11), (7, 5), (6, 7), (2, 13), (4, 11), (7, 6), (5, 8), (3, 12), (4, 10), (2, 14),
    (6, 8), (7, 7), (3, 13), (5, 9), (5, 10), (4, 12), (5, 11), (2, 15), (6, 9), (3, 14), (4, 13), (7, 8), (6, 10),
    (4, 14), (6, 11), (3, 15), (5, 12), (7, 10), (7, 9), (5, 14), (4, 15), (6, 12), (5, 13), (6, 14), (7, 11),
    (5, 15), (7, 12), (6, 13), (6, 15), (7, 14), (7, 13), (7, 15),
)


def tail_body(
    qkv,
    mixed,
    probs,
    state_cells,
    act_two,
    qkv_two,
    mixed_two,
    grad_temporal,
    act_three,
    grad_lifted,
    hidden,
    grad_branch,
    grad_state_two,
    probs_two,
    modulation,
    biases,
    w_qkv_t,
    w_out_t,
    w_qkv,
    w_out,
    grad_home,
    totals,
    gathered,
    x_scr,
    state_scr,
    sums,
    sums_in_scr,
    sums_low,
    core_in,
    first_in,
    second_in,
    edge_in,
    middle_in,
    left_scr,
    right_scr,
    qkv_scr,
    mixed_scr,
    spatial_scr,
    time_scr,
    wqkv_scr,
    wout_scr,
    grad_mixed,
    chunk_state,
    chunk_grad,
    chunk_temporal,
    probs_scr,
    own,
    first_out,
    kept,
    load_sem,
    frame_sem,
    probs_sem,
    side_sem,
    chunk_sem,
    cell_send,
    cell_recv,
    home_send,
    home_recv,
    unit_send,
    unit_recv,
    sum_send,
    sum_recv,
):
    slot = lax.axis_index("dp")
    rank = lax.axis_index("seq")
    core = lax.rem(rank, 2)
    over_x = rank // 2
    over_y = lax.rem(slot, 2)
    over_z = slot // 2
    at_edge = jnp.logical_or(over_z == 0, over_z == 3)
    low_side = over_z < 2
    core_peer = (slot, rank + 1 - 2 * core)
    x_peer = (slot, lax.rem(rank + 2, RANKS))
    y_peer = (slot + 1 - 2 * over_y, rank)
    inner_peer = (jnp.where(low_side, 2, 4) + over_y, rank)
    middle_peer = (jnp.where(low_side, 4, 2) + over_y, rank)
    outer_peer = (jnp.where(low_side, 0, 6) + over_y, rank)

    def piece(index):
        return modulation[index : index + 1]

    def remote(source, target, send, recv, peer):
        return pltpu.make_async_remote_copy(
            src_ref=source, dst_ref=target, send_sem=send, recv_sem=recv, device_id=peer, device_id_type=MESH
        )


    turned = over_z // 2

    def spots(unit):
        mine = {"P": over_y, "S": over_x, "M": turned}[KINDS[unit]]
        return mine, 1 - mine

    def half_rows(which):
        return pl.ds(pl.multiple_of(which * HALF_ROWS, HALF_ROWS), HALF_ROWS)

    def send(kind, unit, source, target, peer, landing=None):
        landing = kind if landing is None else landing
        return remote(source, target, unit_send.at[kind, unit], unit_recv.at[landing, unit], peer)

    def core_copy(unit):
        return send(0, unit, own.at[unit % 4, 1 - core], core_in.at[unit % 6], core_peer)

    def first_copy(unit):
        peer = y_peer if KINDS[unit] == "S" else x_peer
        return send(1, unit, first_out.at[unit % 8], first_in.at[unit % 10], peer)

    def second_copy(unit):
        mine, other = spots(unit)
        if KINDS[unit] == "M":
            return send(2, unit, kept.at[unit, mine], second_in.at[unit % 10], y_peer)
        peer = x_peer if KINDS[unit] == "S" else y_peer
        return send(2, unit, kept.at[unit, other], second_in.at[unit % 10], peer)

    def edge_copy(unit):
        if KINDS[unit] == "M":
            return send(3, unit, kept.at[unit], edge_in.at[unit % 8], inner_peer)
        mine, _ = spots(unit)
        return send(3, unit, kept.at[unit, mine], edge_in.at[unit % 8, 0], inner_peer)

    def middle_copy(unit):
        mine, other = spots(unit)
        source = kept.at[unit, other if KINDS[unit] == "M" else mine]
        return send(4, unit, source, middle_in.at[unit % 10], middle_peer)

    def outer_copy(unit):
        _, other = spots(unit)
        return send(5, unit, kept.at[unit, other], middle_in.at[unit % 10], outer_peer, 4)

    def share_copy(unit, source):
        return send(6, unit, source, totals.at[unit, half_rows(over_y)], y_peer)

    def keep_copy(unit, source, which):
        return pltpu.make_async_copy(source, totals.at[unit, half_rows(which)], unit_send.at[7, unit])

    def cross_copy(unit):
        mine, other = spots(unit)
        return send(6, unit, kept.at[unit, other], totals.at[unit, half_rows(mine)], middle_peer)

    def near_copy(unit):
        mine, other = spots(unit)
        return send(5, unit, kept.at[unit, other], totals.at[unit, half_rows(mine)], outer_peer)

    def far_copy(unit):
        _, other = spots(unit)
        place = totals.at[unit, half_rows(other)]
        return send(8, unit, place, place, outer_peer)

    def plus(left, right):
        return bf16(f32(left) + f32(right))

    def stage_one(unit):
        core_copy(unit).wait()
        held, came = own.at[unit % 4, core], core_in.at[unit % 6]
        if KINDS[unit] == "S":
            for part in range(2):
                first_out[unit % 8, part] = plus(held[part, 1 - over_y], came[part, 1 - over_y])
            first_copy(unit).start()
            for part in range(2):
                kept[unit, part] = plus(held[part, over_y], came[part, over_y])
        else:
            first_out[unit % 8] = plus(held[1 - over_x], came[1 - over_x])
            first_copy(unit).start()
            kept[unit] = plus(held[over_x], came[over_x])

    def stage_two(unit):
        first_copy(unit).wait()
        mine, other = spots(unit)
        if KINDS[unit] == "M":
            kept[unit] = plus(kept[unit], first_in[unit % 10])

            @pl.when(at_edge)
            def _():
                edge_copy(unit).start()

        else:
            kept[unit, other] = plus(kept[unit, other], first_in[unit % 10, other])
            second_copy(unit).start()
            kept[unit, mine] = plus(kept[unit, mine], first_in[unit % 10, mine])

    def stage_three(unit):
        mine, _ = spots(unit)
        if KINDS[unit] == "M":

            @pl.when(jnp.logical_not(at_edge))
            def _():
                edge_copy(unit).wait_recv()
                kept[unit] = plus(kept[unit], edge_in[unit % 8])
                middle_copy(unit).start()

        else:
            second_copy(unit).wait()
            kept[unit, mine] = plus(kept[unit, mine], second_in[unit % 10])

            @pl.when(at_edge)
            def _():
                edge_copy(unit).start()

    def stage_four(unit):
        mine, _ = spots(unit)

        @pl.when(jnp.logical_not(at_edge))
        def _():
            if KINDS[unit] == "M":
                middle_copy(unit).wait()
                kept[unit, mine] = plus(kept[unit, mine], middle_in[unit % 10])
                second_copy(unit).start()
            else:
                edge_copy(unit).wait_recv()
                kept[unit, mine] = plus(kept[unit, mine], edge_in[unit % 8, 0])
                middle_copy(unit).start()

    def stage_five(unit):
        mine, other = spots(unit)

        @pl.when(jnp.logical_not(at_edge))
        def _():
            if KINDS[unit] == "M":
                second_copy(unit).wait()
                kept[unit, other] = plus(kept[unit, mine], second_in[unit % 10])
                cross_copy(unit).start()
                near_copy(unit).start()
                keep_copy(unit, kept.at[unit, other], mine).start()
            else:
                middle_copy(unit).wait()
                kept[unit, other] = plus(kept[unit, mine], middle_in[unit % 10])
                share_copy(unit, kept.at[unit, other]).start()
                outer_copy(unit).start()
                keep_copy(unit, kept.at[unit, other], over_y).start()

    def stage_six(unit):
        if KINDS[unit] == "M":

            @pl.when(jnp.logical_not(at_edge))
            def _():
                cross_copy(unit).wait_recv()
                far_copy(unit).start()

        else:

            @pl.when(at_edge)
            def _():
                outer_copy(unit).wait_recv()
                share_copy(unit, middle_in.at[unit % 10]).start()
                keep_copy(unit, middle_in.at[unit % 10], over_y).start()

    def stage_seven(unit):
        mine, other = spots(unit)
        source = kept.at[unit, other]
        if KINDS[unit] == "M":

            @pl.when(at_edge)
            def _():
                edge_copy(unit).wait_send()
                near_copy(unit).wait_recv()
                far_copy(unit).wait_recv()

            @pl.when(jnp.logical_not(at_edge))
            def _():
                cross_copy(unit).wait_send()
                near_copy(unit).wait_send()
                far_copy(unit).wait_send()
                keep_copy(unit, source, mine).wait()

        else:

            @pl.when(at_edge)
            def _():
                edge_copy(unit).wait_send()

            @pl.when(jnp.logical_not(at_edge))
            def _():
                outer_copy(unit).wait_send()

            share_copy(unit, source).wait()
            keep_copy(unit, source, over_y).wait()

    stages = (
        lambda unit: core_copy(unit).start(),
        stage_one,
        stage_two,
        stage_three,
        stage_four,
        stage_five,
        stage_six,
        stage_seven,
    )


    def put_quarter(unit, quarter, rows):
        own[unit % 4, quarter % 2, quarter // 2] = bf16(rows).reshape(2, HALF_ROWS, D)

    def put_unit(unit, block):
        for quarter in range(RANKS):
            put_quarter(unit, quarter, block[quarter * ROWS : (quarter + 1) * ROWS])

    def flat(block):
        return block.reshape(CHUNKS * TOKENS, block.shape[-1])

    def unit_loads(unit):
        if unit < 8:
            left, right, column = act_three, grad_lifted, unit - 4
        elif unit < 11:
            left, right, column = act_two, time_scr, unit - 8
        else:
            left, right, column = mixed_two, grad_temporal, 0
        return (
            pltpu.make_async_copy(left, left_scr.at[unit % 2], load_sem.at[0, unit % 2]),
            pltpu.make_async_copy(
                right.at[:, :, pl.ds(column * D, D)], right_scr.at[unit % 2], load_sem.at[1, unit % 2]
            ),
        )

    def make_unit(unit):
        if unit < 12:
            for load in unit_loads(unit):
                load.wait()
            left, right = left_scr[unit % 2], right_scr[unit % 2]
        elif unit < 15:
            left, right = x_scr[...], qkv_scr[:, :, pl.ds((unit - 12) * D, D)]
        else:
            left, right = mixed_scr[...], spatial_scr[...]
        put_unit(unit, dot_tn(flat(left), flat(right)))
        if 4 <= unit < 10:
            for load in unit_loads(unit + 2):
                load.start()

    def hidden_load(block):
        spot = block % 2
        lanes = pl.ds(block % RANKS * D, D)
        return pltpu.make_async_copy(hidden.at[:, :, lanes], right_scr.at[spot], load_sem.at[1, spot])

    def double_unit(double):
        for block in range(RANKS):
            hidden_load(block).wait()
            left = left_scr[0, :, :, pl.ds(double * 2 * ROWS, 2 * ROWS)]
            columns = dot_tn(flat(left), flat(right_scr[block % 2]))
            if block + 2 < RANKS or double == 0:
                hidden_load(block + 2).start()
            for part in range(2):
                put_quarter(2 * double + part, block, columns[part * ROWS : (part + 1) * ROWS])
        if double == 1:
            for unit in (4, 5):
                for load in unit_loads(unit):
                    load.start()


    def chunk_loads(order):
        spot = order % 2
        return (
            pltpu.make_async_copy(state_cells.at[order], chunk_state.at[spot], chunk_sem.at[0, spot]),
            pltpu.make_async_copy(grad_state_two.at[order], chunk_grad.at[spot], chunk_sem.at[1, spot]),
            pltpu.make_async_copy(grad_temporal.at[order], chunk_temporal.at[spot], chunk_sem.at[2, spot]),
            pltpu.make_async_copy(qkv_two.at[order], time_scr.at[order], chunk_sem.at[3, spot]),
        )

    def cell_place(order, frame):
        return state_scr.at[frame, chunk_cells(order, rank)]

    def cell_rows(order, target, frame):
        start = (target * FRAME_PART + frame) * CHUNK_CELLS
        return spatial_scr.at[order, pl.ds(pl.multiple_of(start, CHUNK_CELLS), CHUNK_CELLS)]

    def cell_copy(order, hop, frame):
        target = lax.rem(rank + hop, RANKS)
        return remote(
            cell_rows(order, target, frame),
            cell_place(order, frame),
            cell_send.at[order, hop, frame],
            cell_recv.at[order, hop, frame],
            (slot, target),
        )

    def cell_keep(order, frame):
        return pltpu.make_async_copy(
            cell_rows(order, rank, frame), cell_place(order, frame), cell_recv.at[order, 0, frame]
        )

    def probs_load(step):
        source = probs_two.at[step] if step < CHUNKS else probs.at[step - CHUNKS]
        return pltpu.make_async_copy(source, probs_scr, probs_sem.at[0])

    def probs_next(step):
        if step < CHUNKS + FRAME_PART:
            probs_load(step).start()

    def time_backward(order):
        spot = order % 2
        for load in chunk_loads(order):
            load.wait()
        probs_load(order).wait()
        if order < CHUNKS - 1:
            for load in chunk_loads(order + 1):
                load.start()

        grad_mixed[...] = bf16(dot_nt(chunk_temporal[spot], wout_scr[...]))
        heads_backward(time_scr.at[order], grad_mixed, probs_scr, range(HEADS // 2))
        probs_next(order + 1)
        grad_act = dot_nt(time_scr[order], wqkv_scr[...])
        normed, inverse = standardise(f32(chunk_state[spot]).reshape(TOKENS, D))
        add(3, column_sum(grad_act))
        add(4, column_sum(grad_act * normed))
        spatial_scr[order] = bf16(
            chunk_grad[spot] + standard_back(normed, inverse, grad_act * (1.0 + piece(4)))
        )
        for frame in range(FRAME_PART):
            for hop in range(1, RANKS):
                cell_copy(order, hop, frame).start()
            cell_keep(order, frame).start()


    def add(row, value):
        sums[pl.ds(row, 1)] += value

    def frame_loads(frame):
        return (
            pltpu.make_async_copy(qkv.at[frame], qkv_scr.at[frame], frame_sem.at[0, frame]),
            pltpu.make_async_copy(mixed.at[frame], mixed_scr.at[frame], frame_sem.at[1, frame]),
        )

    def home_copy(frame, hop):
        peer = lax.rem(slot + hop, CLIPS)
        rows = pl.ds(pl.multiple_of(peer * CELL_HOME, CELL_HOME), CELL_HOME)
        return remote(
            state_scr.at[frame, rows],
            grad_home.at[slot, frame],
            home_send.at[frame, hop],
            home_recv.at[frame, hop],
            (peer, rank),
        )

    def home_keep(frame):
        rows = pl.ds(pl.multiple_of(slot * CELL_HOME, CELL_HOME), CELL_HOME)
        return pltpu.make_async_copy(state_scr.at[frame, rows], grad_home.at[slot, frame], home_recv.at[frame, 0])

    def frame_first(frame):
        for load in frame_loads(frame):
            load.wait()
        for order in range(CHUNKS):
            for hop in range(1, RANKS):
                cell_copy(order, hop, frame).wait_recv()
        grad_state = f32(state_scr[frame])
        spatial = dot(mixed_scr[frame], wout_scr[...]) + bias_rows[9:10]
        add(2, column_sum(grad_state * spatial))
        low_spatial = bf16(piece(2) * grad_state)
        spatial_scr[frame] = low_spatial
        add(15, column_sum(f32(low_spatial)))
        grad_mixed[...] = bf16(dot_nt(low_spatial, wout_scr[...]))
        probs_load(CHUNKS + frame).wait()
        heads_backward(qkv_scr.at[frame], grad_mixed, probs_scr, range(HEADS // 4))

    def frame_second(frame):
        heads_backward(qkv_scr.at[frame], grad_mixed, probs_scr, range(HEADS // 4, HEADS // 2))
        probs_next(CHUNKS + frame + 1)
        grad_act = dot_nt(qkv_scr[frame], wqkv_scr[...])
        normed, inverse = standardise(f32(x_scr[frame]))
        x_scr[frame] = bf16(normed * (1.0 + piece(1)) + piece(0))
        add(0, column_sum(grad_act))
        add(1, column_sum(grad_act * normed))
        state_scr[frame] = bf16(
            f32(state_scr[frame]) + standard_back(normed, inverse, grad_act * (1.0 + piece(1)))
        )
        for hop in range(1, CLIPS):
            home_copy(frame, hop).start()
        home_keep(frame).start()


    def sum_exchange(step):
        peer = core_peer if step == 0 else x_peer
        return remote(sums, sums_in_scr.at[step], sum_send.at[step], sum_recv.at[step], peer)

    def sum_add(step):
        sum_exchange(step).wait()
        sums[...] = sums[...] + sums_in_scr[step]

    def sum_spread(hop):
        peer = lax.rem(slot + hop, CLIPS)
        return remote(sums_low, gathered.at[slot], sum_send.at[1 + hop], sum_recv.at[1 + hop], (peer, rank))

    def sum_keep():
        return pltpu.make_async_copy(sums_low, gathered.at[slot], sum_send.at[9])


    time_weights = (
        pltpu.make_async_copy(w_qkv_t, wqkv_scr, side_sem.at[0]),
        pltpu.make_async_copy(w_out_t, wout_scr, side_sem.at[1]),
    )
    space_weights = (
        pltpu.make_async_copy(w_qkv, wqkv_scr, side_sem.at[0]),
        pltpu.make_async_copy(w_out, wout_scr, side_sem.at[1]),
    )
    branch_load = pltpu.make_async_copy(grad_branch, left_scr.at[0], load_sem.at[0, 0])
    for load in chunk_loads(0):
        load.start()
    probs_load(0).start()
    for load in time_weights:
        load.start()
    bias_rows = f32(biases[...])
    branch_load.wait()

    def first_of_frames():
        for load in space_weights:
            load.start()
        for order in range(CHUNKS):
            for frame in range(FRAME_PART):
                for hop in range(1, RANKS):
                    cell_copy(order, hop, frame).wait_send()
                cell_keep(order, frame).wait()
        for load in space_weights:
            load.wait()

    for action, index in SCHEDULE:
        if action == "double":
            double_unit(index)
        elif action == "chunk":
            if index == 0:
                for load in time_weights:
                    load.wait()
            if index == 2:
                for frame in range(FRAME_PART):
                    for load in frame_loads(frame):
                        load.start()
            time_backward(index)
        elif action == "first":
            if index == 0:
                first_of_frames()
            frame_first(index)
        elif action == "second":
            frame_second(index)
            if index == FRAME_PART - 1:
                sum_exchange(0).start()
        elif action == "unit":
            make_unit(index)
        elif action == "sums":
            sum_add(index)
            if index == 0:
                sum_exchange(1).start()
            else:
                sums_low[...] = bf16(sums[...])
                for hop in range(1, CLIPS):
                    sum_spread(hop).start()
                sum_keep().start()
        else:
            stages[action](index)

    for hop in range(1, CLIPS):
        sum_spread(hop).wait()
    sum_keep().wait()

    def frame_end(frame, carry):
        for hop in range(1, CLIPS):
            home_copy(frame, hop).wait()
        home_keep(frame).wait()
        return carry

    lax.fori_loop(0, FRAME_PART, frame_end, 0)


def block_body(
    destinations,
    cell_counts,
    frame_tasks,
    tokens,
    loss_grad,
    condition,
    biases,
    w_ada,
    w_qkv_s,
    w_out_s,
    w_qkv_t,
    w_out_t,
    w_up,
    w_down,
    layer_home,
    grad_home,
    totals,
    gathered,
    qkv_one,
    mixed_one,
    probs_one,
    state_cells,
    loss_cells,
    layer_cells,
    act_two,
    qkv_two,
    mixed_two,
    grad_temporal,
    act_three,
    grad_lifted,
    hidden,
    grad_branch,
    grad_state_two,
    probs_two,
    modulation,
    sums,
    sums_in,
    sums_low,
    x_scr,
    state_scr,
    core_in,
    first_in,
    second_in,
    edge_in,
    middle_in,
    left_scr,
    right_scr,
    local_sem,
    ada_sem,
    in_send,
    in_recv,
    out_send,
    out_recv,
    save_one_sem,
    loss_send_sem,
    loss_recv_sem,
    weight_sem,
    stage_sem,
    save_two_sem,
    layer_send_sem,
    layer_recv_sem,
    *tail_sems,
):
    slot = lax.axis_index("dp")
    rank = lax.axis_index("seq")
    low = jnp.bfloat16
    frames = FRAME_PART * RANKS


    def loss_source(half, hop):
        return loss_grad.at[lax.rem(slot + hop, CLIPS), :, pl.ds(half * CHUNK_CELLS, CHUNK_CELLS)]

    def loss_place(order):
        return loss_cells.at[order, pl.ds(rank * FRAME_PART, FRAME_PART)]

    def loss_send(half, hop):
        target, order = loss_target(slot, half)
        return pltpu.make_async_remote_copy(
            src_ref=loss_source(half, hop),
            dst_ref=loss_place(order),
            send_sem=loss_send_sem.at[half, hop],
            recv_sem=loss_recv_sem.at[order, rank],
            device_id=(lax.rem(slot + hop, CLIPS), target),
            device_id_type=MESH,
        )

    def loss_keep(half):
        _, order = loss_target(slot, half)
        return pltpu.make_async_copy(loss_source(half, 0), loss_place(order), loss_recv_sem.at[order, rank])

    def send_loss(early):
        for half in range(2):
            target, order = loss_target(slot, half)

            @pl.when((order < 2) if early else (order >= 2))
            def _():
                @pl.when(target == rank)
                def _():
                    loss_keep(half).start()

                @pl.when(target != rank)
                def _():
                    loss_send(half, 0).start()

                for hop in range(1, CLIPS):
                    loss_send(half, hop).start()

    def loss_sent():
        for half in range(2):
            target, _ = loss_target(slot, half)

            @pl.when(target != rank)
            def _():
                loss_send(half, 0).wait_send()

            for hop in range(1, CLIPS):
                loss_send(half, hop).wait_send()

    def loss_arrive(order):
        for source in range(RANKS):
            place = loss_cells.at[order, pl.ds(source * FRAME_PART, FRAME_PART)]
            pltpu.make_async_copy(
                loss_grad.at[0, :, pl.ds(0, CHUNK_CELLS)], place, loss_recv_sem.at[order, source]
            ).wait()


    def cells_arrive(order):
        for frame in range(FRAME_PART):
            for hop in range(1, RANKS):
                place = state_cells.at[order, frame]
                pltpu.make_async_copy(place, place, out_recv.at[frame, hop, order]).wait()


    def layer_home_of(order):
        chunk = chunk_of(order, rank)
        share = share_of(chunk, rank)
        return 2 * chunk + share // 2, lax.rem(share, 2)

    def layer_copies(order, target):
        home, half = layer_home_of(order)
        source = layer_cells.at[order, pl.ds(target * FRAME_PART, FRAME_PART)]
        place = layer_home.at[slot, :, pl.ds(pl.multiple_of(half * CHUNK_CELLS, CHUNK_CELLS), CHUNK_CELLS)]
        arrival = layer_recv_sem.at[slot, half]
        local = jnp.logical_and(home == slot, rank == target)
        keep = functools.partial(pltpu.make_async_copy, source, place, arrival)
        leave = functools.partial(
            pltpu.make_async_remote_copy,
            src_ref=source,
            dst_ref=place,
            send_sem=layer_send_sem.at[order, target],
            recv_sem=arrival,
            device_id=(home, target),
            device_id_type=MESH,
        )
        return local, keep, leave

    def send_layer(order):
        for target in range(RANKS):
            local, keep, leave = layer_copies(order, target)

            @pl.when(local)
            def _():
                keep().start()

            @pl.when(jnp.logical_not(local))
            def _():
                leave().start()

    def layer_sent(order, carry):
        for target in range(RANKS):
            local, _, leave = layer_copies(order, target)

            @pl.when(jnp.logical_not(local))
            def _():
                leave().wait_send()

        return carry

    def layer_arrive():
        for clip in range(CLIPS):
            for half in range(2):
                place = layer_home.at[clip, :, pl.ds(half * CHUNK_CELLS, CHUNK_CELLS)]
                pltpu.make_async_copy(place, place, layer_recv_sem.at[clip, half]).wait()


    def load_ahead():
        load_sem = tail_sems[0]
        pltpu.make_async_copy(grad_branch, left_scr.at[0], load_sem.at[0, 0]).start()
        for block in range(2):
            lanes = pl.ds(block * D, D)
            pltpu.make_async_copy(hidden.at[:, :, lanes], right_scr.at[block], load_sem.at[1, block]).start()

    def front(wqkv_scr, wout_scr, wup_scr, wdown_scr):
        sources = (w_qkv_t, w_out_t, w_up, w_down)
        places = (wqkv_scr, wout_scr, wup_scr, wdown_scr)
        weight_loads = [
            pltpu.make_async_copy(source, place, weight_sem.at[which])
            for which, (source, place) in enumerate(zip(sources, places))
        ]

        def load_later():
            for load in weight_loads:
                load.start()

        def space(*scoped):
            space_forward_body(
                destinations,
                cell_counts,
                tokens,
                condition,
                biases,
                w_ada,
                w_qkv_s,
                w_out_s,
                qkv_one,
                mixed_one,
                probs_one,
                state_cells,
                modulation,
                x_scr,
                *scoped,
                local_sem,
                ada_sem,
                in_send,
                in_recv,
                out_send,
                out_recv,
                save_one_sem,
                load_later,
                send_loss,
            )

        pl.run_scoped(
            space,
            pltpu.VMEM((3, D, D), low),
            pltpu.VMEM((D, 3 * D), low),
            pltpu.VMEM((D, D), low),
            pltpu.VMEM((FRAME_PART, CELLS, 3 * D), low),
            pltpu.VMEM((FRAME_PART, CELLS, D), low),
            pltpu.VMEM((2, HEADS, CELLS, CELLS), low),
            pltpu.VMEM((FRAME_PART, CELLS, D), low),
        )
        send_loss(False)

        def time(*scoped):
            time_forward_body(
                cell_counts,
                frame_tasks,
                state_cells,
                loss_cells,
                layer_cells,
                modulation,
                biases,
                (
                    act_two,
                    qkv_two,
                    mixed_two,
                    grad_temporal,
                    act_three,
                    grad_lifted,
                    hidden,
                    grad_branch,
                    grad_state_two,
                    probs_two,
                ),
                sums,
                wqkv_scr,
                wout_scr,
                wup_scr,
                wdown_scr,
                *scoped,
                stage_sem,
                save_two_sem,
                weight_loads,
                cells_arrive,
                loss_arrive,
                send_layer,
                load_ahead,
            )

        pl.run_scoped(
            time,
            pltpu.VMEM((TOKENS, FF), jnp.float32),
            pltpu.VMEM((2, frames, CHUNK_CELLS, D), low),
            pltpu.VMEM((frames, CHUNK_CELLS, D), low),
            pltpu.VMEM((frames, CHUNK_CELLS, D), low),
            *[pltpu.VMEM((2, TOKENS, width), low) for width in SAVED_WIDTHS],
            pltpu.VMEM((2, TOKENS, D), jnp.float32),
            pltpu.VMEM((2, HEADS, TOKENS, TOKENS), low),
        )

    pl.run_scoped(
        front,
        pltpu.VMEM((D, 3 * D), low),
        pltpu.VMEM((D, D), low),
        pltpu.VMEM((D, FF), low),
        pltpu.VMEM((FF, D), low),
    )

    def tail(*scoped):
        tail_body(
            qkv_one,
            mixed_one,
            probs_one,
            state_cells,
            act_two,
            qkv_two,
            mixed_two,
            grad_temporal,
            act_three,
            grad_lifted,
            hidden,
            grad_branch,
            grad_state_two,
            probs_two,
            modulation,
            biases,
            w_qkv_t,
            w_out_t,
            w_qkv_s,
            w_out_s,
            grad_home,
            totals,
            gathered,
            x_scr,
            state_scr,
            sums,
            sums_in,
            sums_low,
            core_in,
            first_in,
            second_in,
            edge_in,
            middle_in,
            left_scr,
            right_scr,
            *scoped,
            *tail_sems,
        )

    pl.run_scoped(
        tail,
        pltpu.VMEM((FRAME_PART, CELLS, 3 * D), low),
        pltpu.VMEM((FRAME_PART, CELLS, D), low),
        pltpu.VMEM((FRAME_PART, CELLS, D), low),
        pltpu.VMEM((CHUNKS, TOKENS, 3 * D), low),
        pltpu.VMEM((D, 3 * D), low),
        pltpu.VMEM((D, D), low),
        pltpu.VMEM((CELLS, D), low),
        pltpu.VMEM((2, frames, CHUNK_CELLS, D), low),
        pltpu.VMEM((2, TOKENS, D), jnp.float32),
        pltpu.VMEM((2, TOKENS, D), low),
        pltpu.VMEM((HEADS, TOKENS, TOKENS), low),
        pltpu.VMEM((4, 2, 2, 2, HALF_ROWS, D), low),
        pltpu.VMEM((8, 2, HALF_ROWS, D), low),
        pltpu.VMEM((UNITS, 2, HALF_ROWS, D), low),
    )
    loss_sent()
    lax.fori_loop(0, CHUNKS, layer_sent, 0)
    layer_arrive()


def block(destinations, cell_counts, frame_tasks, tokens, loss_grad, condition, biases, *weights):
    low = jnp.bfloat16
    frames = FRAME_PART * RANKS
    dma = pltpu.SemaphoreType.DMA

    def cells():
        return jax.ShapeDtypeStruct((CHUNKS, frames, CHUNK_CELLS, D), low)

    def home():
        return jax.ShapeDtypeStruct((CLIPS, FRAME_PART, CELL_HOME, D), low)

    def probs():
        return jax.ShapeDtypeStruct((CHUNKS, HEADS, TOKENS, TOKENS), low)

    out_shape = (
        home(),
        home(),
        jax.ShapeDtypeStruct((UNITS, ROWS, D), low),
        jax.ShapeDtypeStruct((CLIPS, 16, D), low),
        jax.ShapeDtypeStruct((FRAME_PART, CELLS, 3 * D), low),
        jax.ShapeDtypeStruct((FRAME_PART, CELLS, D), low),
        probs(),
        cells(),
        cells(),
        cells(),
        *[jax.ShapeDtypeStruct((CHUNKS, TOKENS, width), low) for width in SAVED_WIDTHS],
        jax.ShapeDtypeStruct((CHUNKS, TOKENS, D), jnp.float32),
        probs(),
    )
    return pl.pallas_call(
        block_body,
        out_shape=out_shape,
        in_specs=[SMEM, SMEM, SMEM, ANY, ANY, VMEM, VMEM] + [ANY] * 7,
        out_specs=(ANY,) * len(out_shape),
        scratch_shapes=[
            pltpu.VMEM((16, D), jnp.float32),
            pltpu.VMEM((16, D), jnp.float32),
            pltpu.VMEM((2, 16, D), jnp.float32),
            pltpu.VMEM((16, D), low),
            pltpu.VMEM((FRAME_PART, CELLS, D), low),
            pltpu.VMEM((FRAME_PART, CELLS, D), low),
            pltpu.VMEM((6, 2, 2, HALF_ROWS, D), low),
            pltpu.VMEM((10, 2, HALF_ROWS, D), low),
            pltpu.VMEM((10, HALF_ROWS, D), low),
            pltpu.VMEM((8, 2, HALF_ROWS, D), low),
            pltpu.VMEM((10, HALF_ROWS, D), low),
            pltpu.VMEM((2, CHUNKS, TOKENS, D), low),
            pltpu.VMEM((2, CHUNKS, TOKENS, D), low),
            dma((4,)),
            dma((3,)),
            dma((FRAME_PART, CLIPS)),
            dma((FRAME_PART, CLIPS)),
            dma((FRAME_PART, RANKS, CHUNKS)),
            dma((FRAME_PART, RANKS, CHUNKS)),
            dma((FRAME_PART, 4)),
            dma((2, CLIPS)),
            dma((CHUNKS, RANKS)),
            dma((4,)),
            dma((3,)),
            dma((10, 2)),
            dma((CHUNKS, RANKS)),
            dma((CLIPS, 2)),
            dma((2, 2)),
            dma((2, FRAME_PART)),
            dma((1,)),
            dma((2,)),
            dma((4, 2)),
            dma((CHUNKS, RANKS, FRAME_PART)),
            dma((CHUNKS, RANKS, FRAME_PART)),
            dma((FRAME_PART, CLIPS)),
            dma((FRAME_PART, CLIPS)),
            dma((9, UNITS)),
            dma((9, UNITS)),
            dma((10,)),
            dma((9,)),
        ],
        compiler_params=pltpu.CompilerParams(
            collective_id=0, has_side_effects=True, vmem_limit_bytes=62 * 1024 * 1024
        ),
        cost_estimate=pl.CostEstimate(flops=70 * 10**9, bytes_accessed=150 * 10**6, transcendentals=10**7),
        name="block",
    )(destinations, cell_counts, frame_tasks, tokens, loss_grad, condition, biases, *weights)


def finish_body(
    destinations,
    condition,
    gathered,
    totals,
    layer_home,
    grad_home,
    layer_out,
    grad_tokens,
    grad_w_ada,
    grad_w_qkv_s,
    grad_w_out_s,
    grad_w_qkv_t,
    grad_w_out_t,
    grad_w_up,
    grad_w_down,
    sums_all,
    gathered_scr,
    home_scr,
    totals_scr,
    ada_scr,
    wide_scr,
    cond_scr,
    sem,
    ada_sem,
    wide_sem,
):
    rank = lax.axis_index("seq")
    brings = (
        pltpu.make_async_copy(layer_home, home_scr.at[0], sem.at[0]),
        pltpu.make_async_copy(grad_home, home_scr.at[1], sem.at[1]),
    )
    moves = (
        pltpu.make_async_copy(home_scr.at[0], layer_out, sem.at[0]),
        pltpu.make_async_copy(home_scr.at[1], grad_tokens, sem.at[1]),
    )
    load = pltpu.make_async_copy(totals, totals_scr, sem.at[2])
    gathered_load = pltpu.make_async_copy(gathered, gathered_scr, sem.at[3])
    gathered_load.start()
    load.start()
    for bring in brings:
        bring.start()
    clips = lax.broadcasted_iota(jnp.int32, (CLIPS, 1), 0)
    rows = f32(condition[...])
    cond = jnp.zeros((CLIPS, D), jnp.float32)
    for clip in range(CLIPS):
        row = column_sum(jnp.where(clips == destinations[clip], rows, 0.0))
        cond = jnp.where(clips == clip, row, cond)
    cond = cond / (1.0 + jnp.exp(-cond))
    for which in range(RANKS):

        @pl.when(rank == which)
        def _():
            cond_scr[...] = cond[:, which * ROWS : (which + 1) * ROWS]

    own_cond = bf16(cond_scr[...])
    pieces = []
    gathered_load.wait()
    clip_rows = f32(gathered_scr[...])
    for piece in range(9):
        grads = jnp.concatenate([clip_rows[clip, piece : piece + 1] for clip in range(CLIPS)], axis=0)
        lanes = pl.ds(piece * D, D)
        ada_scr[:, lanes] = dot_tn(own_cond, bf16(grads))
        pieces.append(pltpu.make_async_copy(ada_scr.at[:, lanes], grad_w_ada.at[:, lanes], ada_sem.at[piece]))
        pieces[-1].start()
    total = clip_rows[0]
    for clip in range(1, CLIPS):
        total = total + clip_rows[clip]
    sums_all[...] = total
    for bring, move in zip(brings, moves):
        bring.wait()
        move.start()
    load.wait()
    places = [(grad_w_up, part) for part in range(4)] + [(grad_w_qkv_t, part) for part in range(3)]
    places += [(grad_w_out_t, 0)] + [(grad_w_qkv_s, part) for part in range(3)] + [(grad_w_out_s, 0)]
    for unit, (target, part) in enumerate(places, start=4):
        wide_scr[unit - 4] = f32(totals_scr[unit])
        pieces.append(
            pltpu.make_async_copy(wide_scr.at[unit - 4], target.at[:, pl.ds(part * D, D)], wide_sem.at[unit - 4])
        )
        pieces[-1].start()
    for unit in range(4):
        spot = UNITS - 4 + unit
        lanes = pl.ds(unit * ROWS, ROWS)
        wide_scr[spot] = f32(totals_scr[unit])
    turned = jnp.concatenate([wide_scr[UNITS - 4 + unit] for unit in range(4)], axis=0).T
    for unit in range(4):
        spot = UNITS - 4 + unit
        wide_scr[spot] = turned[unit * ROWS : (unit + 1) * ROWS]
        pieces.append(
            pltpu.make_async_copy(wide_scr.at[spot], grad_w_down.at[pl.ds(unit * ROWS, ROWS)], wide_sem.at[spot])
        )
        pieces[-1].start()
    for move in moves:
        move.wait()
    for copy in pieces:
        copy.wait()


def finish(destinations, condition, gathered, totals, layer_home, grad_home):
    shapes = [(ROWS, 9 * D), (ROWS, 3 * D), (ROWS, D), (ROWS, 3 * D), (ROWS, D), (ROWS, FF), (D, D)]
    dma = pltpu.SemaphoreType.DMA
    return pl.pallas_call(
        finish_body,
        out_shape=(
            jax.ShapeDtypeStruct(layer_home.shape, layer_home.dtype),
            jax.ShapeDtypeStruct(grad_home.shape, grad_home.dtype),
            *[jax.ShapeDtypeStruct(shape, jnp.float32) for shape in shapes],
            jax.ShapeDtypeStruct((16, D), jnp.float32),
        ),
        in_specs=[SMEM, VMEM, ANY, ANY, ANY, ANY],
        out_specs=(ANY,) * 9 + (VMEM,),
        scratch_shapes=[
            pltpu.VMEM((CLIPS, 16, D), jnp.bfloat16),
            pltpu.VMEM((2, *layer_home.shape), layer_home.dtype),
            pltpu.VMEM((UNITS, ROWS, D), jnp.bfloat16),
            pltpu.VMEM((ROWS, 9 * D), jnp.float32),
            pltpu.VMEM((UNITS, ROWS, D), jnp.float32),
            pltpu.VMEM((CLIPS, ROWS), jnp.float32),
            dma((4,)),
            dma((9,)),
            dma((UNITS,)),
        ],
        compiler_params=pltpu.CompilerParams(vmem_limit_bytes=62 * 1024 * 1024),
        cost_estimate=pl.CostEstimate(flops=10**8, bytes_accessed=30 * 10**6, transcendentals=0),
        name="finish",
    )(destinations, condition, gathered, totals, layer_home, grad_home)


def per_device_fast(
    tokens,
    condition,
    loss_grad,
    cell_counts,
    frame_tasks,
    destinations,
    w_ada,
    b_ada,
    w_qkv_s,
    w_out_s,
    b_out_s,
    w_qkv_t,
    w_out_t,
    b_out_t,
    w_up,
    b_up,
    w_down,
    b_down,
):
    rank = lax.axis_index("seq")
    parts = (b_ada, b_out_s, b_out_t, b_up, b_down)
    biases, start = 0.0, 0
    for part in parts:
        biases = biases + jnp.pad(f32(part), (start, 16 * D - start - part.shape[0]))
        start += part.shape[0]
    biases = biases.reshape(16, D)
    layer_home, grad_home, totals, gathered = block(
        destinations,
        cell_counts,
        frame_tasks,
        tokens,
        loss_grad,
        condition,
        biases,
        w_ada,
        w_qkv_s,
        w_out_s,
        w_qkv_t,
        w_out_t,
        w_up,
        w_down,
    )[:4]
    results = finish(destinations, condition, gathered, totals, layer_home, grad_home)
    layer_out, grad_tokens, grad_w_ada, grad_w_qkv_s, grad_w_out_s, grad_w_qkv_t, grad_w_out_t = results[:7]
    grad_w_up, grad_w_down, sums = results[7:]
    grad_b_ada = lax.dynamic_slice_in_dim(sums[:9].reshape(9 * D), rank * 9 * ROWS, 9 * ROWS)
    grad_b_up = lax.dynamic_index_in_dim(sums[9:13], rank, 0, keepdims=False)
    quarters = lax.dynamic_slice_in_dim(sums, rank * ROWS, ROWS, axis=1)
    return (
        layer_out,
        grad_tokens,
        grad_w_ada,
        grad_b_ada,
        grad_w_qkv_s,
        grad_w_out_s,
        quarters[15],
        grad_w_qkv_t,
        grad_w_out_t,
        quarters[14],
        grad_w_up,
        grad_b_up,
        grad_w_down,
        quarters[13],
    )


def solution(mesh):
    placed = (
        P(None, "seq", "dp", None),
        P(),
        P(None, "seq", "dp", None),
        P(),
        P(),
        P(),
        P(),
        P(),
        P(),
        P(),
        P(),
        P(),
        P(),
        P(),
        P(),
        P(),
        P(),
        P(),
    )
    fast = mesh.shape["dp"] == 8 and mesh.shape["seq"] == 4
    return jax.shard_map(
        per_device_fast if fast else per_device_general,
        mesh=mesh,
        in_specs=placed,
        out_specs=(
            P(None, "seq", "dp", None),
            P(None, "seq", "dp", None),
            P("seq", None),
            P("seq"),
            P("seq", None),
            P("seq", None),
            P("seq"),
            P("seq", None),
            P("seq", None),
            P("seq"),
            P("seq", None),
            P("seq"),
            P("seq", None),
            P("seq"),
        ),
        check_vma=False,
    )
```
